32 devices in a mesh: fsdp: 16 (over z, y, core), dp: 2 (over x).
Axes of the slice: x: 2, y: 2, z: 4, core: 2. Of those that a mesh axis runs over, the one named last changes fastest.
Arguments:
- tokens: bfloat16 [32, 512, 768], P(('fsdp', 'dp')), may hold values from -6 to 6
- cotangent: bfloat16 [32, 512, 768], P(('fsdp', 'dp')), may hold values from -6 to 6
- lengths: int32 [32], P(('fsdp', 'dp')), may hold values from 64 to 512, as said below
- matrices: float32 [48, 384, 384], P(None, 'fsdp')
- first_moment: float32 [48, 384, 384], P(None, 'fsdp')
- second_moment: float32 [48, 384, 384], P(None, 'fsdp'), as said below
- left_stat: float32 [48, 384, 384], P(None, 'fsdp'), as said below
- right_stat: float32 [48, 384, 384], P(None, 'fsdp'), as said below
- left_basis: float32 [48, 384, 384], P(None, 'fsdp'), as said below
- right_basis: float32 [48, 384, 384], P(None, 'fsdp'), as said below
- vectors: float32 [9216], P('fsdp')
- vector_first: float32 [9216], P('fsdp')
- vector_second: float32 [9216], P('fsdp'), as said below
Outputs:
- block_out: bfloat16 [32, 512, 768], P(('fsdp', 'dp'))
- input_grad: float32 [32, 512, 768], P(('fsdp', 'dp'))
- new_matrices: float32 [48, 384, 384], P(None, 'fsdp')
- matrices_low: bfloat16 [48, 384, 384], P(None, 'fsdp')
- new_first: float32 [48, 384, 384], P(None, 'fsdp')
- new_second: float32 [48, 384, 384], P(None, 'fsdp')
- new_left_stat: float32 [48, 384, 384], P(None, 'fsdp')
- new_right_stat: float32 [48, 384, 384], P(None, 'fsdp')
- new_left_basis: float32 [48, 384, 384], P(None, 'fsdp')
- new_right_basis: float32 [48, 384, 384], P(None, 'fsdp')
- vector_first_new: float32 [9216], P('fsdp')
- vector_second_new: float32 [9216], P('fsdp')
- vector_new: float32 [9216], P('fsdp')
The draws below stay inside these ranges and needn't reach their ends.
Inputs may be any that keep to these rules, and one draw needn't show every extreme that they name: `lengths`: positions from a sequence's length to 512 are padding; in every draw some sequence is full. `left_basis`: each block is orthogonal. `right_basis`: each block is orthogonal. `left_stat`: each block is symmetric and diagonally dominant with a positive diagonal. `right_stat`: each block is symmetric and diagonally dominant with a positive diagonal. `second_moment`: Positive. `vector_second`: Positive.
All inputs are finite; a program needn't handle non-finite values.
Results may differ from the reference program's by a relative error of at most 0.014.
The reference program's roundings to bfloat16 on the way count: a program that leaves them out, or rounds other values in their place, can miss the bound.
Values may be sent and summed in bfloat16 or wider, within the bound.
A program may use at most 256 MiB of HBM per device.

```python
import math
import jax
import jax.numpy as jnp
from jax import lax

D = 768
HEADS = 12
HEAD_DIM = 64
FF = 3072
SEQ = 512
ADAM_STEP = 10
BLOCK = 384
BLOCKS = 48
VECTOR = 9216
SEQS = 32
TOKENS = 16384


def block_kinds():
    row_blocks = D // BLOCK
    square = row_blocks * row_blocks
    down_start = 4 * square + row_blocks * (FF // BLOCK)
    index_list = jnp.arange(BLOCKS)
    return jnp.where(index_list < 4 * square, index_list // square, jnp.where(index_list < down_start, 4, 5))


def gradient_sizes():
    table = jnp.array([1.0, 1.0, 1.0, 2.4 / math.sqrt(SEQ), 0.4, 0.55], jnp.float32)
    return jnp.take(table, block_kinds()) * math.sqrt(0.56 * TOKENS)


def vector_sizes():
    unit_ratio = FF // D
    row_index = jnp.arange(8 + unit_ratio)
    row_size = jnp.where(row_index == 0, 1.0, jnp.where(row_index == 1, 1.2, jnp.where(row_index == 2, 1.1, jnp.where(row_index < 5, 1.2, jnp.where(row_index < 5 + unit_ratio, 0.4, jnp.where(row_index == 5 + unit_ratio, 0.9, 1.0))))))
    whole = jnp.broadcast_to(row_size[:, None], (8 + unit_ratio, D)).reshape(VECTOR)
    return whole.astype(jnp.float32) * math.sqrt(0.56 * TOKENS)


def statistic(key):
    level = 0.05 * BLOCK * gradient_sizes() ** 2
    key_one, key_two = jax.random.split(key)
    diagonal = jnp.exp(jax.random.uniform(key_one, (BLOCKS, BLOCK), jnp.float32, 0.0, math.log(4.0)))
    raw = jax.random.uniform(key_two, (BLOCKS, BLOCK, BLOCK), jnp.float32, -1.0, 1.0)
    symmetric = 0.5 * (raw + jnp.swapaxes(raw, 1, 2)) * (0.9 / BLOCK)
    identity = jnp.eye(BLOCK, dtype=jnp.float32)
    return (symmetric * (1.0 - identity) + identity * diagonal[:, :, None]) * level[:, None, None]


def rotation(key):
    key_one, key_two, key_three = jax.random.split(key, 3)

    def shuffle(part_key):
        return jax.random.permutation(part_key, BLOCK)
    orders = jax.vmap(shuffle)(jax.random.split(key_one, BLOCKS)).astype(jnp.int32)
    column = jnp.arange(BLOCK, dtype=jnp.int32)
    phase = (2 * column[None, None, :] + 1) * orders[:, :, None] % (4 * BLOCK)
    angles = math.pi * phase.astype(jnp.float32) / (2.0 * BLOCK)
    row_scale = jnp.where(orders == 0, math.sqrt(1.0 / BLOCK), math.sqrt(2.0 / BLOCK)).astype(jnp.float32)
    sign_rows = (jax.random.randint(key_two, (BLOCKS, BLOCK), 0, 2) * 2 - 1).astype(jnp.float32)
    sign_columns = (jax.random.randint(key_three, (BLOCKS, BLOCK), 0, 2) * 2 - 1).astype(jnp.float32)
    return jnp.cos(angles) * row_scale[:, :, None] * sign_rows[:, :, None] * sign_columns[:, None, :]


def draw_lengths(key, part):
    key = jax.random.fold_in(key, 3)
    key_one, key_two = jax.random.split(key)
    drawn = jax.random.randint(key_one, (SEQS,), SEQ // 8, SEQ + 1)
    chosen = jax.random.randint(key_two, (), 0, SEQS)
    return jnp.where(jnp.arange(SEQS) == chosen, SEQ, drawn).astype(jnp.int32)


def draw_matrices(key, part):
    key = jax.random.fold_in(key, 7)
    table = jnp.array([D ** (-0.5), D ** (-0.5), D ** (-0.5), math.sqrt(SEQ / 4.0) * D ** (-0.5), D ** (-0.5), 1.5 * FF ** (-0.5)], jnp.float32)
    scales = jnp.take(table, block_kinds())[:, None, None]
    noise = jax.random.normal(key, (BLOCKS, BLOCK, BLOCK), jnp.float32)
    return noise * scales


def draw_first_moment(key, part):
    key = jax.random.fold_in(key, 11)
    noise = jax.random.normal(key, (BLOCKS, BLOCK, BLOCK), jnp.float32)
    return noise * (0.11 * gradient_sizes())[:, None, None]


def draw_second_moment(key, part):
    key = jax.random.fold_in(key, 13)
    factor = jnp.exp(jax.random.uniform(key, (BLOCKS, BLOCK, BLOCK), jnp.float32, 0.0, math.log(4.0)))
    return factor * (0.001001 * gradient_sizes() ** 2)[:, None, None]


def draw_left_stat(key, part):
    key = jax.random.fold_in(key, 17)
    return statistic(key)


def draw_right_stat(key, part):
    key = jax.random.fold_in(key, 19)
    return statistic(key)


def draw_left_basis(key, part):
    key = jax.random.fold_in(key, 23)
    return rotation(key)


def draw_right_basis(key, part):
    key = jax.random.fold_in(key, 29)
    return rotation(key)


def draw_vectors(key, part):
    key = jax.random.fold_in(key, 31)
    key_one, key_two = jax.random.split(key)
    unit_ratio = FF // D
    row_index = jnp.arange(8 + unit_ratio)
    is_gain = (row_index == 3) | (row_index == 6 + unit_ratio)
    biases = 0.3 * jax.random.normal(key_one, (8 + unit_ratio, D), jnp.float32)
    gains = 1.0 + 0.25 * jax.random.uniform(key_two, (8 + unit_ratio, D), jnp.float32, -1.0, 1.0)
    return jnp.where(is_gain[:, None], gains, biases).reshape(VECTOR)


def draw_vector_first(key, part):
    key = jax.random.fold_in(key, 37)
    return jax.random.normal(key, (VECTOR,), jnp.float32) * 0.11 * vector_sizes()


def draw_vector_second(key, part):
    key = jax.random.fold_in(key, 41)
    factor = jnp.exp(jax.random.uniform(key, (VECTOR,), jnp.float32, 0.0, math.log(4.0)))
    return factor * 0.001001 * vector_sizes() ** 2


def level_of(key, extent, cuts, smallest, top_value):
    def one(position, shards_of):
        heights = jax.random.uniform(jax.random.fold_in(jax.random.fold_in(key, 6), position), (shards_of,), jnp.float32, smallest / len(cuts), top_value / len(cuts))
        return jnp.repeat(jnp.exp(heights), extent[position] // shards_of).reshape((-1,) + (1,) * (len(extent) - position - 1))

    factor_of = one(*cuts[0])
    for cut in cuts[1:]:
        factor_of = factor_of * one(*cut)
    return factor_of


def bell_draw(key, shape, scale, bound, cuts=(), kind=jnp.bfloat16):
    values = jax.random.normal(key, shape, jnp.float32) * scale
    if len(cuts) > 0:
        values = level_of(key, shape, cuts, -0.22, 0.18) * values
    return jnp.clip(values, min=-bound, max=bound).astype(kind)


def setup_inputs(seed: int = 0) -> dict:
    arg_keys = jax.random.split(jax.random.key(seed), 14)
    tokens = bell_draw(arg_keys[0], (SEQS, SEQ, D), 1.0, 6.0, ((0, 32),))
    cotangent = bell_draw(arg_keys[1], (SEQS, SEQ, D), 1.0, 6.0, ((0, 32),))
    lengths = draw_lengths(jax.random.fold_in(arg_keys[13], 71), 0)
    matrices = draw_matrices(jax.random.fold_in(arg_keys[13], 71), 0)
    first_moment = draw_first_moment(jax.random.fold_in(arg_keys[13], 71), 0)
    second_moment = draw_second_moment(jax.random.fold_in(arg_keys[13], 71), 0)
    left_stat = draw_left_stat(jax.random.fold_in(arg_keys[13], 71), 0)
    right_stat = draw_right_stat(jax.random.fold_in(arg_keys[13], 71), 0)
    left_basis = draw_left_basis(jax.random.fold_in(arg_keys[13], 71), 0)
    right_basis = draw_right_basis(jax.random.fold_in(arg_keys[13], 71), 0)
    vectors = draw_vectors(jax.random.fold_in(arg_keys[13], 71), 0)
    vector_first = draw_vector_first(jax.random.fold_in(arg_keys[13], 71), 0)
    vector_second = draw_vector_second(jax.random.fold_in(arg_keys[13], 71), 0)
    return {"tokens": tokens, "cotangent": cotangent, "lengths": lengths, "matrices": matrices, "first_moment": first_moment, "second_moment": second_moment, "left_stat": left_stat, "right_stat": right_stat, "left_basis": left_basis, "right_basis": right_basis, "vectors": vectors, "vector_first": vector_first, "vector_second": vector_second}


PRECISE = lax.Precision.HIGHEST
FIRST_DECAY = 0.9
SECOND_DECAY = 0.999
STAT_DECAY = 0.95
ADAM_EPSILON = 1e-08
NORM_EPSILON = 1e-05
MATRIX_RATE = 0.03
VECTOR_RATE = 0.2
WEIGHT_DECAY = 0.01

@jax.custom_vjp
def low(v):
    return lax.optimization_barrier(v.astype(jnp.bfloat16)).astype(jnp.float32)

@jax.custom_vjp
def low_back(v):
    return v

def low_keep(v):
    return (low(v), None)

def low_pass(kept, grad):
    return (grad,)

def back_keep(v):
    return (v, None)

def back_low(kept, grad):
    return (low(grad),)
low.defvjp(low_keep, low_pass)
low_back.defvjp(back_keep, back_low)

def assemble(blocks, row_count, column_count):
    block_side = blocks.shape[-1]
    shaped = blocks.reshape(row_count, column_count, block_side, block_side)
    return shaped.transpose(0, 2, 1, 3).reshape(row_count * block_side, column_count * block_side)

def layer_norm(values, gain_row, shift_row):
    center = lax.optimization_barrier(jnp.mean(values, axis=-1, keepdims=True))
    centered = values - center
    spread = lax.optimization_barrier(jnp.mean(centered * centered, axis=-1, keepdims=True))
    return centered * lax.rsqrt(spread + NORM_EPSILON) * gain_row + shift_row

def product(left_side, right_side):
    return jnp.matmul(left_side, right_side, precision=PRECISE)

def group_forward(weights, inputs, lengths):
    weight_qkv, weight_out, weight_up, weight_down, vector_rows = weights
    group_size, slots, model_width = inputs.shape
    unit_ratio = FF // model_width
    joined = product(inputs, weight_qkv)
    query_rows = low(low_back(joined[..., :model_width] + vector_rows[0]))
    key_rows = low(low_back(joined[..., model_width:2 * model_width]))
    value_rows = low(low_back(joined[..., 2 * model_width:] + vector_rows[1]))
    heads_query = query_rows.reshape(group_size, slots, HEADS, HEAD_DIM)
    heads_key = key_rows.reshape(group_size, slots, HEADS, HEAD_DIM)
    heads_value = value_rows.reshape(group_size, slots, HEADS, HEAD_DIM)
    scores = low_back(jnp.einsum('gqhd,gkhd->ghqk', heads_query, heads_key, precision=PRECISE) * HEAD_DIM ** (-0.5))
    visible = lax.iota(jnp.int32, slots)[None, :] < lengths[:, None]
    scores = jnp.where(visible[:, None, None, :], scores, -1e+30)
    row_max = lax.optimization_barrier(jnp.max(scores, axis=-1, keepdims=True))
    shifted = jnp.exp(scores - row_max)
    attention_weights = shifted / lax.optimization_barrier(jnp.sum(shifted, axis=-1, keepdims=True))
    context = jnp.einsum('ghqk,gkhd->gqhd', low(attention_weights), heads_value, precision=PRECISE)
    context = low(low_back(context.reshape(group_size, slots, model_width)))
    attended = low_back(product(context, weight_out)) + vector_rows[2]
    normed = layer_norm(inputs + attended, vector_rows[3], vector_rows[4])
    hidden = low_back(product(low(normed), weight_up)) + vector_rows[5:5 + unit_ratio].reshape(FF)
    active = jax.nn.gelu(hidden, approximate=False)
    result = low_back(product(low(active), weight_down)) + vector_rows[5 + unit_ratio]
    return layer_norm(normed + result, vector_rows[6 + unit_ratio], vector_rows[7 + unit_ratio])

def forward_all(inputs, matrices, vectors, lengths):
    model_width = inputs.shape[-1]
    block_side = matrices.shape[-1]
    row_blocks = model_width // block_side
    column_blocks = FF // block_side
    square = row_blocks * row_blocks
    down_start = 4 * square + row_blocks * column_blocks
    rounded = low(matrices)
    parts = [assemble(rounded[block_index * square:(block_index + 1) * square], row_blocks, row_blocks) for block_index in range(4)]
    weights = (jnp.concatenate(parts[:3], axis=1), parts[3], assemble(rounded[4 * square:down_start], row_blocks, column_blocks), assemble(rounded[down_start:], column_blocks, row_blocks), low(vectors).reshape(-1, model_width))
    group_size = math.gcd(inputs.shape[0], max(1, 4096 // inputs.shape[1]))
    group_count = inputs.shape[0] // group_size
    checked = jax.checkpoint(group_forward)

    def advance(carry, pieces):
        return (carry, checked(weights, pieces[0], pieces[1]))
    finished, outputs = lax.scan(advance, None, (inputs.reshape(group_count, group_size, inputs.shape[1], model_width), lengths.reshape(group_count, group_size)))
    return outputs.reshape(inputs.shape)

def orthonormal(matrix):
    gram_matrix = jnp.einsum('kai,kaj->kij', matrix, matrix, precision=PRECISE)
    lower_factor = jnp.linalg.cholesky(gram_matrix)

    def solve_one(factor, target):
        return jax.scipy.linalg.solve_triangular(factor, target, lower=True)
    solved = jax.vmap(solve_one)(lower_factor, jnp.swapaxes(matrix, 1, 2))
    return jnp.swapaxes(solved, 1, 2)

def soap_update(gradient, first_moment, second_moment, left_stat, right_stat, left_basis, right_basis):
    rotated = jnp.einsum('kai,kab->kib', left_basis, gradient, precision=PRECISE)
    rotated = jnp.einsum('kib,kbj->kij', rotated, right_basis, precision=PRECISE)
    first_new = FIRST_DECAY * first_moment + (1.0 - FIRST_DECAY) * rotated
    second_new = SECOND_DECAY * second_moment + (1.0 - SECOND_DECAY) * rotated * rotated
    direction = first_new / (1.0 - FIRST_DECAY ** ADAM_STEP) / (jnp.sqrt(second_new / (1.0 - SECOND_DECAY ** ADAM_STEP)) + ADAM_EPSILON)
    turned = jnp.einsum('kia,kab->kib', left_basis, direction, precision=PRECISE)
    update = jnp.einsum('kib,kjb->kij', turned, right_basis, precision=PRECISE)
    left_new = STAT_DECAY * left_stat + (1.0 - STAT_DECAY) * jnp.einsum('kia,kja->kij', gradient, gradient, precision=PRECISE)
    right_new = STAT_DECAY * right_stat + (1.0 - STAT_DECAY) * jnp.einsum('kai,kaj->kij', gradient, gradient, precision=PRECISE)
    left_turn = orthonormal(jnp.einsum('kia,kaj->kij', left_new, left_basis, precision=PRECISE))
    right_turn = orthonormal(jnp.einsum('kia,kaj->kij', right_new, right_basis, precision=PRECISE))
    return (update, first_new, second_new, left_new, right_new, left_turn, right_turn)

def reference(tokens, cotangent, lengths, matrices, first_moment, second_moment, left_stat, right_stat, left_basis, right_basis, vectors, vector_first, vector_second):
    inputs = tokens.astype(jnp.float32)

    def forward(values, blocks, biases):
        return forward_all(values, blocks, biases, lengths)
    outputs, pull = jax.vjp(forward, inputs, matrices, vectors)
    slots = tokens.shape[1]
    visible = (lax.iota(jnp.int32, slots)[None, :] < lengths[:, None]).astype(jnp.float32)
    grad_input, grad_matrices, grad_vectors = pull(cotangent.astype(jnp.float32) * visible[:, :, None])
    update, first_new, second_new, left_new, right_new, left_turn, right_turn = soap_update(grad_matrices, first_moment, second_moment, left_stat, right_stat, left_basis, right_basis)
    new_matrices = matrices - MATRIX_RATE * (update + WEIGHT_DECAY * matrices)
    vfirst_new = FIRST_DECAY * vector_first + (1.0 - FIRST_DECAY) * grad_vectors
    vsecond_new = SECOND_DECAY * vector_second + (1.0 - SECOND_DECAY) * grad_vectors * grad_vectors
    vector_new = vectors - VECTOR_RATE * (vfirst_new / (1.0 - FIRST_DECAY ** ADAM_STEP)) / (jnp.sqrt(vsecond_new / (1.0 - SECOND_DECAY ** ADAM_STEP)) + ADAM_EPSILON)
    return (outputs.astype(jnp.bfloat16), grad_input, new_matrices, new_matrices.astype(jnp.bfloat16), first_new, second_new, left_new, right_new, left_turn, right_turn, vfirst_new, vsecond_new, vector_new)
```

```python
import functools

import jax
import jax.numpy as jnp
from jax import lax
from jax.experimental import pallas as pl
from jax.experimental.pallas import tpu as pltpu
from jax.sharding import PartitionSpec as P

F32 = jnp.float32
BF16 = jnp.bfloat16
MESH = pl.DeviceIdType.MESH

HEADS = 12
HEAD_DIM = 64
FF = 3072
ADAM_STEP = 10


FIRST_DECAY = 0.9
SECOND_DECAY = 0.999
STAT_DECAY = 0.95
ADAM_EPSILON = 1e-08
NORM_EPSILON = 1e-05
MATRIX_RATE = 0.03
VECTOR_RATE = 0.2
WEIGHT_DECAY = 0.01


def assemble(blocks, row_count, column_count):
    block_side = blocks.shape[-1]
    shaped = blocks.reshape(row_count, column_count, block_side, block_side)
    return shaped.transpose(0, 2, 1, 3).reshape(row_count * block_side, column_count * block_side)


def split_blocks(matrix, row_count, column_count, block_side):
    shaped = matrix.reshape(row_count, block_side, column_count, block_side)
    return shaped.transpose(0, 2, 1, 3).reshape(row_count * column_count, block_side, block_side)


def layer_norm(values, gain_row, shift_row):
    center = jnp.mean(values, axis=-1, keepdims=True)
    centered = values - center
    spread = jnp.mean(centered * centered, axis=-1, keepdims=True)
    return centered * lax.rsqrt(spread + NORM_EPSILON) * gain_row + shift_row


def exact_gelu(hidden):
    return jax.nn.gelu(hidden, approximate=False)


def masked_scores(heads_query, heads_key, length):
    slots = heads_query.shape[0]
    scores = jnp.einsum(
        "qhd,khd->hqk", heads_query, heads_key, preferred_element_type=jnp.float32
    ) * HEAD_DIM ** (-0.5)
    visible = lax.iota(jnp.int32, slots) < length
    return jnp.where(visible[None, None, :], scores, -1e30)


def attend(pieces):
    query_rows, key_rows, value_rows, length = pieces
    slots = query_rows.shape[0]
    heads_query = query_rows.reshape(slots, HEADS, HEAD_DIM)
    heads_key = key_rows.reshape(slots, HEADS, HEAD_DIM)
    heads_value = value_rows.reshape(slots, HEADS, HEAD_DIM)
    scores = masked_scores(heads_query, heads_key, length)
    row_max = jnp.max(scores, axis=-1, keepdims=True)
    shifted = jnp.exp(scores - row_max)
    row_total = jnp.sum(shifted, axis=-1, keepdims=True)
    attention_weights = (shifted / row_total).astype(jnp.bfloat16)
    context = jnp.einsum(
        "hqk,khd->qhd", attention_weights, heads_value, preferred_element_type=jnp.float32
    )
    return (
        context.reshape(slots, -1).astype(jnp.bfloat16),
        row_max[..., 0] + jnp.log(row_total[..., 0]),
    )


def attend_back(pieces):
    query_rows, key_rows, value_rows, logsum, grad_context, length = pieces
    slots = query_rows.shape[0]
    heads_query = query_rows.reshape(slots, HEADS, HEAD_DIM)
    heads_key = key_rows.reshape(slots, HEADS, HEAD_DIM)
    heads_value = value_rows.reshape(slots, HEADS, HEAD_DIM)
    heads_grad = grad_context.reshape(slots, HEADS, HEAD_DIM)
    scores = masked_scores(heads_query, heads_key, length)
    attention_weights = jnp.exp(scores - logsum[..., None])
    weights_low = attention_weights.astype(jnp.bfloat16)
    grad_values = jnp.einsum(
        "hqk,qhd->khd", weights_low, heads_grad, preferred_element_type=jnp.float32
    )
    grad_weights = jnp.einsum(
        "qhd,khd->hqk", heads_grad, heads_value, preferred_element_type=jnp.float32
    )
    grad_scores = attention_weights * (
        grad_weights - jnp.sum(grad_weights * attention_weights, axis=-1, keepdims=True)
    )
    scores_low = grad_scores.astype(jnp.bfloat16)
    grad_query = jnp.einsum(
        "hqk,khd->qhd", scores_low, heads_key, preferred_element_type=jnp.float32
    ) * HEAD_DIM ** (-0.5)
    grad_keys = jnp.einsum(
        "hqk,qhd->khd", scores_low, heads_query, preferred_element_type=jnp.float32
    ) * HEAD_DIM ** (-0.5)
    return (
        grad_query.reshape(slots, -1).astype(jnp.bfloat16),
        grad_keys.reshape(slots, -1).astype(jnp.bfloat16),
        grad_values.reshape(slots, -1).astype(jnp.bfloat16),
    )


def dg(a,b,ca,cb):
    return lax.dot_general(a,b,(((ca,),(cb,)),((),())),preferred_element_type=F32)

def halves(a):
    hi=a.astype(BF16)
    return hi,(a-hi.astype(F32)).astype(BF16)

def mm3(a,b,ca,cb):
    ah,al=halves(a); bh,bl=halves(b)
    return dg(ah,bh,ca,cb)+(dg(ah,bl,ca,cb)+dg(al,bh,ca,cb))

def thirds(u):
    h=u.astype(BF16).astype(F32); r=u-h
    m=r.astype(BF16).astype(F32)
    return h,m,r-m

def factor_panels(aug, slots, side=128):
    sub=lax.broadcasted_iota(jnp.int32,(8,side),0)
    def spread(v): return jnp.broadcast_to(v,(8,side))
    for p in range(side//8):
        k=8*p
        panels=[]
        for s in range(slots):
            pw=aug[s,k:k+8,:side]; pv=aug[s,k:k+8,side:]
            cols=[spread(pw[:,k+i:k+i+1]) for i in range(8)]
            S=[[spread(cols[i][j:j+1,:]) if j>=i else None for i in range(8)] for j in range(8)]
            rw=[spread(pw[i:i+1,:]) for i in range(8)]
            rv=[spread(pv[i:i+1,:]) for i in range(8)]
            panels.append((S,rw,rv))
        for i in range(8):
            for S,rw,rv in panels:
                r=lax.rsqrt(S[i][i])
                for j in range(i+1,8): S[j][i]=S[j][i]*r
                for m in range(i+1,8):
                    for j in range(m,8):
                        S[j][m]=S[j][m]-S[j][i]*S[m][i]
                rw[i]=rw[i]*r; rv[i]=rv[i]*r
                for j in range(i+1,8):
                    rw[j]=rw[j]-S[j][i]*rw[i]
                    rv[j]=rv[j]-S[j][i]*rv[i]
        for s,(S,rw,rv) in enumerate(panels):
            uw,uv=rw[0],rv[0]
            for i in range(1,8):
                uw=jnp.where(sub==i,rw[i],uw); uv=jnp.where(sub==i,rv[i],uv)
            aug[s,k:k+8,side:]=uv
            if k+8<side:
                h,m,l=thirds(uw); vh,vm,vl=thirds(uv)
                a=jnp.concatenate([h,h,m,m,h,l],0).astype(BF16)
                b=jnp.concatenate([jnp.concatenate([h,m,h,m,l,h],0),jnp.concatenate([vh,vm,vh,vm,vl,vh],0)],1).astype(BF16)
                t=dg(a,b,0,0)
                aug[s,k+8:,:]=aug[s,k+8:,:]-t[k+8:,:]

def orthonormal_cols(mat, aug, slots, side=128):
    n=mat.shape[-1]
    r=lax.broadcasted_iota(jnp.int32,(side,side),0); c=lax.broadcasted_iota(jnp.int32,(side,side),1)
    eye=(r==c).astype(F32)
    steps=n//side
    for o in range(steps):
        lo=o*side
        for s in range(slots):
            mo=mat[s,:,lo:lo+side]
            aug[s,:,:side]=mm3(mo,mo,0,0)
            aug[s,:,side:]=eye
        factor_panels(aug,slots,side)
        for s in range(slots):
            q=mm3(mat[s,:,lo:lo+side],aug[s,:,side:],1,1)
            mat[s,:,lo:lo+side]=q
            if o+1<steps:
                rest=mat[s,:,lo+side:]
                mat[s,:,lo+side:]=rest-mm3(q,mm3(q,rest,0,0),1,0)


def soap_kernel(grad, stat, own, other, first, second, outer_out, basis_out, turned_out, update_out, mat, aug):
    slots = grad.shape[0]
    right_side = lax.rem(lax.axis_index("dp"), 2) == 1

    def run(is_right):
        near, far = (0, 1) if is_right else (1, 0)

        def one(s, carry):
            g = grad[s].astype(BF16)
            outer = dg(g, g, near, near)
            outer_out[s] = outer.astype(BF16)
            mixed = STAT_DECAY * stat[s].astype(F32) + (1.0 - STAT_DECAY) * outer
            high, rest = halves(mixed)
            mat[s] = dg(high, own[s], 1, 0) + dg(rest, own[s], 1, 0)
            left, right = (other[s], own[s]) if is_right else (own[s], other[s])
            rotated = dg(dg(left, g, 0, 0).astype(BF16), right, 1, 0)
            turned_out[s] = rotated.astype(BF16)
            first_new = FIRST_DECAY * first[s].astype(F32) + (1.0 - FIRST_DECAY) * rotated
            second_new = SECOND_DECAY * second[s].astype(F32) + (1.0 - SECOND_DECAY) * rotated * rotated
            direction = (
                first_new
                / (1.0 - FIRST_DECAY**ADAM_STEP)
                / (jnp.sqrt(second_new / (1.0 - SECOND_DECAY**ADAM_STEP)) + ADAM_EPSILON)
            )
            back = dg(left, direction.astype(BF16), 1, 0).astype(BF16)
            update_out[s] = dg(back, right, 1, 1).astype(BF16)
            return carry

        lax.fori_loop(0, slots, one, 0)

    @pl.when(right_side)
    def _():
        run(True)

    @pl.when(jnp.logical_not(right_side))
    def _():
        run(False)

    orthonormal_cols(mat, aug, slots)
    basis_out[...] = mat[...].astype(BF16)


def soap_blocks(grad, stat, own, other, first, second):
    slots, side, _ = grad.shape
    shape = jax.ShapeDtypeStruct(grad.shape, BF16)
    whole = pl.BlockSpec(memory_space=pltpu.VMEM)
    return pl.pallas_call(
        soap_kernel,
        out_shape=[shape] * 4,
        in_specs=[whole] * 6,
        out_specs=[whole] * 4,
        scratch_shapes=[
            pltpu.VMEM((slots, side, side), F32),
            pltpu.VMEM((slots, 128, 256), F32),
        ],
        compiler_params=pltpu.CompilerParams(vmem_limit_bytes=48 * 2**20),
        name="soap_blocks",
    )(grad, stat, own, other, first, second)


def ring_place(chip, chips):
    along, across = chip // 2, lax.rem(chip, 2)
    return along * (1 - across) + (chips - 1 - along) * across


def ring_chip(place, chips):
    place = lax.rem(place + 8 * chips, chips)
    across = place // (chips // 2)
    along = place * (1 - across) + (chips - 1 - place) * across
    return 2 * along + across


def whereabouts(chips):
    device, replica = lax.axis_index("fsdp"), lax.axis_index("dp")
    chip, core = device // 2, lax.rem(device, 2)
    place = ring_place(chip, chips)
    turn = 1 - 2 * core
    after = (2 * ring_chip(place + turn, chips) + core, replica)
    before = (2 * ring_chip(place - turn, chips) + core, replica)
    sibling = (2 * chip + 1 - core, replica)
    return device, replica, chip, core, place, turn, after, before, sibling


def greet(neighbours):
    barrier = pltpu.get_barrier_semaphore()
    for neighbour in neighbours:
        pl.semaphore_signal(barrier, inc=1, device_id=neighbour, device_id_type=MESH)
    pl.semaphore_wait(barrier, len(neighbours))


def gather_kernel(chips, share, mat_ref, vec_ref, attn, up, down, vecs, raw_a, raw_u, raw_d, low_a, low_u, low_d,
                  low_v, trade_send, trade_recv, own_sem, ring_send, ring_recv, sib_send, sib_recv):
    device, replica, chip, core, place, turn, after, before, sibling = whereabouts(chips)
    side = mat_ref.shape[-1]
    wide = attn.shape[-1] // 2
    slim = down.shape[-1] // 2
    both = 2 * share
    rows = pl.ds(pl.multiple_of(share * core, 8), share)
    for b in range(16):
        raw_a[(b % 4) // 2, rows, (b // 4) * 2 * side + (b % 2) * side : (b // 4) * 2 * side + (b % 2 + 1) * side] = mat_ref[b]
        raw_u[b // 8, rows, (b % 8) * side : (b % 8 + 1) * side] = mat_ref[16 + b]
        raw_d[b // 2, rows, (b % 2) * side : (b % 2 + 1) * side] = mat_ref[32 + b]
    low_v[...] = vec_ref[...].astype(BF16).astype(F32)
    greet((after, before, sibling))
    groups = ((raw_a, low_a, attn, wide), (raw_u, low_u, up, wide), (raw_d, low_d, down, slim))

    def half(which, width):
        return pl.ds(pl.multiple_of(which * width, 128), width)

    trades = []
    for g, (raw, low, out, width) in enumerate(groups):
        part = raw.at[:, rows, half(1 - core, width)]
        trade = pltpu.make_async_remote_copy(
            src_ref=part, dst_ref=part, send_sem=trade_send.at[g], recv_sem=trade_recv.at[g],
            device_id=sibling, device_id_type=MESH)
        trade.start()
        trades.append(trade)

    def slab(g, origin):
        raw, low, out, width = groups[g]
        return out.at[:, pl.ds(pl.multiple_of(origin * both, 16), both), half(core, width)]

    def vec_of(origin):
        return vecs.at[2 * origin + core]

    def piece(g, origin):
        return vec_of(origin) if g == 3 else slab(g, origin)

    def forward(g, t, origin, source):
        return pltpu.make_async_remote_copy(
            src_ref=source, dst_ref=piece(g, origin), send_sem=ring_send.at[t, g], recv_sem=ring_recv.at[t, g],
            device_id=after, device_id_type=MESH)

    def pass_on(g, t, origin, source):
        return pltpu.make_async_remote_copy(
            src_ref=source, dst_ref=piece(g, origin), send_sem=sib_send.at[t, g], recv_sem=sib_recv.at[t, g],
            device_id=sibling, device_id_type=MESH)

    sources = [low_a, low_u, low_d, low_v]
    owns = []
    for g in (3, 0, 1, 2):
        if g < 3:
            raw, low, out, width = groups[g]
            trades[g].wait()
            low[...] = raw[:, :, half(core, width)].astype(BF16)
        forward(g, 0, chip, sources[g]).start()
        pass_on(g, 0, chip, sources[g]).start()
        own = pltpu.make_async_copy(sources[g], piece(g, chip), own_sem.at[g])
        own.start()
        owns.append(own)

    def step(t, carry):
        origin = ring_chip(place - turn * t, chips)
        for g in (3, 0, 1, 2):
            arrived = piece(g, origin)
            forward(g, t - 1, origin, arrived).wait_recv()

            @pl.when(t < chips - 1)
            def _():
                forward(g, t, origin, arrived).start()

            pass_on(g, t, origin, arrived).start()
        return carry

    lax.fori_loop(1, chips, step, 0)
    for own in owns:
        own.wait()

    def finish(t, carry):
        for g in range(4):
            @pl.when(t < chips - 1)
            def _():
                forward(g, t, chip, piece(g, chip)).wait_send()

            pass_on(g, t, chip, piece(g, chip)).wait()
        return carry

    lax.fori_loop(0, chips, finish, 0)


def gather_weights(matrices, vector_tile, chips):
    total, share, side = matrices.shape
    both = 2 * share
    anywhere = pl.BlockSpec(memory_space=pl.ANY)
    whole = pl.BlockSpec(memory_space=pltpu.VMEM)
    dma = pltpu.SemaphoreType.DMA
    return pl.pallas_call(
        functools.partial(gather_kernel, chips, share),
        out_shape=[
            jax.ShapeDtypeStruct((2, side, 8 * side), BF16),
            jax.ShapeDtypeStruct((2, side, 8 * side), BF16),
            jax.ShapeDtypeStruct((8, side, 2 * side), BF16),
            jax.ShapeDtypeStruct((2 * chips, 8, 128), F32),
        ],
        in_specs=[whole, whole],
        out_specs=[anywhere] * 4,
        scratch_shapes=[
            pltpu.VMEM((2, both, 8 * side), F32),
            pltpu.VMEM((2, both, 8 * side), F32),
            pltpu.VMEM((8, both, 2 * side), F32),
            pltpu.VMEM((2, both, 4 * side), BF16),
            pltpu.VMEM((2, both, 4 * side), BF16),
            pltpu.VMEM((8, both, side), BF16),
            pltpu.VMEM((8, 128), F32),
            dma((3,)), dma((3,)), dma((4,)),
            dma((chips - 1, 4)), dma((chips - 1, 4)), dma((chips, 4)), dma((chips, 4)),
        ],
        compiler_params=pltpu.CompilerParams(collective_id=1, has_side_effects=True, vmem_limit_bytes=40 * 2**20),
        name="gather_weights",
    )(matrices, vector_tile)


def reduce_kernel(chips, g_qkv, g_out, g_up, g_down, g_vec, owned, vec_sum, mine, theirs, ring, peer, vmine, vring, vpeer,
                  mine_sem, sib_send, sib_recv, ring_send, ring_recv, peer_send, peer_recv):
    device, replica, chip, core, place, turn, after, before, sibling = whereabouts(chips)
    other = (device, 1 - replica)
    side = mine.shape[-1]
    greet((after, before, sibling, other))

    def column(index):
        return pl.ds(pl.multiple_of(index * side, 128), side)

    def fetch(owner, start):
        which = owner // 4
        i, j = lax.rem(owner, 4) // 2, lax.rem(owner, 2)

        @pl.when(which < 3)
        def _():
            start(0, g_qkv.at[i, :, column(2 * which + j)])

        @pl.when(which == 3)
        def _():
            start(0, g_out.at[i, :, column(j)])

        start(1, g_up.at[owner // 8, :, column(lax.rem(owner, 8))])
        start(2, g_down.at[owner // 2, :, column(lax.rem(owner, 2))])
        start(3, g_vec.at[owner])

    def local(t, slot, source):
        target = vmine.at[0, t] if slot == 3 else mine.at[t, slot]
        return pltpu.make_async_copy(source, target, mine_sem.at[t, slot])

    def to_sibling(t, slot, source):
        target = vmine.at[1, t] if slot == 3 else theirs.at[t, slot]
        return pltpu.make_async_remote_copy(
            src_ref=source, dst_ref=target, send_sem=sib_send.at[t, slot], recv_sem=sib_recv.at[t, slot],
            device_id=sibling, device_id_type=MESH)

    def to_next(t, slot):
        source, target = (vmine.at[0, t], vring.at[t]) if slot == 3 else (mine.at[t, slot], ring.at[t, slot])
        return pltpu.make_async_remote_copy(
            src_ref=source, dst_ref=target, send_sem=ring_send.at[t, slot], recv_sem=ring_recv.at[t, slot],
            device_id=after, device_id_type=MESH)

    def to_other(slot):
        source, target = (vmine.at[0, chips - 1], vpeer) if slot == 3 else (mine.at[chips - 1, slot], peer.at[slot])
        return pltpu.make_async_remote_copy(
            src_ref=source, dst_ref=target, send_sem=peer_send.at[slot], recv_sem=peer_recv.at[slot],
            device_id=other, device_id_type=MESH)

    def begin(t, carry):
        fetch(2 * ring_chip(place + turn * (t + 1), chips) + 1 - core, lambda slot, source: to_sibling(t, slot, source).start())
        fetch(2 * ring_chip(place - turn * (t + 1), chips) + core, lambda slot, source: local(t, slot, source).start())
        return carry

    lax.fori_loop(0, chips, begin, 0)

    def sources(slot):
        return g_vec.at[0] if slot == 3 else g_up.at[0, :, :side]

    def ready(t, slot):
        local(t, slot, sources(slot)).wait()
        to_sibling(t, slot, sources(slot)).wait_recv()

    for slot in (3, 0, 1, 2):
        ready(0, slot)
        if slot == 3:
            vmine[0, 0] = vmine[0, 0] + vmine[1, 0]
        else:
            mine[0, slot] = (mine[0, slot].astype(F32) + theirs[0, slot].astype(F32)).astype(BF16)
        to_next(0, slot).start()

    def step(t, carry):
        for slot in (3, 0, 1, 2):
            ready(t, slot)
            to_next(t - 1, slot).wait_recv()
            if slot == 3:
                vmine[0, t] = vmine[0, t] + vmine[1, t] + vring[t - 1]
            else:
                total = mine[t, slot].astype(F32) + theirs[t, slot].astype(F32) + ring[t - 1, slot].astype(F32)
                mine[t, slot] = total.astype(BF16)

            @pl.when(t < chips - 1)
            def _():
                to_next(t, slot).start()

            @pl.when(t == chips - 1)
            def _():
                to_other(slot).start()
        return carry

    lax.fori_loop(1, chips, step, 0)
    for slot in (3, 0, 1, 2):
        to_other(slot).wait()
        if slot == 3:
            vec_sum[...] = vmine[0, chips - 1] + vpeer[...]
        else:
            owned[slot] = (mine[chips - 1, slot].astype(F32) + peer[slot].astype(F32)).astype(BF16)

    def finish(t, carry):
        for slot in range(4):
            to_sibling(t, slot, sources(slot)).wait_send()

            @pl.when(t < chips - 1)
            def _():
                to_next(t, slot).wait_send()
        return carry

    lax.fori_loop(0, chips, finish, 0)


def reduce_gradients(g_qkv, g_out, g_up, g_down, g_vec, chips):
    side = g_up.shape[1]
    anywhere = pl.BlockSpec(memory_space=pl.ANY)
    whole = pl.BlockSpec(memory_space=pltpu.VMEM)
    dma = pltpu.SemaphoreType.DMA
    return pl.pallas_call(
        functools.partial(reduce_kernel, chips),
        out_shape=[jax.ShapeDtypeStruct((3, side, side), BF16), jax.ShapeDtypeStruct((8, 128), F32)],
        in_specs=[anywhere] * 5,
        out_specs=[whole] * 2,
        scratch_shapes=[
            pltpu.VMEM((chips, 3, side, side), BF16),
            pltpu.VMEM((chips, 3, side, side), BF16),
            pltpu.VMEM((chips - 1, 3, side, side), BF16),
            pltpu.VMEM((3, side, side), BF16),
            pltpu.VMEM((2, chips, 8, 128), F32),
            pltpu.VMEM((chips - 1, 8, 128), F32),
            pltpu.VMEM((8, 128), F32),
            dma((chips, 4)), dma((chips, 4)), dma((chips, 4)),
            dma((chips - 1, 4)), dma((chips - 1, 4)), dma((4,)), dma((4,)),
        ],
        compiler_params=pltpu.CompilerParams(collective_id=2, has_side_effects=True, vmem_limit_bytes=48 * 2**20),
        name="reduce_gradients",
    )(g_qkv, g_out, g_up, g_down, g_vec)


def plain_gather(matrices, vectors):
    side = matrices.shape[-1]
    blocks = lax.all_gather(matrices.astype(BF16), "fsdp", axis=1, tiled=True)
    attn = jnp.concatenate([assemble(blocks[4 * part : 4 * part + 4], 2, 2) for part in range(4)], axis=1)
    up = assemble(blocks[16:32], 2, 8)
    down = assemble(blocks[32:], 8, 2)
    rows = lax.all_gather(vectors.astype(BF16), "fsdp", axis=0, tiled=True)
    return attn, up, down, rows.astype(F32).reshape(-1, 2 * side)


def plain_reduce(grad_qkv, grad_out, grad_up, grad_down, vector_grad, capacity):
    shard_count = lax.axis_size("fsdp")
    width = grad_up.shape[0]
    side = width // 2
    blocks = jnp.concatenate(
        [split_blocks(grad_qkv[:, part * width : (part + 1) * width], 2, 2, side) for part in range(3)]
        + [split_blocks(grad_out, 2, 2, side), split_blocks(grad_up, 2, 8, side), split_blocks(grad_down, 8, 2, side)],
        axis=0,
    )
    owned = lax.psum_scatter(
        to_owners(blocks, capacity, shard_count), "fsdp", scatter_dimension=1, tiled=True
    )
    owned = lax.psum(owned, "dp")[:, 0]
    share = lax.psum_scatter(vector_grad, "fsdp", scatter_dimension=0, tiled=True)
    return owned, lax.psum(share, "dp")


def to_owners(blocks, capacity, shard_count):
    spare = capacity * shard_count - blocks.shape[0]
    blocks = jnp.pad(blocks, ((0, spare),) + ((0, 0),) * (blocks.ndim - 1))
    return blocks.reshape((capacity, shard_count) + blocks.shape[1:])


def shards(
    tokens,
    cotangent,
    lengths,
    matrices,
    first_moment,
    second_moment,
    left_stat,
    right_stat,
    left_basis,
    right_basis,
    vectors,
    vector_first,
    vector_second,
):
    shard_count = lax.axis_size("fsdp")
    replicas = lax.axis_size("dp")
    sequences, slots, model_width = tokens.shape
    block_total, share_rows, block_side = matrices.shape
    unit_ratio = FF // model_width
    rows_total = sequences * slots
    capacity = -(-block_total // shard_count)
    ringed = replicas == 2 and capacity * shard_count == block_total == 48 and share_rows % 8 == 0 and capacity == 3
    vector_share = vectors.shape[0]

    def shaped(array):
        return array.reshape(sequences, slots, array.shape[-1])

    right_side = lax.axis_index("dp") % 2 == 1
    chosen = [
        jnp.where(right_side, right_stat, left_stat),
        jnp.where(right_side, right_basis, left_basis),
        jnp.where(right_side, left_basis, right_basis),
        first_moment,
        second_moment,
    ]
    states = jnp.stack([to_owners(part.astype(BF16), capacity, shard_count) for part in chosen])
    states = lax.all_to_all(states, "fsdp", split_axis=2, concat_axis=3, tiled=True)[:, :, 0]

    if ringed:
        vector_tile = jnp.pad(vectors, (0, 1024 - vector_share)).reshape(8, 128)
        attn, up, down, vector_tiles = gather_weights(matrices, vector_tile, shard_count // 2)
        attn = attn.reshape(model_width, 4 * model_width)
        up = up.reshape(model_width, FF)
        down = down.reshape(FF, model_width)
        vector_rows = vector_tiles.reshape(shard_count, 1024)[:, :vector_share].reshape(-1, model_width)
    else:
        attn, up, down, vector_rows = plain_gather(matrices, vectors)
    weight_qkv, weight_out = attn[:, : 3 * model_width], attn[:, 3 * model_width :]
    inputs = tokens.reshape(rows_total, model_width)
    joined = jnp.dot(inputs, weight_qkv, preferred_element_type=F32)
    query_rows = (joined[:, :model_width] + vector_rows[0]).astype(BF16)
    key_rows = joined[:, model_width : 2 * model_width].astype(BF16)
    value_rows = (joined[:, 2 * model_width :] + vector_rows[1]).astype(BF16)
    context, logsum = lax.map(
        attend, (shaped(query_rows), shaped(key_rows), shaped(value_rows), lengths)
    )
    context = context.reshape(rows_total, model_width)
    attended = jnp.dot(context, weight_out, preferred_element_type=F32) + vector_rows[2]
    normed, pull_one = jax.vjp(
        layer_norm, inputs.astype(F32) + attended, vector_rows[3], vector_rows[4]
    )
    normed_low = normed.astype(BF16)
    hidden = jnp.dot(normed_low, up, preferred_element_type=F32) + vector_rows[
        5 : 5 + unit_ratio
    ].reshape(FF)
    active, pull_gelu = jax.vjp(exact_gelu, hidden)
    active_low = active.astype(BF16)
    result = jnp.dot(active_low, down, preferred_element_type=F32) + vector_rows[5 + unit_ratio]
    output, pull_two = jax.vjp(
        layer_norm, normed + result, vector_rows[6 + unit_ratio], vector_rows[7 + unit_ratio]
    )
    block_out = output.reshape(sequences, slots, model_width).astype(BF16)
    visible = (lax.iota(jnp.int32, slots)[None, :] < lengths[:, None]).astype(F32)
    grad_output = (cotangent.astype(F32) * visible[:, :, None]).reshape(rows_total, model_width)
    grad_second, grad_gain_two, grad_shift_two = pull_two(grad_output)
    second_low = grad_second.astype(BF16)
    grad_down = jnp.einsum("tf,td->fd", active_low, second_low, preferred_element_type=F32)
    grad_active = jnp.einsum("td,fd->tf", second_low, down, preferred_element_type=F32)
    (grad_hidden,) = pull_gelu(grad_active)
    hidden_low = grad_hidden.astype(BF16)
    grad_up = jnp.einsum("td,tf->df", normed_low, hidden_low, preferred_element_type=F32)
    grad_normed = grad_second + jnp.einsum("tf,df->td", hidden_low, up, preferred_element_type=F32)
    grad_mixed, grad_gain_one, grad_shift_one = pull_one(grad_normed)
    mixed_low = grad_mixed.astype(BF16)
    grad_out_weight = jnp.einsum("td,te->de", context, mixed_low, preferred_element_type=F32)
    grad_context = jnp.einsum(
        "te,de->td", mixed_low, weight_out, preferred_element_type=F32
    ).astype(BF16)
    grad_query, grad_keys, grad_values = lax.map(
        attend_back,
        (
            shaped(query_rows),
            shaped(key_rows),
            shaped(value_rows),
            logsum,
            shaped(grad_context),
            lengths,
        ),
    )
    grad_joined = jnp.concatenate(
        [
            grad_query.reshape(rows_total, model_width),
            grad_keys.reshape(rows_total, model_width),
            grad_values.reshape(rows_total, model_width),
        ],
        axis=1,
    )
    grad_qkv = jnp.einsum("td,te->de", inputs, grad_joined, preferred_element_type=F32)
    input_grad = grad_mixed + jnp.einsum(
        "te,de->td", grad_joined, weight_qkv, preferred_element_type=F32
    )
    vector_grad = jnp.concatenate(
        [
            jnp.sum(grad_joined[:, :model_width], axis=0, dtype=F32)[None],
            jnp.sum(grad_joined[:, 2 * model_width :], axis=0, dtype=F32)[None],
            jnp.sum(grad_mixed, axis=0)[None],
            grad_gain_one[None],
            grad_shift_one[None],
            jnp.sum(grad_hidden, axis=0).reshape(unit_ratio, model_width),
            jnp.sum(grad_second, axis=0)[None],
            grad_gain_two[None],
            grad_shift_two[None],
        ],
        axis=0,
    ).reshape(-1)
    weight_grads = [part.astype(BF16) for part in (grad_qkv, grad_out_weight, grad_up, grad_down)]
    if ringed:
        tiles = jnp.pad(
            vector_grad.reshape(shard_count, vector_share), ((0, 0), (0, 1024 - vector_share))
        ).reshape(shard_count, 8, 128)
        slabs = [part.reshape(-1, block_side, part.shape[1]) for part in weight_grads]
        owned, vector_sum = reduce_gradients(*slabs, tiles, shard_count // 2)
        vector_sum = vector_sum.reshape(1024)[:vector_share]
    else:
        owned, vector_sum = plain_reduce(*weight_grads, vector_grad, capacity)
    filler = (lax.iota(jnp.int32, capacity) * shard_count + lax.axis_index("fsdp")) >= block_total
    stat = jnp.where(
        filler[:, None, None], jnp.eye(block_side, dtype=jnp.bfloat16), states[0]
    )
    basis = jnp.where(
        filler[:, None, None], jnp.eye(block_side, dtype=jnp.bfloat16), states[1]
    )
    outer, new_basis, turned, update = soap_blocks(
        owned, stat, basis, states[2], states[3], states[4]
    )
    returned = lax.all_to_all(
        jnp.stack([outer, new_basis, turned, update])[:, :, None],
        "fsdp",
        split_axis=3,
        concat_axis=2,
        tiled=True,
    ).reshape(4, capacity * shard_count, -1, block_side)[:, :block_total]
    mirror = lax.ppermute(
        returned[:2], "dp", [(place, place ^ 1) for place in range(lax.axis_size("dp"))]
    )
    returned = returned.astype(jnp.float32)
    mirror = mirror.astype(jnp.float32)
    left_pair = jnp.where(right_side, mirror, returned[:2])
    right_pair = jnp.where(right_side, returned[:2], mirror)
    turned = returned[2]
    local = [
        returned[3],
        FIRST_DECAY * first_moment + (1.0 - FIRST_DECAY) * turned,
        SECOND_DECAY * second_moment + (1.0 - SECOND_DECAY) * turned * turned,
        STAT_DECAY * left_stat + (1.0 - STAT_DECAY) * left_pair[0],
        STAT_DECAY * right_stat + (1.0 - STAT_DECAY) * right_pair[0],
        left_pair[1],
        right_pair[1],
    ]
    new_matrices = matrices - MATRIX_RATE * (local[0] + WEIGHT_DECAY * matrices)
    vfirst_new = FIRST_DECAY * vector_first + (1.0 - FIRST_DECAY) * vector_sum
    vsecond_new = SECOND_DECAY * vector_second + (1.0 - SECOND_DECAY) * vector_sum * vector_sum
    vector_new = vectors - VECTOR_RATE * (vfirst_new / (1.0 - FIRST_DECAY**ADAM_STEP)) / (
        jnp.sqrt(vsecond_new / (1.0 - SECOND_DECAY**ADAM_STEP)) + ADAM_EPSILON
    )
    return (
        block_out,
        input_grad.reshape(sequences, slots, model_width),
        new_matrices,
        new_matrices.astype(jnp.bfloat16),
        local[1],
        local[2],
        local[3],
        local[4],
        local[5],
        local[6],
        vfirst_new,
        vsecond_new,
        vector_new,
    )


def solution(mesh):
    return jax.shard_map(
        shards,
        mesh=mesh,
        in_specs=(
            P(("fsdp", "dp"), None, None),
            P(("fsdp", "dp"), None, None),
            P(("fsdp", "dp")),
            P(None, "fsdp", None),
            P(None, "fsdp", None),
            P(None, "fsdp", None),
            P(None, "fsdp", None),
            P(None, "fsdp", None),
            P(None, "fsdp", None),
            P(None, "fsdp", None),
            P("fsdp"),
            P("fsdp"),
            P("fsdp"),
        ),
        out_specs=(
            P(("fsdp", "dp"), None, None),
            P(("fsdp", "dp"), None, None),
            P(None, "fsdp", None),
            P(None, "fsdp", None),
            P(None, "fsdp", None),
            P(None, "fsdp", None),
            P(None, "fsdp", None),
            P(None, "fsdp", None),
            P(None, "fsdp", None),
            P(None, "fsdp", None),
            P("fsdp"),
            P("fsdp"),
            P("fsdp"),
        ),
        check_vma=False,
    )
```

```python
import functools

import jax
import jax.numpy as jnp
from jax import lax
from jax.experimental import pallas as pl
from jax.experimental.pallas import tpu as pltpu
from jax.sharding import PartitionSpec as P

F32 = jnp.float32
BF16 = jnp.bfloat16
MESH = pl.DeviceIdType.MESH

HEADS = 12
HEAD_DIM = 64
FF = 3072
ADAM_STEP = 10


FIRST_DECAY = 0.9
SECOND_DECAY = 0.999
STAT_DECAY = 0.95
ADAM_EPSILON = 1e-08
NORM_EPSILON = 1e-05
MATRIX_RATE = 0.03
VECTOR_RATE = 0.2
WEIGHT_DECAY = 0.01


def assemble(blocks, row_count, column_count):
    block_side = blocks.shape[-1]
    shaped = blocks.reshape(row_count, column_count, block_side, block_side)
    return shaped.transpose(0, 2, 1, 3).reshape(row_count * block_side, column_count * block_side)


def split_blocks(matrix, row_count, column_count, block_side):
    shaped = matrix.reshape(row_count, block_side, column_count, block_side)
    return shaped.transpose(0, 2, 1, 3).reshape(row_count * column_count, block_side, block_side)


def layer_norm(values, gain_row, shift_row):
    center = jnp.mean(values, axis=-1, keepdims=True)
    centered = values - center
    spread = jnp.mean(centered * centered, axis=-1, keepdims=True)
    return centered * lax.rsqrt(spread + NORM_EPSILON) * gain_row + shift_row


def exact_gelu(hidden):
    return jax.nn.gelu(hidden, approximate=False)


def masked_scores(heads_query, heads_key, length):
    slots = heads_query.shape[0]
    scores = jnp.einsum(
        "qhd,khd->hqk", heads_query, heads_key, preferred_element_type=jnp.float32
    ) * HEAD_DIM ** (-0.5)
    visible = lax.iota(jnp.int32, slots) < length
    return jnp.where(visible[None, None, :], scores, -1e30)


def attend(pieces):
    query_rows, key_rows, value_rows, length = pieces
    slots = query_rows.shape[0]
    heads_query = query_rows.reshape(slots, HEADS, HEAD_DIM)
    heads_key = key_rows.reshape(slots, HEADS, HEAD_DIM)
    heads_value = value_rows.reshape(slots, HEADS, HEAD_DIM)
    scores = masked_scores(heads_query, heads_key, length)
    row_max = jnp.max(scores, axis=-1, keepdims=True)
    shifted = jnp.exp(scores - row_max)
    row_total = jnp.sum(shifted, axis=-1, keepdims=True)
    attention_weights = (shifted / row_total).astype(jnp.bfloat16)
    context = jnp.einsum(
        "hqk,khd->qhd", attention_weights, heads_value, preferred_element_type=jnp.float32
    )
    return (
        context.reshape(slots, -1).astype(jnp.bfloat16),
        row_max[..., 0] + jnp.log(row_total[..., 0]),
    )


def attend_back(pieces):
    query_rows, key_rows, value_rows, logsum, grad_context, length = pieces
    slots = query_rows.shape[0]
    heads_query = query_rows.reshape(slots, HEADS, HEAD_DIM)
    heads_key = key_rows.reshape(slots, HEADS, HEAD_DIM)
    heads_value = value_rows.reshape(slots, HEADS, HEAD_DIM)
    heads_grad = grad_context.reshape(slots, HEADS, HEAD_DIM)
    scores = masked_scores(heads_query, heads_key, length)
    attention_weights = jnp.exp(scores - logsum[..., None])
    weights_low = attention_weights.astype(jnp.bfloat16)
    grad_values = jnp.einsum(
        "hqk,qhd->khd", weights_low, heads_grad, preferred_element_type=jnp.float32
    )
    grad_weights = jnp.einsum(
        "qhd,khd->hqk", heads_grad, heads_value, preferred_element_type=jnp.float32
    )
    grad_scores = attention_weights * (
        grad_weights - jnp.sum(grad_weights * attention_weights, axis=-1, keepdims=True)
    )
    scores_low = grad_scores.astype(jnp.bfloat16)
    grad_query = jnp.einsum(
        "hqk,khd->qhd", scores_low, heads_key, preferred_element_type=jnp.float32
    ) * HEAD_DIM ** (-0.5)
    grad_keys = jnp.einsum(
        "hqk,qhd->khd", scores_low, heads_query, preferred_element_type=jnp.float32
    ) * HEAD_DIM ** (-0.5)
    return (
        grad_query.reshape(slots, -1).astype(jnp.bfloat16),
        grad_keys.reshape(slots, -1).astype(jnp.bfloat16),
        grad_values.reshape(slots, -1).astype(jnp.bfloat16),
    )


def dg(a,b,ca,cb):
    return lax.dot_general(a,b,(((ca,),(cb,)),((),())),preferred_element_type=F32)

def halves(a):
    hi=a.astype(BF16)
    return hi,(a-hi.astype(F32)).astype(BF16)

def mm3(a,b,ca,cb):
    ah,al=halves(a); bh,bl=halves(b)
    return dg(ah,bh,ca,cb)+(dg(ah,bl,ca,cb)+dg(al,bh,ca,cb))

def thirds(u):
    h=u.astype(BF16).astype(F32); r=u-h
    m=r.astype(BF16).astype(F32)
    return h,m,r-m

def factor_panels(aug, slots, side=128, between=None):
    sub=lax.broadcasted_iota(jnp.int32,(8,side),0)
    def spread(v): return jnp.broadcast_to(v,(8,side))
    for p in range(side//8):
        k=8*p
        if between is not None:
            between(p)
        panels=[]
        for s in range(slots):
            pw=aug[s,k:k+8,:side]; pv=aug[s,k:k+8,side:]
            cols=[spread(pw[:,k+i:k+i+1]) for i in range(8)]
            S=[[spread(cols[i][j:j+1,:]) if j>=i else None for i in range(8)] for j in range(8)]
            rw=[spread(pw[i:i+1,:]) for i in range(8)]
            rv=[spread(pv[i:i+1,:]) for i in range(8)]
            panels.append((S,rw,rv))
        for i in range(8):
            for S,rw,rv in panels:
                r=lax.rsqrt(S[i][i])
                for j in range(i+1,8): S[j][i]=S[j][i]*r
                for m in range(i+1,8):
                    for j in range(m,8):
                        S[j][m]=S[j][m]-S[j][i]*S[m][i]
                rw[i]=rw[i]*r; rv[i]=rv[i]*r
                for j in range(i+1,8):
                    rw[j]=rw[j]-S[j][i]*rw[i]
                    rv[j]=rv[j]-S[j][i]*rv[i]
        for s,(S,rw,rv) in enumerate(panels):
            uw,uv=rw[0],rv[0]
            for i in range(1,8):
                uw=jnp.where(sub==i,rw[i],uw); uv=jnp.where(sub==i,rv[i],uv)
            aug[s,k:k+8,side:]=uv
            if k+8<side:
                h,m,l=thirds(uw); vh,vm,vl=thirds(uv)
                a=jnp.concatenate([h,h,m,m,h,l],0).astype(BF16)
                b=jnp.concatenate([jnp.concatenate([h,m,h,m,l,h],0),jnp.concatenate([vh,vm,vh,vm,vl,vh],0)],1).astype(BF16)
                t=dg(a,b,0,0)
                aug[s,k+8:,:]=aug[s,k+8:,:]-t[k+8:,:]

def orthonormal_cols(mat, aug, slots, side=128):
    n=mat.shape[-1]
    r=lax.broadcasted_iota(jnp.int32,(side,side),0); c=lax.broadcasted_iota(jnp.int32,(side,side),1)
    eye=(r==c).astype(F32)
    steps=n//side
    for o in range(steps):
        lo=o*side
        for s in range(slots):
            mo=mat[s,:,lo:lo+side]
            aug[s,:,:side]=mm3(mo,mo,0,0)
            aug[s,:,side:]=eye
        factor_panels(aug,slots,side)
        for s in range(slots):
            q=mm3(mat[s,:,lo:lo+side],aug[s,:,side:],1,1)
            mat[s,:,lo:lo+side]=q
            if o+1<steps:
                rest=mat[s,:,lo+side:]
                mat[s,:,lo+side:]=rest-mm3(q,mm3(q,rest,0,0),1,0)


def soap_kernel(grad, stat, own, other, first, second, outer_out, basis_out, turned_out, update_out, mat, aug):
    slots = grad.shape[0]
    right_side = lax.rem(lax.axis_index("dp"), 2) == 1

    def run(is_right):
        near, far = (0, 1) if is_right else (1, 0)

        def one(s, carry):
            g = grad[s].astype(BF16)
            outer = dg(g, g, near, near)
            outer_out[s] = outer.astype(BF16)
            mixed = STAT_DECAY * stat[s].astype(F32) + (1.0 - STAT_DECAY) * outer
            high, rest = halves(mixed)
            mat[s] = dg(high, own[s], 1, 0) + dg(rest, own[s], 1, 0)
            left, right = (other[s], own[s]) if is_right else (own[s], other[s])
            rotated = dg(dg(left, g, 0, 0).astype(BF16), right, 1, 0)
            turned_out[s] = rotated.astype(BF16)
            first_new = FIRST_DECAY * first[s].astype(F32) + (1.0 - FIRST_DECAY) * rotated
            second_new = SECOND_DECAY * second[s].astype(F32) + (1.0 - SECOND_DECAY) * rotated * rotated
            direction = (
                first_new
                / (1.0 - FIRST_DECAY**ADAM_STEP)
                / (jnp.sqrt(second_new / (1.0 - SECOND_DECAY**ADAM_STEP)) + ADAM_EPSILON)
            )
            back = dg(left, direction.astype(BF16), 1, 0).astype(BF16)
            update_out[s] = dg(back, right, 1, 1).astype(BF16)
            return carry

        lax.fori_loop(0, slots, one, 0)

    @pl.when(right_side)
    def _():
        run(True)

    @pl.when(jnp.logical_not(right_side))
    def _():
        run(False)

    orthonormal_cols(mat, aug, slots)
    basis_out[...] = mat[...].astype(BF16)


def soap_blocks(grad, stat, own, other, first, second):
    slots, side, _ = grad.shape
    shape = jax.ShapeDtypeStruct(grad.shape, BF16)
    whole = pl.BlockSpec(memory_space=pltpu.VMEM)
    return pl.pallas_call(
        soap_kernel,
        out_shape=[shape] * 4,
        in_specs=[whole] * 6,
        out_specs=[whole] * 4,
        scratch_shapes=[
            pltpu.VMEM((slots, side, side), F32),
            pltpu.VMEM((slots, 128, 256), F32),
        ],
        compiler_params=pltpu.CompilerParams(vmem_limit_bytes=48 * 2**20),
        name="soap_blocks",
    )(grad, stat, own, other, first, second)


def ring_place(chip, chips):
    along, across = chip // 2, lax.rem(chip, 2)
    return along * (1 - across) + (chips - 1 - along) * across


def ring_chip(place, chips):
    place = lax.rem(place + 8 * chips, chips)
    across = place // (chips // 2)
    along = place * (1 - across) + (chips - 1 - place) * across
    return 2 * along + across


def whereabouts(chips):
    device, replica = lax.axis_index("fsdp"), lax.axis_index("dp")
    chip, core = device // 2, lax.rem(device, 2)
    place = ring_place(chip, chips)
    turn = 1 - 2 * core
    after = (2 * ring_chip(place + turn, chips) + core, replica)
    before = (2 * ring_chip(place - turn, chips) + core, replica)
    sibling = (2 * chip + 1 - core, replica)
    return device, replica, chip, core, place, turn, after, before, sibling


def greet(neighbours):
    barrier = pltpu.get_barrier_semaphore()
    for neighbour in neighbours:
        pl.semaphore_signal(barrier, inc=1, device_id=neighbour, device_id_type=MESH)
    pl.semaphore_wait(barrier, len(neighbours))


def gather_kernel(chips, share, mat_ref, vec_ref, attn, up, down, vecs, raw_a, raw_u, raw_d, low_a, low_u, low_d,
                  low_v, trade_send, trade_recv, own_sem, ring_send, ring_recv, sib_send, sib_recv):
    device, replica, chip, core, place, turn, after, before, sibling = whereabouts(chips)
    side = mat_ref.shape[-1]
    wide = attn.shape[-1] // 2
    slim = down.shape[-1] // 2
    both = 2 * share
    rows = pl.ds(pl.multiple_of(share * core, 8), share)
    for b in range(16):
        raw_a[(b % 4) // 2, rows, (b // 4) * 2 * side + (b % 2) * side : (b // 4) * 2 * side + (b % 2 + 1) * side] = mat_ref[b]
        raw_u[b // 8, rows, (b % 8) * side : (b % 8 + 1) * side] = mat_ref[16 + b]
        raw_d[b // 2, rows, (b % 2) * side : (b % 2 + 1) * side] = mat_ref[32 + b]
    low_v[...] = vec_ref[...].astype(BF16).astype(F32)
    greet((after, before, sibling))
    groups = ((raw_a, low_a, attn, wide), (raw_u, low_u, up, wide), (raw_d, low_d, down, slim))

    def half(which, width):
        return pl.ds(pl.multiple_of(which * width, 128), width)

    trades = []
    for g, (raw, low, out, width) in enumerate(groups):
        part = raw.at[:, rows, half(1 - core, width)]
        trade = pltpu.make_async_remote_copy(
            src_ref=part, dst_ref=part, send_sem=trade_send.at[g], recv_sem=trade_recv.at[g],
            device_id=sibling, device_id_type=MESH)
        trade.start()
        trades.append(trade)

    def slab(g, origin):
        raw, low, out, width = groups[g]
        return out.at[:, pl.ds(pl.multiple_of(origin * both, 16), both), half(core, width)]

    def vec_of(origin):
        return vecs.at[2 * origin + core]

    def piece(g, origin):
        return vec_of(origin) if g == 3 else slab(g, origin)

    def forward(g, t, origin, source):
        return pltpu.make_async_remote_copy(
            src_ref=source, dst_ref=piece(g, origin), send_sem=ring_send.at[t, g], recv_sem=ring_recv.at[t, g],
            device_id=after, device_id_type=MESH)

    def pass_on(g, t, origin, source):
        return pltpu.make_async_remote_copy(
            src_ref=source, dst_ref=piece(g, origin), send_sem=sib_send.at[t, g], recv_sem=sib_recv.at[t, g],
            device_id=sibling, device_id_type=MESH)

    sources = [low_a, low_u, low_d, low_v]
    owns = []
    for g in (3, 0, 1, 2):
        if g < 3:
            raw, low, out, width = groups[g]
            trades[g].wait()
            low[...] = raw[:, :, half(core, width)].astype(BF16)
        forward(g, 0, chip, sources[g]).start()
        pass_on(g, 0, chip, sources[g]).start()
        own = pltpu.make_async_copy(sources[g], piece(g, chip), own_sem.at[g])
        own.start()
        owns.append(own)

    def step(t, carry):
        origin = ring_chip(place - turn * t, chips)
        for g in (3, 0, 1, 2):
            arrived = piece(g, origin)
            forward(g, t - 1, origin, arrived).wait_recv()

            @pl.when(t < chips - 1)
            def _():
                forward(g, t, origin, arrived).start()

            pass_on(g, t, origin, arrived).start()
        return carry

    lax.fori_loop(1, chips, step, 0)
    for own in owns:
        own.wait()

    def finish(t, carry):
        for g in range(4):
            @pl.when(t < chips - 1)
            def _():
                forward(g, t, chip, piece(g, chip)).wait_send()

            pass_on(g, t, chip, piece(g, chip)).wait()
        return carry

    lax.fori_loop(0, chips, finish, 0)


def gather_weights(matrices, vector_tile, chips):
    total, share, side = matrices.shape
    both = 2 * share
    anywhere = pl.BlockSpec(memory_space=pl.ANY)
    whole = pl.BlockSpec(memory_space=pltpu.VMEM)
    dma = pltpu.SemaphoreType.DMA
    return pl.pallas_call(
        functools.partial(gather_kernel, chips, share),
        out_shape=[
            jax.ShapeDtypeStruct((2, side, 8 * side), BF16),
            jax.ShapeDtypeStruct((2, side, 8 * side), BF16),
            jax.ShapeDtypeStruct((8, side, 2 * side), BF16),
            jax.ShapeDtypeStruct((2 * chips, 8, 128), F32),
        ],
        in_specs=[whole, whole],
        out_specs=[anywhere] * 4,
        scratch_shapes=[
            pltpu.VMEM((2, both, 8 * side), F32),
            pltpu.VMEM((2, both, 8 * side), F32),
            pltpu.VMEM((8, both, 2 * side), F32),
            pltpu.VMEM((2, both, 4 * side), BF16),
            pltpu.VMEM((2, both, 4 * side), BF16),
            pltpu.VMEM((8, both, side), BF16),
            pltpu.VMEM((8, 128), F32),
            dma((3,)), dma((3,)), dma((4,)),
            dma((chips - 1, 4)), dma((chips - 1, 4)), dma((chips, 4)), dma((chips, 4)),
        ],
        compiler_params=pltpu.CompilerParams(collective_id=1, has_side_effects=True, vmem_limit_bytes=40 * 2**20),
        name="gather_weights",
    )(matrices, vector_tile)


def reduce_kernel(chips, g_qkv, g_out, g_up, g_down, g_vec, owned, vec_sum, mine, theirs, ring, peer, vmine, vring, vpeer,
                  mine_sem, sib_send, sib_recv, ring_send, ring_recv, peer_send, peer_recv):
    device, replica, chip, core, place, turn, after, before, sibling = whereabouts(chips)
    other = (device, 1 - replica)
    side = mine.shape[-1]
    greet((after, before, sibling, other))

    def column(index):
        return pl.ds(pl.multiple_of(index * side, 128), side)

    def fetch(owner, start):
        which = owner // 4
        i, j = lax.rem(owner, 4) // 2, lax.rem(owner, 2)

        @pl.when(which < 3)
        def _():
            start(0, g_qkv.at[i, :, column(2 * which + j)])

        @pl.when(which == 3)
        def _():
            start(0, g_out.at[i, :, column(j)])

        start(1, g_up.at[owner // 8, :, column(lax.rem(owner, 8))])
        start(2, g_down.at[owner // 2, :, column(lax.rem(owner, 2))])
        start(3, g_vec.at[owner])

    def local(t, slot, source):
        target = vmine.at[0, t] if slot == 3 else mine.at[t, slot]
        return pltpu.make_async_copy(source, target, mine_sem.at[t, slot])

    def to_sibling(t, slot, source):
        target = vmine.at[1, t] if slot == 3 else theirs.at[t, slot]
        return pltpu.make_async_remote_copy(
            src_ref=source, dst_ref=target, send_sem=sib_send.at[t, slot], recv_sem=sib_recv.at[t, slot],
            device_id=sibling, device_id_type=MESH)

    def to_next(t, slot):
        source, target = (vmine.at[0, t], vring.at[t]) if slot == 3 else (mine.at[t, slot], ring.at[t, slot])
        return pltpu.make_async_remote_copy(
            src_ref=source, dst_ref=target, send_sem=ring_send.at[t, slot], recv_sem=ring_recv.at[t, slot],
            device_id=after, device_id_type=MESH)

    def to_other(slot):
        source, target = (vmine.at[0, chips - 1], vpeer) if slot == 3 else (mine.at[chips - 1, slot], peer.at[slot])
        return pltpu.make_async_remote_copy(
            src_ref=source, dst_ref=target, send_sem=peer_send.at[slot], recv_sem=peer_recv.at[slot],
            device_id=other, device_id_type=MESH)

    def begin(t, carry):
        fetch(2 * ring_chip(place + turn * (t + 1), chips) + 1 - core, lambda slot, source: to_sibling(t, slot, source).start())
        fetch(2 * ring_chip(place - turn * (t + 1), chips) + core, lambda slot, source: local(t, slot, source).start())
        return carry

    lax.fori_loop(0, chips, begin, 0)

    def sources(slot):
        return g_vec.at[0] if slot == 3 else g_up.at[0, :, :side]

    def ready(t, slot):
        local(t, slot, sources(slot)).wait()
        to_sibling(t, slot, sources(slot)).wait_recv()

    for slot in (3, 0, 1, 2):
        ready(0, slot)
        if slot == 3:
            vmine[0, 0] = vmine[0, 0] + vmine[1, 0]
        else:
            mine[0, slot] = (mine[0, slot].astype(F32) + theirs[0, slot].astype(F32)).astype(BF16)
        to_next(0, slot).start()

    def step(t, carry):
        for slot in (3, 0, 1, 2):
            ready(t, slot)
            to_next(t - 1, slot).wait_recv()
            if slot == 3:
                vmine[0, t] = vmine[0, t] + vmine[1, t] + vring[t - 1]
            else:
                total = mine[t, slot].astype(F32) + theirs[t, slot].astype(F32) + ring[t - 1, slot].astype(F32)
                mine[t, slot] = total.astype(BF16)

            @pl.when(t < chips - 1)
            def _():
                to_next(t, slot).start()

            @pl.when(t == chips - 1)
            def _():
                to_other(slot).start()
        return carry

    lax.fori_loop(1, chips, step, 0)
    for slot in (3, 0, 1, 2):
        to_other(slot).wait()
        if slot == 3:
            vec_sum[...] = vmine[0, chips - 1] + vpeer[...]
        else:
            owned[slot] = (mine[chips - 1, slot].astype(F32) + peer[slot].astype(F32)).astype(BF16)

    def finish(t, carry):
        for slot in range(4):
            to_sibling(t, slot, sources(slot)).wait_send()

            @pl.when(t < chips - 1)
            def _():
                to_next(t, slot).wait_send()
        return carry

    lax.fori_loop(0, chips, finish, 0)


def reduce_gradients(g_qkv, g_out, g_up, g_down, g_vec, chips):
    side = g_up.shape[1]
    anywhere = pl.BlockSpec(memory_space=pl.ANY)
    whole = pl.BlockSpec(memory_space=pltpu.VMEM)
    dma = pltpu.SemaphoreType.DMA
    return pl.pallas_call(
        functools.partial(reduce_kernel, chips),
        out_shape=[jax.ShapeDtypeStruct((3, side, side), BF16), jax.ShapeDtypeStruct((8, 128), F32)],
        in_specs=[anywhere] * 5,
        out_specs=[whole] * 2,
        scratch_shapes=[
            pltpu.VMEM((chips, 3, side, side), BF16),
            pltpu.VMEM((chips, 3, side, side), BF16),
            pltpu.VMEM((chips - 1, 3, side, side), BF16),
            pltpu.VMEM((3, side, side), BF16),
            pltpu.VMEM((2, chips, 8, 128), F32),
            pltpu.VMEM((chips - 1, 8, 128), F32),
            pltpu.VMEM((8, 128), F32),
            dma((chips, 4)), dma((chips, 4)), dma((chips, 4)),
            dma((chips - 1, 4)), dma((chips - 1, 4)), dma((4,)), dma((4,)),
        ],
        compiler_params=pltpu.CompilerParams(collective_id=2, has_side_effects=True, vmem_limit_bytes=48 * 2**20),
        name="reduce_gradients",
    )(g_qkv, g_out, g_up, g_down, g_vec)


def opposite(device, step, count):
    result, bit = 0, 1
    while bit < count:
        one, two = lax.rem(device // bit, 2), lax.rem(step // bit, 2)
        result = result + bit * (one + two - 2 * one * two)
        bit *= 2
    return result


def renew_kernel(count, share, grad, stat, own, other, first, second, early, late, items, mat, aug, out_early, out_late,
                 early_send, early_recv, early_own, late_send, late_recv, late_own,
                 cross_send, cross_recv, cross_late_send, cross_late_recv):
    device, replica = lax.axis_index("fsdp"), lax.axis_index("dp")
    mirror = (device, 1 - replica)
    slots, side, _ = grad.shape
    part = 128

    def partner(step):
        return opposite(device, step, count), replica

    barrier = pltpu.get_barrier_semaphore()

    def hail(step, carry):
        pl.semaphore_signal(barrier, inc=1, device_id=partner(step), device_id_type=MESH)
        return carry

    lax.fori_loop(1, count, hail, 0)
    pl.semaphore_signal(barrier, inc=1, device_id=mirror, device_id_type=MESH)
    pl.semaphore_wait(barrier, count)

    def run(is_right):
        near, far = (0, 1) if is_right else (1, 0)

        def outer_one(s, carry):
            g = grad[s]
            outer = dg(g, g, near, near)
            items[s] = outer
            mixed = STAT_DECAY * stat[s].astype(F32) + (1.0 - STAT_DECAY) * outer
            high, rest = halves(mixed)
            mat[s] = dg(high, own[s], 1, 0) + dg(rest, own[s], 1, 0)
            return carry

        lax.fori_loop(0, slots, outer_one, 0)
        for e, s in enumerate((1, 2) if is_right else (0, 2)):
            left, right = (other[e], own[s]) if is_right else (own[s], other[e])
            rotated = dg(dg(left, grad[s], 0, 0).astype(BF16), right, 1, 0)
            if e == 0:
                items[3] = rotated
            elif not is_right:
                items[5] = rotated
                continue
            first_new = FIRST_DECAY * first[e].astype(F32) + (1.0 - FIRST_DECAY) * rotated
            second_new = SECOND_DECAY * second[e].astype(F32) + (1.0 - SECOND_DECAY) * rotated * rotated
            direction = (
                first_new
                / (1.0 - FIRST_DECAY**ADAM_STEP)
                / (jnp.sqrt(second_new / (1.0 - SECOND_DECAY**ADAM_STEP)) + ADAM_EPSILON)
            )
            back = dg(left, direction.astype(BF16), 1, 0).astype(BF16)
            items[4 + e] = dg(back, right, 1, 1)

    @pl.when(replica == 1)
    def _():
        run(True)

    @pl.when(replica == 0)
    def _():
        run(False)

    def rows_of(holder):
        return pl.ds(pl.multiple_of(holder * share, 8), share)

    def pack_early(holder, carry):
        for pair in range(3):
            two = jnp.concatenate([items[2 * pair, rows_of(holder), :], items[2 * pair + 1, rows_of(holder), :]], axis=0)
            out_early[holder, 2 * share * pair : 2 * share * (pair + 1), :] = two.astype(BF16)
        return carry

    def send_early(step, target):
        return pltpu.make_async_remote_copy(
            src_ref=out_early.at[target[0]], dst_ref=early.at[replica, device], send_sem=early_send.at[step],
            recv_sem=early_recv.at[step], device_id=target, device_id_type=MESH)

    def send_late(panel, step, target):
        return pltpu.make_async_remote_copy(
            src_ref=out_late.at[panel, target[0]], dst_ref=late.at[panel, replica, device],
            send_sem=late_send.at[panel, step], recv_sem=late_recv.at[panel, step], device_id=target, device_id_type=MESH)

    def cross_early(step):
        block = early.at[replica, partner(step)[0]]
        return pltpu.make_async_remote_copy(
            src_ref=block, dst_ref=block, send_sem=cross_send.at[step], recv_sem=cross_recv.at[step],
            device_id=mirror, device_id_type=MESH)

    def cross_late(panel, step):
        block = late.at[panel, replica, partner(step)[0]]
        return pltpu.make_async_remote_copy(
            src_ref=block, dst_ref=block, send_sem=cross_late_send.at[panel, step], recv_sem=cross_late_recv.at[panel, step],
            device_id=mirror, device_id_type=MESH)

    def keep_early():
        return pltpu.make_async_copy(out_early.at[device], early.at[replica, device], early_own)

    def keep_late(panel):
        return pltpu.make_async_copy(out_late.at[panel, device], late.at[panel, replica, device], late_own.at[panel])

    lax.fori_loop(0, count, pack_early, 0)

    def launch_early(index, carry):
        step = count - 1 - index
        send_early(step, partner(step)).start()
        return carry

    lax.fori_loop(0, count - 1, launch_early, 0)
    keep_early().start()

    def relay_early(step):
        if step == 0:
            keep_early().wait()
        else:
            send_early(step, partner(step)).wait_recv()
        cross_early(step).start()

    relayed = []

    def between(moment):
        if moment % 4 == 0 and len(relayed) < min(count, 11):
            relay_early(len(relayed))
            relayed.append(moment)

    row_index = lax.broadcasted_iota(jnp.int32, (part, part), 0)
    column_index = lax.broadcasted_iota(jnp.int32, (part, part), 1)
    eye = (row_index == column_index).astype(F32)
    panels = side // part
    for o in range(panels):
        lo = o * part
        for s in range(slots):
            block = mat[s, :, lo : lo + part]
            aug[s, :, :part] = mm3(block, block, 0, 0)
            aug[s, :, part:] = eye
        factor_panels(aug, slots, part, lambda p: between(16 * o + p))
        for s in range(slots):
            mat[s, :, lo : lo + part] = mm3(mat[s, :, lo : lo + part], aug[s, :, part:], 1, 1)

        def pack_late(holder, carry):
            rows = rows_of(holder)
            stacked = [mat[s, rows, lo : lo + part] for s in range(slots)]
            stacked.append(jnp.zeros((8, part), F32))
            out_late[o, holder] = jnp.concatenate(stacked, axis=0).astype(BF16)
            return carry

        lax.fori_loop(0, count, pack_late, 0)

        def launch_late(index, carry):
            step = count - 1 - index
            send_late(o, step, partner(step)).start()
            return carry

        lax.fori_loop(0, count - 1, launch_late, 0)
        keep_late(o).start()
        if o + 1 < panels:
            for s in range(slots):
                q, rest = mat[s, :, lo : lo + part], mat[s, :, lo + part :]
                mat[s, :, lo + part :] = rest - mm3(q, mm3(q, rest, 0, 0), 1, 0)
    for step in range(len(relayed), count):
        relay_early(step)
    for o in range(panels):
        keep_late(o).wait()
        cross_late(o, 0).start()

        def relay_late(step, carry):
            send_late(o, step, partner(step)).wait_recv()
            cross_late(o, step).start()
            return carry

        lax.fori_loop(1, count, relay_late, 0)

    def finish(step, carry):
        cross_early(step).wait()
        for o in range(panels):
            cross_late(o, step).wait()

        @pl.when(step > 0)
        def _():
            send_early(step, partner(step)).wait_send()
            for o in range(panels):
                send_late(o, step, partner(step)).wait_send()
        return carry

    lax.fori_loop(0, count, finish, 0)


def renew_blocks(grad, stat, own, other, first, second, count, share):
    slots, side, _ = grad.shape
    anywhere = pl.BlockSpec(memory_space=pl.ANY)
    whole = pl.BlockSpec(memory_space=pltpu.VMEM)
    dma = pltpu.SemaphoreType.DMA
    tall = -(-slots * share // 16) * 16
    panels = side // 128
    return pl.pallas_call(
        functools.partial(renew_kernel, count, share),
        out_shape=[
            jax.ShapeDtypeStruct((2, count, 6 * share, side), BF16),
            jax.ShapeDtypeStruct((panels, 2, count, tall, 128), BF16),
        ],
        in_specs=[whole] * 6,
        out_specs=[anywhere] * 2,
        scratch_shapes=[
            pltpu.VMEM((6, side, side), F32),
            pltpu.VMEM((slots, side, side), F32),
            pltpu.VMEM((slots, 128, 256), F32),
            pltpu.VMEM((count, 6 * share, side), BF16),
            pltpu.VMEM((panels, count, tall, 128), BF16),
            dma((count,)), dma((count,)), dma,
            dma((panels, count)), dma((panels, count)), dma((panels,)),
            dma((count,)), dma((count,)), dma((panels, count)), dma((panels, count)),
        ],
        compiler_params=pltpu.CompilerParams(collective_id=3, has_side_effects=True, vmem_limit_bytes=48 * 2**20),
        name="renew_blocks",
    )(grad, stat, own, other, first, second)


def settle_kernel(early, late, mat, first, second, left, right, mat_new, mat_low, first_new, second_new, left_new, right_new,
                  left_basis, right_basis):
    share = mat.shape[2]
    for s in range(3):
        def item(plane, index):
            return early[plane, 0, index * share : (index + 1) * share, :].astype(F32)

        turned = (item(0, 3), item(1, 3), item(0, 5))[s]
        update = (item(0, 4), item(1, 4), item(1, 5))[s]
        fresh = mat[s, 0] - MATRIX_RATE * (update + WEIGHT_DECAY * mat[s, 0])
        mat_new[s, 0] = fresh
        mat_low[s, 0] = fresh.astype(BF16)
        first_new[s, 0] = FIRST_DECAY * first[s, 0] + (1.0 - FIRST_DECAY) * turned
        second_new[s, 0] = SECOND_DECAY * second[s, 0] + (1.0 - SECOND_DECAY) * turned * turned
        left_new[s, 0] = STAT_DECAY * left[s, 0] + (1.0 - STAT_DECAY) * item(0, s)
        right_new[s, 0] = STAT_DECAY * right[s, 0] + (1.0 - STAT_DECAY) * item(1, s)
        for panel in range(late.shape[0]):
            lanes = slice(128 * panel, 128 * (panel + 1))
            left_basis[s, 0, :, lanes] = late[panel, 0, 0, s * share : (s + 1) * share, :].astype(F32)
            right_basis[s, 0, :, lanes] = late[panel, 1, 0, s * share : (s + 1) * share, :].astype(F32)


def settle(early, late, matrices, first, second, left, right):
    _, count, tall, side = early.shape
    panels, share = late.shape[0], matrices.shape[1]
    state = pl.BlockSpec((3, 1, share, side), lambda f: (0, f, 0, 0))
    shape = jax.ShapeDtypeStruct((3, count, share, side), F32)
    low = jax.ShapeDtypeStruct((3, count, share, side), BF16)
    results = pl.pallas_call(
        settle_kernel,
        grid=(count,),
        out_shape=[shape, low] + [shape] * 6,
        in_specs=[
            pl.BlockSpec((2, 1, tall, side), lambda f: (0, f, 0, 0)),
            pl.BlockSpec((panels, 2, 1, late.shape[3], 128), lambda f: (0, 0, f, 0, 0)),
        ]
        + [state] * 5,
        out_specs=[state] * 8,
        compiler_params=pltpu.CompilerParams(vmem_limit_bytes=32 * 2**20),
        name="settle",
    )(early, late, *[part.reshape(3, count, share, side) for part in (matrices, first, second, left, right)])
    return [part.reshape(matrices.shape) for part in results]


def plain_gather(matrices, vectors):
    side = matrices.shape[-1]
    blocks = lax.all_gather(matrices.astype(BF16), "fsdp", axis=1, tiled=True)
    attn = jnp.concatenate([assemble(blocks[4 * part : 4 * part + 4], 2, 2) for part in range(4)], axis=1)
    up = assemble(blocks[16:32], 2, 8)
    down = assemble(blocks[32:], 8, 2)
    rows = lax.all_gather(vectors.astype(BF16), "fsdp", axis=0, tiled=True)
    return attn, up, down, rows.astype(F32).reshape(-1, 2 * side)


def plain_reduce(grad_qkv, grad_out, grad_up, grad_down, vector_grad, capacity):
    shard_count = lax.axis_size("fsdp")
    width = grad_up.shape[0]
    side = width // 2
    blocks = jnp.concatenate(
        [split_blocks(grad_qkv[:, part * width : (part + 1) * width], 2, 2, side) for part in range(3)]
        + [split_blocks(grad_out, 2, 2, side), split_blocks(grad_up, 2, 8, side), split_blocks(grad_down, 8, 2, side)],
        axis=0,
    )
    owned = lax.psum_scatter(
        to_owners(blocks, capacity, shard_count), "fsdp", scatter_dimension=1, tiled=True
    )
    owned = lax.psum(owned, "dp")[:, 0]
    share = lax.psum_scatter(vector_grad, "fsdp", scatter_dimension=0, tiled=True)
    return owned, lax.psum(share, "dp")


def to_owners(blocks, capacity, shard_count):
    spare = capacity * shard_count - blocks.shape[0]
    blocks = jnp.pad(blocks, ((0, spare),) + ((0, 0),) * (blocks.ndim - 1))
    return blocks.reshape((capacity, shard_count) + blocks.shape[1:])


def shards(
    tokens,
    cotangent,
    lengths,
    matrices,
    first_moment,
    second_moment,
    left_stat,
    right_stat,
    left_basis,
    right_basis,
    vectors,
    vector_first,
    vector_second,
):
    shard_count = lax.axis_size("fsdp")
    replicas = lax.axis_size("dp")
    sequences, slots, model_width = tokens.shape
    block_total, share_rows, block_side = matrices.shape
    unit_ratio = FF // model_width
    rows_total = sequences * slots
    capacity = -(-block_total // shard_count)
    ringed = replicas == 2 and capacity * shard_count == block_total == 48 and share_rows % 8 == 0 and capacity == 3
    vector_share = vectors.shape[0]

    def shaped(array):
        return array.reshape(sequences, slots, array.shape[-1])

    right_side = lax.axis_index("dp") % 2 == 1
    chosen = [
        jnp.where(right_side, right_stat, left_stat),
        jnp.where(right_side, right_basis, left_basis),
    ]
    turning = [jnp.where(right_side, left_basis, right_basis), first_moment, second_moment]
    if ringed:
        split = [part.reshape(capacity, shard_count, share_rows, block_side) for part in chosen + turning]
        states = jnp.concatenate(
            [part.astype(BF16) for part in split[:2]]
            + [
                piece.astype(BF16)
                for part in split[2:]
                for piece in (jnp.where(right_side, part[1:2], part[0:1]), part[2:])
            ]
        )
    else:
        states = jnp.stack([to_owners(part.astype(BF16), capacity, shard_count) for part in chosen + turning])

    if ringed:
        vector_tile = jnp.pad(vectors, (0, 1024 - vector_share)).reshape(8, 128)
        attn, up, down, vector_tiles = gather_weights(matrices, vector_tile, shard_count // 2)
        attn = attn.reshape(model_width, 4 * model_width)
        up = up.reshape(model_width, FF)
        down = down.reshape(FF, model_width)
        states, attn = lax.optimization_barrier((states, attn))
        states = lax.all_to_all(states, "fsdp", split_axis=1, concat_axis=2, tiled=True)[:, 0]
        vector_rows = vector_tiles.reshape(shard_count, 1024)[:, :vector_share].reshape(-1, model_width)
    else:
        attn, up, down, vector_rows = plain_gather(matrices, vectors)
        states = lax.all_to_all(states, "fsdp", split_axis=2, concat_axis=3, tiled=True)[:, :, 0]
    weight_qkv, weight_out = attn[:, : 3 * model_width], attn[:, 3 * model_width :]
    inputs = tokens.reshape(rows_total, model_width)
    joined = jnp.dot(inputs, weight_qkv, preferred_element_type=F32)
    query_rows = (joined[:, :model_width] + vector_rows[0]).astype(BF16)
    key_rows = joined[:, model_width : 2 * model_width].astype(BF16)
    value_rows = (joined[:, 2 * model_width :] + vector_rows[1]).astype(BF16)
    context, logsum = lax.map(
        attend, (shaped(query_rows), shaped(key_rows), shaped(value_rows), lengths)
    )
    context = context.reshape(rows_total, model_width)
    attended = jnp.dot(context, weight_out, preferred_element_type=F32) + vector_rows[2]
    normed, pull_one = jax.vjp(
        layer_norm, inputs.astype(F32) + attended, vector_rows[3], vector_rows[4]
    )
    normed_low = normed.astype(BF16)
    hidden = jnp.dot(normed_low, up, preferred_element_type=F32) + vector_rows[
        5 : 5 + unit_ratio
    ].reshape(FF)
    active, pull_gelu = jax.vjp(exact_gelu, hidden)
    active_low = active.astype(BF16)
    result = jnp.dot(active_low, down, preferred_element_type=F32) + vector_rows[5 + unit_ratio]
    output, pull_two = jax.vjp(
        layer_norm, normed + result, vector_rows[6 + unit_ratio], vector_rows[7 + unit_ratio]
    )
    block_out = output.reshape(sequences, slots, model_width).astype(BF16)
    visible = (lax.iota(jnp.int32, slots)[None, :] < lengths[:, None]).astype(F32)
    grad_output = (cotangent.astype(F32) * visible[:, :, None]).reshape(rows_total, model_width)
    grad_second, grad_gain_two, grad_shift_two = pull_two(grad_output)
    second_low = grad_second.astype(BF16)
    grad_down = jnp.einsum("tf,td->fd", active_low, second_low, preferred_element_type=F32)
    grad_active = jnp.einsum("td,fd->tf", second_low, down, preferred_element_type=F32)
    (grad_hidden,) = pull_gelu(grad_active)
    hidden_low = grad_hidden.astype(BF16)
    grad_up = jnp.einsum("td,tf->df", normed_low, hidden_low, preferred_element_type=F32)
    grad_normed = grad_second + jnp.einsum("tf,df->td", hidden_low, up, preferred_element_type=F32)
    grad_mixed, grad_gain_one, grad_shift_one = pull_one(grad_normed)
    mixed_low = grad_mixed.astype(BF16)
    grad_out_weight = jnp.einsum("td,te->de", context, mixed_low, preferred_element_type=F32)
    grad_context = jnp.einsum(
        "te,de->td", mixed_low, weight_out, preferred_element_type=F32
    ).astype(BF16)
    grad_query, grad_keys, grad_values = lax.map(
        attend_back,
        (
            shaped(query_rows),
            shaped(key_rows),
            shaped(value_rows),
            logsum,
            shaped(grad_context),
            lengths,
        ),
    )
    grad_joined = jnp.concatenate(
        [
            grad_query.reshape(rows_total, model_width),
            grad_keys.reshape(rows_total, model_width),
            grad_values.reshape(rows_total, model_width),
        ],
        axis=1,
    )
    grad_qkv = jnp.einsum("td,te->de", inputs, grad_joined, preferred_element_type=F32)
    input_grad = grad_mixed + jnp.einsum(
        "te,de->td", grad_joined, weight_qkv, preferred_element_type=F32
    )
    vector_grad = jnp.concatenate(
        [
            jnp.sum(grad_joined[:, :model_width], axis=0, dtype=F32)[None],
            jnp.sum(grad_joined[:, 2 * model_width :], axis=0, dtype=F32)[None],
            jnp.sum(grad_mixed, axis=0)[None],
            grad_gain_one[None],
            grad_shift_one[None],
            jnp.sum(grad_hidden, axis=0).reshape(unit_ratio, model_width),
            jnp.sum(grad_second, axis=0)[None],
            grad_gain_two[None],
            grad_shift_two[None],
        ],
        axis=0,
    ).reshape(-1)
    weight_grads = [part.astype(BF16) for part in (grad_qkv, grad_out_weight, grad_up, grad_down)]
    if ringed:
        tiles = jnp.pad(
            vector_grad.reshape(shard_count, vector_share), ((0, 0), (0, 1024 - vector_share))
        ).reshape(shard_count, 8, 128)
        slabs = [part.reshape(-1, block_side, part.shape[1]) for part in weight_grads]
        owned, vector_sum = reduce_gradients(*slabs, tiles, shard_count // 2)
        vector_sum = vector_sum.reshape(1024)[:vector_share]
    else:
        owned, vector_sum = plain_reduce(*weight_grads, vector_grad, capacity)
    if ringed:
        early, late = renew_blocks(
            owned, states[0:3], states[3:6], states[6:8], states[8:10], states[10:12], shard_count, share_rows
        )
        local = settle(early, late, matrices, first_moment, second_moment, left_stat, right_stat)
    else:
        filler = (lax.iota(jnp.int32, capacity) * shard_count + lax.axis_index("fsdp")) >= block_total
        stat = jnp.where(
            filler[:, None, None], jnp.eye(block_side, dtype=jnp.bfloat16), states[0]
        )
        basis = jnp.where(
            filler[:, None, None], jnp.eye(block_side, dtype=jnp.bfloat16), states[1]
        )
        outer, new_basis, turned, update = soap_blocks(
            owned, stat, basis, states[2], states[3], states[4]
        )
        returned = lax.all_to_all(
            jnp.stack([outer, new_basis, turned, update])[:, :, None],
            "fsdp",
            split_axis=3,
            concat_axis=2,
            tiled=True,
        ).reshape(4, capacity * shard_count, -1, block_side)[:, :block_total]
        mirror = lax.ppermute(
            returned[:2], "dp", [(place, place ^ 1) for place in range(lax.axis_size("dp"))]
        )
        returned = returned.astype(jnp.float32)
        mirror = mirror.astype(jnp.float32)
        left_pair = jnp.where(right_side, mirror, returned[:2])
        right_pair = jnp.where(right_side, returned[:2], mirror)
        turned = returned[2]
        local = [
            returned[3],
            FIRST_DECAY * first_moment + (1.0 - FIRST_DECAY) * turned,
            SECOND_DECAY * second_moment + (1.0 - SECOND_DECAY) * turned * turned,
            STAT_DECAY * left_stat + (1.0 - STAT_DECAY) * left_pair[0],
            STAT_DECAY * right_stat + (1.0 - STAT_DECAY) * right_pair[0],
            left_pair[1],
            right_pair[1],
        ]
        local = [matrices - MATRIX_RATE * (local[0] + WEIGHT_DECAY * matrices)] + local
        local[1] = local[0].astype(BF16)
    vfirst_new = FIRST_DECAY * vector_first + (1.0 - FIRST_DECAY) * vector_sum
    vsecond_new = SECOND_DECAY * vector_second + (1.0 - SECOND_DECAY) * vector_sum * vector_sum
    vector_new = vectors - VECTOR_RATE * (vfirst_new / (1.0 - FIRST_DECAY**ADAM_STEP)) / (
        jnp.sqrt(vsecond_new / (1.0 - SECOND_DECAY**ADAM_STEP)) + ADAM_EPSILON
    )
    return (
        block_out,
        input_grad.reshape(sequences, slots, model_width),
        *local,
        vfirst_new,
        vsecond_new,
        vector_new,
    )


def solution(mesh):
    return jax.shard_map(
        shards,
        mesh=mesh,
        in_specs=(
            P(("fsdp", "dp"), None, None),
            P(("fsdp", "dp"), None, None),
            P(("fsdp", "dp")),
            P(None, "fsdp", None),
            P(None, "fsdp", None),
            P(None, "fsdp", None),
            P(None, "fsdp", None),
            P(None, "fsdp", None),
            P(None, "fsdp", None),
            P(None, "fsdp", None),
            P("fsdp"),
            P("fsdp"),
            P("fsdp"),
        ),
        out_specs=(
            P(("fsdp", "dp"), None, None),
            P(("fsdp", "dp"), None, None),
            P(None, "fsdp", None),
            P(None, "fsdp", None),
            P(None, "fsdp", None),
            P(None, "fsdp", None),
            P(None, "fsdp", None),
            P(None, "fsdp", None),
            P(None, "fsdp", None),
            P(None, "fsdp", None),
            P("fsdp"),
            P("fsdp"),
            P("fsdp"),
        ),
        check_vma=False,
    )
```

```python
import functools

import jax
import jax.numpy as jnp
from jax import lax
from jax.experimental import pallas as pl
from jax.experimental.pallas import tpu as pltpu
from jax.sharding import PartitionSpec as P

F32 = jnp.float32
BF16 = jnp.bfloat16
MESH = pl.DeviceIdType.MESH

HEADS = 12
HEAD_DIM = 64
FF = 3072
ADAM_STEP = 10


FIRST_DECAY = 0.9
SECOND_DECAY = 0.999
STAT_DECAY = 0.95
ADAM_EPSILON = 1e-08
NORM_EPSILON = 1e-05
MATRIX_RATE = 0.03
VECTOR_RATE = 0.2
WEIGHT_DECAY = 0.01


def assemble(blocks, row_count, column_count):
    block_side = blocks.shape[-1]
    shaped = blocks.reshape(row_count, column_count, block_side, block_side)
    return shaped.transpose(0, 2, 1, 3).reshape(row_count * block_side, column_count * block_side)


def split_blocks(matrix, row_count, column_count, block_side):
    shaped = matrix.reshape(row_count, block_side, column_count, block_side)
    return shaped.transpose(0, 2, 1, 3).reshape(row_count * column_count, block_side, block_side)


def layer_norm(values, gain_row, shift_row):
    center = jnp.mean(values, axis=-1, keepdims=True)
    centered = values - center
    spread = jnp.mean(centered * centered, axis=-1, keepdims=True)
    return centered * lax.rsqrt(spread + NORM_EPSILON) * gain_row + shift_row


def exact_gelu(hidden):
    return jax.nn.gelu(hidden, approximate=False)


def masked_scores(heads_query, heads_key, length):
    slots = heads_query.shape[0]
    scores = jnp.einsum(
        "qhd,khd->hqk", heads_query, heads_key, preferred_element_type=jnp.float32
    ) * HEAD_DIM ** (-0.5)
    visible = lax.iota(jnp.int32, slots) < length
    return jnp.where(visible[None, None, :], scores, -1e30)


def attend(pieces):
    query_rows, key_rows, value_rows, length = pieces
    slots = query_rows.shape[0]
    heads_query = query_rows.reshape(slots, HEADS, HEAD_DIM)
    heads_key = key_rows.reshape(slots, HEADS, HEAD_DIM)
    heads_value = value_rows.reshape(slots, HEADS, HEAD_DIM)
    scores = masked_scores(heads_query, heads_key, length)
    row_max = jnp.max(scores, axis=-1, keepdims=True)
    shifted = jnp.exp(scores - row_max)
    row_total = jnp.sum(shifted, axis=-1, keepdims=True)
    attention_weights = (shifted / row_total).astype(jnp.bfloat16)
    context = jnp.einsum(
        "hqk,khd->qhd", attention_weights, heads_value, preferred_element_type=jnp.float32
    )
    return (
        context.reshape(slots, -1).astype(jnp.bfloat16),
        row_max[..., 0] + jnp.log(row_total[..., 0]),
    )


def attend_back(pieces):
    query_rows, key_rows, value_rows, logsum, grad_context, length = pieces
    slots = query_rows.shape[0]
    heads_query = query_rows.reshape(slots, HEADS, HEAD_DIM)
    heads_key = key_rows.reshape(slots, HEADS, HEAD_DIM)
    heads_value = value_rows.reshape(slots, HEADS, HEAD_DIM)
    heads_grad = grad_context.reshape(slots, HEADS, HEAD_DIM)
    scores = masked_scores(heads_query, heads_key, length)
    attention_weights = jnp.exp(scores - logsum[..., None])
    weights_low = attention_weights.astype(jnp.bfloat16)
    grad_values = jnp.einsum(
        "hqk,qhd->khd", weights_low, heads_grad, preferred_element_type=jnp.float32
    )
    grad_weights = jnp.einsum(
        "qhd,khd->hqk", heads_grad, heads_value, preferred_element_type=jnp.float32
    )
    grad_scores = attention_weights * (
        grad_weights - jnp.sum(grad_weights * attention_weights, axis=-1, keepdims=True)
    )
    scores_low = grad_scores.astype(jnp.bfloat16)
    grad_query = jnp.einsum(
        "hqk,khd->qhd", scores_low, heads_key, preferred_element_type=jnp.float32
    ) * HEAD_DIM ** (-0.5)
    grad_keys = jnp.einsum(
        "hqk,qhd->khd", scores_low, heads_query, preferred_element_type=jnp.float32
    ) * HEAD_DIM ** (-0.5)
    return (
        grad_query.reshape(slots, -1).astype(jnp.bfloat16),
        grad_keys.reshape(slots, -1).astype(jnp.bfloat16),
        grad_values.reshape(slots, -1).astype(jnp.bfloat16),
    )


def dg(a,b,ca,cb):
    return lax.dot_general(a,b,(((ca,),(cb,)),((),())),preferred_element_type=F32)

def halves(a):
    hi=a.astype(BF16)
    return hi,(a-hi.astype(F32)).astype(BF16)

def mm3(a,b,ca,cb):
    ah,al=halves(a); bh,bl=halves(b)
    return dg(ah,bh,ca,cb)+(dg(ah,bl,ca,cb)+dg(al,bh,ca,cb))

def thirds(u):
    h=u.astype(BF16).astype(F32); r=u-h
    m=r.astype(BF16).astype(F32)
    return h,m,r-m

def factor_panels(aug, slots, side=128, between=None):
    sub=lax.broadcasted_iota(jnp.int32,(8,side),0)
    def spread(v): return jnp.broadcast_to(v,(8,side))
    for p in range(side//8):
        k=8*p
        if between is not None:
            between(p)
        panels=[]
        for s in range(slots):
            pw=aug[s,k:k+8,:side]; pv=aug[s,k:k+8,side:]
            cols=[spread(pw[:,k+i:k+i+1]) for i in range(8)]
            S=[[spread(cols[i][j:j+1,:]) if j>=i else None for i in range(8)] for j in range(8)]
            rw=[spread(pw[i:i+1,:]) for i in range(8)]
            rv=[spread(pv[i:i+1,:]) for i in range(8)]
            panels.append((S,rw,rv))
        for i in range(8):
            for S,rw,rv in panels:
                r=lax.rsqrt(S[i][i])
                for j in range(i+1,8): S[j][i]=S[j][i]*r
                for m in range(i+1,8):
                    for j in range(m,8):
                        S[j][m]=S[j][m]-S[j][i]*S[m][i]
                rw[i]=rw[i]*r; rv[i]=rv[i]*r
                for j in range(i+1,8):
                    rw[j]=rw[j]-S[j][i]*rw[i]
                    rv[j]=rv[j]-S[j][i]*rv[i]
        for s,(S,rw,rv) in enumerate(panels):
            uw,uv=rw[0],rv[0]
            for i in range(1,8):
                uw=jnp.where(sub==i,rw[i],uw); uv=jnp.where(sub==i,rv[i],uv)
            aug[s,k:k+8,side:]=uv
            if k+8<side:
                h,m,l=thirds(uw); vh,vm,vl=thirds(uv)
                a=jnp.concatenate([h,h,m,m,h,l],0).astype(BF16)
                b=jnp.concatenate([jnp.concatenate([h,m,h,m,l,h],0),jnp.concatenate([vh,vm,vh,vm,vl,vh],0)],1).astype(BF16)
                t=dg(a,b,0,0)
                aug[s,k+8:,:]=aug[s,k+8:,:]-t[k+8:,:]

def orthonormal_cols(mat, aug, slots, side=128):
    n=mat.shape[-1]
    r=lax.broadcasted_iota(jnp.int32,(side,side),0); c=lax.broadcasted_iota(jnp.int32,(side,side),1)
    eye=(r==c).astype(F32)
    steps=n//side
    for o in range(steps):
        lo=o*side
        for s in range(slots):
            mo=mat[s,:,lo:lo+side]
            aug[s,:,:side]=mm3(mo,mo,0,0)
            aug[s,:,side:]=eye
        factor_panels(aug,slots,side)
        for s in range(slots):
            q=mm3(mat[s,:,lo:lo+side],aug[s,:,side:],1,1)
            mat[s,:,lo:lo+side]=q
            if o+1<steps:
                rest=mat[s,:,lo+side:]
                mat[s,:,lo+side:]=rest-mm3(q,mm3(q,rest,0,0),1,0)


def soap_kernel(grad, stat, own, other, first, second, outer_out, basis_out, turned_out, update_out, mat, aug):
    slots = grad.shape[0]
    right_side = lax.rem(lax.axis_index("dp"), 2) == 1

    def run(is_right):
        near, far = (0, 1) if is_right else (1, 0)

        def one(s, carry):
            g = grad[s].astype(BF16)
            outer = dg(g, g, near, near)
            outer_out[s] = outer.astype(BF16)
            mixed = STAT_DECAY * stat[s].astype(F32) + (1.0 - STAT_DECAY) * outer
            high, rest = halves(mixed)
            mat[s] = dg(high, own[s], 1, 0) + dg(rest, own[s], 1, 0)
            left, right = (other[s], own[s]) if is_right else (own[s], other[s])
            rotated = dg(dg(left, g, 0, 0).astype(BF16), right, 1, 0)
            turned_out[s] = rotated.astype(BF16)
            first_new = FIRST_DECAY * first[s].astype(F32) + (1.0 - FIRST_DECAY) * rotated
            second_new = SECOND_DECAY * second[s].astype(F32) + (1.0 - SECOND_DECAY) * rotated * rotated
            direction = (
                first_new
                / (1.0 - FIRST_DECAY**ADAM_STEP)
                / (jnp.sqrt(second_new / (1.0 - SECOND_DECAY**ADAM_STEP)) + ADAM_EPSILON)
            )
            back = dg(left, direction.astype(BF16), 1, 0).astype(BF16)
            update_out[s] = dg(back, right, 1, 1).astype(BF16)
            return carry

        lax.fori_loop(0, slots, one, 0)

    @pl.when(right_side)
    def _():
        run(True)

    @pl.when(jnp.logical_not(right_side))
    def _():
        run(False)

    orthonormal_cols(mat, aug, slots)
    basis_out[...] = mat[...].astype(BF16)


def soap_blocks(grad, stat, own, other, first, second):
    slots, side, _ = grad.shape
    shape = jax.ShapeDtypeStruct(grad.shape, BF16)
    whole = pl.BlockSpec(memory_space=pltpu.VMEM)
    return pl.pallas_call(
        soap_kernel,
        out_shape=[shape] * 4,
        in_specs=[whole] * 6,
        out_specs=[whole] * 4,
        scratch_shapes=[
            pltpu.VMEM((slots, side, side), F32),
            pltpu.VMEM((slots, 128, 256), F32),
        ],
        compiler_params=pltpu.CompilerParams(vmem_limit_bytes=48 * 2**20),
        name="soap_blocks",
    )(grad, stat, own, other, first, second)


def ring_place(chip, chips):
    along, across = chip // 2, lax.rem(chip, 2)
    return along * (1 - across) + (chips - 1 - along) * across


def ring_chip(place, chips):
    place = lax.rem(place + 8 * chips, chips)
    across = place // (chips // 2)
    along = place * (1 - across) + (chips - 1 - place) * across
    return 2 * along + across


def whereabouts(chips):
    device, replica = lax.axis_index("fsdp"), lax.axis_index("dp")
    chip, core = device // 2, lax.rem(device, 2)
    place = ring_place(chip, chips)
    turn = 1 - 2 * core
    after = (2 * ring_chip(place + turn, chips) + core, replica)
    before = (2 * ring_chip(place - turn, chips) + core, replica)
    sibling = (2 * chip + 1 - core, replica)
    return device, replica, chip, core, place, turn, after, before, sibling


def greet(neighbours):
    barrier = pltpu.get_barrier_semaphore()
    for neighbour in neighbours:
        pl.semaphore_signal(barrier, inc=1, device_id=neighbour, device_id_type=MESH)
    pl.semaphore_wait(barrier, len(neighbours))


def gather_kernel(chips, share, mat_ref, vec_ref, attn, up, down, vecs, raw_a, raw_u, raw_d, low_a, low_u, low_d,
                  low_v, trade_send, trade_recv, own_sem, ring_send, ring_recv, sib_send, sib_recv, cross_send, cross_recv,
                  vec_send, vec_recv, vec_sib_send, vec_sib_recv):
    device, replica, chip, core, place, turn, after, before, sibling = whereabouts(chips)
    mirror = (device, 1 - replica)
    side = mat_ref.shape[-1]
    both = 2 * share
    rows = pl.ds(pl.multiple_of(share * core, 8), share)
    greet((after, before, sibling, mirror))
    groups = ((raw_a, low_a, attn), (raw_u, low_u, up), (raw_d, low_d, down))
    trades = []
    for g, (raw, low, out) in enumerate(groups):
        for b in range(16):
            if g == 0:
                raw[(b % 4) // 2, rows, (b // 4) * 2 * side + (b % 2) * side : (b // 4) * 2 * side + (b % 2 + 1) * side] = mat_ref[b]
            elif g == 1:
                raw[b // 8, rows, (b % 8) * side : (b % 8 + 1) * side] = mat_ref[16 + b]
            else:
                raw[b // 2, rows, (b % 2) * side : (b % 2 + 1) * side] = mat_ref[32 + b]
        part = raw.at[:, rows, :]
        trade = pltpu.make_async_remote_copy(
            src_ref=part, dst_ref=part, send_sem=trade_send.at[g], recv_sem=trade_recv.at[g],
            device_id=sibling, device_id_type=MESH)
        trade.start()
        trades.append(trade)
    low_v[...] = vec_ref[...].astype(BF16).astype(F32)

    def units(kind):
        return ((6 * replica + core, 1), (2 + 2 * core, 2), (6 * (1 - replica) + core, 1))[kind]

    def cut(ref, g, row, kind):
        first, number = units(kind)
        if g == 2:
            return ref.at[pl.ds(first, number), row, :]
        return ref.at[:, row, pl.ds(pl.multiple_of(first * side, 128), number * side)]

    def slab(g, origin, kind):
        return cut(groups[g][2], g, pl.ds(pl.multiple_of(origin * both, 16), both), kind)

    def forward(g, t, kind, origin, source):
        return pltpu.make_async_remote_copy(
            src_ref=source, dst_ref=slab(g, origin, kind), send_sem=ring_send.at[t, g, kind],
            recv_sem=ring_recv.at[t, g, kind], device_id=after, device_id_type=MESH)

    def pass_on(g, t, kind, origin):
        part = slab(g, origin, kind)
        return pltpu.make_async_remote_copy(
            src_ref=part, dst_ref=part, send_sem=sib_send.at[t, g, kind], recv_sem=sib_recv.at[t, g, kind],
            device_id=sibling, device_id_type=MESH)

    def across(g, t, origin, kind):
        part = slab(g, origin, kind)
        return pltpu.make_async_remote_copy(
            src_ref=part, dst_ref=part, send_sem=cross_send.at[t, g], recv_sem=cross_recv.at[t, g],
            device_id=mirror, device_id_type=MESH)

    def vec_of(origin):
        return vecs.at[2 * origin + core]

    def vec_forward(t, origin, source):
        return pltpu.make_async_remote_copy(
            src_ref=source, dst_ref=vec_of(origin), send_sem=vec_send.at[t], recv_sem=vec_recv.at[t],
            device_id=after, device_id_type=MESH)

    def vec_pass_on(t, origin, source):
        return pltpu.make_async_remote_copy(
            src_ref=source, dst_ref=vec_of(origin), send_sem=vec_sib_send.at[t], recv_sem=vec_sib_recv.at[t],
            device_id=sibling, device_id_type=MESH)

    vec_forward(0, chip, low_v).start()
    vec_pass_on(0, chip, low_v).start()
    owns = [pltpu.make_async_copy(low_v, vec_of(chip), own_sem.at[3])]
    owns[0].start()
    for g, (raw, low, out) in enumerate(groups):
        trades[g].wait()
        low[...] = raw[...].astype(BF16)
        for kind in range(2):
            forward(g, 0, kind, chip, cut(low, g, slice(None), kind)).start()
        own = pltpu.make_async_copy(low, out.at[:, pl.ds(pl.multiple_of(chip * both, 16), both), :], own_sem.at[g])
        own.start()
        owns.append(own)

    def take_crossed(t):
        origin = ring_chip(place - turn * t, chips)
        for g in range(3):
            across(g, t, origin, 2).wait_recv()
            pass_on(g, t, 2, origin).start()

    def step(t, carry):
        origin = ring_chip(place - turn * t, chips)
        vec_forward(t - 1, origin, vec_of(origin)).wait_recv()

        @pl.when(t < chips - 1)
        def _():
            vec_forward(t, origin, vec_of(origin)).start()

        vec_pass_on(t, origin, vec_of(origin)).start()
        for g in range(3):
            for kind in range(2):
                arrived = slab(g, origin, kind)
                forward(g, t - 1, kind, origin, arrived).wait_recv()

                @pl.when(t < chips - 1)
                def _():
                    forward(g, t, kind, origin, arrived).start()

                if kind == 0:
                    across(g, t, origin, 0).start()
                pass_on(g, t, kind, origin).start()

        @pl.when(t > 1)
        def _():
            take_crossed(t - 1)
        return carry

    lax.fori_loop(1, chips, step, 0)
    take_crossed(chips - 1)
    for own in owns:
        own.wait()

    def finish(t, carry):
        @pl.when(t < chips - 1)
        def _():
            vec_forward(t, chip, vec_of(chip)).wait_send()

        vec_pass_on(t, chip, vec_of(chip)).wait()
        for g in range(3):
            @pl.when(t < chips - 1)
            def _():
                for kind in range(2):
                    forward(g, t, kind, chip, slab(g, chip, kind)).wait_send()

            @pl.when(t > 0)
            def _():
                across(g, t, chip, 0).wait_send()
                for kind in range(3):
                    pass_on(g, t, kind, chip).wait()
        return carry

    lax.fori_loop(0, chips, finish, 0)


def gather_weights(matrices, vector_tile, chips):
    total, share, side = matrices.shape
    both = 2 * share
    anywhere = pl.BlockSpec(memory_space=pl.ANY)
    whole = pl.BlockSpec(memory_space=pltpu.VMEM)
    dma = pltpu.SemaphoreType.DMA
    return pl.pallas_call(
        functools.partial(gather_kernel, chips, share),
        out_shape=[
            jax.ShapeDtypeStruct((2, side, 8 * side), BF16),
            jax.ShapeDtypeStruct((2, side, 8 * side), BF16),
            jax.ShapeDtypeStruct((8, side, 2 * side), BF16),
            jax.ShapeDtypeStruct((2 * chips, 8, 128), F32),
        ],
        in_specs=[whole, whole],
        out_specs=[anywhere] * 4,
        scratch_shapes=[
            pltpu.VMEM((2, both, 8 * side), F32),
            pltpu.VMEM((2, both, 8 * side), F32),
            pltpu.VMEM((8, both, 2 * side), F32),
            pltpu.VMEM((2, both, 8 * side), BF16),
            pltpu.VMEM((2, both, 8 * side), BF16),
            pltpu.VMEM((8, both, 2 * side), BF16),
            pltpu.VMEM((8, 128), F32),
            dma((3,)), dma((3,)), dma((4,)),
            dma((chips - 1, 3, 2)), dma((chips - 1, 3, 2)), dma((chips, 3, 3)), dma((chips, 3, 3)),
            dma((chips, 3)), dma((chips, 3)),
            dma((chips - 1,)), dma((chips - 1,)), dma((chips,)), dma((chips,)),
        ],
        compiler_params=pltpu.CompilerParams(collective_id=1, has_side_effects=True, vmem_limit_bytes=40 * 2**20),
        name="gather_weights",
    )(matrices, vector_tile)


def reduce_kernel(chips, g_qkv, g_out, g_up, g_down, g_vec, owned, vec_sum, mine, theirs, ring, crossed, peer, vmine, vring,
                  vpeer, mine_sem, sib_send, sib_recv, ring_send, ring_recv, cross_send, cross_recv, peer_send, peer_recv):
    device, replica, chip, core, place, turn, after, before, sibling = whereabouts(chips)
    mirror = (device, 1 - replica)
    side = mine.shape[-1]
    quarter = side // 4
    last = chips - 1
    greet((after, before, sibling, mirror))

    def quarters(first, number):
        return pl.ds(pl.multiple_of(first * quarter, 16), number * quarter)

    carried = quarters(replica, 3)
    private = quarters(3 * replica, 1)
    foreign = quarters(3 * (1 - replica), 1)

    def column(index):
        return pl.ds(pl.multiple_of(index * side, 128), side)

    def fetch(owner, start):
        which = owner // 4
        i, j = lax.rem(owner, 4) // 2, lax.rem(owner, 2)

        @pl.when(which < 3)
        def _():
            start(0, g_qkv.at[i, :, column(2 * which + j)])

        @pl.when(which == 3)
        def _():
            start(0, g_out.at[i, :, column(j)])

        start(1, g_up.at[owner // 8, :, column(lax.rem(owner, 8))])
        start(2, g_down.at[owner // 2, :, column(lax.rem(owner, 2))])
        start(3, g_vec.at[owner])

    def local(t, slot, source):
        target = vmine.at[0, t] if slot == 3 else mine.at[t, slot]
        return pltpu.make_async_copy(source, target, mine_sem.at[t, slot])

    def to_sibling(t, slot, source):
        target = vmine.at[1, t] if slot == 3 else theirs.at[t, slot]
        return pltpu.make_async_remote_copy(
            src_ref=source, dst_ref=target, send_sem=sib_send.at[t, slot], recv_sem=sib_recv.at[t, slot],
            device_id=sibling, device_id_type=MESH)

    def to_next(t, slot):
        source, target = (vmine.at[0, t], vring.at[t]) if slot == 3 else (mine.at[t, slot, carried, :], ring.at[t, slot])
        return pltpu.make_async_remote_copy(
            src_ref=source, dst_ref=target, send_sem=ring_send.at[t, slot], recv_sem=ring_recv.at[t, slot],
            device_id=after, device_id_type=MESH)

    def across(t, slot):
        return pltpu.make_async_remote_copy(
            src_ref=mine.at[t, slot, foreign, :], dst_ref=crossed.at[t, slot], send_sem=cross_send.at[t, slot],
            recv_sem=cross_recv.at[t, slot], device_id=mirror, device_id_type=MESH)

    def to_mirror(slot):
        source, target = (vmine.at[0, last], vpeer) if slot == 3 else (mine.at[last, slot, carried, :], peer.at[slot, carried, :])
        return pltpu.make_async_remote_copy(
            src_ref=source, dst_ref=target, send_sem=peer_send.at[slot], recv_sem=peer_recv.at[slot],
            device_id=mirror, device_id_type=MESH)

    def begin(t):
        fetch(2 * ring_chip(place + turn * (t + 1), chips) + 1 - core, lambda slot, source: to_sibling(t, slot, source).start())
        fetch(2 * ring_chip(place - turn * (t + 1), chips) + core, lambda slot, source: local(t, slot, source).start())

    def sources(slot):
        return g_vec.at[0] if slot == 3 else g_up.at[0, :, :side]

    def pair(t):
        for slot in (3, 0, 1, 2):
            local(t, slot, sources(slot)).wait()
            to_sibling(t, slot, sources(slot)).wait_recv()
            if slot == 3:
                vmine[0, t] = vmine[0, t] + vmine[1, t]
            else:
                mine[t, slot] = (mine[t, slot].astype(F32) + theirs[t, slot].astype(F32)).astype(BF16)
                across(t, slot).start()

    def add(t, slot, hold, extra):
        mine[t, slot, hold, :] = (mine[t, slot, hold, :].astype(F32) + extra.astype(F32)).astype(BF16)

    def step(t, carry):
        @pl.when(t + 2 < chips)
        def _():
            begin(t + 2)

        @pl.when(t + 1 < chips)
        def _():
            pair(t + 1)

        for slot in (3, 0, 1, 2):
            if slot < 3:
                across(t, slot).wait_recv()
                add(t, slot, private, crossed[t, slot])

            @pl.when(t > 0)
            def _():
                to_next(t - 1, slot).wait_recv()
                if slot == 3:
                    vmine[0, t] = vmine[0, t] + vring[t - 1]
                else:
                    add(t, slot, carried, ring[t - 1, slot])

            @pl.when(t < last)
            def _():
                to_next(t, slot).start()

            @pl.when(t == last)
            def _():
                to_mirror(slot).start()
        return carry

    begin(0)
    begin(1)
    pair(0)
    lax.fori_loop(0, chips, step, 0)
    for slot in (3, 0, 1, 2):
        to_mirror(slot).wait()
        if slot == 3:
            vec_sum[...] = vmine[0, last] + vpeer[...]
        else:
            shared = slice(quarter, 3 * quarter)
            owned[slot, shared, :] = (mine[last, slot, shared, :].astype(F32) + peer[slot, shared, :].astype(F32)).astype(BF16)
            owned[slot, private, :] = mine[last, slot, private, :]
            owned[slot, foreign, :] = peer[slot, foreign, :]

    def finish(t, carry):
        for slot in range(4):
            to_sibling(t, slot, sources(slot)).wait_send()
            if slot < 3:
                across(t, slot).wait_send()

            @pl.when(t < last)
            def _():
                to_next(t, slot).wait_send()
        return carry

    lax.fori_loop(0, chips, finish, 0)


def reduce_gradients(g_qkv, g_out, g_up, g_down, g_vec, chips):
    side = g_up.shape[1]
    anywhere = pl.BlockSpec(memory_space=pl.ANY)
    whole = pl.BlockSpec(memory_space=pltpu.VMEM)
    dma = pltpu.SemaphoreType.DMA
    return pl.pallas_call(
        functools.partial(reduce_kernel, chips),
        out_shape=[jax.ShapeDtypeStruct((3, side, side), BF16), jax.ShapeDtypeStruct((8, 128), F32)],
        in_specs=[anywhere] * 5,
        out_specs=[whole] * 2,
        scratch_shapes=[
            pltpu.VMEM((chips, 3, side, side), BF16),
            pltpu.VMEM((chips, 3, side, side), BF16),
            pltpu.VMEM((chips - 1, 3, 3 * side // 4, side), BF16),
            pltpu.VMEM((chips, 3, side // 4, side), BF16),
            pltpu.VMEM((3, side, side), BF16),
            pltpu.VMEM((2, chips, 8, 128), F32),
            pltpu.VMEM((chips - 1, 8, 128), F32),
            pltpu.VMEM((8, 128), F32),
            dma((chips, 4)), dma((chips, 4)), dma((chips, 4)),
            dma((chips - 1, 4)), dma((chips - 1, 4)), dma((chips, 3)), dma((chips, 3)), dma((4,)), dma((4,)),
        ],
        compiler_params=pltpu.CompilerParams(collective_id=2, has_side_effects=True, vmem_limit_bytes=48 * 2**20),
        name="reduce_gradients",
    )(g_qkv, g_out, g_up, g_down, g_vec)


def opposite(device, step, count):
    result, bit = 0, 1
    while bit < count:
        one, two = lax.rem(device // bit, 2), lax.rem(step // bit, 2)
        result = result + bit * (one + two - 2 * one * two)
        bit *= 2
    return result


def renew_kernel(count, share, grad, stat, own, other, first, second, early, late, items, mat, aug, out_early, out_late,
                 early_send, early_recv, early_own, late_send, late_recv, late_own,
                 cross_send, cross_recv, cross_late_send, cross_late_recv):
    device, replica = lax.axis_index("fsdp"), lax.axis_index("dp")
    mirror = (device, 1 - replica)
    slots, side, _ = grad.shape
    part = 128

    def partner(step):
        return opposite(device, step, count), replica

    barrier = pltpu.get_barrier_semaphore()

    def hail(step, carry):
        pl.semaphore_signal(barrier, inc=1, device_id=partner(step), device_id_type=MESH)
        return carry

    lax.fori_loop(1, count, hail, 0)
    pl.semaphore_signal(barrier, inc=1, device_id=mirror, device_id_type=MESH)
    pl.semaphore_wait(barrier, count)

    def run(is_right):
        near, far = (0, 1) if is_right else (1, 0)

        def outer_one(s, carry):
            g = grad[s]
            outer = dg(g, g, near, near)
            items[s] = outer
            mixed = STAT_DECAY * stat[s].astype(F32) + (1.0 - STAT_DECAY) * outer
            high, rest = halves(mixed)
            mat[s] = dg(high, own[s], 1, 0) + dg(rest, own[s], 1, 0)
            return carry

        lax.fori_loop(0, slots, outer_one, 0)
        for e, s in enumerate((1, 2) if is_right else (0, 2)):
            left, right = (other[e], own[s]) if is_right else (own[s], other[e])
            rotated = dg(dg(left, grad[s], 0, 0).astype(BF16), right, 1, 0)
            if e == 0:
                items[3] = rotated
            elif not is_right:
                items[5] = rotated
                continue
            first_new = FIRST_DECAY * first[e].astype(F32) + (1.0 - FIRST_DECAY) * rotated
            second_new = SECOND_DECAY * second[e].astype(F32) + (1.0 - SECOND_DECAY) * rotated * rotated
            direction = (
                first_new
                / (1.0 - FIRST_DECAY**ADAM_STEP)
                / (jnp.sqrt(second_new / (1.0 - SECOND_DECAY**ADAM_STEP)) + ADAM_EPSILON)
            )
            back = dg(left, direction.astype(BF16), 1, 0).astype(BF16)
            items[4 + e] = dg(back, right, 1, 1)

    @pl.when(replica == 1)
    def _():
        run(True)

    @pl.when(replica == 0)
    def _():
        run(False)

    def rows_of(holder):
        return pl.ds(pl.multiple_of(holder * share, 8), share)

    def pack_early(holder, carry):
        for pair in range(3):
            two = jnp.concatenate([items[2 * pair, rows_of(holder), :], items[2 * pair + 1, rows_of(holder), :]], axis=0)
            out_early[holder, 2 * share * pair : 2 * share * (pair + 1), :] = two.astype(BF16)
        return carry

    def send_early(step, target):
        return pltpu.make_async_remote_copy(
            src_ref=out_early.at[target[0]], dst_ref=early.at[replica, device], send_sem=early_send.at[step],
            recv_sem=early_recv.at[step], device_id=target, device_id_type=MESH)

    def send_late(panel, step, target):
        return pltpu.make_async_remote_copy(
            src_ref=out_late.at[panel, target[0]], dst_ref=late.at[panel, replica, device],
            send_sem=late_send.at[panel, step], recv_sem=late_recv.at[panel, step], device_id=target, device_id_type=MESH)

    def cross_early(step):
        block = early.at[replica, partner(step)[0]]
        return pltpu.make_async_remote_copy(
            src_ref=block, dst_ref=block, send_sem=cross_send.at[step], recv_sem=cross_recv.at[step],
            device_id=mirror, device_id_type=MESH)

    def cross_late(panel, step):
        block = late.at[panel, replica, partner(step)[0]]
        return pltpu.make_async_remote_copy(
            src_ref=block, dst_ref=block, send_sem=cross_late_send.at[panel, step], recv_sem=cross_late_recv.at[panel, step],
            device_id=mirror, device_id_type=MESH)

    def keep_early():
        return pltpu.make_async_copy(out_early.at[device], early.at[replica, device], early_own)

    def keep_late(panel):
        return pltpu.make_async_copy(out_late.at[panel, device], late.at[panel, replica, device], late_own.at[panel])

    lax.fori_loop(0, count, pack_early, 0)

    def launch_early(index, carry):
        step = index + 1
        send_early(step, partner(step)).start()
        return carry

    lax.fori_loop(0, count - 1, launch_early, 0)
    keep_early().start()

    def relay_early(step):
        if step == 0:
            keep_early().wait()
        else:
            send_early(step, partner(step)).wait_recv()
        cross_early(step).start()

    relayed = []

    def between(moment):
        if moment % 4 == 0 and len(relayed) < min(count, 11):
            relay_early(len(relayed))
            relayed.append(moment)

    row_index = lax.broadcasted_iota(jnp.int32, (part, part), 0)
    column_index = lax.broadcasted_iota(jnp.int32, (part, part), 1)
    eye = (row_index == column_index).astype(F32)
    panels = side // part
    for o in range(panels):
        lo = o * part
        for s in range(slots):
            block = mat[s, :, lo : lo + part]
            aug[s, :, :part] = mm3(block, block, 0, 0)
            aug[s, :, part:] = eye
        factor_panels(aug, slots, part, lambda p: between(16 * o + p))
        for s in range(slots):
            mat[s, :, lo : lo + part] = mm3(mat[s, :, lo : lo + part], aug[s, :, part:], 1, 1)

        def pack_late(holder, carry):
            rows = rows_of(holder)
            stacked = [mat[s, rows, lo : lo + part] for s in range(slots)]
            stacked.append(jnp.zeros((8, part), F32))
            out_late[o, holder] = jnp.concatenate(stacked, axis=0).astype(BF16)
            return carry

        lax.fori_loop(0, count, pack_late, 0)

        def launch_late(index, carry):
            step = index + 1
            send_late(o, step, partner(step)).start()
            return carry

        lax.fori_loop(0, count - 1, launch_late, 0)
        keep_late(o).start()
        if o + 1 < panels:
            for s in range(slots):
                q, rest = mat[s, :, lo : lo + part], mat[s, :, lo + part :]
                mat[s, :, lo + part :] = rest - mm3(q, mm3(q, rest, 0, 0), 1, 0)
    for step in range(len(relayed), count):
        relay_early(step)
    for o in range(panels):
        keep_late(o).wait()
        cross_late(o, 0).start()

        def relay_late(step, carry):
            send_late(o, step, partner(step)).wait_recv()
            cross_late(o, step).start()
            return carry

        lax.fori_loop(1, count, relay_late, 0)

    def finish(step, carry):
        cross_early(step).wait()
        for o in range(panels):
            cross_late(o, step).wait()

        @pl.when(step > 0)
        def _():
            send_early(step, partner(step)).wait_send()
            for o in range(panels):
                send_late(o, step, partner(step)).wait_send()
        return carry

    lax.fori_loop(0, count, finish, 0)


def renew_blocks(grad, stat, own, other, first, second, count, share):
    slots, side, _ = grad.shape
    anywhere = pl.BlockSpec(memory_space=pl.ANY)
    whole = pl.BlockSpec(memory_space=pltpu.VMEM)
    dma = pltpu.SemaphoreType.DMA
    tall = -(-slots * share // 16) * 16
    panels = side // 128
    return pl.pallas_call(
        functools.partial(renew_kernel, count, share),
        out_shape=[
            jax.ShapeDtypeStruct((2, count, 6 * share, side), BF16),
            jax.ShapeDtypeStruct((panels, 2, count, tall, 128), BF16),
        ],
        in_specs=[whole] * 6,
        out_specs=[anywhere] * 2,
        scratch_shapes=[
            pltpu.VMEM((6, side, side), F32),
            pltpu.VMEM((slots, side, side), F32),
            pltpu.VMEM((slots, 128, 256), F32),
            pltpu.VMEM((count, 6 * share, side), BF16),
            pltpu.VMEM((panels, count, tall, 128), BF16),
            dma((count,)), dma((count,)), dma,
            dma((panels, count)), dma((panels, count)), dma((panels,)),
            dma((count,)), dma((count,)), dma((panels, count)), dma((panels, count)),
        ],
        compiler_params=pltpu.CompilerParams(collective_id=3, has_side_effects=True, vmem_limit_bytes=48 * 2**20),
        name="renew_blocks",
    )(grad, stat, own, other, first, second)


def settle_kernel(early, late, mat, first, second, left, right, mat_new, mat_low, first_new, second_new, left_new, right_new,
                  left_basis, right_basis):
    share = mat.shape[2]
    for s in range(3):
        def item(plane, index):
            return early[plane, 0, index * share : (index + 1) * share, :].astype(F32)

        turned = (item(0, 3), item(1, 3), item(0, 5))[s]
        update = (item(0, 4), item(1, 4), item(1, 5))[s]
        fresh = mat[s, 0] - MATRIX_RATE * (update + WEIGHT_DECAY * mat[s, 0])
        mat_new[s, 0] = fresh
        mat_low[s, 0] = fresh.astype(BF16)
        first_new[s, 0] = FIRST_DECAY * first[s, 0] + (1.0 - FIRST_DECAY) * turned
        second_new[s, 0] = SECOND_DECAY * second[s, 0] + (1.0 - SECOND_DECAY) * turned * turned
        left_new[s, 0] = STAT_DECAY * left[s, 0] + (1.0 - STAT_DECAY) * item(0, s)
        right_new[s, 0] = STAT_DECAY * right[s, 0] + (1.0 - STAT_DECAY) * item(1, s)
        for panel in range(late.shape[0]):
            lanes = slice(128 * panel, 128 * (panel + 1))
            left_basis[s, 0, :, lanes] = late[panel, 0, 0, s * share : (s + 1) * share, :].astype(F32)
            right_basis[s, 0, :, lanes] = late[panel, 1, 0, s * share : (s + 1) * share, :].astype(F32)


def settle(early, late, matrices, first, second, left, right):
    _, count, tall, side = early.shape
    panels, share = late.shape[0], matrices.shape[1]
    state = pl.BlockSpec((3, 1, share, side), lambda f: (0, f, 0, 0))
    shape = jax.ShapeDtypeStruct((3, count, share, side), F32)
    low = jax.ShapeDtypeStruct((3, count, share, side), BF16)
    results = pl.pallas_call(
        settle_kernel,
        grid=(count,),
        out_shape=[shape, low] + [shape] * 6,
        in_specs=[
            pl.BlockSpec((2, 1, tall, side), lambda f: (0, f, 0, 0)),
            pl.BlockSpec((panels, 2, 1, late.shape[3], 128), lambda f: (0, 0, f, 0, 0)),
        ]
        + [state] * 5,
        out_specs=[state] * 8,
        compiler_params=pltpu.CompilerParams(vmem_limit_bytes=32 * 2**20),
        name="settle",
    )(early, late, *[part.reshape(3, count, share, side) for part in (matrices, first, second, left, right)])
    return [part.reshape(matrices.shape) for part in results]


def plain_gather(matrices, vectors):
    side = matrices.shape[-1]
    blocks = lax.all_gather(matrices.astype(BF16), "fsdp", axis=1, tiled=True)
    attn = jnp.concatenate([assemble(blocks[4 * part : 4 * part + 4], 2, 2) for part in range(4)], axis=1)
    up = assemble(blocks[16:32], 2, 8)
    down = assemble(blocks[32:], 8, 2)
    rows = lax.all_gather(vectors.astype(BF16), "fsdp", axis=0, tiled=True)
    return attn, up, down, rows.astype(F32).reshape(-1, 2 * side)


def plain_reduce(grad_qkv, grad_out, grad_up, grad_down, vector_grad, capacity):
    shard_count = lax.axis_size("fsdp")
    width = grad_up.shape[0]
    side = width // 2
    blocks = jnp.concatenate(
        [split_blocks(grad_qkv[:, part * width : (part + 1) * width], 2, 2, side) for part in range(3)]
        + [split_blocks(grad_out, 2, 2, side), split_blocks(grad_up, 2, 8, side), split_blocks(grad_down, 8, 2, side)],
        axis=0,
    )
    owned = lax.psum_scatter(
        to_owners(blocks, capacity, shard_count), "fsdp", scatter_dimension=1, tiled=True
    )
    owned = lax.psum(owned, "dp")[:, 0]
    share = lax.psum_scatter(vector_grad, "fsdp", scatter_dimension=0, tiled=True)
    return owned, lax.psum(share, "dp")


def to_owners(blocks, capacity, shard_count):
    spare = capacity * shard_count - blocks.shape[0]
    blocks = jnp.pad(blocks, ((0, spare),) + ((0, 0),) * (blocks.ndim - 1))
    return blocks.reshape((capacity, shard_count) + blocks.shape[1:])


def shards(
    tokens,
    cotangent,
    lengths,
    matrices,
    first_moment,
    second_moment,
    left_stat,
    right_stat,
    left_basis,
    right_basis,
    vectors,
    vector_first,
    vector_second,
):
    shard_count = lax.axis_size("fsdp")
    replicas = lax.axis_size("dp")
    sequences, slots, model_width = tokens.shape
    block_total, share_rows, block_side = matrices.shape
    unit_ratio = FF // model_width
    rows_total = sequences * slots
    capacity = -(-block_total // shard_count)
    ringed = replicas == 2 and capacity * shard_count == block_total == 48 and share_rows % 8 == 0 and capacity == 3
    vector_share = vectors.shape[0]

    def shaped(array):
        return array.reshape(sequences, slots, array.shape[-1])

    right_side = lax.axis_index("dp") % 2 == 1
    chosen = [
        jnp.where(right_side, right_stat, left_stat),
        jnp.where(right_side, right_basis, left_basis),
    ]
    turning = [jnp.where(right_side, left_basis, right_basis), first_moment, second_moment]
    if ringed:
        split = [part.reshape(capacity, shard_count, share_rows, block_side) for part in chosen + turning]
        states = jnp.concatenate(
            [part.astype(BF16) for part in split[:2]]
            + [
                piece.astype(BF16)
                for part in split[2:]
                for piece in (jnp.where(right_side, part[1:2], part[0:1]), part[2:])
            ]
        )
    else:
        states = jnp.stack([to_owners(part.astype(BF16), capacity, shard_count) for part in chosen + turning])

    if ringed:
        vector_tile = jnp.pad(vectors, (0, 1024 - vector_share)).reshape(8, 128)
        attn, up, down, vector_tiles = gather_weights(matrices, vector_tile, shard_count // 2)
        attn = attn.reshape(model_width, 4 * model_width)
        up = up.reshape(model_width, FF)
        down = down.reshape(FF, model_width)
        states, attn = lax.optimization_barrier((states, attn))
        states = lax.all_to_all(states, "fsdp", split_axis=1, concat_axis=2, tiled=True)[:, 0]
        vector_rows = vector_tiles.reshape(shard_count, 1024)[:, :vector_share].reshape(-1, model_width)
    else:
        attn, up, down, vector_rows = plain_gather(matrices, vectors)
        states = lax.all_to_all(states, "fsdp", split_axis=2, concat_axis=3, tiled=True)[:, :, 0]
    weight_qkv, weight_out = attn[:, : 3 * model_width], attn[:, 3 * model_width :]
    inputs = tokens.reshape(rows_total, model_width)
    joined = jnp.dot(inputs, weight_qkv, preferred_element_type=F32)
    query_rows = (joined[:, :model_width] + vector_rows[0]).astype(BF16)
    key_rows = joined[:, model_width : 2 * model_width].astype(BF16)
    value_rows = (joined[:, 2 * model_width :] + vector_rows[1]).astype(BF16)
    context, logsum = lax.map(
        attend, (shaped(query_rows), shaped(key_rows), shaped(value_rows), lengths)
    )
    context = context.reshape(rows_total, model_width)
    attended = jnp.dot(context, weight_out, preferred_element_type=F32) + vector_rows[2]
    normed, pull_one = jax.vjp(
        layer_norm, inputs.astype(F32) + attended, vector_rows[3], vector_rows[4]
    )
    normed_low = normed.astype(BF16)
    hidden = jnp.dot(normed_low, up, preferred_element_type=F32) + vector_rows[
        5 : 5 + unit_ratio
    ].reshape(FF)
    active, pull_gelu = jax.vjp(exact_gelu, hidden)
    active_low = active.astype(BF16)
    result = jnp.dot(active_low, down, preferred_element_type=F32) + vector_rows[5 + unit_ratio]
    output, pull_two = jax.vjp(
        layer_norm, normed + result, vector_rows[6 + unit_ratio], vector_rows[7 + unit_ratio]
    )
    block_out = output.reshape(sequences, slots, model_width).astype(BF16)
    visible = (lax.iota(jnp.int32, slots)[None, :] < lengths[:, None]).astype(F32)
    grad_output = (cotangent.astype(F32) * visible[:, :, None]).reshape(rows_total, model_width)
    grad_second, grad_gain_two, grad_shift_two = pull_two(grad_output)
    second_low = grad_second.astype(BF16)
    grad_down = jnp.einsum("tf,td->fd", active_low, second_low, preferred_element_type=F32)
    grad_active = jnp.einsum("td,fd->tf", second_low, down, preferred_element_type=F32)
    (grad_hidden,) = pull_gelu(grad_active)
    hidden_low = grad_hidden.astype(BF16)
    grad_up = jnp.einsum("td,tf->df", normed_low, hidden_low, preferred_element_type=F32)
    grad_normed = grad_second + jnp.einsum("tf,df->td", hidden_low, up, preferred_element_type=F32)
    grad_mixed, grad_gain_one, grad_shift_one = pull_one(grad_normed)
    mixed_low = grad_mixed.astype(BF16)
    grad_out_weight = jnp.einsum("td,te->de", context, mixed_low, preferred_element_type=F32)
    grad_context = jnp.einsum(
        "te,de->td", mixed_low, weight_out, preferred_element_type=F32
    ).astype(BF16)
    grad_query, grad_keys, grad_values = lax.map(
        attend_back,
        (
            shaped(query_rows),
            shaped(key_rows),
            shaped(value_rows),
            logsum,
            shaped(grad_context),
            lengths,
        ),
    )
    grad_joined = jnp.concatenate(
        [
            grad_query.reshape(rows_total, model_width),
            grad_keys.reshape(rows_total, model_width),
            grad_values.reshape(rows_total, model_width),
        ],
        axis=1,
    )
    grad_qkv = jnp.einsum("td,te->de", inputs, grad_joined, preferred_element_type=F32)
    input_grad = grad_mixed + jnp.einsum(
        "te,de->td", grad_joined, weight_qkv, preferred_element_type=F32
    )
    vector_grad = jnp.concatenate(
        [
            jnp.sum(grad_joined[:, :model_width], axis=0, dtype=F32)[None],
            jnp.sum(grad_joined[:, 2 * model_width :], axis=0, dtype=F32)[None],
            jnp.sum(grad_mixed, axis=0)[None],
            grad_gain_one[None],
            grad_shift_one[None],
            jnp.sum(grad_hidden, axis=0).reshape(unit_ratio, model_width),
            jnp.sum(grad_second, axis=0)[None],
            grad_gain_two[None],
            grad_shift_two[None],
        ],
        axis=0,
    ).reshape(-1)
    weight_grads = [part.astype(BF16) for part in (grad_qkv, grad_out_weight, grad_up, grad_down)]
    if ringed:
        tiles = jnp.pad(
            vector_grad.reshape(shard_count, vector_share), ((0, 0), (0, 1024 - vector_share))
        ).reshape(shard_count, 8, 128)
        slabs = [part.reshape(-1, block_side, part.shape[1]) for part in weight_grads]
        owned, vector_sum = reduce_gradients(*slabs, tiles, shard_count // 2)
        vector_sum = vector_sum.reshape(1024)[:vector_share]
    else:
        owned, vector_sum = plain_reduce(*weight_grads, vector_grad, capacity)
    if ringed:
        early, late = renew_blocks(
            owned, states[0:3], states[3:6], states[6:8], states[8:10], states[10:12], shard_count, share_rows
        )
        local = settle(early, late, matrices, first_moment, second_moment, left_stat, right_stat)
    else:
        filler = (lax.iota(jnp.int32, capacity) * shard_count + lax.axis_index("fsdp")) >= block_total
        stat = jnp.where(
            filler[:, None, None], jnp.eye(block_side, dtype=jnp.bfloat16), states[0]
        )
        basis = jnp.where(
            filler[:, None, None], jnp.eye(block_side, dtype=jnp.bfloat16), states[1]
        )
        outer, new_basis, turned, update = soap_blocks(
            owned, stat, basis, states[2], states[3], states[4]
        )
        returned = lax.all_to_all(
            jnp.stack([outer, new_basis, turned, update])[:, :, None],
            "fsdp",
            split_axis=3,
            concat_axis=2,
            tiled=True,
        ).reshape(4, capacity * shard_count, -1, block_side)[:, :block_total]
        mirror = lax.ppermute(
            returned[:2], "dp", [(place, place ^ 1) for place in range(lax.axis_size("dp"))]
        )
        returned = returned.astype(jnp.float32)
        mirror = mirror.astype(jnp.float32)
        left_pair = jnp.where(right_side, mirror, returned[:2])
        right_pair = jnp.where(right_side, returned[:2], mirror)
        turned = returned[2]
        local = [
            returned[3],
            FIRST_DECAY * first_moment + (1.0 - FIRST_DECAY) * turned,
            SECOND_DECAY * second_moment + (1.0 - SECOND_DECAY) * turned * turned,
            STAT_DECAY * left_stat + (1.0 - STAT_DECAY) * left_pair[0],
            STAT_DECAY * right_stat + (1.0 - STAT_DECAY) * right_pair[0],
            left_pair[1],
            right_pair[1],
        ]
        local = [matrices - MATRIX_RATE * (local[0] + WEIGHT_DECAY * matrices)] + local
        local[1] = local[0].astype(BF16)
    vfirst_new = FIRST_DECAY * vector_first + (1.0 - FIRST_DECAY) * vector_sum
    vsecond_new = SECOND_DECAY * vector_second + (1.0 - SECOND_DECAY) * vector_sum * vector_sum
    vector_new = vectors - VECTOR_RATE * (vfirst_new / (1.0 - FIRST_DECAY**ADAM_STEP)) / (
        jnp.sqrt(vsecond_new / (1.0 - SECOND_DECAY**ADAM_STEP)) + ADAM_EPSILON
    )
    return (
        block_out,
        input_grad.reshape(sequences, slots, model_width),
        *local,
        vfirst_new,
        vsecond_new,
        vector_new,
    )


def solution(mesh):
    return jax.shard_map(
        shards,
        mesh=mesh,
        in_specs=(
            P(("fsdp", "dp"), None, None),
            P(("fsdp", "dp"), None, None),
            P(("fsdp", "dp")),
            P(None, "fsdp", None),
            P(None, "fsdp", None),
            P(None, "fsdp", None),
            P(None, "fsdp", None),
            P(None, "fsdp", None),
            P(None, "fsdp", None),
            P(None, "fsdp", None),
            P("fsdp"),
            P("fsdp"),
            P("fsdp"),
        ),
        out_specs=(
            P(("fsdp", "dp"), None, None),
            P(("fsdp", "dp"), None, None),
            P(None, "fsdp", None),
            P(None, "fsdp", None),
            P(None, "fsdp", None),
            P(None, "fsdp", None),
            P(None, "fsdp", None),
            P(None, "fsdp", None),
            P(None, "fsdp", None),
            P(None, "fsdp", None),
            P("fsdp"),
            P("fsdp"),
            P("fsdp"),
        ),
        check_vma=False,
    )
```

```python
import functools

import jax
import jax.numpy as jnp
from jax import lax
from jax.experimental import pallas as pl
from jax.experimental.pallas import tpu as pltpu
from jax.sharding import PartitionSpec as P

F32 = jnp.float32
BF16 = jnp.bfloat16
MESH = pl.DeviceIdType.MESH
OWNERS = 4

HEADS = 12
HEAD_DIM = 64
FF = 3072
ADAM_STEP = 10


FIRST_DECAY = 0.9
SECOND_DECAY = 0.999
STAT_DECAY = 0.95
ADAM_EPSILON = 1e-08
NORM_EPSILON = 1e-05
MATRIX_RATE = 0.03
VECTOR_RATE = 0.2
WEIGHT_DECAY = 0.01


def assemble(blocks, row_count, column_count):
    block_side = blocks.shape[-1]
    shaped = blocks.reshape(row_count, column_count, block_side, block_side)
    return shaped.transpose(0, 2, 1, 3).reshape(row_count * block_side, column_count * block_side)


def split_blocks(matrix, row_count, column_count, block_side):
    shaped = matrix.reshape(row_count, block_side, column_count, block_side)
    return shaped.transpose(0, 2, 1, 3).reshape(row_count * column_count, block_side, block_side)


def layer_norm(values, gain_row, shift_row):
    center = jnp.mean(values, axis=-1, keepdims=True)
    centered = values - center
    spread = jnp.mean(centered * centered, axis=-1, keepdims=True)
    return centered * lax.rsqrt(spread + NORM_EPSILON) * gain_row + shift_row


def exact_gelu(hidden):
    return jax.nn.gelu(hidden, approximate=False)


def masked_scores(heads_query, heads_key, length):
    slots = heads_query.shape[0]
    scores = jnp.einsum(
        "qhd,khd->hqk", heads_query, heads_key, preferred_element_type=jnp.float32
    ) * HEAD_DIM ** (-0.5)
    visible = lax.iota(jnp.int32, slots) < length
    return jnp.where(visible[None, None, :], scores, -1e30)


def attend(pieces):
    query_rows, key_rows, value_rows, length = pieces
    slots = query_rows.shape[0]
    heads_query = query_rows.reshape(slots, HEADS, HEAD_DIM)
    heads_key = key_rows.reshape(slots, HEADS, HEAD_DIM)
    heads_value = value_rows.reshape(slots, HEADS, HEAD_DIM)
    scores = masked_scores(heads_query, heads_key, length)
    row_max = jnp.max(scores, axis=-1, keepdims=True)
    shifted = jnp.exp(scores - row_max)
    row_total = jnp.sum(shifted, axis=-1, keepdims=True)
    attention_weights = (shifted / row_total).astype(jnp.bfloat16)
    context = jnp.einsum(
        "hqk,khd->qhd", attention_weights, heads_value, preferred_element_type=jnp.float32
    )
    return (
        context.reshape(slots, -1).astype(jnp.bfloat16),
        row_max[..., 0] + jnp.log(row_total[..., 0]),
    )


def attend_back(pieces):
    query_rows, key_rows, value_rows, logsum, grad_context, length = pieces
    slots = query_rows.shape[0]
    heads_query = query_rows.reshape(slots, HEADS, HEAD_DIM)
    heads_key = key_rows.reshape(slots, HEADS, HEAD_DIM)
    heads_value = value_rows.reshape(slots, HEADS, HEAD_DIM)
    heads_grad = grad_context.reshape(slots, HEADS, HEAD_DIM)
    scores = masked_scores(heads_query, heads_key, length)
    attention_weights = jnp.exp(scores - logsum[..., None])
    weights_low = attention_weights.astype(jnp.bfloat16)
    grad_values = jnp.einsum(
        "hqk,qhd->khd", weights_low, heads_grad, preferred_element_type=jnp.float32
    )
    grad_weights = jnp.einsum(
        "qhd,khd->hqk", heads_grad, heads_value, preferred_element_type=jnp.float32
    )
    grad_scores = attention_weights * (
        grad_weights - jnp.sum(grad_weights * attention_weights, axis=-1, keepdims=True)
    )
    scores_low = grad_scores.astype(jnp.bfloat16)
    grad_query = jnp.einsum(
        "hqk,khd->qhd", scores_low, heads_key, preferred_element_type=jnp.float32
    ) * HEAD_DIM ** (-0.5)
    grad_keys = jnp.einsum(
        "hqk,qhd->khd", scores_low, heads_query, preferred_element_type=jnp.float32
    ) * HEAD_DIM ** (-0.5)
    return (
        grad_query.reshape(slots, -1).astype(jnp.bfloat16),
        grad_keys.reshape(slots, -1).astype(jnp.bfloat16),
        grad_values.reshape(slots, -1).astype(jnp.bfloat16),
    )


def dg(a,b,ca,cb):
    return lax.dot_general(a,b,(((ca,),(cb,)),((),())),preferred_element_type=F32)

def halves(a):
    hi=a.astype(BF16)
    return hi,(a-hi.astype(F32)).astype(BF16)

def mm3(a,b,ca,cb):
    ah,al=halves(a); bh,bl=halves(b)
    return dg(ah,bh,ca,cb)+(dg(ah,bl,ca,cb)+dg(al,bh,ca,cb))

def thirds(u):
    h=u.astype(BF16).astype(F32); r=u-h
    m=r.astype(BF16).astype(F32)
    return h,m,r-m

def factor_panels(aug, slots, side=128, between=None):
    sub=lax.broadcasted_iota(jnp.int32,(8,side),0)
    def spread(v): return jnp.broadcast_to(v,(8,side))
    for p in range(side//8):
        k=8*p
        if between is not None:
            between(p)
        panels=[]
        for s in range(slots):
            pw=aug[s,k:k+8,:side]; pv=aug[s,k:k+8,side:]
            cols=[spread(pw[:,k+i:k+i+1]) for i in range(8)]
            S=[[spread(cols[i][j:j+1,:]) if j>=i else None for i in range(8)] for j in range(8)]
            rw=[spread(pw[i:i+1,:]) for i in range(8)]
            rv=[spread(pv[i:i+1,:]) for i in range(8)]
            panels.append((S,rw,rv))
        for i in range(8):
            for S,rw,rv in panels:
                r=lax.rsqrt(S[i][i])
                for j in range(i+1,8): S[j][i]=S[j][i]*r
                for m in range(i+1,8):
                    for j in range(m,8):
                        S[j][m]=S[j][m]-S[j][i]*S[m][i]
                rw[i]=rw[i]*r; rv[i]=rv[i]*r
                for j in range(i+1,8):
                    rw[j]=rw[j]-S[j][i]*rw[i]
                    rv[j]=rv[j]-S[j][i]*rv[i]
        for s,(S,rw,rv) in enumerate(panels):
            uw,uv=rw[0],rv[0]
            for i in range(1,8):
                uw=jnp.where(sub==i,rw[i],uw); uv=jnp.where(sub==i,rv[i],uv)
            aug[s,k:k+8,side:]=uv
            if k+8<side:
                h,m,l=thirds(uw); vh,vm,vl=thirds(uv)
                a=jnp.concatenate([h,h,m,m,h,l],0).astype(BF16)
                b=jnp.concatenate([jnp.concatenate([h,m,h,m,l,h],0),jnp.concatenate([vh,vm,vh,vm,vl,vh],0)],1).astype(BF16)
                t=dg(a,b,0,0)
                aug[s,k+8:,:]=aug[s,k+8:,:]-t[k+8:,:]

def orthonormal_cols(mat, aug, slots, side=128):
    n=mat.shape[-1]
    r=lax.broadcasted_iota(jnp.int32,(side,side),0); c=lax.broadcasted_iota(jnp.int32,(side,side),1)
    eye=(r==c).astype(F32)
    steps=n//side
    for o in range(steps):
        lo=o*side
        for s in range(slots):
            mo=mat[s,:,lo:lo+side]
            aug[s,:,:side]=mm3(mo,mo,0,0)
            aug[s,:,side:]=eye
        factor_panels(aug,slots,side)
        for s in range(slots):
            q=mm3(mat[s,:,lo:lo+side],aug[s,:,side:],1,1)
            mat[s,:,lo:lo+side]=q
            if o+1<steps:
                rest=mat[s,:,lo+side:]
                mat[s,:,lo+side:]=rest-mm3(q,mm3(q,rest,0,0),1,0)


def soap_kernel(grad, stat, own, other, first, second, outer_out, basis_out, turned_out, update_out, mat, aug):
    slots = grad.shape[0]
    right_side = lax.rem(lax.axis_index("dp"), 2) == 1

    def run(is_right):
        near, far = (0, 1) if is_right else (1, 0)

        def one(s, carry):
            g = grad[s].astype(BF16)
            outer = dg(g, g, near, near)
            outer_out[s] = outer.astype(BF16)
            mixed = STAT_DECAY * stat[s].astype(F32) + (1.0 - STAT_DECAY) * outer
            high, rest = halves(mixed)
            mat[s] = dg(high, own[s], 1, 0) + dg(rest, own[s], 1, 0)
            left, right = (other[s], own[s]) if is_right else (own[s], other[s])
            rotated = dg(dg(left, g, 0, 0).astype(BF16), right, 1, 0)
            turned_out[s] = rotated.astype(BF16)
            first_new = FIRST_DECAY * first[s].astype(F32) + (1.0 - FIRST_DECAY) * rotated
            second_new = SECOND_DECAY * second[s].astype(F32) + (1.0 - SECOND_DECAY) * rotated * rotated
            direction = (
                first_new
                / (1.0 - FIRST_DECAY**ADAM_STEP)
                / (jnp.sqrt(second_new / (1.0 - SECOND_DECAY**ADAM_STEP)) + ADAM_EPSILON)
            )
            back = dg(left, direction.astype(BF16), 1, 0).astype(BF16)
            update_out[s] = dg(back, right, 1, 1).astype(BF16)
            return carry

        lax.fori_loop(0, slots, one, 0)

    @pl.when(right_side)
    def _():
        run(True)

    @pl.when(jnp.logical_not(right_side))
    def _():
        run(False)

    orthonormal_cols(mat, aug, slots)
    basis_out[...] = mat[...].astype(BF16)


def soap_blocks(grad, stat, own, other, first, second):
    slots, side, _ = grad.shape
    shape = jax.ShapeDtypeStruct(grad.shape, BF16)
    whole = pl.BlockSpec(memory_space=pltpu.VMEM)
    return pl.pallas_call(
        soap_kernel,
        out_shape=[shape] * 4,
        in_specs=[whole] * 6,
        out_specs=[whole] * 4,
        scratch_shapes=[
            pltpu.VMEM((slots, side, side), F32),
            pltpu.VMEM((slots, 128, 256), F32),
        ],
        compiler_params=pltpu.CompilerParams(vmem_limit_bytes=60 * 2**20),
        name="soap_blocks",
    )(grad, stat, own, other, first, second)


def ring_place(chip, chips):
    along, across = chip // 2, lax.rem(chip, 2)
    return along * (1 - across) + (chips - 1 - along) * across


def ring_chip(place, chips):
    place = lax.rem(place + 8 * chips, chips)
    across = place // (chips // 2)
    along = place * (1 - across) + (chips - 1 - place) * across
    return 2 * along + across


def whereabouts(chips):
    device, replica = lax.axis_index("fsdp"), lax.axis_index("dp")
    chip, core = device // 2, lax.rem(device, 2)
    place = ring_place(chip, chips)
    turn = 1 - 2 * core
    after = (2 * ring_chip(place + turn, chips) + core, replica)
    before = (2 * ring_chip(place - turn, chips) + core, replica)
    sibling = (2 * chip + 1 - core, replica)
    return device, replica, chip, core, place, turn, after, before, sibling


def greet(neighbours):
    barrier = pltpu.get_barrier_semaphore()
    for neighbour in neighbours:
        pl.semaphore_signal(barrier, inc=1, device_id=neighbour, device_id_type=MESH)
    pl.semaphore_wait(barrier, len(neighbours))


def gather_kernel(chips, share, mat_ref, vec_ref, left_stat, right_stat, left_basis, right_basis, first, second,
                  attn, up, down, vecs, states, wide, raw_a, raw_u, raw_d, low_a, low_u, low_d,
                  low_v, trade_send, trade_recv, own_sem, ring_send, ring_recv, sib_send, sib_recv, cross_send, cross_recv,
                  vec_send, vec_recv, vec_sib_send, vec_sib_recv, state_sem):
    device, replica, chip, core, place, turn, after, before, sibling = whereabouts(chips)
    mirror = (device, 1 - replica)
    side = mat_ref.shape[-1]
    both = 2 * share
    rows = pl.ds(pl.multiple_of(share * core, 8), share)
    greet((after, before, sibling, mirror))

    def state(source, slot, item):
        return pltpu.make_async_copy(source.at[slot], wide.at[item], state_sem.at[item])

    def fetch_states(stat, basis, other, mine):
        for slot in range(3):
            state(stat, slot, slot).start()
            state(basis, slot, 3 + slot).start()
        for index, slot in enumerate((mine, 2)):
            state(other, slot, 6 + index).start()
            state(first, slot, 8 + index).start()
            state(second, slot, 10 + index).start()

    @pl.when(replica == 0)
    def _():
        fetch_states(left_stat, left_basis, right_basis, 0)

    @pl.when(replica == 1)
    def _():
        fetch_states(right_stat, right_basis, left_basis, 1)

    groups = ((raw_a, low_a, attn), (raw_u, low_u, up), (raw_d, low_d, down))
    trades = []
    for g, (raw, low, out) in enumerate(groups):
        for b in range(16):
            if g == 0:
                raw[(b % 4) // 2, rows, (b // 4) * 2 * side + (b % 2) * side : (b // 4) * 2 * side + (b % 2 + 1) * side] = mat_ref[b]
            elif g == 1:
                raw[b // 8, rows, (b % 8) * side : (b % 8 + 1) * side] = mat_ref[16 + b]
            else:
                raw[b // 2, rows, (b % 2) * side : (b % 2 + 1) * side] = mat_ref[32 + b]
        part = raw.at[:, rows, :]
        trade = pltpu.make_async_remote_copy(
            src_ref=part, dst_ref=part, send_sem=trade_send.at[g], recv_sem=trade_recv.at[g],
            device_id=sibling, device_id_type=MESH)
        trade.start()
        trades.append(trade)
    low_v[...] = vec_ref[...].astype(BF16).astype(F32)

    def units(kind):
        return ((6 * replica + core, 1), (2 + 2 * core, 2), (6 * (1 - replica) + core, 1))[kind]

    def cut(ref, g, row, kind):
        first, number = units(kind)
        if g == 2:
            return ref.at[pl.ds(first, number), row, :]
        return ref.at[:, row, pl.ds(pl.multiple_of(first * side, 128), number * side)]

    def slab(g, origin, kind):
        return cut(groups[g][2], g, pl.ds(pl.multiple_of(origin * both, 16), both), kind)

    def forward(g, t, kind, origin, source):
        return pltpu.make_async_remote_copy(
            src_ref=source, dst_ref=slab(g, origin, kind), send_sem=ring_send.at[t, g, kind],
            recv_sem=ring_recv.at[t, g, kind], device_id=after, device_id_type=MESH)

    def pass_on(g, t, kind, origin):
        part = slab(g, origin, kind)
        return pltpu.make_async_remote_copy(
            src_ref=part, dst_ref=part, send_sem=sib_send.at[t, g, kind], recv_sem=sib_recv.at[t, g, kind],
            device_id=sibling, device_id_type=MESH)

    def across(g, t, origin, kind):
        part = slab(g, origin, kind)
        return pltpu.make_async_remote_copy(
            src_ref=part, dst_ref=part, send_sem=cross_send.at[t, g], recv_sem=cross_recv.at[t, g],
            device_id=mirror, device_id_type=MESH)

    def vec_of(origin):
        return vecs.at[2 * origin + core]

    def vec_forward(t, origin, source):
        return pltpu.make_async_remote_copy(
            src_ref=source, dst_ref=vec_of(origin), send_sem=vec_send.at[t], recv_sem=vec_recv.at[t],
            device_id=after, device_id_type=MESH)

    def vec_pass_on(t, origin, source):
        return pltpu.make_async_remote_copy(
            src_ref=source, dst_ref=vec_of(origin), send_sem=vec_sib_send.at[t], recv_sem=vec_sib_recv.at[t],
            device_id=sibling, device_id_type=MESH)

    vec_forward(0, chip, low_v).start()
    vec_pass_on(0, chip, low_v).start()
    owns = [pltpu.make_async_copy(low_v, vec_of(chip), own_sem.at[3])]
    owns[0].start()
    for g, (raw, low, out) in enumerate(groups):
        trades[g].wait()
        low[...] = raw[...].astype(BF16)
        for kind in range(2):
            forward(g, 0, kind, chip, cut(low, g, slice(None), kind)).start()
        own = pltpu.make_async_copy(low, out.at[:, pl.ds(pl.multiple_of(chip * both, 16), both), :], own_sem.at[g])
        own.start()
        owns.append(own)

    def take_crossed(t):
        origin = ring_chip(place - turn * t, chips)
        for g in range(3):
            across(g, t, origin, 2).wait_recv()
            pass_on(g, t, 2, origin).start()

    def step(t, carry):
        origin = ring_chip(place - turn * t, chips)
        vec_forward(t - 1, origin, vec_of(origin)).wait_recv()

        @pl.when(t < chips - 1)
        def _():
            vec_forward(t, origin, vec_of(origin)).start()

        vec_pass_on(t, origin, vec_of(origin)).start()
        for g in range(3):
            for kind in range(2):
                arrived = slab(g, origin, kind)
                forward(g, t - 1, kind, origin, arrived).wait_recv()

                @pl.when(t < chips - 1)
                def _():
                    forward(g, t, kind, origin, arrived).start()

                if kind == 0:
                    across(g, t, origin, 0).start()
                pass_on(g, t, kind, origin).start()

        @pl.when(t > 1)
        def _():
            take_crossed(t - 1)

        @pl.when(t < chips - 1)
        def _():
            for item in (2 * t - 2, 2 * t - 1):
                state(first, 0, item).wait()
                for holder in range(2 * chips):
                    states[holder, item] = wide[item, holder].astype(BF16)
        return carry

    lax.fori_loop(1, chips, step, 0)
    take_crossed(chips - 1)
    for own in owns:
        own.wait()

    def finish(t, carry):
        @pl.when(t < chips - 1)
        def _():
            vec_forward(t, chip, vec_of(chip)).wait_send()

        vec_pass_on(t, chip, vec_of(chip)).wait()
        for g in range(3):
            @pl.when(t < chips - 1)
            def _():
                for kind in range(2):
                    forward(g, t, kind, chip, slab(g, chip, kind)).wait_send()

            @pl.when(t > 0)
            def _():
                across(g, t, chip, 0).wait_send()
                for kind in range(3):
                    pass_on(g, t, kind, chip).wait()
        return carry

    lax.fori_loop(0, chips, finish, 0)


def gather_weights(matrices, vector_tile, states, chips):
    total, share, side = matrices.shape
    both = 2 * share
    anywhere = pl.BlockSpec(memory_space=pl.ANY)
    whole = pl.BlockSpec(memory_space=pltpu.VMEM)
    dma = pltpu.SemaphoreType.DMA
    return pl.pallas_call(
        functools.partial(gather_kernel, chips, share),
        out_shape=[
            jax.ShapeDtypeStruct((2, side, 8 * side), BF16),
            jax.ShapeDtypeStruct((2, side, 8 * side), BF16),
            jax.ShapeDtypeStruct((8, side, 2 * side), BF16),
            jax.ShapeDtypeStruct((2 * chips, 16, 128), F32),
            jax.ShapeDtypeStruct((2 * chips, 12, share, side), BF16),
        ],
        in_specs=[whole, whole] + [anywhere] * 6,
        out_specs=[anywhere] * 4 + [whole],
        scratch_shapes=[
            pltpu.VMEM((12, 2 * chips, share, side), F32),
            pltpu.VMEM((2, both, 8 * side), F32),
            pltpu.VMEM((2, both, 8 * side), F32),
            pltpu.VMEM((8, both, 2 * side), F32),
            pltpu.VMEM((2, both, 8 * side), BF16),
            pltpu.VMEM((2, both, 8 * side), BF16),
            pltpu.VMEM((8, both, 2 * side), BF16),
            pltpu.VMEM((16, 128), F32),
            dma((3,)), dma((3,)), dma((4,)),
            dma((chips - 1, 3, 2)), dma((chips - 1, 3, 2)), dma((chips, 3, 3)), dma((chips, 3, 3)),
            dma((chips, 3)), dma((chips, 3)),
            dma((chips - 1,)), dma((chips - 1,)), dma((chips,)), dma((chips,)), dma((12,)),
        ],
        compiler_params=pltpu.CompilerParams(collective_id=1, has_side_effects=True, vmem_limit_bytes=60 * 2**20),
        name="gather_weights",
    )(matrices, vector_tile, *[part.reshape(3, 2 * chips, share, side) for part in states])


def reduce_kernel(chips, g_qkv, g_out, g_up, g_down, g_vec, owned, vec_sum, mine, theirs, ring, crossed, peer, vmine, vring,
                  vpeer, mine_sem, sib_send, sib_recv, ring_send, ring_recv, cross_send, cross_recv, peer_send, peer_recv):
    device, replica, chip, core, place, turn, after, before, sibling = whereabouts(chips)
    mirror = (device, 1 - replica)
    side = mine.shape[-1]
    quarter = side // 4
    last = chips - 1
    greet((after, before, sibling, mirror))

    def quarters(first, number):
        return pl.ds(pl.multiple_of(first * quarter, 16), number * quarter)

    carried = quarters(replica, 3)
    private = quarters(3 * replica, 1)
    foreign = quarters(3 * (1 - replica), 1)

    def column(index):
        return pl.ds(pl.multiple_of(index * side, 128), side)

    def fetch(owner, start):
        which = owner // 4
        i, j = lax.rem(owner, 4) // 2, lax.rem(owner, 2)

        @pl.when(which < 3)
        def _():
            start(0, g_qkv.at[i, :, column(2 * which + j)])

        @pl.when(which == 3)
        def _():
            start(0, g_out.at[i, :, column(j)])

        start(1, g_up.at[owner // 8, :, column(lax.rem(owner, 8))])
        start(2, g_down.at[owner // 2, :, column(lax.rem(owner, 2))])
        start(3, g_vec.at[owner])

    def local(t, slot, source):
        target = vmine.at[0, t] if slot == 3 else mine.at[t, slot]
        return pltpu.make_async_copy(source, target, mine_sem.at[t, slot])

    def to_sibling(t, slot, source):
        target = vmine.at[1, t] if slot == 3 else theirs.at[t, slot]
        return pltpu.make_async_remote_copy(
            src_ref=source, dst_ref=target, send_sem=sib_send.at[t, slot], recv_sem=sib_recv.at[t, slot],
            device_id=sibling, device_id_type=MESH)

    def to_next(t, slot):
        source, target = (vmine.at[0, t], vring.at[t]) if slot == 3 else (mine.at[t, slot, carried, :], ring.at[t, slot])
        return pltpu.make_async_remote_copy(
            src_ref=source, dst_ref=target, send_sem=ring_send.at[t, slot], recv_sem=ring_recv.at[t, slot],
            device_id=after, device_id_type=MESH)

    def across(t, slot):
        return pltpu.make_async_remote_copy(
            src_ref=mine.at[t, slot, foreign, :], dst_ref=crossed.at[t, slot], send_sem=cross_send.at[t, slot],
            recv_sem=cross_recv.at[t, slot], device_id=mirror, device_id_type=MESH)

    def to_mirror(slot):
        source, target = (vmine.at[0, last], vpeer) if slot == 3 else (mine.at[last, slot, carried, :], peer.at[slot, carried, :])
        return pltpu.make_async_remote_copy(
            src_ref=source, dst_ref=target, send_sem=peer_send.at[slot], recv_sem=peer_recv.at[slot],
            device_id=mirror, device_id_type=MESH)

    def begin(t):
        fetch(2 * ring_chip(place + turn * (t + 1), chips) + 1 - core, lambda slot, source: to_sibling(t, slot, source).start())
        fetch(2 * ring_chip(place - turn * (t + 1), chips) + core, lambda slot, source: local(t, slot, source).start())

    def sources(slot):
        return g_vec.at[0] if slot == 3 else g_up.at[0, :, :side]

    def pair(t):
        for slot in (3, 0, 1, 2):
            local(t, slot, sources(slot)).wait()
            to_sibling(t, slot, sources(slot)).wait_recv()
            if slot == 3:
                vmine[0, t] = vmine[0, t] + vmine[1, t]
            else:
                mine[t, slot] = (mine[t, slot].astype(F32) + theirs[t, slot].astype(F32)).astype(BF16)
                across(t, slot).start()

    def add(t, slot, hold, extra):
        mine[t, slot, hold, :] = (mine[t, slot, hold, :].astype(F32) + extra.astype(F32)).astype(BF16)

    def step(t, carry):
        @pl.when(t + 2 < chips)
        def _():
            begin(t + 2)

        @pl.when(t + 1 < chips)
        def _():
            pair(t + 1)

        for slot in (3, 0, 1, 2):
            if slot < 3:
                across(t, slot).wait_recv()
                add(t, slot, private, crossed[t, slot])

            @pl.when(t > 0)
            def _():
                to_next(t - 1, slot).wait_recv()
                if slot == 3:
                    vmine[0, t] = vmine[0, t] + vring[t - 1]
                else:
                    add(t, slot, carried, ring[t - 1, slot])

            @pl.when(t < last)
            def _():
                to_next(t, slot).start()

            @pl.when(t == last)
            def _():
                to_mirror(slot).start()
        return carry

    begin(0)
    begin(1)
    pair(0)
    lax.fori_loop(0, chips, step, 0)
    for slot in (3, 0, 1, 2):
        to_mirror(slot).wait()
        if slot == 3:
            vec_sum[...] = vmine[0, last] + vpeer[...]
        else:
            shared = slice(quarter, 3 * quarter)
            owned[slot, shared, :] = (mine[last, slot, shared, :].astype(F32) + peer[slot, shared, :].astype(F32)).astype(BF16)
            owned[slot, private, :] = mine[last, slot, private, :]
            owned[slot, foreign, :] = peer[slot, foreign, :]

    def finish(t, carry):
        for slot in range(4):
            to_sibling(t, slot, sources(slot)).wait_send()
            if slot < 3:
                across(t, slot).wait_send()

            @pl.when(t < last)
            def _():
                to_next(t, slot).wait_send()
        return carry

    lax.fori_loop(0, chips, finish, 0)


def reduce_gradients(g_qkv, g_out, g_up, g_down, g_vec, chips):
    side = g_up.shape[1]
    anywhere = pl.BlockSpec(memory_space=pl.ANY)
    whole = pl.BlockSpec(memory_space=pltpu.VMEM)
    dma = pltpu.SemaphoreType.DMA
    return pl.pallas_call(
        functools.partial(reduce_kernel, chips),
        out_shape=[jax.ShapeDtypeStruct((3, side, side), BF16), jax.ShapeDtypeStruct((16, 128), F32)],
        in_specs=[anywhere] * 5,
        out_specs=[whole] * 2,
        scratch_shapes=[
            pltpu.VMEM((chips, 3, side, side), BF16),
            pltpu.VMEM((chips, 3, side, side), BF16),
            pltpu.VMEM((chips - 1, 3, 3 * side // 4, side), BF16),
            pltpu.VMEM((chips, 3, side // 4, side), BF16),
            pltpu.VMEM((3, side, side), BF16),
            pltpu.VMEM((2, chips, 16, 128), F32),
            pltpu.VMEM((chips - 1, 16, 128), F32),
            pltpu.VMEM((16, 128), F32),
            dma((chips, 4)), dma((chips, 4)), dma((chips, 4)),
            dma((chips - 1, 4)), dma((chips - 1, 4)), dma((chips, 3)), dma((chips, 3)), dma((4,)), dma((4,)),
        ],
        compiler_params=pltpu.CompilerParams(collective_id=2, has_side_effects=True, vmem_limit_bytes=60 * 2**20),
        name="reduce_gradients",
    )(g_qkv, g_out, g_up, g_down, g_vec)


def opposite(device, step, count):
    result, bit = 0, 1
    while bit < count:
        one, two = lax.rem(device // bit, 2), lax.rem(step // bit, 2)
        result = result + bit * (one + two - 2 * one * two)
        bit *= 2
    return result


def renew_kernel(count, share, grad, parts, early, late, states, items, mat, aug, out_early, out_late,
                 early_send, early_recv, early_own, late_send, late_recv, late_own,
                 cross_send, cross_recv, cross_late_send, cross_late_recv):
    device, replica = lax.axis_index("fsdp"), lax.axis_index("dp")
    mirror = (device, 1 - replica)
    slots, side, _ = grad.shape
    part = 128

    def partner(step):
        return opposite(device, step, count), replica

    barrier = pltpu.get_barrier_semaphore()

    def hail(step, carry):
        pl.semaphore_signal(barrier, inc=1, device_id=partner(step), device_id_type=MESH)
        return carry

    lax.fori_loop(1, count, hail, 0)
    pl.semaphore_signal(barrier, inc=1, device_id=mirror, device_id_type=MESH)
    pl.semaphore_wait(barrier, count)

    def join(pair, carry):
        rows = pl.ds(pl.multiple_of(2 * share * pair, 16), 2 * share)
        for item in range(12):
            two = [parts[2 * pair + index, item].astype(F32) for index in range(2)]
            states[item, rows, :] = jnp.concatenate(two, axis=0).astype(BF16)
        return carry

    lax.fori_loop(0, count // 2, join, 0)

    def run(is_right):
        near, far = (0, 1) if is_right else (1, 0)

        def outer_one(s, carry):
            g = grad[s]
            outer = dg(g, g, near, near)
            items[s] = outer
            mixed = STAT_DECAY * states[s].astype(F32) + (1.0 - STAT_DECAY) * outer
            high, rest = halves(mixed)
            mat[s] = dg(high, states[3 + s], 1, 0) + dg(rest, states[3 + s], 1, 0)
            return carry

        lax.fori_loop(0, slots, outer_one, 0)
        for e, s in enumerate((1, 2) if is_right else (0, 2)):
            left, right = (states[6 + e], states[3 + s]) if is_right else (states[3 + s], states[6 + e])
            rotated = dg(dg(left, grad[s], 0, 0).astype(BF16), right, 1, 0)
            if e == 0:
                items[3] = rotated
            elif not is_right:
                items[5] = rotated
                continue
            first_new = FIRST_DECAY * states[8 + e].astype(F32) + (1.0 - FIRST_DECAY) * rotated
            second_new = SECOND_DECAY * states[10 + e].astype(F32) + (1.0 - SECOND_DECAY) * rotated * rotated
            direction = (
                first_new
                / (1.0 - FIRST_DECAY**ADAM_STEP)
                / (jnp.sqrt(second_new / (1.0 - SECOND_DECAY**ADAM_STEP)) + ADAM_EPSILON)
            )
            back = dg(left, direction.astype(BF16), 1, 0).astype(BF16)
            items[4 + e] = dg(back, right, 1, 1)

    @pl.when(replica == 1)
    def _():
        run(True)

    @pl.when(replica == 0)
    def _():
        run(False)

    def rows_of(holder):
        return pl.ds(pl.multiple_of(holder * share, 8), share)

    def pack_early(holder, carry):
        for pair in range(3):
            two = jnp.concatenate([items[2 * pair, rows_of(holder), :], items[2 * pair + 1, rows_of(holder), :]], axis=0)
            out_early[holder, 2 * share * pair : 2 * share * (pair + 1), :] = two.astype(BF16)
        return carry

    def send_early(step, target):
        return pltpu.make_async_remote_copy(
            src_ref=out_early.at[target[0]], dst_ref=early.at[replica, device], send_sem=early_send.at[step],
            recv_sem=early_recv.at[step], device_id=target, device_id_type=MESH)

    def send_late(panel, step, target):
        return pltpu.make_async_remote_copy(
            src_ref=out_late.at[panel, target[0]], dst_ref=late.at[panel, replica, device],
            send_sem=late_send.at[panel, step], recv_sem=late_recv.at[panel, step], device_id=target, device_id_type=MESH)

    def cross_early(step):
        block = early.at[replica, partner(step)[0]]
        return pltpu.make_async_remote_copy(
            src_ref=block, dst_ref=block, send_sem=cross_send.at[step], recv_sem=cross_recv.at[step],
            device_id=mirror, device_id_type=MESH)

    def cross_late(panel, step):
        block = late.at[panel, replica, partner(step)[0]]
        return pltpu.make_async_remote_copy(
            src_ref=block, dst_ref=block, send_sem=cross_late_send.at[panel, step], recv_sem=cross_late_recv.at[panel, step],
            device_id=mirror, device_id_type=MESH)

    def keep_early():
        return pltpu.make_async_copy(out_early.at[device], early.at[replica, device], early_own)

    def keep_late(panel):
        return pltpu.make_async_copy(out_late.at[panel, device], late.at[panel, replica, device], late_own.at[panel])

    lax.fori_loop(0, count, pack_early, 0)

    def launch_early(index, carry):
        step = index + 1
        send_early(step, partner(step)).start()
        return carry

    lax.fori_loop(0, count - 1, launch_early, 0)
    keep_early().start()

    def relay_early(step):
        if step == 0:
            keep_early().wait()
        else:
            send_early(step, partner(step)).wait_recv()
        cross_early(step).start()

    relayed = []

    def between(moment):
        if moment % 4 == 0 and len(relayed) < min(count, 11):
            relay_early(len(relayed))
            relayed.append(moment)

    row_index = lax.broadcasted_iota(jnp.int32, (part, part), 0)
    column_index = lax.broadcasted_iota(jnp.int32, (part, part), 1)
    eye = (row_index == column_index).astype(F32)
    panels = side // part
    for o in range(panels):
        lo = o * part
        for s in range(slots):
            block = mat[s, :, lo : lo + part]
            aug[s, :, :part] = mm3(block, block, 0, 0)
            aug[s, :, part:] = eye
        factor_panels(aug, slots, part, lambda p: between(16 * o + p))
        for s in range(slots):
            mat[s, :, lo : lo + part] = mm3(mat[s, :, lo : lo + part], aug[s, :, part:], 1, 1)

        def pack_late(holder, carry):
            rows = rows_of(holder)
            stacked = [mat[s, rows, lo : lo + part] for s in range(slots)]
            stacked.append(jnp.zeros((8, part), F32))
            out_late[o, holder] = jnp.concatenate(stacked, axis=0).astype(BF16)
            return carry

        lax.fori_loop(0, count, pack_late, 0)

        def launch_late(index, carry):
            step = index + 1
            send_late(o, step, partner(step)).start()
            return carry

        lax.fori_loop(0, count - 1, launch_late, 0)
        keep_late(o).start()
        if o + 1 < panels:
            for s in range(slots):
                q, rest = mat[s, :, lo : lo + part], mat[s, :, lo + part :]
                mat[s, :, lo + part :] = rest - mm3(q, mm3(q, rest, 0, 0), 1, 0)
    for step in range(len(relayed), count):
        relay_early(step)
    for o in range(panels):
        keep_late(o).wait()
        cross_late(o, 0).start()

        def relay_late(step, carry):
            send_late(o, step, partner(step)).wait_recv()
            cross_late(o, step).start()
            return carry

        lax.fori_loop(1, count, relay_late, 0)

    def finish(step, carry):
        cross_early(step).wait()
        for o in range(panels):
            cross_late(o, step).wait()

        @pl.when(step > 0)
        def _():
            send_early(step, partner(step)).wait_send()
            for o in range(panels):
                send_late(o, step, partner(step)).wait_send()
        return carry

    lax.fori_loop(0, count, finish, 0)


def renew_blocks(grad, states, count, share):
    slots, side, _ = grad.shape
    anywhere = pl.BlockSpec(memory_space=pl.ANY)
    whole = pl.BlockSpec(memory_space=pltpu.VMEM)
    dma = pltpu.SemaphoreType.DMA
    tall = -(-slots * share // 16) * 16
    panels = side // 128
    return pl.pallas_call(
        functools.partial(renew_kernel, count, share),
        out_shape=[
            jax.ShapeDtypeStruct((2, count, 6 * share, side), BF16),
            jax.ShapeDtypeStruct((panels, 2, count, tall, 128), BF16),
        ],
        in_specs=[whole] * 2,
        out_specs=[anywhere] * 2,
        scratch_shapes=[
            pltpu.VMEM((12, side, side), BF16),
            pltpu.VMEM((6, side, side), F32),
            pltpu.VMEM((slots, side, side), F32),
            pltpu.VMEM((slots, 128, 256), F32),
            pltpu.VMEM((count, 6 * share, side), BF16),
            pltpu.VMEM((panels, count, tall, 128), BF16),
            dma((count,)), dma((count,)), dma,
            dma((panels, count)), dma((panels, count)), dma((panels,)),
            dma((count,)), dma((count,)), dma((panels, count)), dma((panels, count)),
        ],
        compiler_params=pltpu.CompilerParams(collective_id=3, has_side_effects=True, vmem_limit_bytes=60 * 2**20),
        name="renew_blocks",
    )(grad, states)


def settle_kernel(early, late, mat, first, second, left, right, mat_new, mat_low, first_new, second_new, left_new, right_new,
                  left_basis, right_basis):
    share = mat.shape[2]
    for f in range(mat.shape[1]):
        for s in range(3):
            def item(plane, index):
                return early[plane, f, index * share : (index + 1) * share, :].astype(F32)

            turned = (item(0, 3), item(1, 3), item(0, 5))[s]
            update = (item(0, 4), item(1, 4), item(1, 5))[s]
            fresh = mat[s, f] - MATRIX_RATE * (update + WEIGHT_DECAY * mat[s, f])
            mat_new[s, f] = fresh
            mat_low[s, f] = fresh.astype(BF16)
            first_new[s, f] = FIRST_DECAY * first[s, f] + (1.0 - FIRST_DECAY) * turned
            second_new[s, f] = SECOND_DECAY * second[s, f] + (1.0 - SECOND_DECAY) * turned * turned
            left_new[s, f] = STAT_DECAY * left[s, f] + (1.0 - STAT_DECAY) * item(0, s)
            right_new[s, f] = STAT_DECAY * right[s, f] + (1.0 - STAT_DECAY) * item(1, s)
            for panel in range(late.shape[0]):
                lanes = slice(128 * panel, 128 * (panel + 1))
                left_basis[s, f, :, lanes] = late[panel, 0, f, s * share : (s + 1) * share, :].astype(F32)
                right_basis[s, f, :, lanes] = late[panel, 1, f, s * share : (s + 1) * share, :].astype(F32)


def settle(early, late, matrices, first, second, left, right):
    _, count, tall, side = early.shape
    panels, share = late.shape[0], matrices.shape[1]
    state = pl.BlockSpec((3, OWNERS, share, side), lambda f: (0, f, 0, 0))
    shape = jax.ShapeDtypeStruct((3, count, share, side), F32)
    low = jax.ShapeDtypeStruct((3, count, share, side), BF16)
    results = pl.pallas_call(
        settle_kernel,
        grid=(count // OWNERS,),
        out_shape=[shape, low] + [shape] * 6,
        in_specs=[
            pl.BlockSpec((2, OWNERS, tall, side), lambda f: (0, f, 0, 0)),
            pl.BlockSpec((panels, 2, OWNERS, late.shape[3], 128), lambda f: (0, 0, f, 0, 0)),
        ]
        + [state] * 5,
        out_specs=[state] * 8,
        compiler_params=pltpu.CompilerParams(vmem_limit_bytes=60 * 2**20),
        name="settle",
    )(early, late, *[part.reshape(3, count, share, side) for part in (matrices, first, second, left, right)])
    return [part.reshape(matrices.shape) for part in results]


def normal_parts(value):
    size = jnp.abs(value) * 0.7071067811865476
    t = 1.0 / (1.0 + 0.3275911 * size)
    bell = jnp.exp(-size * size)
    series = t * (0.254829592 + t * (-0.284496736 + t * (1.421413741 + t * (-1.453152027 + t * 1.061405429))))
    tail = 0.5 * series * bell
    return jnp.where(value >= 0.0, 1.0 - tail, tail), bell * 0.3989422804014327


def span(index, size):
    return pl.ds(pl.multiple_of(index * size, size), size)


def looped(count, body):
    def step(index, carry):
        body(index)
        return carry

    lax.fori_loop(0, count, step, 0)


def vector_row(vecs, row, width):
    lane = lax.broadcasted_iota(jnp.int32, (1, 128), 1)
    pieces = []
    for pair in range(width // 128):
        chunk = row * (width // 64) + 2 * pair
        one = vecs[chunk // 9, chunk % 9 : chunk % 9 + 1, :]
        chunk += 1
        two = vecs[chunk // 9, chunk % 9 : chunk % 9 + 1, :]
        pieces.append(jnp.where(lane < 64, one, pltpu.roll(two, 64, 1)))
    return jnp.concatenate(pieces, axis=1)


def vector_tiles_of(rows, row_up, tiles):
    chunks = rows.shape[1] // 64
    for f in range(tiles.shape[0]):
        for i in range(9):
            row, place = divmod(9 * f + i, chunks)
            if 5 <= row < 9:
                spot = (row - 5) * chunks + place
                piece = row_up[spot // 4, :, 128 * (spot % 4 // 2) : 128 * (spot % 4 // 2) + 128]
            else:
                piece = rows[row : row + 1, 128 * (place // 2) : 128 * (place // 2) + 128]
            tiles[f, i : i + 1, :] = pltpu.roll(piece, 64, 1) if place % 2 else piece


def layer_kernel(length_ref, x_ref, cot_ref, tiles, attn_hbm, up_hbm, down_hbm,
                 out_ref, grad_x, grad_tiles, grad_qkv, grad_out, grad_up, grad_down,
                 w_attn, w_up, w_down, qkv, context, logs, hat_one, scale_one, normed, active, slope, hidden_low,
                 grad_r, low_e, grad_c, grad_heads, turned_x, turned_n, turned_c, probs, dscores, stage_w, stage_t,
                 vec, vec_up, grad_vec, grad_vec_up, load_sem, wide_sem, tall_sem):
    slots, width = x_ref.shape
    length = length_ref[0]
    chunks = w_up.shape[1] // 256
    thirds_of = width // 256
    loads = [pltpu.make_async_copy(source, target, load_sem.at[i])
             for i, (source, target) in enumerate(((attn_hbm, w_attn), (up_hbm, w_up), (down_hbm, w_down)))]
    for load in loads:
        load.start()

    def turn(source, target):
        def one(index):
            target[:, span(index, 128)] = source[span(index, 128), :].T

        looped(slots // 128, one)

    def wide_copy(target, slot, index):
        return pltpu.make_async_copy(stage_w.at[slot], target.at[:, span(index, 256)], wide_sem.at[slot])

    def tall_copy(slot, index):
        return pltpu.make_async_copy(stage_t.at[slot], grad_down.at[span(index, 256), :], tall_sem.at[slot])

    def put_wide(target, index, value, first):
        slot = lax.rem(index, 2)

        @pl.when(jnp.logical_not(first))
        def _():
            wide_copy(target, slot, index).wait()

        stage_w[slot] = value.astype(BF16)
        wide_copy(target, slot, index).start()

    grad_vec[...] = jnp.zeros_like(grad_vec)
    for row in range(12):
        vec[row : row + 1, :] = vector_row(tiles, row, width)
        if 5 <= row < 9:
            for third in range(thirds_of):
                vec_up[(row - 5) * thirds_of + third] = vec[row : row + 1, 256 * third : 256 * (third + 1)]
    turn(x_ref, turned_x)
    loads[0].wait()

    def project(index):
        lanes = span(index, 256)
        part = index // thirds_of
        row = jnp.where(part == 0, vec[0:1, span(lax.rem(index, thirds_of), 256)],
                        jnp.where(part == 2, vec[1:2, span(lax.rem(index, thirds_of), 256)], 0.0))
        qkv[:, lanes] = (jnp.dot(x_ref[...], w_attn[:, lanes], preferred_element_type=F32) + row).astype(BF16)

    looped(3 * thirds_of, project)

    lane = lax.broadcasted_iota(jnp.int32, (slots, 128), 1)
    tall_lane = lax.broadcasted_iota(jnp.int32, (128, 128), 0)
    seen = lax.broadcasted_iota(jnp.int32, (slots, 128), 0) < length

    def head_lanes(head, value):
        keep = (lane < HEAD_DIM) if head == 0 else (lane >= HEAD_DIM)
        return jnp.where(keep, value, jnp.zeros_like(value))

    def lanes_of(pair, part):
        return pl.ds(pl.multiple_of(part * width + pair * 128, 128), 128)

    def attend(pair):
        key, value = qkv[:, lanes_of(pair, 1)], qkv[:, lanes_of(pair, 2)]
        turned_value = value.T
        keys = [head_lanes(head, key * HEAD_DIM ** (-0.5)) for head in range(2)]
        for block in range(slots // 128):
            rows = slice(128 * block, 128 * (block + 1))
            query = qkv[rows, lanes_of(pair, 0)]
            both = []
            for head in range(2):
                scores = jnp.where(seen, dg(keys[head], query, 1, 1), -1e30)
                top = jnp.max(scores, axis=0, keepdims=True)
                shifted = jnp.exp(scores - top)
                total = jnp.sum(shifted, axis=0, keepdims=True)
                weights = (shifted * (1.0 / total)).astype(BF16)
                both.append(jnp.dot(turned_value, weights, preferred_element_type=F32))
                logs[2 * pair + head, :, rows] = top + jnp.log(total)
            merged = jnp.where(tall_lane < HEAD_DIM, both[0], both[1])
            context[rows, lanes_of(pair, 0)] = merged.T.astype(BF16)

    looped(width // 128, attend)
    turn(context, turned_c)

    def mix(index):
        lanes = span(index, 256)
        away = pl.ds(pl.multiple_of(3 * width + index * 256, 256), 256)
        value = jnp.dot(context[...], w_attn[:, away], preferred_element_type=F32) + vec[2:3, lanes]
        hat_one[:, lanes] = x_ref[:, lanes].astype(F32) + value

    looped(thirds_of, mix)

    def standard(value):
        centered = value - jnp.mean(value, axis=-1, keepdims=True)
        scale = lax.rsqrt(jnp.mean(centered * centered, axis=-1, keepdims=True) + NORM_EPSILON)
        return centered * scale, scale

    def norm_one(index):
        rows = span(index, 128)
        hat, scale = standard(hat_one[rows, :])
        hat_one[rows, :] = hat
        scale_one[rows, :] = jnp.broadcast_to(scale, (128, 128))
        normed[rows, :] = (hat * vec[3:4, :] + vec[4:5, :]).astype(BF16)

    looped(slots // 128, norm_one)
    turn(normed, turned_n)
    loads[1].wait()

    def rise(index):
        lanes = span(index, 256)
        hidden = jnp.dot(normed[...], w_up[:, lanes], preferred_element_type=F32) + vec_up[index]
        below, density = normal_parts(hidden)
        active[:, lanes] = (hidden * below).astype(BF16)
        slope[:, lanes] = below + hidden * density

    looped(chunks, rise)
    loads[2].wait()

    def fall(index):
        lanes = span(index, 256)
        value = jnp.dot(active[...], w_down[:, lanes], preferred_element_type=F32)
        grad_r[:, lanes] = hat_one[:, lanes] * vec[3:4, lanes] + vec[4:5, lanes] + value + vec[9:10, lanes]

    looped(thirds_of, fall)

    def unstandard(grad_hat, hat, scale):
        return scale * (grad_hat - jnp.mean(grad_hat, axis=-1, keepdims=True)
                        - hat * jnp.mean(grad_hat * hat, axis=-1, keepdims=True))

    def add_row(row, value):
        grad_vec[row : row + 1, :] += jnp.sum(value, axis=0, keepdims=True)

    def norm_two(index):
        rows = span(index, 128)
        hat, scale = standard(grad_r[rows, :])
        out_ref[rows, :] = (hat * vec[10:11, :] + vec[11:12, :]).astype(BF16)
        place = lax.broadcasted_iota(jnp.int32, (128, width), 0) + index * 128
        grad = jnp.where(place < length, cot_ref[rows, :].astype(F32), 0.0)
        add_row(10, grad * hat)
        add_row(11, grad)
        back = unstandard(grad * vec[10:11, :], hat, scale)
        add_row(9, back)
        grad_r[rows, :] = back
        low_e[rows, :] = back.astype(BF16)

    looped(slots // 128, norm_two)

    def sink(index):
        lanes = span(index, 256)
        grad = dg(low_e[...], w_down[lanes, :], 1, 1) * slope[:, lanes]
        grad_vec_up[index] = jnp.sum(grad, axis=0, keepdims=True)
        low = grad.astype(BF16)
        hidden_low[:, lanes] = low
        put_wide(grad_up, index, jnp.dot(turned_n[...], low, preferred_element_type=F32), index < 2)
        slot = lax.rem(index, 2)

        @pl.when(index >= 2)
        def _():
            tall_copy(slot, index).wait()

        stage_t[slot] = dg(active[:, lanes], low_e[...], 0, 0).astype(BF16)
        tall_copy(slot, index).start()

    looped(chunks, sink)

    def rise_back(index):
        lanes = span(index, 256)
        grad_r[:, lanes] += dg(hidden_low[...], w_up[lanes, :], 1, 1)

    looped(thirds_of, rise_back)

    def norm_one_back(index):
        rows = span(index, 128)
        hat, grad = hat_one[rows, :], grad_r[rows, :]
        add_row(3, grad * hat)
        add_row(4, grad)
        back = unstandard(grad * vec[3:4, :], hat, scale_one[rows, 0:1])
        add_row(2, back)
        grad_r[rows, :] = back
        low_e[rows, :] = back.astype(BF16)

    looped(slots // 128, norm_one_back)

    def mix_back(index):
        lanes = span(index, 256)
        put_wide(grad_out, index, jnp.dot(turned_c[...], low_e[:, lanes], preferred_element_type=F32), False)
        away = pl.ds(3 * width, width)
        grad_c[:, lanes] = dg(low_e[...], w_attn[lanes, away], 1, 1).astype(BF16)

    looped(thirds_of, mix_back)

    def attend_back(pair):
        query, key, value = [qkv[:, lanes_of(pair, part)] for part in range(3)]
        grad = grad_c[:, lanes_of(pair, 0)]
        turned_key = key.T
        found = []
        for head in range(2):
            near_key = head_lanes(head, key * HEAD_DIM ** (-0.5))
            near_value = head_lanes(head, value)
            for block in range(slots // 128):
                rows = slice(128 * block, 128 * (block + 1))
                scores = jnp.where(seen, dg(near_key, query[rows], 1, 1), -1e30)
                weights = jnp.exp(scores - logs[2 * pair + head, :, rows])
                back = dg(near_value, grad[rows], 1, 1)
                scores_back = weights * (back - jnp.sum(back * weights, axis=0, keepdims=True))
                probs[head, :, rows] = weights.astype(BF16)
                dscores[head, :, rows] = scores_back.astype(BF16)
            found.append((
                jnp.dot(turned_key, dscores[head], preferred_element_type=F32),
                jnp.dot(dscores[head], query, preferred_element_type=F32),
                jnp.dot(probs[head], grad, preferred_element_type=F32),
            ))
        top = lax.broadcasted_iota(jnp.int32, (128, slots), 0) < HEAD_DIM
        turned_query = jnp.where(top, found[0][0], found[1][0]) * HEAD_DIM ** (-0.5)
        grad_heads[:, lanes_of(pair, 0)] = turned_query.T.astype(BF16)
        grad_heads[:, lanes_of(pair, 1)] = (jnp.where(lane < HEAD_DIM, found[0][1], found[1][1]) * HEAD_DIM ** (-0.5)).astype(BF16)
        grad_heads[:, lanes_of(pair, 2)] = jnp.where(lane < HEAD_DIM, found[0][2], found[1][2]).astype(BF16)

    looped(width // 128, attend_back)
    grad_vec[0:1, :] = jnp.sum(grad_heads[:, :width].astype(F32), axis=0, keepdims=True)
    grad_vec[1:2, :] = jnp.sum(grad_heads[:, 2 * width :].astype(F32), axis=0, keepdims=True)

    def project_shifted(index):
        lanes = span(index, 256)
        slot = lax.rem(index + 1, 2)
        wide_copy(grad_qkv, slot, index).wait()
        stage_w[slot] = jnp.dot(turned_x[...], grad_heads[:, lanes], preferred_element_type=F32).astype(BF16)
        wide_copy(grad_qkv, slot, index).start()

    looped(3 * thirds_of, project_shifted)
    vector_tiles_of(grad_vec, grad_vec_up, grad_tiles)

    def input_back(index):
        lanes = span(index, 256)
        grad_x[:, lanes] = grad_r[:, lanes] + dg(grad_heads[...], w_attn[lanes, : 3 * width], 1, 1)

    looped(thirds_of, input_back)
    for slot in range(2):
        wide_copy(grad_qkv, slot, 0).wait()
        tall_copy(slot, 0).wait()


def layer(length, inputs, cotangent, tiles, attn, up, down):
    slots, width = inputs.shape
    tall = down.shape[0]
    anywhere = pl.BlockSpec(memory_space=pl.ANY)
    whole = pl.BlockSpec(memory_space=pltpu.VMEM)
    vmem = pltpu.VMEM
    dma = pltpu.SemaphoreType.DMA
    return pl.pallas_call(
        layer_kernel,
        out_shape=[
            jax.ShapeDtypeStruct((slots, width), BF16),
            jax.ShapeDtypeStruct((slots, width), F32),
            jax.ShapeDtypeStruct(tiles.shape, F32),
            jax.ShapeDtypeStruct((width, 3 * width), BF16),
            jax.ShapeDtypeStruct((width, width), BF16),
            jax.ShapeDtypeStruct((width, tall), BF16),
            jax.ShapeDtypeStruct((tall, width), BF16),
        ],
        in_specs=[pl.BlockSpec(memory_space=pltpu.SMEM)] + [whole] * 3 + [anywhere] * 3,
        out_specs=[whole] * 3 + [anywhere] * 4,
        scratch_shapes=[
            vmem((width, 4 * width), BF16), vmem((width, tall), BF16), vmem((tall, width), BF16),
            vmem((slots, 3 * width), BF16), vmem((slots, width), BF16), vmem((width // HEAD_DIM, 1, slots), F32),
            vmem((slots, width), F32), vmem((slots, 128), F32), vmem((slots, width), BF16),
            vmem((slots, tall), BF16), vmem((slots, tall), F32), vmem((slots, tall), BF16),
            vmem((slots, width), F32), vmem((slots, width), BF16), vmem((slots, width), BF16),
            vmem((slots, 3 * width), BF16), vmem((width, slots), BF16), vmem((width, slots), BF16), vmem((width, slots), BF16),
            vmem((2, slots, slots), BF16), vmem((2, slots, slots), BF16),
            vmem((2, width, 256), BF16), vmem((2, 256, width), BF16),
            vmem((16, width), F32), vmem((tall // 256, 1, 256), F32), vmem((16, width), F32), vmem((tall // 256, 1, 256), F32),
            dma((3,)), dma((2,)), dma((2,)),
        ],
        compiler_params=pltpu.CompilerParams(vmem_limit_bytes=60 * 2**20),
        cost_estimate=pl.CostEstimate(flops=25_000_000_000, bytes_accessed=40_000_000, transcendentals=8_000_000),
        name="layer",
    )(length, inputs, cotangent, tiles, attn, up, down)


def plain_gather(matrices, vectors):
    side = matrices.shape[-1]
    blocks = lax.all_gather(matrices.astype(BF16), "fsdp", axis=1, tiled=True)
    attn = jnp.concatenate([assemble(blocks[4 * part : 4 * part + 4], 2, 2) for part in range(4)], axis=1)
    up = assemble(blocks[16:32], 2, 8)
    down = assemble(blocks[32:], 8, 2)
    rows = lax.all_gather(vectors.astype(BF16), "fsdp", axis=0, tiled=True)
    return attn, up, down, rows.astype(F32).reshape(-1, 2 * side)


def plain_reduce(grad_qkv, grad_out, grad_up, grad_down, vector_grad, capacity):
    shard_count = lax.axis_size("fsdp")
    width = grad_up.shape[0]
    side = width // 2
    blocks = jnp.concatenate(
        [split_blocks(grad_qkv[:, part * width : (part + 1) * width], 2, 2, side) for part in range(3)]
        + [split_blocks(grad_out, 2, 2, side), split_blocks(grad_up, 2, 8, side), split_blocks(grad_down, 8, 2, side)],
        axis=0,
    )
    owned = lax.psum_scatter(
        to_owners(blocks, capacity, shard_count), "fsdp", scatter_dimension=1, tiled=True
    )
    owned = lax.psum(owned, "dp")[:, 0]
    share = lax.psum_scatter(vector_grad, "fsdp", scatter_dimension=0, tiled=True)
    return owned, lax.psum(share, "dp")


def to_owners(blocks, capacity, shard_count):
    spare = capacity * shard_count - blocks.shape[0]
    blocks = jnp.pad(blocks, ((0, spare),) + ((0, 0),) * (blocks.ndim - 1))
    return blocks.reshape((capacity, shard_count) + blocks.shape[1:])


def plain_layer(tokens, cotangent, lengths, attn, up, down, vector_rows):
    sequences, slots, model_width = tokens.shape
    rows_total = sequences * slots
    unit_ratio = FF // model_width

    def shaped(array):
        return array.reshape(sequences, slots, array.shape[-1])

    weight_qkv, weight_out = attn[:, : 3 * model_width], attn[:, 3 * model_width :]
    inputs = tokens.reshape(rows_total, model_width)
    joined = jnp.dot(inputs, weight_qkv, preferred_element_type=F32)
    query_rows = (joined[:, :model_width] + vector_rows[0]).astype(BF16)
    key_rows = joined[:, model_width : 2 * model_width].astype(BF16)
    value_rows = (joined[:, 2 * model_width :] + vector_rows[1]).astype(BF16)
    context, logsum = lax.map(
        attend, (shaped(query_rows), shaped(key_rows), shaped(value_rows), lengths)
    )
    context = context.reshape(rows_total, model_width)
    attended = jnp.dot(context, weight_out, preferred_element_type=F32) + vector_rows[2]
    normed, pull_one = jax.vjp(
        layer_norm, inputs.astype(F32) + attended, vector_rows[3], vector_rows[4]
    )
    normed_low = normed.astype(BF16)
    hidden = jnp.dot(normed_low, up, preferred_element_type=F32) + vector_rows[
        5 : 5 + unit_ratio
    ].reshape(FF)
    active, pull_gelu = jax.vjp(exact_gelu, hidden)
    active_low = active.astype(BF16)
    result = jnp.dot(active_low, down, preferred_element_type=F32) + vector_rows[5 + unit_ratio]
    output, pull_two = jax.vjp(
        layer_norm, normed + result, vector_rows[6 + unit_ratio], vector_rows[7 + unit_ratio]
    )
    block_out = output.reshape(sequences, slots, model_width).astype(BF16)
    visible = (lax.iota(jnp.int32, slots)[None, :] < lengths[:, None]).astype(F32)
    grad_output = (cotangent.astype(F32) * visible[:, :, None]).reshape(rows_total, model_width)
    grad_second, grad_gain_two, grad_shift_two = pull_two(grad_output)
    second_low = grad_second.astype(BF16)
    grad_down = jnp.einsum("tf,td->fd", active_low, second_low, preferred_element_type=F32)
    grad_active = jnp.einsum("td,fd->tf", second_low, down, preferred_element_type=F32)
    (grad_hidden,) = pull_gelu(grad_active)
    hidden_low = grad_hidden.astype(BF16)
    grad_up = jnp.einsum("td,tf->df", normed_low, hidden_low, preferred_element_type=F32)
    grad_normed = grad_second + jnp.einsum("tf,df->td", hidden_low, up, preferred_element_type=F32)
    grad_mixed, grad_gain_one, grad_shift_one = pull_one(grad_normed)
    mixed_low = grad_mixed.astype(BF16)
    grad_out_weight = jnp.einsum("td,te->de", context, mixed_low, preferred_element_type=F32)
    grad_context = jnp.einsum(
        "te,de->td", mixed_low, weight_out, preferred_element_type=F32
    ).astype(BF16)
    grad_query, grad_keys, grad_values = lax.map(
        attend_back,
        (
            shaped(query_rows),
            shaped(key_rows),
            shaped(value_rows),
            logsum,
            shaped(grad_context),
            lengths,
        ),
    )
    grad_joined = jnp.concatenate(
        [
            grad_query.reshape(rows_total, model_width),
            grad_keys.reshape(rows_total, model_width),
            grad_values.reshape(rows_total, model_width),
        ],
        axis=1,
    )
    grad_qkv = jnp.einsum("td,te->de", inputs, grad_joined, preferred_element_type=F32)
    input_grad = grad_mixed + jnp.einsum(
        "te,de->td", grad_joined, weight_qkv, preferred_element_type=F32
    )
    vector_grad = jnp.concatenate(
        [
            jnp.sum(grad_joined[:, :model_width], axis=0, dtype=F32)[None],
            jnp.sum(grad_joined[:, 2 * model_width :], axis=0, dtype=F32)[None],
            jnp.sum(grad_mixed, axis=0)[None],
            grad_gain_one[None],
            grad_shift_one[None],
            jnp.sum(grad_hidden, axis=0).reshape(unit_ratio, model_width),
            jnp.sum(grad_second, axis=0)[None],
            grad_gain_two[None],
            grad_shift_two[None],
        ],
        axis=0,
    ).reshape(-1)
    weight_grads = [part.astype(BF16) for part in (grad_qkv, grad_out_weight, grad_up, grad_down)]
    return block_out, input_grad.reshape(tokens.shape), vector_grad, weight_grads


def shards(
    tokens,
    cotangent,
    lengths,
    matrices,
    first_moment,
    second_moment,
    left_stat,
    right_stat,
    left_basis,
    right_basis,
    vectors,
    vector_first,
    vector_second,
):
    shard_count = lax.axis_size("fsdp")
    replicas = lax.axis_size("dp")
    sequences, slots, model_width = tokens.shape
    block_total, share_rows, block_side = matrices.shape
    capacity = -(-block_total // shard_count)
    ringed = replicas == 2 and sequences == 1 and vectors.shape[0] == 576 and capacity * shard_count == block_total == 48 and share_rows % 8 == 0 and capacity == 3

    right_side = lax.axis_index("dp") % 2 == 1
    if ringed:
        vector_tile = jnp.pad(vectors.reshape(9, 64), ((0, 7), (0, 64)))
        attn, up, down, tiles, states = gather_weights(
            matrices,
            vector_tile,
            (left_stat, right_stat, left_basis, right_basis, first_moment, second_moment),
            shard_count // 2,
        )
        states = lax.all_to_all(states, "fsdp", split_axis=0, concat_axis=0, tiled=True)
        block_out, input_grad, grad_tiles, *weight_grads = layer(
            lengths,
            tokens[0],
            cotangent[0],
            tiles,
            attn.reshape(model_width, 4 * model_width),
            up.reshape(model_width, FF),
            down.reshape(FF, model_width),
        )
        block_out, input_grad = block_out[None], input_grad[None]
        slabs = [part.reshape(-1, block_side, part.shape[1]) for part in weight_grads]
        owned, vector_sum = reduce_gradients(*slabs, grad_tiles, shard_count // 2)
        vector_sum = vector_sum[:9, :64].reshape(-1)
    else:
        chosen = [
            jnp.where(right_side, right_stat, left_stat),
            jnp.where(right_side, right_basis, left_basis),
            jnp.where(right_side, left_basis, right_basis),
            first_moment,
            second_moment,
        ]
        states = jnp.stack([to_owners(part.astype(BF16), capacity, shard_count) for part in chosen])
        attn, up, down, vector_rows = plain_gather(matrices, vectors)
        states = lax.all_to_all(states, "fsdp", split_axis=2, concat_axis=3, tiled=True)[:, :, 0]
        block_out, input_grad, vector_grad, weight_grads = plain_layer(
            tokens, cotangent, lengths, attn, up, down, vector_rows
        )
        owned, vector_sum = plain_reduce(*weight_grads, vector_grad, capacity)
    if ringed:
        early, late = renew_blocks(owned, states, shard_count, share_rows)
        local = settle(early, late, matrices, first_moment, second_moment, left_stat, right_stat)
    else:
        filler = (lax.iota(jnp.int32, capacity) * shard_count + lax.axis_index("fsdp")) >= block_total
        stat = jnp.where(
            filler[:, None, None], jnp.eye(block_side, dtype=jnp.bfloat16), states[0]
        )
        basis = jnp.where(
            filler[:, None, None], jnp.eye(block_side, dtype=jnp.bfloat16), states[1]
        )
        outer, new_basis, turned, update = soap_blocks(
            owned, stat, basis, states[2], states[3], states[4]
        )
        returned = lax.all_to_all(
            jnp.stack([outer, new_basis, turned, update])[:, :, None],
            "fsdp",
            split_axis=3,
            concat_axis=2,
            tiled=True,
        ).reshape(4, capacity * shard_count, -1, block_side)[:, :block_total]
        mirror = lax.ppermute(
            returned[:2], "dp", [(place, place ^ 1) for place in range(lax.axis_size("dp"))]
        )
        returned = returned.astype(jnp.float32)
        mirror = mirror.astype(jnp.float32)
        left_pair = jnp.where(right_side, mirror, returned[:2])
        right_pair = jnp.where(right_side, returned[:2], mirror)
        turned = returned[2]
        local = [
            returned[3],
            FIRST_DECAY * first_moment + (1.0 - FIRST_DECAY) * turned,
            SECOND_DECAY * second_moment + (1.0 - SECOND_DECAY) * turned * turned,
            STAT_DECAY * left_stat + (1.0 - STAT_DECAY) * left_pair[0],
            STAT_DECAY * right_stat + (1.0 - STAT_DECAY) * right_pair[0],
            left_pair[1],
            right_pair[1],
        ]
        local = [matrices - MATRIX_RATE * (local[0] + WEIGHT_DECAY * matrices)] + local
        local[1] = local[0].astype(BF16)
    vfirst_new = FIRST_DECAY * vector_first + (1.0 - FIRST_DECAY) * vector_sum
    vsecond_new = SECOND_DECAY * vector_second + (1.0 - SECOND_DECAY) * vector_sum * vector_sum
    vector_new = vectors - VECTOR_RATE * (vfirst_new / (1.0 - FIRST_DECAY**ADAM_STEP)) / (
        jnp.sqrt(vsecond_new / (1.0 - SECOND_DECAY**ADAM_STEP)) + ADAM_EPSILON
    )
    return (
        block_out,
        input_grad,
        *local,
        vfirst_new,
        vsecond_new,
        vector_new,
    )


def solution(mesh):
    return jax.shard_map(
        shards,
        mesh=mesh,
        in_specs=(
            P(("fsdp", "dp"), None, None),
            P(("fsdp", "dp"), None, None),
            P(("fsdp", "dp")),
            P(None, "fsdp", None),
            P(None, "fsdp", None),
            P(None, "fsdp", None),
            P(None, "fsdp", None),
            P(None, "fsdp", None),
            P(None, "fsdp", None),
            P(None, "fsdp", None),
            P("fsdp"),
            P("fsdp"),
            P("fsdp"),
        ),
        out_specs=(
            P(("fsdp", "dp"), None, None),
            P(("fsdp", "dp"), None, None),
            P(None, "fsdp", None),
            P(None, "fsdp", None),
            P(None, "fsdp", None),
            P(None, "fsdp", None),
            P(None, "fsdp", None),
            P(None, "fsdp", None),
            P(None, "fsdp", None),
            P(None, "fsdp", None),
            P("fsdp"),
            P("fsdp"),
            P("fsdp"),
        ),
        check_vma=False,
    )
```

```python
import functools

import jax
import jax.numpy as jnp
from jax import lax
from jax.experimental import pallas as pl
from jax.experimental.pallas import tpu as pltpu
from jax.sharding import PartitionSpec as P

F32 = jnp.float32
BF16 = jnp.bfloat16
MESH = pl.DeviceIdType.MESH
TRADE = 5
WINDOW = 4
OWNERS = 4

HEADS = 12
HEAD_DIM = 64
FF = 3072
ADAM_STEP = 10


FIRST_DECAY = 0.9
SECOND_DECAY = 0.999
STAT_DECAY = 0.95
ADAM_EPSILON = 1e-08
NORM_EPSILON = 1e-05
MATRIX_RATE = 0.03
VECTOR_RATE = 0.2
WEIGHT_DECAY = 0.01


def assemble(blocks, row_count, column_count):
    block_side = blocks.shape[-1]
    shaped = blocks.reshape(row_count, column_count, block_side, block_side)
    return shaped.transpose(0, 2, 1, 3).reshape(row_count * block_side, column_count * block_side)


def split_blocks(matrix, row_count, column_count, block_side):
    shaped = matrix.reshape(row_count, block_side, column_count, block_side)
    return shaped.transpose(0, 2, 1, 3).reshape(row_count * column_count, block_side, block_side)


def layer_norm(values, gain_row, shift_row):
    center = jnp.mean(values, axis=-1, keepdims=True)
    centered = values - center
    spread = jnp.mean(centered * centered, axis=-1, keepdims=True)
    return centered * lax.rsqrt(spread + NORM_EPSILON) * gain_row + shift_row


def exact_gelu(hidden):
    return jax.nn.gelu(hidden, approximate=False)


def masked_scores(heads_query, heads_key, length):
    slots = heads_query.shape[0]
    scores = jnp.einsum(
        "qhd,khd->hqk", heads_query, heads_key, preferred_element_type=jnp.float32
    ) * HEAD_DIM ** (-0.5)
    visible = lax.iota(jnp.int32, slots) < length
    return jnp.where(visible[None, None, :], scores, -1e30)


def attend(pieces):
    query_rows, key_rows, value_rows, length = pieces
    slots = query_rows.shape[0]
    heads_query = query_rows.reshape(slots, HEADS, HEAD_DIM)
    heads_key = key_rows.reshape(slots, HEADS, HEAD_DIM)
    heads_value = value_rows.reshape(slots, HEADS, HEAD_DIM)
    scores = masked_scores(heads_query, heads_key, length)
    row_max = jnp.max(scores, axis=-1, keepdims=True)
    shifted = jnp.exp(scores - row_max)
    row_total = jnp.sum(shifted, axis=-1, keepdims=True)
    attention_weights = (shifted / row_total).astype(jnp.bfloat16)
    context = jnp.einsum(
        "hqk,khd->qhd", attention_weights, heads_value, preferred_element_type=jnp.float32
    )
    return (
        context.reshape(slots, -1).astype(jnp.bfloat16),
        row_max[..., 0] + jnp.log(row_total[..., 0]),
    )


def attend_back(pieces):
    query_rows, key_rows, value_rows, logsum, grad_context, length = pieces
    slots = query_rows.shape[0]
    heads_query = query_rows.reshape(slots, HEADS, HEAD_DIM)
    heads_key = key_rows.reshape(slots, HEADS, HEAD_DIM)
    heads_value = value_rows.reshape(slots, HEADS, HEAD_DIM)
    heads_grad = grad_context.reshape(slots, HEADS, HEAD_DIM)
    scores = masked_scores(heads_query, heads_key, length)
    attention_weights = jnp.exp(scores - logsum[..., None])
    weights_low = attention_weights.astype(jnp.bfloat16)
    grad_values = jnp.einsum(
        "hqk,qhd->khd", weights_low, heads_grad, preferred_element_type=jnp.float32
    )
    grad_weights = jnp.einsum(
        "qhd,khd->hqk", heads_grad, heads_value, preferred_element_type=jnp.float32
    )
    grad_scores = attention_weights * (
        grad_weights - jnp.sum(grad_weights * attention_weights, axis=-1, keepdims=True)
    )
    scores_low = grad_scores.astype(jnp.bfloat16)
    grad_query = jnp.einsum(
        "hqk,khd->qhd", scores_low, heads_key, preferred_element_type=jnp.float32
    ) * HEAD_DIM ** (-0.5)
    grad_keys = jnp.einsum(
        "hqk,qhd->khd", scores_low, heads_query, preferred_element_type=jnp.float32
    ) * HEAD_DIM ** (-0.5)
    return (
        grad_query.reshape(slots, -1).astype(jnp.bfloat16),
        grad_keys.reshape(slots, -1).astype(jnp.bfloat16),
        grad_values.reshape(slots, -1).astype(jnp.bfloat16),
    )


def dg(a,b,ca,cb):
    return lax.dot_general(a,b,(((ca,),(cb,)),((),())),preferred_element_type=F32)

def halves(a):
    hi=a.astype(BF16)
    return hi,(a-hi.astype(F32)).astype(BF16)

def mm3(a,b,ca,cb):
    ah,al=halves(a); bh,bl=halves(b)
    return dg(ah,bh,ca,cb)+(dg(ah,bl,ca,cb)+dg(al,bh,ca,cb))

def thirds(u):
    h=u.astype(BF16).astype(F32); r=u-h
    m=r.astype(BF16).astype(F32)
    return h,m,r-m

def factor_panels(aug, slots, side=128, between=None):
    sub=lax.broadcasted_iota(jnp.int32,(8,side),0)
    def spread(v): return jnp.broadcast_to(v,(8,side))
    for p in range(side//8):
        k=8*p
        if between is not None:
            between(p)
        panels=[]
        for s in range(slots):
            pw=aug[s,k:k+8,:side]; pv=aug[s,k:k+8,side:]
            cols=[spread(pw[:,k+i:k+i+1]) for i in range(8)]
            S=[[spread(cols[i][j:j+1,:]) if j>=i else None for i in range(8)] for j in range(8)]
            rw=[spread(pw[i:i+1,:]) for i in range(8)]
            rv=[spread(pv[i:i+1,:]) for i in range(8)]
            panels.append((S,rw,rv))
        for i in range(8):
            for S,rw,rv in panels:
                r=lax.rsqrt(S[i][i])
                for j in range(i+1,8): S[j][i]=S[j][i]*r
                for m in range(i+1,8):
                    for j in range(m,8):
                        S[j][m]=S[j][m]-S[j][i]*S[m][i]
                rw[i]=rw[i]*r; rv[i]=rv[i]*r
                for j in range(i+1,8):
                    rw[j]=rw[j]-S[j][i]*rw[i]
                    rv[j]=rv[j]-S[j][i]*rv[i]
        for s,(S,rw,rv) in enumerate(panels):
            uw,uv=rw[0],rv[0]
            for i in range(1,8):
                uw=jnp.where(sub==i,rw[i],uw); uv=jnp.where(sub==i,rv[i],uv)
            aug[s,k:k+8,side:]=uv
            if k+8<side:
                h,m,l=thirds(uw); vh,vm,vl=thirds(uv)
                a=jnp.concatenate([h,h,m,m,h,l],0).astype(BF16)
                b=jnp.concatenate([jnp.concatenate([h,m,h,m,l,h],0),jnp.concatenate([vh,vm,vh,vm,vl,vh],0)],1).astype(BF16)
                t=dg(a,b,0,0)
                aug[s,k+8:,:]=aug[s,k+8:,:]-t[k+8:,:]

def orthonormal_cols(mat, aug, slots, side=128):
    n=mat.shape[-1]
    r=lax.broadcasted_iota(jnp.int32,(side,side),0); c=lax.broadcasted_iota(jnp.int32,(side,side),1)
    eye=(r==c).astype(F32)
    steps=n//side
    for o in range(steps):
        lo=o*side
        for s in range(slots):
            mo=mat[s,:,lo:lo+side]
            aug[s,:,:side]=mm3(mo,mo,0,0)
            aug[s,:,side:]=eye
        factor_panels(aug,slots,side)
        for s in range(slots):
            q=mm3(mat[s,:,lo:lo+side],aug[s,:,side:],1,1)
            mat[s,:,lo:lo+side]=q
            if o+1<steps:
                rest=mat[s,:,lo+side:]
                mat[s,:,lo+side:]=rest-mm3(q,mm3(q,rest,0,0),1,0)


def soap_kernel(grad, stat, own, other, first, second, outer_out, basis_out, turned_out, update_out, mat, aug):
    slots = grad.shape[0]
    right_side = lax.rem(lax.axis_index("dp"), 2) == 1

    def run(is_right):
        near, far = (0, 1) if is_right else (1, 0)

        def one(s, carry):
            g = grad[s].astype(BF16)
            outer = dg(g, g, near, near)
            outer_out[s] = outer.astype(BF16)
            mixed = STAT_DECAY * stat[s].astype(F32) + (1.0 - STAT_DECAY) * outer
            high, rest = halves(mixed)
            mat[s] = dg(high, own[s], 1, 0) + dg(rest, own[s], 1, 0)
            left, right = (other[s], own[s]) if is_right else (own[s], other[s])
            rotated = dg(dg(left, g, 0, 0).astype(BF16), right, 1, 0)
            turned_out[s] = rotated.astype(BF16)
            first_new = FIRST_DECAY * first[s].astype(F32) + (1.0 - FIRST_DECAY) * rotated
            second_new = SECOND_DECAY * second[s].astype(F32) + (1.0 - SECOND_DECAY) * rotated * rotated
            direction = (
                first_new
                / (1.0 - FIRST_DECAY**ADAM_STEP)
                / (jnp.sqrt(second_new / (1.0 - SECOND_DECAY**ADAM_STEP)) + ADAM_EPSILON)
            )
            back = dg(left, direction.astype(BF16), 1, 0).astype(BF16)
            update_out[s] = dg(back, right, 1, 1).astype(BF16)
            return carry

        lax.fori_loop(0, slots, one, 0)

    @pl.when(right_side)
    def _():
        run(True)

    @pl.when(jnp.logical_not(right_side))
    def _():
        run(False)

    orthonormal_cols(mat, aug, slots)
    basis_out[...] = mat[...].astype(BF16)


def soap_blocks(grad, stat, own, other, first, second):
    slots, side, _ = grad.shape
    shape = jax.ShapeDtypeStruct(grad.shape, BF16)
    whole = pl.BlockSpec(memory_space=pltpu.VMEM)
    return pl.pallas_call(
        soap_kernel,
        out_shape=[shape] * 4,
        in_specs=[whole] * 6,
        out_specs=[whole] * 4,
        scratch_shapes=[
            pltpu.VMEM((slots, side, side), F32),
            pltpu.VMEM((slots, 128, 256), F32),
        ],
        compiler_params=pltpu.CompilerParams(vmem_limit_bytes=60 * 2**20),
        name="soap_blocks",
    )(grad, stat, own, other, first, second)


def ring_place(chip, chips):
    along, across = chip // 2, lax.rem(chip, 2)
    return along * (1 - across) + (chips - 1 - along) * across


def ring_chip(place, chips):
    place = lax.rem(place + 8 * chips, chips)
    across = place // (chips // 2)
    along = place * (1 - across) + (chips - 1 - place) * across
    return 2 * along + across


def whereabouts(chips):
    device, replica = lax.axis_index("fsdp"), lax.axis_index("dp")
    chip, core = device // 2, lax.rem(device, 2)
    place = ring_place(chip, chips)
    turn = 1 - 2 * core
    after = (2 * ring_chip(place + turn, chips) + core, replica)
    before = (2 * ring_chip(place - turn, chips) + core, replica)
    sibling = (2 * chip + 1 - core, replica)
    return device, replica, chip, core, place, turn, after, before, sibling


def greet(neighbours):
    barrier = pltpu.get_barrier_semaphore()
    for neighbour in neighbours:
        pl.semaphore_signal(barrier, inc=1, device_id=neighbour, device_id_type=MESH)
    pl.semaphore_wait(barrier, len(neighbours))


def gather_kernel(chips, share, mat_ref, vec_ref, left_stat, right_stat, left_basis, right_basis, first, second,
                  attn, up, down, vecs, states, wide, raw_a, raw_u, raw_d, low_a, low_u, low_d,
                  low_v, trade_send, trade_recv, own_sem, ring_send, ring_recv, sib_send, sib_recv, cross_send, cross_recv,
                  vec_send, vec_recv, vec_sib_send, vec_sib_recv, state_sem):
    device, replica, chip, core, place, turn, after, before, sibling = whereabouts(chips)
    mirror = (device, 1 - replica)
    side = mat_ref.shape[-1]
    both = 2 * share
    rows = pl.ds(pl.multiple_of(share * core, 8), share)
    greet((after, before, sibling, mirror))

    def state(source, slot, item):
        return pltpu.make_async_copy(source.at[slot], wide.at[item], state_sem.at[item])

    def fetch_states(stat, basis, spare, mine):
        for slot in range(3):
            state(stat, slot, slot).start()
            state(basis, slot, 3 + slot).start()
        state(first, mine, 6).start()
        state(second, mine, 7).start()
        state(spare, 0, 8).start()

    @pl.when(replica == 0)
    def _():
        fetch_states(left_stat, left_basis, second, 1)

    @pl.when(replica == 1)
    def _():
        fetch_states(right_stat, right_basis, first, 2)

    groups = ((raw_a, low_a, attn), (raw_u, low_u, up), (raw_d, low_d, down))
    trades = []
    for g, (raw, low, out) in enumerate(groups):
        for b in range(16):
            if g == 0:
                raw[(b % 4) // 2, rows, (b // 4) * 2 * side + (b % 2) * side : (b // 4) * 2 * side + (b % 2 + 1) * side] = mat_ref[b]
            elif g == 1:
                raw[b // 8, rows, (b % 8) * side : (b % 8 + 1) * side] = mat_ref[16 + b]
            else:
                raw[b // 2, rows, (b % 2) * side : (b % 2 + 1) * side] = mat_ref[32 + b]
        part = raw.at[:, rows, :]
        trade = pltpu.make_async_remote_copy(
            src_ref=part, dst_ref=part, send_sem=trade_send.at[g], recv_sem=trade_recv.at[g],
            device_id=sibling, device_id_type=MESH)
        trade.start()
        trades.append(trade)
    low_v[...] = vec_ref[...].astype(BF16).astype(F32)

    def units(kind):
        return ((6 * replica + core, 1), (2 + 2 * core, 2), (6 * (1 - replica) + core, 1))[kind]

    def cut(ref, g, row, kind):
        first, number = units(kind)
        if g == 2:
            return ref.at[pl.ds(first, number), row, :]
        return ref.at[:, row, pl.ds(pl.multiple_of(first * side, 128), number * side)]

    def slab(g, origin, kind):
        return cut(groups[g][2], g, pl.ds(pl.multiple_of(origin * both, 16), both), kind)

    def forward(g, t, kind, origin, source):
        return pltpu.make_async_remote_copy(
            src_ref=source, dst_ref=slab(g, origin, kind), send_sem=ring_send.at[t, g, kind],
            recv_sem=ring_recv.at[t, g, kind], device_id=after, device_id_type=MESH)

    def pass_on(g, t, kind, origin):
        part = slab(g, origin, kind)
        return pltpu.make_async_remote_copy(
            src_ref=part, dst_ref=part, send_sem=sib_send.at[t, g, kind], recv_sem=sib_recv.at[t, g, kind],
            device_id=sibling, device_id_type=MESH)

    def across(g, t, origin, kind):
        part = slab(g, origin, kind)
        return pltpu.make_async_remote_copy(
            src_ref=part, dst_ref=part, send_sem=cross_send.at[t, g], recv_sem=cross_recv.at[t, g],
            device_id=mirror, device_id_type=MESH)

    def vec_of(origin):
        return vecs.at[2 * origin + core]

    def vec_forward(t, origin, source):
        return pltpu.make_async_remote_copy(
            src_ref=source, dst_ref=vec_of(origin), send_sem=vec_send.at[t], recv_sem=vec_recv.at[t],
            device_id=after, device_id_type=MESH)

    def vec_pass_on(t, origin, source):
        return pltpu.make_async_remote_copy(
            src_ref=source, dst_ref=vec_of(origin), send_sem=vec_sib_send.at[t], recv_sem=vec_sib_recv.at[t],
            device_id=sibling, device_id_type=MESH)

    vec_forward(0, chip, low_v).start()
    vec_pass_on(0, chip, low_v).start()
    owns = [pltpu.make_async_copy(low_v, vec_of(chip), own_sem.at[3])]
    owns[0].start()
    for g, (raw, low, out) in enumerate(groups):
        trades[g].wait()
        low[...] = raw[...].astype(BF16)
        for kind in range(2):
            forward(g, 0, kind, chip, cut(low, g, slice(None), kind)).start()
        own = pltpu.make_async_copy(low, out.at[:, pl.ds(pl.multiple_of(chip * both, 16), both), :], own_sem.at[g])
        own.start()
        owns.append(own)

    def take_crossed(t):
        origin = ring_chip(place - turn * t, chips)
        for g in range(3):
            across(g, t, origin, 2).wait_recv()
            pass_on(g, t, 2, origin).start()

    def step(t, carry):
        origin = ring_chip(place - turn * t, chips)
        vec_forward(t - 1, origin, vec_of(origin)).wait_recv()

        @pl.when(t < chips - 1)
        def _():
            vec_forward(t, origin, vec_of(origin)).start()

        vec_pass_on(t, origin, vec_of(origin)).start()
        for g in range(3):
            for kind in range(2):
                arrived = slab(g, origin, kind)
                forward(g, t - 1, kind, origin, arrived).wait_recv()

                @pl.when(t < chips - 1)
                def _():
                    forward(g, t, kind, origin, arrived).start()

                if kind == 0:
                    across(g, t, origin, 0).start()
                pass_on(g, t, kind, origin).start()

        @pl.when(t > 1)
        def _():
            take_crossed(t - 1)

        @pl.when(t < 4)
        def _():
            for item in (3 * t - 3, 3 * t - 2, 3 * t - 1):
                state(first, 0, item).wait()
                for holder in range(2 * chips):
                    states[holder, item] = wide[item, holder].astype(BF16)
        return carry

    lax.fori_loop(1, chips, step, 0)
    take_crossed(chips - 1)
    for own in owns:
        own.wait()

    def finish(t, carry):
        @pl.when(t < chips - 1)
        def _():
            vec_forward(t, chip, vec_of(chip)).wait_send()

        vec_pass_on(t, chip, vec_of(chip)).wait()
        for g in range(3):
            @pl.when(t < chips - 1)
            def _():
                for kind in range(2):
                    forward(g, t, kind, chip, slab(g, chip, kind)).wait_send()

            @pl.when(t > 0)
            def _():
                across(g, t, chip, 0).wait_send()
                for kind in range(3):
                    pass_on(g, t, kind, chip).wait()
        return carry

    lax.fori_loop(0, chips, finish, 0)


def gather_weights(matrices, vector_tile, states, chips):
    total, share, side = matrices.shape
    both = 2 * share
    anywhere = pl.BlockSpec(memory_space=pl.ANY)
    whole = pl.BlockSpec(memory_space=pltpu.VMEM)
    dma = pltpu.SemaphoreType.DMA
    return pl.pallas_call(
        functools.partial(gather_kernel, chips, share),
        out_shape=[
            jax.ShapeDtypeStruct((2, side, 8 * side), BF16),
            jax.ShapeDtypeStruct((2, side, 8 * side), BF16),
            jax.ShapeDtypeStruct((8, side, 2 * side), BF16),
            jax.ShapeDtypeStruct((2 * chips, 16, 128), F32),
            jax.ShapeDtypeStruct((2 * chips, 9, share, side), BF16),
        ],
        in_specs=[whole, whole] + [anywhere] * 6,
        out_specs=[anywhere] * 4 + [whole],
        scratch_shapes=[
            pltpu.VMEM((9, 2 * chips, share, side), F32),
            pltpu.VMEM((2, both, 8 * side), F32),
            pltpu.VMEM((2, both, 8 * side), F32),
            pltpu.VMEM((8, both, 2 * side), F32),
            pltpu.VMEM((2, both, 8 * side), BF16),
            pltpu.VMEM((2, both, 8 * side), BF16),
            pltpu.VMEM((8, both, 2 * side), BF16),
            pltpu.VMEM((16, 128), F32),
            dma((3,)), dma((3,)), dma((4,)),
            dma((chips - 1, 3, 2)), dma((chips - 1, 3, 2)), dma((chips, 3, 3)), dma((chips, 3, 3)),
            dma((chips, 3)), dma((chips, 3)),
            dma((chips - 1,)), dma((chips - 1,)), dma((chips,)), dma((chips,)), dma((9,)),
        ],
        compiler_params=pltpu.CompilerParams(collective_id=1, has_side_effects=True, vmem_limit_bytes=60 * 2**20),
        name="gather_weights",
    )(matrices, vector_tile, *[part.reshape(3, 2 * chips, share, side) for part in states])


def opposite(device, step, count):
    result, bit = 0, 1
    while bit < count:
        one, two = lax.rem(device // bit, 2), lax.rem(step // bit, 2)
        result = result + bit * (one + two - 2 * one * two)
        bit *= 2
    return result


def settle_kernel(early, early_last, late, mat, first, second, left, right, mat_new, mat_low, first_new, second_new, left_new, right_new,
                  left_basis, right_basis):
    share = mat.shape[2]
    for f in range(mat.shape[1]):
        for s in range(3):
            def item(plane, index):
                source, spot = (early, index) if index < 4 else (early_last, index - 4)
                return source[plane, f, spot * share : (spot + 1) * share, :].astype(F32)

            turned = item(*((0, 5), (0, 2), (1, 2))[s])
            update = item(*((1, 5), (0, 3), (1, 3))[s])
            outer = (4, 0, 1)[s]
            fresh = mat[s, f] - MATRIX_RATE * (update + WEIGHT_DECAY * mat[s, f])
            mat_new[s, f] = fresh
            mat_low[s, f] = fresh.astype(BF16)
            first_new[s, f] = FIRST_DECAY * first[s, f] + (1.0 - FIRST_DECAY) * turned
            second_new[s, f] = SECOND_DECAY * second[s, f] + (1.0 - SECOND_DECAY) * turned * turned
            left_new[s, f] = STAT_DECAY * left[s, f] + (1.0 - STAT_DECAY) * item(0, outer)
            right_new[s, f] = STAT_DECAY * right[s, f] + (1.0 - STAT_DECAY) * item(1, outer)
            for panel in range(late.shape[0]):
                lanes = slice(128 * panel, 128 * (panel + 1))
                left_basis[s, f, :, lanes] = late[panel, 0, f, s * share : (s + 1) * share, :].astype(F32)
                right_basis[s, f, :, lanes] = late[panel, 1, f, s * share : (s + 1) * share, :].astype(F32)


def settle(early, early_last, late, matrices, first, second, left, right):
    _, count, tall, side = early.shape
    panels, share = late.shape[0], matrices.shape[1]
    state = pl.BlockSpec((3, OWNERS, share, side), lambda f: (0, f, 0, 0))
    shape = jax.ShapeDtypeStruct((3, count, share, side), F32)
    low = jax.ShapeDtypeStruct((3, count, share, side), BF16)
    results = pl.pallas_call(
        settle_kernel,
        grid=(count // OWNERS,),
        out_shape=[shape, low] + [shape] * 6,
        in_specs=[
            pl.BlockSpec((2, OWNERS, tall, side), lambda f: (0, f, 0, 0)),
            pl.BlockSpec((2, OWNERS, early_last.shape[2], side), lambda f: (0, f, 0, 0)),
            pl.BlockSpec((panels, 2, OWNERS, late.shape[3], 128), lambda f: (0, 0, f, 0, 0)),
        ]
        + [state] * 5,
        out_specs=[state] * 8,
        compiler_params=pltpu.CompilerParams(vmem_limit_bytes=60 * 2**20),
        name="settle",
    )(early, early_last, late, *[part.reshape(3, count, share, side) for part in (matrices, first, second, left, right)])
    return [part.reshape(matrices.shape) for part in results]


def normal_parts(value):
    size = jnp.abs(value) * 0.7071067811865476
    t = 1.0 / (1.0 + 0.3275911 * size)
    bell = jnp.exp(-size * size)
    series = t * (0.254829592 + t * (-0.284496736 + t * (1.421413741 + t * (-1.453152027 + t * 1.061405429))))
    tail = 0.5 * series * bell
    return jnp.where(value >= 0.0, 1.0 - tail, tail), bell * 0.3989422804014327


def span(index, size):
    return pl.ds(pl.multiple_of(index * size, size), size)


def looped(count, body):
    def step(index, carry):
        body(index)
        return carry

    lax.fori_loop(0, count, step, 0)


def vector_row(vecs, row, width):
    lane = lax.broadcasted_iota(jnp.int32, (1, 128), 1)
    pieces = []
    for pair in range(width // 128):
        chunk = row * (width // 64) + 2 * pair
        one = vecs[chunk // 9, chunk % 9 : chunk % 9 + 1, :]
        chunk += 1
        two = vecs[chunk // 9, chunk % 9 : chunk % 9 + 1, :]
        pieces.append(jnp.where(lane < 64, one, pltpu.roll(two, 64, 1)))
    return jnp.concatenate(pieces, axis=1)


def vector_tiles_of(rows, row_up, tiles):
    chunks = rows.shape[1] // 64
    for f in range(tiles.shape[0]):
        for i in range(9):
            row, place = divmod(9 * f + i, chunks)
            if 5 <= row < 9:
                spot = (row - 5) * chunks + place
                piece = row_up[spot // 4, :, 128 * (spot % 4 // 2) : 128 * (spot % 4 // 2) + 128]
            else:
                piece = rows[row : row + 1, 128 * (place // 2) : 128 * (place // 2) + 128]
            tiles[f, i : i + 1, :] = pltpu.roll(piece, 64, 1) if place % 2 else piece


def layer_kernel(length_ref, x_ref, cot_ref, tiles, attn_hbm, up_hbm, down_hbm,
                 out_ref, logs, grad_vec, grad_vec_up, qkv_out, grad_c_out, turned_x_out, grad_r_out, grad_out, grad_up, grad_down,
                 w_attn, w_up, w_down, qkv, context, hat_one, scale_one, normed, active, slope, hidden_low,
                 grad_r, low_e, grad_c, turned_x, turned_n, turned_c, stage_w, stage_t,
                 vec, vec_up, load_sem, wide_sem, tall_sem, save_sem):
    slots, width = x_ref.shape
    length = length_ref[0]
    chunks = w_up.shape[1] // 256
    thirds_of = width // 256
    loads = [pltpu.make_async_copy(source, target, load_sem.at[i])
             for i, (source, target) in enumerate(((attn_hbm, w_attn), (up_hbm, w_up), (down_hbm, w_down)))]
    for load in loads:
        load.start()

    def turn(source, target):
        def one(index):
            target[:, span(index, 128)] = source[span(index, 128), :].T

        looped(slots // 128, one)

    def wide_copy(target, slot, index):
        return pltpu.make_async_copy(stage_w.at[slot], target.at[:, span(index, 256)], wide_sem.at[slot])

    def tall_copy(slot, index):
        return pltpu.make_async_copy(stage_t.at[slot], grad_down.at[span(index, 256), :], tall_sem.at[slot])

    def put_wide(target, index, value, first):
        slot = lax.rem(index, 2)

        @pl.when(jnp.logical_not(first))
        def _():
            wide_copy(target, slot, index).wait()

        stage_w[slot] = value.astype(BF16)
        wide_copy(target, slot, index).start()

    grad_vec[...] = jnp.zeros_like(grad_vec)
    for row in range(12):
        vec[row : row + 1, :] = vector_row(tiles, row, width)
        if 5 <= row < 9:
            for third in range(thirds_of):
                vec_up[(row - 5) * thirds_of + third] = vec[row : row + 1, 256 * third : 256 * (third + 1)]
    turn(x_ref, turned_x)
    loads[0].wait()

    def project(index):
        lanes = span(index, 256)
        part = index // thirds_of
        row = jnp.where(part == 0, vec[0:1, span(lax.rem(index, thirds_of), 256)],
                        jnp.where(part == 2, vec[1:2, span(lax.rem(index, thirds_of), 256)], 0.0))
        qkv[:, lanes] = (jnp.dot(x_ref[...], w_attn[:, lanes], preferred_element_type=F32) + row).astype(BF16)

    looped(3 * thirds_of, project)
    saves = [pltpu.make_async_copy(source, target, save_sem.at[i]) for i, (source, target) in enumerate((
        (qkv, qkv_out), (turned_x, turned_x_out), (grad_c, grad_c_out), (grad_r, grad_r_out)))]
    saves[0].start()
    saves[1].start()

    lane = lax.broadcasted_iota(jnp.int32, (slots, 128), 1)
    tall_lane = lax.broadcasted_iota(jnp.int32, (128, 128), 0)
    seen = lax.broadcasted_iota(jnp.int32, (slots, 128), 0) < length

    def head_lanes(head, value):
        keep = (lane < HEAD_DIM) if head == 0 else (lane >= HEAD_DIM)
        return jnp.where(keep, value, jnp.zeros_like(value))

    def lanes_of(pair, part):
        return pl.ds(pl.multiple_of(part * width + pair * 128, 128), 128)

    def attend(pair):
        key, value = qkv[:, lanes_of(pair, 1)], qkv[:, lanes_of(pair, 2)]
        turned_value = value.T
        keys = [head_lanes(head, key * HEAD_DIM ** (-0.5)) for head in range(2)]
        for block in range(slots // 128):
            rows = slice(128 * block, 128 * (block + 1))
            query = qkv[rows, lanes_of(pair, 0)]
            both = []
            for head in range(2):
                scores = jnp.where(seen, dg(keys[head], query, 1, 1), -1e30)
                top = jnp.max(scores, axis=0, keepdims=True)
                shifted = jnp.exp(scores - top)
                total = jnp.sum(shifted, axis=0, keepdims=True)
                weights = (shifted * (1.0 / total)).astype(BF16)
                both.append(jnp.dot(turned_value, weights, preferred_element_type=F32))
                logs[2 * pair + head, :, rows] = top + jnp.log(total)
            merged = jnp.where(tall_lane < HEAD_DIM, both[0], both[1])
            context[rows, lanes_of(pair, 0)] = merged.T.astype(BF16)

    looped(width // 128, attend)
    turn(context, turned_c)

    def mix(index):
        lanes = span(index, 256)
        away = pl.ds(pl.multiple_of(3 * width + index * 256, 256), 256)
        value = jnp.dot(context[...], w_attn[:, away], preferred_element_type=F32) + vec[2:3, lanes]
        hat_one[:, lanes] = x_ref[:, lanes].astype(F32) + value

    looped(thirds_of, mix)

    def standard(value):
        centered = value - jnp.mean(value, axis=-1, keepdims=True)
        scale = lax.rsqrt(jnp.mean(centered * centered, axis=-1, keepdims=True) + NORM_EPSILON)
        return centered * scale, scale

    def norm_one(index):
        rows = span(index, 128)
        hat, scale = standard(hat_one[rows, :])
        hat_one[rows, :] = hat
        scale_one[rows, :] = jnp.broadcast_to(scale, (128, 128))
        normed[rows, :] = (hat * vec[3:4, :] + vec[4:5, :]).astype(BF16)

    looped(slots // 128, norm_one)
    turn(normed, turned_n)
    loads[1].wait()

    def rise(index):
        lanes = span(index, 256)
        hidden = jnp.dot(normed[...], w_up[:, lanes], preferred_element_type=F32) + vec_up[index]
        below, density = normal_parts(hidden)
        active[:, lanes] = (hidden * below).astype(BF16)
        slope[:, lanes] = below + hidden * density

    looped(chunks, rise)
    loads[2].wait()

    def fall(index):
        lanes = span(index, 256)
        value = jnp.dot(active[...], w_down[:, lanes], preferred_element_type=F32)
        grad_r[:, lanes] = hat_one[:, lanes] * vec[3:4, lanes] + vec[4:5, lanes] + value + vec[9:10, lanes]

    looped(thirds_of, fall)

    def unstandard(grad_hat, hat, scale):
        return scale * (grad_hat - jnp.mean(grad_hat, axis=-1, keepdims=True)
                        - hat * jnp.mean(grad_hat * hat, axis=-1, keepdims=True))

    def add_row(row, value):
        grad_vec[row : row + 1, :] += jnp.sum(value, axis=0, keepdims=True)

    def norm_two(index):
        rows = span(index, 128)
        hat, scale = standard(grad_r[rows, :])
        out_ref[rows, :] = (hat * vec[10:11, :] + vec[11:12, :]).astype(BF16)
        place = lax.broadcasted_iota(jnp.int32, (128, width), 0) + index * 128
        grad = jnp.where(place < length, cot_ref[rows, :].astype(F32), 0.0)
        add_row(10, grad * hat)
        add_row(11, grad)
        back = unstandard(grad * vec[10:11, :], hat, scale)
        add_row(9, back)
        grad_r[rows, :] = back
        low_e[rows, :] = back.astype(BF16)

    looped(slots // 128, norm_two)

    def sink(index):
        lanes = span(index, 256)
        grad = dg(low_e[...], w_down[lanes, :], 1, 1) * slope[:, lanes]
        grad_vec_up[index] = jnp.sum(grad, axis=0, keepdims=True)
        low = grad.astype(BF16)
        hidden_low[:, lanes] = low
        put_wide(grad_up, index, jnp.dot(turned_n[...], low, preferred_element_type=F32), index < 2)
        slot = lax.rem(index, 2)

        @pl.when(index >= 2)
        def _():
            tall_copy(slot, index).wait()

        stage_t[slot] = dg(active[:, lanes], low_e[...], 0, 0).astype(BF16)
        tall_copy(slot, index).start()

    looped(chunks, sink)

    def rise_back(index):
        lanes = span(index, 256)
        grad_r[:, lanes] += dg(hidden_low[...], w_up[lanes, :], 1, 1)

    looped(thirds_of, rise_back)

    def norm_one_back(index):
        rows = span(index, 128)
        hat, grad = hat_one[rows, :], grad_r[rows, :]
        add_row(3, grad * hat)
        add_row(4, grad)
        back = unstandard(grad * vec[3:4, :], hat, scale_one[rows, 0:1])
        add_row(2, back)
        grad_r[rows, :] = back
        low_e[rows, :] = back.astype(BF16)


    def mix_back(index):
        lanes = span(index, 256)
        put_wide(grad_out, index, jnp.dot(turned_c[...], low_e[:, lanes], preferred_element_type=F32), False)
        away = pl.ds(3 * width, width)
        grad_c[:, lanes] = dg(low_e[...], w_attn[lanes, away], 1, 1).astype(BF16)

    looped(slots // 128, norm_one_back)
    saves[3].start()
    looped(thirds_of, mix_back)
    saves[2].start()
    for slot in range(2):
        wide_copy(grad_out, slot, 0).wait()
        tall_copy(slot, 0).wait()
    for save in saves:
        save.wait()


def layer(length, inputs, cotangent, tiles, attn, up, down):
    slots, width = inputs.shape
    tall = down.shape[0]
    anywhere = pl.BlockSpec(memory_space=pl.ANY)
    whole = pl.BlockSpec(memory_space=pltpu.VMEM)
    vmem = pltpu.VMEM
    dma = pltpu.SemaphoreType.DMA
    return pl.pallas_call(
        layer_kernel,
        out_shape=[
            jax.ShapeDtypeStruct((slots, width), BF16),
            jax.ShapeDtypeStruct((width // HEAD_DIM, 1, slots), F32),
            jax.ShapeDtypeStruct((16, width), F32),
            jax.ShapeDtypeStruct((tall // 256, 1, 256), F32),
            jax.ShapeDtypeStruct((slots, 3 * width), BF16),
            jax.ShapeDtypeStruct((slots, width), BF16),
            jax.ShapeDtypeStruct((width, slots), BF16),
            jax.ShapeDtypeStruct((slots, width), F32),
            jax.ShapeDtypeStruct((width, width), BF16),
            jax.ShapeDtypeStruct((width, tall), BF16),
            jax.ShapeDtypeStruct((tall, width), BF16),
        ],
        in_specs=[pl.BlockSpec(memory_space=pltpu.SMEM)] + [whole] * 3 + [anywhere] * 3,
        out_specs=[whole] * 4 + [anywhere] * 7,
        scratch_shapes=[
            vmem((width, 4 * width), BF16), vmem((width, tall), BF16), vmem((tall, width), BF16),
            vmem((slots, 3 * width), BF16), vmem((slots, width), BF16),
            vmem((slots, width), F32), vmem((slots, 128), F32), vmem((slots, width), BF16),
            vmem((slots, tall), BF16), vmem((slots, tall), F32), vmem((slots, tall), BF16),
            vmem((slots, width), F32), vmem((slots, width), BF16), vmem((slots, width), BF16),
            vmem((width, slots), BF16), vmem((width, slots), BF16), vmem((width, slots), BF16),
            vmem((2, width, 256), BF16), vmem((2, 256, width), BF16),
            vmem((16, width), F32), vmem((tall // 256, 1, 256), F32),
            dma((3,)), dma((2,)), dma((2,)), dma((4,)),
        ],
        compiler_params=pltpu.CompilerParams(vmem_limit_bytes=60 * 2**20),
        cost_estimate=pl.CostEstimate(flops=25_000_000_000, bytes_accessed=40_000_000, transcendentals=8_000_000),
        name="layer",
    )(length, inputs, cotangent, tiles, attn, up, down)


def conclude_kernel(chips, share, length_ref, logs, vec_part, vec_up_part, parts, qkv_hbm, grad_c_hbm, turned_x_hbm, grad_r_hbm,
                    attn_hbm, g_out, g_up, g_down,
                    grad_x, vec_sum, early, early_last, late,
                    qkv, grad_c, turned_x, grad_r, w_qkv, grad_heads, probs, dscores, g_qkv, grad_vec, tiles,
                    mine, theirs, ring, crossed, peer, vmine, vring, vpeer, owned,
                    states, items, mat, aug, out_early, out_last, out_late,
                    load_sem, mine_sem, sib_send, sib_recv, ring_send, ring_recv, cross_send, cross_recv, peer_send, peer_recv,
                    state_send, state_recv, note_send, note_recv, relay_send, relay_recv, keep_sem):
    device, replica, chip, core, place, turn, after, before, sibling = whereabouts(chips)
    count = 2 * chips
    mirror = (device, 1 - replica)
    side = mine.shape[-1]
    width = 2 * side
    slots = qkv.shape[0]
    quarter = side // 4
    last = chips - 1
    part = 128
    panels = side // part
    length = length_ref[0]

    def partner(step):
        return opposite(device, step, count), replica

    barrier = pltpu.get_barrier_semaphore()

    def hail(step, carry):
        pl.semaphore_signal(barrier, inc=1, device_id=partner(step), device_id_type=MESH)
        return carry

    lax.fori_loop(1, count, hail, 0)
    pl.semaphore_signal(barrier, inc=1, device_id=mirror, device_id_type=MESH)
    pl.semaphore_wait(barrier, count)

    loads = [pltpu.make_async_copy(source, target, load_sem.at[i]) for i, (source, target) in enumerate((
        (qkv_hbm, qkv), (grad_c_hbm, grad_c), (turned_x_hbm, turned_x), (grad_r_hbm, grad_r),
        (attn_hbm.at[:, : 3 * width], w_qkv)))]


    def quarters(first, number):
        return pl.ds(pl.multiple_of(first * quarter, 16), number * quarter)

    carried = quarters(replica, 3)
    private = quarters(3 * replica, 1)
    foreign = quarters(3 * (1 - replica), 1)

    def column(index):
        return pl.ds(pl.multiple_of(index * side, 128), side)

    def fetch(owner, wanted, start):
        which = owner // 4
        i, j = lax.rem(owner, 4) // 2, lax.rem(owner, 2)
        if 0 in wanted:
            @pl.when(which < 3)
            def _():
                start(0, g_qkv.at[i, :, column(2 * which + j)])

            @pl.when(which == 3)
            def _():
                start(0, g_out.at[i, :, column(j)])

            start(3, tiles.at[owner])
        else:
            start(1, g_up.at[owner // 8, :, column(lax.rem(owner, 8))])
            start(2, g_down.at[owner // 2, :, column(lax.rem(owner, 2))])

    def local(t, slot, source):
        target = vmine.at[0, t] if slot == 3 else mine.at[t, slot]
        return pltpu.make_async_copy(source, target, mine_sem.at[t, slot])

    def to_sibling(t, slot, source):
        target = vmine.at[1, t] if slot == 3 else theirs.at[t, slot]
        return pltpu.make_async_remote_copy(
            src_ref=source, dst_ref=target, send_sem=sib_send.at[t, slot], recv_sem=sib_recv.at[t, slot],
            device_id=sibling, device_id_type=MESH)

    def to_next(t, slot):
        source, target = (vmine.at[0, t], vring.at[t]) if slot == 3 else (mine.at[t, slot, carried, :], ring.at[t, slot])
        return pltpu.make_async_remote_copy(
            src_ref=source, dst_ref=target, send_sem=ring_send.at[t, slot], recv_sem=ring_recv.at[t, slot],
            device_id=after, device_id_type=MESH)

    def across(t, slot):
        return pltpu.make_async_remote_copy(
            src_ref=mine.at[t, slot, foreign, :], dst_ref=crossed.at[t, slot], send_sem=cross_send.at[t, slot],
            recv_sem=cross_recv.at[t, slot], device_id=mirror, device_id_type=MESH)

    def to_mirror(slot):
        source, target = (vmine.at[0, last], vpeer) if slot == 3 else (mine.at[last, slot, carried, :], peer.at[slot, carried, :])
        return pltpu.make_async_remote_copy(
            src_ref=source, dst_ref=target, send_sem=peer_send.at[slot], recv_sem=peer_recv.at[slot],
            device_id=mirror, device_id_type=MESH)

    def begin(t, wanted):
        fetch(2 * ring_chip(place + turn * (t + 1), chips) + 1 - core, wanted,
              lambda slot, source: to_sibling(t, slot, source).start())
        fetch(2 * ring_chip(place - turn * (t + 1), chips) + core, wanted, lambda slot, source: local(t, slot, source).start())

    def sources(slot):
        return tiles.at[0] if slot == 3 else g_up.at[0, :, :side]

    def pair_up(t, wanted):
        for slot in wanted:
            local(t, slot, sources(slot)).wait()
            to_sibling(t, slot, sources(slot)).wait_recv()
            if slot == 3:
                vmine[0, t] = vmine[0, t] + vmine[1, t]
            else:
                mine[t, slot] = (mine[t, slot].astype(F32) + theirs[t, slot].astype(F32)).astype(BF16)
                across(t, slot).start()

    def add(t, slot, hold, extra):
        mine[t, slot, hold, :] = (mine[t, slot, hold, :].astype(F32) + extra.astype(F32)).astype(BF16)

    def pass_round(t, wanted):
        for slot in wanted:
            if slot < 3:
                across(t, slot).wait_recv()
                add(t, slot, private, crossed[t, slot])

            @pl.when(t > 0)
            def _():
                to_next(t - 1, slot).wait_recv()
                if slot == 3:
                    vmine[0, t] = vmine[0, t] + vring[t - 1]
                else:
                    add(t, slot, carried, ring[t - 1, slot])

            @pl.when(t < last)
            def _():
                to_next(t, slot).start()

            @pl.when(t == last)
            def _():
                to_mirror(slot).start()

    def own_sum(slot):
        to_mirror(slot).wait()
        if slot == 3:
            vec_sum[...] = vmine[0, last] + vpeer[...]
            return
        shared = slice(quarter, 3 * quarter)
        owned[slot, shared, :] = (mine[last, slot, shared, :].astype(F32) + peer[slot, shared, :].astype(F32)).astype(BF16)
        owned[slot, private, :] = mine[last, slot, private, :]
        owned[slot, foreign, :] = peer[slot, foreign, :]

    feed, rest = (1, 2), (3, 0)

    def rest_step(t):
        @pl.when(t + 3 < chips)
        def _():
            begin(t + 3, rest)

        @pl.when(t == 0)
        def _():
            pair_up(1, rest)

        @pl.when(t + 2 < chips)
        def _():
            pair_up(t + 2, rest)

        pass_round(t, rest)


    lane = lax.broadcasted_iota(jnp.int32, (slots, 128), 1)
    seen = lax.broadcasted_iota(jnp.int32, (slots, 128), 0) < length

    def head_lanes(head, value):
        keep = (lane < HEAD_DIM) if head == 0 else (lane >= HEAD_DIM)
        return jnp.where(keep, value, jnp.zeros_like(value))

    def lanes_of(pair, member):
        return pl.ds(pl.multiple_of(member * width + pair * 128, 128), 128)

    def attend_back(pair):
        query, key, value = [qkv[:, lanes_of(pair, member)] for member in range(3)]
        grad = grad_c[:, lanes_of(pair, 0)]
        turned_key = key.T
        found = []
        for head in range(2):
            near_key = head_lanes(head, key * HEAD_DIM ** (-0.5))
            near_value = head_lanes(head, value)
            for block in range(slots // 128):
                rows = slice(128 * block, 128 * (block + 1))
                scores = jnp.where(seen, dg(near_key, query[rows], 1, 1), -1e30)
                weights = jnp.exp(scores - logs[2 * pair + head, :, rows])
                back = dg(near_value, grad[rows], 1, 1)
                scores_back = weights * (back - jnp.sum(back * weights, axis=0, keepdims=True))
                probs[head, :, rows] = weights.astype(BF16)
                dscores[head, :, rows] = scores_back.astype(BF16)
            found.append((
                jnp.dot(turned_key, dscores[head], preferred_element_type=F32),
                jnp.dot(dscores[head], query, preferred_element_type=F32),
                jnp.dot(probs[head], grad, preferred_element_type=F32),
            ))
        top = lax.broadcasted_iota(jnp.int32, (128, slots), 0) < HEAD_DIM
        turned_query = jnp.where(top, found[0][0], found[1][0]) * HEAD_DIM ** (-0.5)
        grad_heads[:, lanes_of(pair, 0)] = turned_query.T.astype(BF16)
        grad_heads[:, lanes_of(pair, 1)] = (jnp.where(lane < HEAD_DIM, found[0][1], found[1][1]) * HEAD_DIM ** (-0.5)).astype(BF16)
        grad_heads[:, lanes_of(pair, 2)] = jnp.where(lane < HEAD_DIM, found[0][2], found[1][2]).astype(BF16)

    def project_back(index):
        lanes = span(index, 256)
        value = jnp.dot(turned_x[...], grad_heads[:, lanes], preferred_element_type=F32)
        g_qkv[:, :, lanes] = value.astype(BF16).reshape(2, side, 256)

    def input_back(index):
        lanes = span(index, 256)
        grad_x[:, lanes] = grad_r[:, lanes] + dg(grad_heads[...], w_qkv[lanes, :], 1, 1)


    def join(pair, carry):
        rows = pl.ds(pl.multiple_of(2 * share * pair, 16), 2 * share)
        for item in range(9):
            two = [parts[2 * pair + index, item].astype(F32) for index in range(2)]
            states[item, rows, :] = jnp.concatenate(two, axis=0).astype(BF16)
        return carry

    def trade(index):
        source = (5 - replica, 3, 8)[index]
        return pltpu.make_async_remote_copy(
            src_ref=states.at[source], dst_ref=states.at[9 + index], send_sem=state_send.at[index],
            recv_sem=state_recv.at[index], device_id=mirror, device_id_type=MESH)

    def update(rotated, left, right, first, second):
        first_new = FIRST_DECAY * first.astype(F32) + (1.0 - FIRST_DECAY) * rotated
        second_new = SECOND_DECAY * second.astype(F32) + (1.0 - SECOND_DECAY) * rotated * rotated
        direction = (
            first_new
            / (1.0 - FIRST_DECAY**ADAM_STEP)
            / (jnp.sqrt(second_new / (1.0 - SECOND_DECAY**ADAM_STEP)) + ADAM_EPSILON)
        )
        back = dg(left, direction.astype(BF16), 1, 0).astype(BF16)
        return dg(back, right, 1, 1)

    def prepare(s):
        for is_right in (False, True):
            @pl.when(replica == int(is_right))
            def _():
                near = 0 if is_right else 1
                g = owned[s]
                outer = dg(g, g, near, near)
                items[(4, 0, 1)[s]] = outer
                mixed = STAT_DECAY * states[s].astype(F32) + (1.0 - STAT_DECAY) * outer
                high, low = halves(mixed)
                mat[s] = dg(high, states[3 + s], 1, 0) + dg(low, states[3 + s], 1, 0)
                if s not in (0, 2 if is_right else 1):
                    return
                other = states[10] if s == 0 else states[9]
                left, right = (other, states[3 + s]) if is_right else (states[3 + s], other)
                rotated = dg(dg(left, g, 0, 0).astype(BF16), right, 1, 0)
                if s > 0:
                    items[2] = rotated
                    items[3] = update(rotated, left, right, states[6], states[7])
                elif is_right:
                    items[5] = update(rotated, left, right, states[8], states[11])
                else:
                    items[5] = rotated

    def rows_of(holder):
        return pl.ds(pl.multiple_of(holder * share, 8), share)

    def outgoing(kind, holder):
        return (out_early.at[holder], out_last.at[holder])[kind] if kind < 2 else out_late.at[kind - 2, holder]

    def incoming(kind, owner):
        return (early.at[replica, owner], early_last.at[replica, owner])[kind] if kind < 2 else late.at[kind - 2, replica, owner]

    def pack(kind):
        def one(holder, carry):
            rows = rows_of(holder)
            if kind < 2:
                for pair in ((0, 1), (2,))[kind]:
                    two = jnp.concatenate([items[2 * pair, rows, :], items[2 * pair + 1, rows, :]], axis=0)
                    spot = pair if kind == 0 else 0
                    (out_early, out_last)[kind][holder, 2 * share * spot : 2 * share * (spot + 1), :] = two.astype(BF16)
            else:
                lo = (kind - 2) * part
                stacked = [mat[s, rows, lo : lo + part] for s in range(3)] + [jnp.zeros((8, part), F32)]
                out_late[kind - 2, holder] = jnp.concatenate(stacked, axis=0).astype(BF16)
            return carry

        lax.fori_loop(0, count, one, 0)

    def note(kind, step):
        target = partner(step)
        return pltpu.make_async_remote_copy(
            src_ref=outgoing(kind, target[0]), dst_ref=incoming(kind, device), send_sem=note_send.at[kind, step],
            recv_sem=note_recv.at[kind, step], device_id=target, device_id_type=MESH)

    def relay(kind, step):
        block = incoming(kind, partner(step)[0])
        return pltpu.make_async_remote_copy(
            src_ref=block, dst_ref=block, send_sem=relay_send.at[kind, step], recv_sem=relay_recv.at[kind, step],
            device_id=mirror, device_id_type=MESH)

    def keep(kind):
        return pltpu.make_async_copy(outgoing(kind, device), incoming(kind, device), keep_sem.at[kind])

    def launch(kind):
        pack(kind)
        keep(kind).start()

        def one(step, carry):
            note(kind, step).start()
            return carry

        lax.fori_loop(1, chips, one, 0)
        near.extend((kind, step) for step in range(chips))
        far.extend((kind, step) for step in range(chips, count))

    def hand_on(kind, step):
        note(kind, step).wait_recv()
        relay(kind, step).start()

    near, far, flying = [], [], []

    def hand_on_near(number):
        for kind, step in near[:number]:
            if step == 0:
                keep(kind).wait()
                relay(kind, 0).start()
            else:
                hand_on(kind, step)
        del near[:number]

    def pump(number):
        for kind, step in far[:number]:
            if len(flying) >= WINDOW:
                hand_on(*flying.pop(0))
            note(kind, step).start()
            flying.append((kind, step))
        del far[:number]


    def first(index, carry):
        begin(index, feed)
        return carry

    lax.fori_loop(0, 3, first, 0)
    for load in loads[:2]:
        load.start()
    lax.fori_loop(0, count // 2, join, 0)
    pair_up(0, feed)
    for load in loads[2:]:
        load.start()
    grad_vec[...] = vec_part[...]

    def main(t, carry):
        @pl.when(t + 3 < chips)
        def _():
            begin(t + 3, feed)

        @pl.when(t == 0)
        def _():
            pair_up(1, feed)

        @pl.when(t + 2 < chips)
        def _():
            pair_up(t + 2, feed)

        pass_round(t, feed)

        @pl.when(t == 0)
        def _():
            for load in loads[:2]:
                load.wait()

        @pl.when(t < 2)
        def _():
            def one(third, carry):
                attend_back(3 * t + third)
                return carry

            lax.fori_loop(0, 3, one, 0)

        @pl.when(t == TRADE)
        def _():
            for index in range(3):
                trade(index).start()

        @pl.when(t == 2)
        def _():
            loads[2].wait()
            grad_vec[0:1, :] = jnp.sum(grad_heads[:, :width].astype(F32), axis=0, keepdims=True)
            grad_vec[1:2, :] = jnp.sum(grad_heads[:, 2 * width :].astype(F32), axis=0, keepdims=True)
            looped(3 * width // 256, project_back)
            vector_tiles_of(grad_vec, vec_up_part, tiles)

            def start_rest(index, carry):
                begin(index, rest)
                return carry

            lax.fori_loop(0, 3, start_rest, 0)
            pair_up(0, rest)

        @pl.when(t > 2)
        def _():
            rest_step(t - 3)
        return carry

    lax.fori_loop(0, chips, main, 0)
    for index in range(3):
        trade(index).wait()
    own_sum(1)
    prepare(1)
    rest_step(jnp.int32(chips - 3))
    own_sum(2)
    prepare(2)
    launch(0)
    pump(WINDOW)
    rest_step(jnp.int32(chips - 2))
    hand_on_near(4)
    pump(1)
    for load in loads[3:]:
        load.wait()
    looped(width // 256, input_back)
    pump(1)
    rest_step(jnp.int32(chips - 1))
    hand_on_near(4)
    pump(1)
    own_sum(0)
    prepare(0)
    launch(1)

    def between(moment):
        if far and moment % (5, 3, 2, 2, 2)[far[0][0]] == 0:
            pump(1)
        elif near and moment % 2 == 1:
            hand_on_near(1)

    row_index = lax.broadcasted_iota(jnp.int32, (part, part), 0)
    column_index = lax.broadcasted_iota(jnp.int32, (part, part), 1)
    eye = (row_index == column_index).astype(F32)
    for o in range(panels):
        lo = o * part
        for s in range(3):
            block = mat[s, :, lo : lo + part]
            aug[s, :, :part] = mm3(block, block, 0, 0)
            aug[s, :, part:] = eye
        factor_panels(aug, 3, part, lambda p: between(16 * o + p))
        for s in range(3):
            mat[s, :, lo : lo + part] = mm3(mat[s, :, lo : lo + part], aug[s, :, part:], 1, 1)
        launch(2 + o)
        if o + 1 < panels:
            for s in range(3):
                q, remaining = mat[s, :, lo : lo + part], mat[s, :, lo + part :]
                mat[s, :, lo + part :] = remaining - mm3(q, mm3(q, remaining, 0, 0), 1, 0)
    while far or near:
        pump(2)
        hand_on_near(2)
    for kind, step in flying:
        hand_on(kind, step)
    own_sum(3)

    def finish(step, carry):
        for kind in range(2 + panels):
            relay(kind, step).wait()

            @pl.when(step > 0)
            def _():
                note(kind, step).wait_send()

        @pl.when(step < chips)
        def _():
            for slot in range(4):
                to_sibling(step, slot, sources(slot)).wait_send()
                if slot < 3:
                    across(step, slot).wait_send()

                @pl.when(step < last)
                def _():
                    to_next(step, slot).wait_send()
        return carry

    lax.fori_loop(0, count, finish, 0)


def conclude(length, logs, vec_part, vec_up_part, parts, qkv, grad_c, turned_x, grad_r, attn, g_out, g_up, g_down, share, chips):
    side = g_up.shape[1]
    width, count = 2 * side, 2 * chips
    slots = qkv.shape[0]
    tall = -(-3 * share // 16) * 16
    panels = side // 128
    anywhere = pl.BlockSpec(memory_space=pl.ANY)
    whole = pl.BlockSpec(memory_space=pltpu.VMEM)
    vmem = pltpu.VMEM
    dma = pltpu.SemaphoreType.DMA
    return pl.pallas_call(
        functools.partial(conclude_kernel, chips, share),
        out_shape=[
            jax.ShapeDtypeStruct((slots, width), F32),
            jax.ShapeDtypeStruct((16, 128), F32),
            jax.ShapeDtypeStruct((2, count, 4 * share, side), BF16),
            jax.ShapeDtypeStruct((2, count, 2 * share, side), BF16),
            jax.ShapeDtypeStruct((panels, 2, count, tall, 128), BF16),
        ],
        in_specs=[pl.BlockSpec(memory_space=pltpu.SMEM)] + [whole] * 4 + [anywhere] * 8,
        out_specs=[whole] * 2 + [anywhere] * 3,
        scratch_shapes=[
            vmem((slots, 3 * width), BF16), vmem((slots, width), BF16), vmem((width, slots), BF16), vmem((slots, width), F32),
            vmem((width, 3 * width), BF16), vmem((slots, 3 * width), BF16), vmem((2, slots, slots), BF16),
            vmem((2, slots, slots), BF16), vmem((2, side, 3 * width), BF16), vmem((16, width), F32), vmem((count, 16, 128), F32),
            vmem((chips, 3, side, side), BF16), vmem((chips, 3, side, side), BF16),
            vmem((chips - 1, 3, 3 * side // 4, side), BF16), vmem((chips, 3, side // 4, side), BF16), vmem((3, side, side), BF16),
            vmem((2, chips, 16, 128), F32), vmem((chips - 1, 16, 128), F32), vmem((16, 128), F32), vmem((3, side, side), BF16),
            vmem((12, side, side), BF16), vmem((6, side, side), F32), vmem((3, side, side), F32), vmem((3, 128, 256), F32),
            vmem((count, 4 * share, side), BF16), vmem((count, 2 * share, side), BF16), vmem((panels, count, tall, 128), BF16),
            dma((5,)), dma((chips, 4)), dma((chips, 4)), dma((chips, 4)), dma((chips - 1, 4)), dma((chips - 1, 4)),
            dma((chips, 3)), dma((chips, 3)), dma((4,)), dma((4,)), dma((3,)), dma((3,)),
            dma((2 + panels, count)), dma((2 + panels, count)), dma((2 + panels, count)), dma((2 + panels, count)),
            dma((2 + panels,)),
        ],
        compiler_params=pltpu.CompilerParams(collective_id=2, has_side_effects=True, vmem_limit_bytes=62 * 2**20),
        name="conclude",
    )(length, logs, vec_part, vec_up_part, parts, qkv, grad_c, turned_x, grad_r, attn, g_out, g_up, g_down)


def plain_gather(matrices, vectors):
    side = matrices.shape[-1]
    blocks = lax.all_gather(matrices.astype(BF16), "fsdp", axis=1, tiled=True)
    attn = jnp.concatenate([assemble(blocks[4 * part : 4 * part + 4], 2, 2) for part in range(4)], axis=1)
    up = assemble(blocks[16:32], 2, 8)
    down = assemble(blocks[32:], 8, 2)
    rows = lax.all_gather(vectors.astype(BF16), "fsdp", axis=0, tiled=True)
    return attn, up, down, rows.astype(F32).reshape(-1, 2 * side)


def plain_reduce(grad_qkv, grad_out, grad_up, grad_down, vector_grad, capacity):
    shard_count = lax.axis_size("fsdp")
    width = grad_up.shape[0]
    side = width // 2
    blocks = jnp.concatenate(
        [split_blocks(grad_qkv[:, part * width : (part + 1) * width], 2, 2, side) for part in range(3)]
        + [split_blocks(grad_out, 2, 2, side), split_blocks(grad_up, 2, 8, side), split_blocks(grad_down, 8, 2, side)],
        axis=0,
    )
    owned = lax.psum_scatter(
        to_owners(blocks, capacity, shard_count), "fsdp", scatter_dimension=1, tiled=True
    )
    owned = lax.psum(owned, "dp")[:, 0]
    share = lax.psum_scatter(vector_grad, "fsdp", scatter_dimension=0, tiled=True)
    return owned, lax.psum(share, "dp")


def to_owners(blocks, capacity, shard_count):
    spare = capacity * shard_count - blocks.shape[0]
    blocks = jnp.pad(blocks, ((0, spare),) + ((0, 0),) * (blocks.ndim - 1))
    return blocks.reshape((capacity, shard_count) + blocks.shape[1:])


def plain_layer(tokens, cotangent, lengths, attn, up, down, vector_rows):
    sequences, slots, model_width = tokens.shape
    rows_total = sequences * slots
    unit_ratio = FF // model_width

    def shaped(array):
        return array.reshape(sequences, slots, array.shape[-1])

    weight_qkv, weight_out = attn[:, : 3 * model_width], attn[:, 3 * model_width :]
    inputs = tokens.reshape(rows_total, model_width)
    joined = jnp.dot(inputs, weight_qkv, preferred_element_type=F32)
    query_rows = (joined[:, :model_width] + vector_rows[0]).astype(BF16)
    key_rows = joined[:, model_width : 2 * model_width].astype(BF16)
    value_rows = (joined[:, 2 * model_width :] + vector_rows[1]).astype(BF16)
    context, logsum = lax.map(
        attend, (shaped(query_rows), shaped(key_rows), shaped(value_rows), lengths)
    )
    context = context.reshape(rows_total, model_width)
    attended = jnp.dot(context, weight_out, preferred_element_type=F32) + vector_rows[2]
    normed, pull_one = jax.vjp(
        layer_norm, inputs.astype(F32) + attended, vector_rows[3], vector_rows[4]
    )
    normed_low = normed.astype(BF16)
    hidden = jnp.dot(normed_low, up, preferred_element_type=F32) + vector_rows[
        5 : 5 + unit_ratio
    ].reshape(FF)
    active, pull_gelu = jax.vjp(exact_gelu, hidden)
    active_low = active.astype(BF16)
    result = jnp.dot(active_low, down, preferred_element_type=F32) + vector_rows[5 + unit_ratio]
    output, pull_two = jax.vjp(
        layer_norm, normed + result, vector_rows[6 + unit_ratio], vector_rows[7 + unit_ratio]
    )
    block_out = output.reshape(sequences, slots, model_width).astype(BF16)
    visible = (lax.iota(jnp.int32, slots)[None, :] < lengths[:, None]).astype(F32)
    grad_output = (cotangent.astype(F32) * visible[:, :, None]).reshape(rows_total, model_width)
    grad_second, grad_gain_two, grad_shift_two = pull_two(grad_output)
    second_low = grad_second.astype(BF16)
    grad_down = jnp.einsum("tf,td->fd", active_low, second_low, preferred_element_type=F32)
    grad_active = jnp.einsum("td,fd->tf", second_low, down, preferred_element_type=F32)
    (grad_hidden,) = pull_gelu(grad_active)
    hidden_low = grad_hidden.astype(BF16)
    grad_up = jnp.einsum("td,tf->df", normed_low, hidden_low, preferred_element_type=F32)
    grad_normed = grad_second + jnp.einsum("tf,df->td", hidden_low, up, preferred_element_type=F32)
    grad_mixed, grad_gain_one, grad_shift_one = pull_one(grad_normed)
    mixed_low = grad_mixed.astype(BF16)
    grad_out_weight = jnp.einsum("td,te->de", context, mixed_low, preferred_element_type=F32)
    grad_context = jnp.einsum(
        "te,de->td", mixed_low, weight_out, preferred_element_type=F32
    ).astype(BF16)
    grad_query, grad_keys, grad_values = lax.map(
        attend_back,
        (
            shaped(query_rows),
            shaped(key_rows),
            shaped(value_rows),
            logsum,
            shaped(grad_context),
            lengths,
        ),
    )
    grad_joined = jnp.concatenate(
        [
            grad_query.reshape(rows_total, model_width),
            grad_keys.reshape(rows_total, model_width),
            grad_values.reshape(rows_total, model_width),
        ],
        axis=1,
    )
    grad_qkv = jnp.einsum("td,te->de", inputs, grad_joined, preferred_element_type=F32)
    input_grad = grad_mixed + jnp.einsum(
        "te,de->td", grad_joined, weight_qkv, preferred_element_type=F32
    )
    vector_grad = jnp.concatenate(
        [
            jnp.sum(grad_joined[:, :model_width], axis=0, dtype=F32)[None],
            jnp.sum(grad_joined[:, 2 * model_width :], axis=0, dtype=F32)[None],
            jnp.sum(grad_mixed, axis=0)[None],
            grad_gain_one[None],
            grad_shift_one[None],
            jnp.sum(grad_hidden, axis=0).reshape(unit_ratio, model_width),
            jnp.sum(grad_second, axis=0)[None],
            grad_gain_two[None],
            grad_shift_two[None],
        ],
        axis=0,
    ).reshape(-1)
    weight_grads = [part.astype(BF16) for part in (grad_qkv, grad_out_weight, grad_up, grad_down)]
    return block_out, input_grad.reshape(tokens.shape), vector_grad, weight_grads


def shards(
    tokens,
    cotangent,
    lengths,
    matrices,
    first_moment,
    second_moment,
    left_stat,
    right_stat,
    left_basis,
    right_basis,
    vectors,
    vector_first,
    vector_second,
):
    shard_count = lax.axis_size("fsdp")
    replicas = lax.axis_size("dp")
    sequences, slots, model_width = tokens.shape
    block_total, share_rows, block_side = matrices.shape
    capacity = -(-block_total // shard_count)
    ringed = replicas == 2 and sequences == 1 and vectors.shape[0] == 576 and capacity * shard_count == block_total == 48 and share_rows % 8 == 0 and capacity == 3

    right_side = lax.axis_index("dp") % 2 == 1
    if ringed:
        vector_tile = jnp.pad(vectors.reshape(9, 64), ((0, 7), (0, 64)))
        attn, up, down, tiles, states = gather_weights(
            matrices,
            vector_tile,
            (left_stat, right_stat, left_basis, right_basis, first_moment, second_moment),
            shard_count // 2,
        )
        states = lax.all_to_all(states, "fsdp", split_axis=0, concat_axis=0, tiled=True)
        weight_attn = attn.reshape(model_width, 4 * model_width)
        block_out, logs, vec_part, vec_up_part, qkv, grad_c, turned_x, grad_r, *weight_grads = layer(
            lengths,
            tokens[0],
            cotangent[0],
            tiles,
            weight_attn,
            up.reshape(model_width, FF),
            down.reshape(FF, model_width),
        )
        slabs = [part.reshape(-1, block_side, part.shape[1]) for part in weight_grads]
        input_grad, vector_sum, early, early_last, late = conclude(
            lengths, logs, vec_part, vec_up_part, states, qkv, grad_c, turned_x, grad_r, weight_attn, *slabs,
            share_rows, shard_count // 2
        )
        block_out, input_grad = block_out[None], input_grad[None]
        vector_sum = vector_sum[:9, :64].reshape(-1)
        local = settle(early, early_last, late, matrices, first_moment, second_moment, left_stat, right_stat)
    else:
        chosen = [
            jnp.where(right_side, right_stat, left_stat),
            jnp.where(right_side, right_basis, left_basis),
            jnp.where(right_side, left_basis, right_basis),
            first_moment,
            second_moment,
        ]
        states = jnp.stack([to_owners(part.astype(BF16), capacity, shard_count) for part in chosen])
        attn, up, down, vector_rows = plain_gather(matrices, vectors)
        states = lax.all_to_all(states, "fsdp", split_axis=2, concat_axis=3, tiled=True)[:, :, 0]
        block_out, input_grad, vector_grad, weight_grads = plain_layer(
            tokens, cotangent, lengths, attn, up, down, vector_rows
        )
        owned, vector_sum = plain_reduce(*weight_grads, vector_grad, capacity)
        filler = (lax.iota(jnp.int32, capacity) * shard_count + lax.axis_index("fsdp")) >= block_total
        stat = jnp.where(
            filler[:, None, None], jnp.eye(block_side, dtype=jnp.bfloat16), states[0]
        )
        basis = jnp.where(
            filler[:, None, None], jnp.eye(block_side, dtype=jnp.bfloat16), states[1]
        )
        outer, new_basis, turned, update = soap_blocks(
            owned, stat, basis, states[2], states[3], states[4]
        )
        returned = lax.all_to_all(
            jnp.stack([outer, new_basis, turned, update])[:, :, None],
            "fsdp",
            split_axis=3,
            concat_axis=2,
            tiled=True,
        ).reshape(4, capacity * shard_count, -1, block_side)[:, :block_total]
        mirror = lax.ppermute(
            returned[:2], "dp", [(place, place ^ 1) for place in range(lax.axis_size("dp"))]
        )
        returned = returned.astype(jnp.float32)
        mirror = mirror.astype(jnp.float32)
        left_pair = jnp.where(right_side, mirror, returned[:2])
        right_pair = jnp.where(right_side, returned[:2], mirror)
        turned = returned[2]
        local = [
            returned[3],
            FIRST_DECAY * first_moment + (1.0 - FIRST_DECAY) * turned,
            SECOND_DECAY * second_moment + (1.0 - SECOND_DECAY) * turned * turned,
            STAT_DECAY * left_stat + (1.0 - STAT_DECAY) * left_pair[0],
            STAT_DECAY * right_stat + (1.0 - STAT_DECAY) * right_pair[0],
            left_pair[1],
            right_pair[1],
        ]
        local = [matrices - MATRIX_RATE * (local[0] + WEIGHT_DECAY * matrices)] + local
        local[1] = local[0].astype(BF16)
    vfirst_new = FIRST_DECAY * vector_first + (1.0 - FIRST_DECAY) * vector_sum
    vsecond_new = SECOND_DECAY * vector_second + (1.0 - SECOND_DECAY) * vector_sum * vector_sum
    vector_new = vectors - VECTOR_RATE * (vfirst_new / (1.0 - FIRST_DECAY**ADAM_STEP)) / (
        jnp.sqrt(vsecond_new / (1.0 - SECOND_DECAY**ADAM_STEP)) + ADAM_EPSILON
    )
    return (
        block_out,
        input_grad,
        *local,
        vfirst_new,
        vsecond_new,
        vector_new,
    )


def solution(mesh):
    return jax.shard_map(
        shards,
        mesh=mesh,
        in_specs=(
            P(("fsdp", "dp"), None, None),
            P(("fsdp", "dp"), None, None),
            P(("fsdp", "dp")),
            P(None, "fsdp", None),
            P(None, "fsdp", None),
            P(None, "fsdp", None),
            P(None, "fsdp", None),
            P(None, "fsdp", None),
            P(None, "fsdp", None),
            P(None, "fsdp", None),
            P("fsdp"),
            P("fsdp"),
            P("fsdp"),
        ),
        out_specs=(
            P(("fsdp", "dp"), None, None),
            P(("fsdp", "dp"), None, None),
            P(None, "fsdp", None),
            P(None, "fsdp", None),
            P(None, "fsdp", None),
            P(None, "fsdp", None),
            P(None, "fsdp", None),
            P(None, "fsdp", None),
            P(None, "fsdp", None),
            P(None, "fsdp", None),
            P("fsdp"),
            P("fsdp"),
            P("fsdp"),
        ),
        check_vma=False,
    )
```

```python
import functools

import jax
import jax.numpy as jnp
from jax import lax
from jax.experimental import pallas as pl
from jax.experimental.pallas import tpu as pltpu
from jax.sharding import PartitionSpec as P

F32 = jnp.float32
BF16 = jnp.bfloat16
MESH = pl.DeviceIdType.MESH
TRADE = 5
WINDOW = 4
OWNERS = 4

HEADS = 12
HEAD_DIM = 64
FF = 3072
ADAM_STEP = 10


FIRST_DECAY = 0.9
SECOND_DECAY = 0.999
STAT_DECAY = 0.95
ADAM_EPSILON = 1e-08
NORM_EPSILON = 1e-05
MATRIX_RATE = 0.03
VECTOR_RATE = 0.2
WEIGHT_DECAY = 0.01


def assemble(blocks, row_count, column_count):
    block_side = blocks.shape[-1]
    shaped = blocks.reshape(row_count, column_count, block_side, block_side)
    return shaped.transpose(0, 2, 1, 3).reshape(row_count * block_side, column_count * block_side)


def split_blocks(matrix, row_count, column_count, block_side):
    shaped = matrix.reshape(row_count, block_side, column_count, block_side)
    return shaped.transpose(0, 2, 1, 3).reshape(row_count * column_count, block_side, block_side)


def layer_norm(values, gain_row, shift_row):
    center = jnp.mean(values, axis=-1, keepdims=True)
    centered = values - center
    spread = jnp.mean(centered * centered, axis=-1, keepdims=True)
    return centered * lax.rsqrt(spread + NORM_EPSILON) * gain_row + shift_row


def exact_gelu(hidden):
    return jax.nn.gelu(hidden, approximate=False)


def masked_scores(heads_query, heads_key, length):
    slots = heads_query.shape[0]
    scores = jnp.einsum(
        "qhd,khd->hqk", heads_query, heads_key, preferred_element_type=jnp.float32
    ) * HEAD_DIM ** (-0.5)
    visible = lax.iota(jnp.int32, slots) < length
    return jnp.where(visible[None, None, :], scores, -1e30)


def attend(pieces):
    query_rows, key_rows, value_rows, length = pieces
    slots = query_rows.shape[0]
    heads_query = query_rows.reshape(slots, HEADS, HEAD_DIM)
    heads_key = key_rows.reshape(slots, HEADS, HEAD_DIM)
    heads_value = value_rows.reshape(slots, HEADS, HEAD_DIM)
    scores = masked_scores(heads_query, heads_key, length)
    row_max = jnp.max(scores, axis=-1, keepdims=True)
    shifted = jnp.exp(scores - row_max)
    row_total = jnp.sum(shifted, axis=-1, keepdims=True)
    attention_weights = (shifted / row_total).astype(jnp.bfloat16)
    context = jnp.einsum(
        "hqk,khd->qhd", attention_weights, heads_value, preferred_element_type=jnp.float32
    )
    return (
        context.reshape(slots, -1).astype(jnp.bfloat16),
        row_max[..., 0] + jnp.log(row_total[..., 0]),
    )


def attend_back(pieces):
    query_rows, key_rows, value_rows, logsum, grad_context, length = pieces
    slots = query_rows.shape[0]
    heads_query = query_rows.reshape(slots, HEADS, HEAD_DIM)
    heads_key = key_rows.reshape(slots, HEADS, HEAD_DIM)
    heads_value = value_rows.reshape(slots, HEADS, HEAD_DIM)
    heads_grad = grad_context.reshape(slots, HEADS, HEAD_DIM)
    scores = masked_scores(heads_query, heads_key, length)
    attention_weights = jnp.exp(scores - logsum[..., None])
    weights_low = attention_weights.astype(jnp.bfloat16)
    grad_values = jnp.einsum(
        "hqk,qhd->khd", weights_low, heads_grad, preferred_element_type=jnp.float32
    )
    grad_weights = jnp.einsum(
        "qhd,khd->hqk", heads_grad, heads_value, preferred_element_type=jnp.float32
    )
    grad_scores = attention_weights * (
        grad_weights - jnp.sum(grad_weights * attention_weights, axis=-1, keepdims=True)
    )
    scores_low = grad_scores.astype(jnp.bfloat16)
    grad_query = jnp.einsum(
        "hqk,khd->qhd", scores_low, heads_key, preferred_element_type=jnp.float32
    ) * HEAD_DIM ** (-0.5)
    grad_keys = jnp.einsum(
        "hqk,qhd->khd", scores_low, heads_query, preferred_element_type=jnp.float32
    ) * HEAD_DIM ** (-0.5)
    return (
        grad_query.reshape(slots, -1).astype(jnp.bfloat16),
        grad_keys.reshape(slots, -1).astype(jnp.bfloat16),
        grad_values.reshape(slots, -1).astype(jnp.bfloat16),
    )


def dg(a,b,ca,cb):
    return lax.dot_general(a,b,(((ca,),(cb,)),((),())),preferred_element_type=F32)

def halves(a):
    hi=a.astype(BF16)
    return hi,(a-hi.astype(F32)).astype(BF16)

def mm3(a,b,ca,cb):
    ah,al=halves(a); bh,bl=halves(b)
    return dg(ah,bh,ca,cb)+(dg(ah,bl,ca,cb)+dg(al,bh,ca,cb))

def thirds(u):
    h=u.astype(BF16).astype(F32); r=u-h
    m=r.astype(BF16).astype(F32)
    return h,m,r-m

def factor_panels(aug, slots, side=128, between=None):
    sub=lax.broadcasted_iota(jnp.int32,(8,side),0)
    def spread(v): return jnp.broadcast_to(v,(8,side))
    for p in range(side//8):
        k=8*p
        if between is not None:
            between(p)
        panels=[]
        for s in range(slots):
            pw=aug[s,k:k+8,:side]; pv=aug[s,k:k+8,side:]
            cols=[spread(pw[:,k+i:k+i+1]) for i in range(8)]
            S=[[spread(cols[i][j:j+1,:]) if j>=i else None for i in range(8)] for j in range(8)]
            rw=[spread(pw[i:i+1,:]) for i in range(8)]
            rv=[spread(pv[i:i+1,:]) for i in range(8)]
            panels.append((S,rw,rv))
        for i in range(8):
            for S,rw,rv in panels:
                r=lax.rsqrt(S[i][i])
                for j in range(i+1,8): S[j][i]=S[j][i]*r
                for m in range(i+1,8):
                    for j in range(m,8):
                        S[j][m]=S[j][m]-S[j][i]*S[m][i]
                rw[i]=rw[i]*r; rv[i]=rv[i]*r
                for j in range(i+1,8):
                    rw[j]=rw[j]-S[j][i]*rw[i]
                    rv[j]=rv[j]-S[j][i]*rv[i]
        for s,(S,rw,rv) in enumerate(panels):
            uw,uv=rw[0],rv[0]
            for i in range(1,8):
                uw=jnp.where(sub==i,rw[i],uw); uv=jnp.where(sub==i,rv[i],uv)
            aug[s,k:k+8,side:]=uv
            if k+8<side:
                h,m,l=thirds(uw); vh,vm,vl=thirds(uv)
                a=jnp.concatenate([h,h,m,m,h,l],0).astype(BF16)
                b=jnp.concatenate([jnp.concatenate([h,m,h,m,l,h],0),jnp.concatenate([vh,vm,vh,vm,vl,vh],0)],1).astype(BF16)
                t=dg(a,b,0,0)
                aug[s,k+8:,:]=aug[s,k+8:,:]-t[k+8:,:]

def orthonormal_cols(mat, aug, slots, side=128):
    n=mat.shape[-1]
    r=lax.broadcasted_iota(jnp.int32,(side,side),0); c=lax.broadcasted_iota(jnp.int32,(side,side),1)
    eye=(r==c).astype(F32)
    steps=n//side
    for o in range(steps):
        lo=o*side
        for s in range(slots):
            mo=mat[s,:,lo:lo+side]
            aug[s,:,:side]=mm3(mo,mo,0,0)
            aug[s,:,side:]=eye
        factor_panels(aug,slots,side)
        for s in range(slots):
            q=mm3(mat[s,:,lo:lo+side],aug[s,:,side:],1,1)
            mat[s,:,lo:lo+side]=q
            if o+1<steps:
                rest=mat[s,:,lo+side:]
                mat[s,:,lo+side:]=rest-mm3(q,mm3(q,rest,0,0),1,0)


def soap_kernel(grad, stat, own, other, first, second, outer_out, basis_out, turned_out, update_out, mat, aug):
    slots = grad.shape[0]
    right_side = lax.rem(lax.axis_index("dp"), 2) == 1

    def run(is_right):
        near, far = (0, 1) if is_right else (1, 0)

        def one(s, carry):
            g = grad[s].astype(BF16)
            outer = dg(g, g, near, near)
            outer_out[s] = outer.astype(BF16)
            mixed = STAT_DECAY * stat[s].astype(F32) + (1.0 - STAT_DECAY) * outer
            high, rest = halves(mixed)
            mat[s] = dg(high, own[s], 1, 0) + dg(rest, own[s], 1, 0)
            left, right = (other[s], own[s]) if is_right else (own[s], other[s])
            rotated = dg(dg(left, g, 0, 0).astype(BF16), right, 1, 0)
            turned_out[s] = rotated.astype(BF16)
            first_new = FIRST_DECAY * first[s].astype(F32) + (1.0 - FIRST_DECAY) * rotated
            second_new = SECOND_DECAY * second[s].astype(F32) + (1.0 - SECOND_DECAY) * rotated * rotated
            direction = (
                first_new
                / (1.0 - FIRST_DECAY**ADAM_STEP)
                / (jnp.sqrt(second_new / (1.0 - SECOND_DECAY**ADAM_STEP)) + ADAM_EPSILON)
            )
            back = dg(left, direction.astype(BF16), 1, 0).astype(BF16)
            update_out[s] = dg(back, right, 1, 1).astype(BF16)
            return carry

        lax.fori_loop(0, slots, one, 0)

    @pl.when(right_side)
    def _():
        run(True)

    @pl.when(jnp.logical_not(right_side))
    def _():
        run(False)

    orthonormal_cols(mat, aug, slots)
    basis_out[...] = mat[...].astype(BF16)


def soap_blocks(grad, stat, own, other, first, second):
    slots, side, _ = grad.shape
    shape = jax.ShapeDtypeStruct(grad.shape, BF16)
    whole = pl.BlockSpec(memory_space=pltpu.VMEM)
    return pl.pallas_call(
        soap_kernel,
        out_shape=[shape] * 4,
        in_specs=[whole] * 6,
        out_specs=[whole] * 4,
        scratch_shapes=[
            pltpu.VMEM((slots, side, side), F32),
            pltpu.VMEM((slots, 128, 256), F32),
        ],
        compiler_params=pltpu.CompilerParams(vmem_limit_bytes=60 * 2**20),
        name="soap_blocks",
    )(grad, stat, own, other, first, second)


def ring_place(chip, chips):
    along, across = chip // 2, lax.rem(chip, 2)
    return along * (1 - across) + (chips - 1 - along) * across


def ring_chip(place, chips):
    place = lax.rem(place + 8 * chips, chips)
    across = place // (chips // 2)
    along = place * (1 - across) + (chips - 1 - place) * across
    return 2 * along + across


def whereabouts(chips):
    device, replica = lax.axis_index("fsdp"), lax.axis_index("dp")
    chip, core = device // 2, lax.rem(device, 2)
    place = ring_place(chip, chips)
    turn = 1 - 2 * core
    after = (2 * ring_chip(place + turn, chips) + core, replica)
    before = (2 * ring_chip(place - turn, chips) + core, replica)
    sibling = (2 * chip + 1 - core, replica)
    return device, replica, chip, core, place, turn, after, before, sibling


def greet(neighbours):
    barrier = pltpu.get_barrier_semaphore()
    for neighbour in neighbours:
        pl.semaphore_signal(barrier, inc=1, device_id=neighbour, device_id_type=MESH)
    pl.semaphore_wait(barrier, len(neighbours))


def gather_kernel(chips, share, mat_ref, vec_ref, left_stat, right_stat, left_basis, right_basis, first, second,
                  attn, up, down, vecs, states, wide, raw_a, raw_u, raw_d, low_a, low_u, low_d,
                  low_v, trade_send, trade_recv, own_sem, ring_send, ring_recv, sib_send, sib_recv, cross_send, cross_recv,
                  vec_send, vec_recv, vec_sib_send, vec_sib_recv, state_sem):
    device, replica, chip, core, place, turn, after, before, sibling = whereabouts(chips)
    mirror = (device, 1 - replica)
    side = mat_ref.shape[-1]
    both = 2 * share
    rows = pl.ds(pl.multiple_of(share * core, 8), share)
    barrier = pltpu.get_barrier_semaphore()
    for neighbour in (after, before, sibling, mirror):
        pl.semaphore_signal(barrier, inc=1, device_id=neighbour, device_id_type=MESH)

    def state(source, slot, item):
        return pltpu.make_async_copy(source.at[slot], wide.at[item], state_sem.at[item])

    def fetch_states(stat, basis, spare, mine):
        for slot in range(3):
            state(stat, slot, slot).start()
            state(basis, slot, 3 + slot).start()
        state(first, mine, 6).start()
        state(second, mine, 7).start()
        state(spare, 0, 8).start()

    @pl.when(replica == 0)
    def _():
        fetch_states(left_stat, left_basis, second, 1)

    @pl.when(replica == 1)
    def _():
        fetch_states(right_stat, right_basis, first, 2)

    groups = ((raw_a, low_a, attn), (raw_u, low_u, up), (raw_d, low_d, down))
    for g, (raw, low, out) in enumerate(groups):
        for b in range(16):
            if g == 0:
                raw[(b % 4) // 2, rows, (b // 4) * 2 * side + (b % 2) * side : (b // 4) * 2 * side + (b % 2 + 1) * side] = mat_ref[b]
            elif g == 1:
                raw[b // 8, rows, (b % 8) * side : (b % 8 + 1) * side] = mat_ref[16 + b]
            else:
                raw[b // 2, rows, (b % 2) * side : (b % 2 + 1) * side] = mat_ref[32 + b]
    pl.semaphore_wait(barrier, 4)
    trades = []
    for g, (raw, low, out) in enumerate(groups):
        part = raw.at[:, rows, :]
        trade = pltpu.make_async_remote_copy(
            src_ref=part, dst_ref=part, send_sem=trade_send.at[g], recv_sem=trade_recv.at[g],
            device_id=sibling, device_id_type=MESH)
        trade.start()
        trades.append(trade)
    low_v[...] = vec_ref[...].astype(BF16).astype(F32)

    def units(kind):
        return ((6 * replica + core, 1), (2 + 2 * core, 2), (6 * (1 - replica) + core, 1))[kind]

    def cut(ref, g, row, kind):
        first, number = units(kind)
        if g == 2:
            return ref.at[pl.ds(first, number), row, :]
        return ref.at[:, row, pl.ds(pl.multiple_of(first * side, 128), number * side)]

    def slab(g, origin, kind):
        return cut(groups[g][2], g, pl.ds(pl.multiple_of(origin * both, 16), both), kind)

    def forward(g, t, kind, origin, source):
        return pltpu.make_async_remote_copy(
            src_ref=source, dst_ref=slab(g, origin, kind), send_sem=ring_send.at[t, g, kind],
            recv_sem=ring_recv.at[t, g, kind], device_id=after, device_id_type=MESH)

    def pass_on(g, t, kind, origin):
        part = slab(g, origin, kind)
        return pltpu.make_async_remote_copy(
            src_ref=part, dst_ref=part, send_sem=sib_send.at[t, g, kind], recv_sem=sib_recv.at[t, g, kind],
            device_id=sibling, device_id_type=MESH)

    def across(g, t, origin, kind):
        part = slab(g, origin, kind)
        return pltpu.make_async_remote_copy(
            src_ref=part, dst_ref=part, send_sem=cross_send.at[t, g], recv_sem=cross_recv.at[t, g],
            device_id=mirror, device_id_type=MESH)

    def vec_of(origin):
        return vecs.at[2 * origin + core]

    def vec_forward(t, origin, source):
        return pltpu.make_async_remote_copy(
            src_ref=source, dst_ref=vec_of(origin), send_sem=vec_send.at[t], recv_sem=vec_recv.at[t],
            device_id=after, device_id_type=MESH)

    def vec_pass_on(t, origin, source):
        return pltpu.make_async_remote_copy(
            src_ref=source, dst_ref=vec_of(origin), send_sem=vec_sib_send.at[t], recv_sem=vec_sib_recv.at[t],
            device_id=sibling, device_id_type=MESH)

    vec_forward(0, chip, low_v).start()
    vec_pass_on(0, chip, low_v).start()
    owns = [pltpu.make_async_copy(low_v, vec_of(chip), own_sem.at[3])]
    owns[0].start()
    for g, (raw, low, out) in enumerate(groups):
        trades[g].wait()
        low[...] = raw[...].astype(BF16)
        for kind in range(2):
            forward(g, 0, kind, chip, cut(low, g, slice(None), kind)).start()
        own = pltpu.make_async_copy(low, out.at[:, pl.ds(pl.multiple_of(chip * both, 16), both), :], own_sem.at[g])
        own.start()
        owns.append(own)

    def take_crossed(t):
        origin = ring_chip(place - turn * t, chips)
        for g in range(3):
            across(g, t, origin, 2).wait_recv()
            pass_on(g, t, 2, origin).start()

    def step(t, carry):
        origin = ring_chip(place - turn * t, chips)
        vec_forward(t - 1, origin, vec_of(origin)).wait_recv()

        @pl.when(t < chips - 1)
        def _():
            vec_forward(t, origin, vec_of(origin)).start()

        vec_pass_on(t, origin, vec_of(origin)).start()
        for g in range(3):
            for kind in range(2):
                arrived = slab(g, origin, kind)
                forward(g, t - 1, kind, origin, arrived).wait_recv()

                @pl.when(t < chips - 1)
                def _():
                    forward(g, t, kind, origin, arrived).start()

                if kind == 0:
                    across(g, t, origin, 0).start()
                pass_on(g, t, kind, origin).start()

        @pl.when(t > 1)
        def _():
            take_crossed(t - 1)

        @pl.when(t < 4)
        def _():
            for item in (3 * t - 3, 3 * t - 2, 3 * t - 1):
                state(first, 0, item).wait()
                for holder in range(2 * chips):
                    states[holder, item] = wide[item, holder].astype(BF16)
        return carry

    lax.fori_loop(1, chips, step, 0)
    take_crossed(chips - 1)
    for own in owns:
        own.wait()

    def finish(t, carry):
        @pl.when(t < chips - 1)
        def _():
            vec_forward(t, chip, vec_of(chip)).wait_send()

        vec_pass_on(t, chip, vec_of(chip)).wait()
        for g in range(3):
            @pl.when(t < chips - 1)
            def _():
                for kind in range(2):
                    forward(g, t, kind, chip, slab(g, chip, kind)).wait_send()

            @pl.when(t > 0)
            def _():
                across(g, t, chip, 0).wait_send()
                for kind in range(3):
                    pass_on(g, t, kind, chip).wait()
        return carry

    lax.fori_loop(0, chips, finish, 0)


def gather_weights(matrices, vector_tile, states, chips):
    total, share, side = matrices.shape
    both = 2 * share
    anywhere = pl.BlockSpec(memory_space=pl.ANY)
    whole = pl.BlockSpec(memory_space=pltpu.VMEM)
    dma = pltpu.SemaphoreType.DMA
    return pl.pallas_call(
        functools.partial(gather_kernel, chips, share),
        out_shape=[
            jax.ShapeDtypeStruct((2, side, 8 * side), BF16),
            jax.ShapeDtypeStruct((2, side, 8 * side), BF16),
            jax.ShapeDtypeStruct((8, side, 2 * side), BF16),
            jax.ShapeDtypeStruct((2 * chips, 16, 128), F32),
            jax.ShapeDtypeStruct((2 * chips, 9, share, side), BF16),
        ],
        in_specs=[whole, whole] + [anywhere] * 6,
        out_specs=[anywhere] * 4 + [whole],
        scratch_shapes=[
            pltpu.VMEM((9, 2 * chips, share, side), F32),
            pltpu.VMEM((2, both, 8 * side), F32),
            pltpu.VMEM((2, both, 8 * side), F32),
            pltpu.VMEM((8, both, 2 * side), F32),
            pltpu.VMEM((2, both, 8 * side), BF16),
            pltpu.VMEM((2, both, 8 * side), BF16),
            pltpu.VMEM((8, both, 2 * side), BF16),
            pltpu.VMEM((16, 128), F32),
            dma((3,)), dma((3,)), dma((4,)),
            dma((chips - 1, 3, 2)), dma((chips - 1, 3, 2)), dma((chips, 3, 3)), dma((chips, 3, 3)),
            dma((chips, 3)), dma((chips, 3)),
            dma((chips - 1,)), dma((chips - 1,)), dma((chips,)), dma((chips,)), dma((9,)),
        ],
        compiler_params=pltpu.CompilerParams(collective_id=1, has_side_effects=True, vmem_limit_bytes=60 * 2**20),
        name="gather_weights",
    )(matrices, vector_tile, *[part.reshape(3, 2 * chips, share, side) for part in states])


def opposite(device, step, count):
    result, bit = 0, 1
    while bit < count:
        one, two = lax.rem(device // bit, 2), lax.rem(step // bit, 2)
        result = result + bit * (one + two - 2 * one * two)
        bit *= 2
    return result


def settle_kernel(early, early_last, late_two, late_one, mat, first, second, left, right, mat_new, mat_low, first_new, second_new, left_new, right_new,
                  left_basis, right_basis):
    share = mat.shape[2]
    for f in range(mat.shape[1]):
        for s in range(3):
            def item(plane, index):
                source, spot = (early, index) if index < 4 else (early_last, index - 4)
                return source[plane, f, spot * share : (spot + 1) * share, :].astype(F32)

            turned = item(*((0, 5), (0, 2), (1, 2))[s])
            update = item(*((1, 5), (0, 3), (1, 3))[s])
            outer = (4, 0, 1)[s]
            fresh = mat[s, f] - MATRIX_RATE * (update + WEIGHT_DECAY * mat[s, f])
            mat_new[s, f] = fresh
            mat_low[s, f] = fresh.astype(BF16)
            first_new[s, f] = FIRST_DECAY * first[s, f] + (1.0 - FIRST_DECAY) * turned
            second_new[s, f] = SECOND_DECAY * second[s, f] + (1.0 - SECOND_DECAY) * turned * turned
            left_new[s, f] = STAT_DECAY * left[s, f] + (1.0 - STAT_DECAY) * item(0, outer)
            right_new[s, f] = STAT_DECAY * right[s, f] + (1.0 - STAT_DECAY) * item(1, outer)
            for panel in range(3):
                lanes = slice(128 * panel, 128 * (panel + 1))
                source, spot = (late_two, 3 * panel + s) if panel < 2 else (late_one, s)
                left_basis[s, f, :, lanes] = source[0, f, spot * share : (spot + 1) * share, :].astype(F32)
                right_basis[s, f, :, lanes] = source[1, f, spot * share : (spot + 1) * share, :].astype(F32)


def settle(early, early_last, late_two, late_one, matrices, first, second, left, right):
    _, count, tall, side = early.shape
    share = matrices.shape[1]
    state = pl.BlockSpec((3, OWNERS, share, side), lambda f: (0, f, 0, 0))
    shape = jax.ShapeDtypeStruct((3, count, share, side), F32)
    low = jax.ShapeDtypeStruct((3, count, share, side), BF16)
    results = pl.pallas_call(
        settle_kernel,
        grid=(count // OWNERS,),
        out_shape=[shape, low] + [shape] * 6,
        in_specs=[
            pl.BlockSpec((2, OWNERS, tall, side), lambda f: (0, f, 0, 0)),
            pl.BlockSpec((2, OWNERS, early_last.shape[2], side), lambda f: (0, f, 0, 0)),
            pl.BlockSpec((2, OWNERS, late_two.shape[2], 128), lambda f: (0, f, 0, 0)),
            pl.BlockSpec((2, OWNERS, late_one.shape[2], 128), lambda f: (0, f, 0, 0)),
        ]
        + [state] * 5,
        out_specs=[state] * 8,
        compiler_params=pltpu.CompilerParams(vmem_limit_bytes=60 * 2**20),
        name="settle",
    )(early, early_last, late_two, late_one, *[part.reshape(3, count, share, side) for part in (matrices, first, second, left, right)])
    return [part.reshape(matrices.shape) for part in results]


def normal_parts(value):
    size = jnp.abs(value) * 0.7071067811865476
    t = 1.0 / (1.0 + 0.3275911 * size)
    bell = jnp.exp(-size * size)
    series = t * (0.254829592 + t * (-0.284496736 + t * (1.421413741 + t * (-1.453152027 + t * 1.061405429))))
    tail = 0.5 * series * bell
    return jnp.where(value >= 0.0, 1.0 - tail, tail), bell * 0.3989422804014327


def span(index, size):
    return pl.ds(pl.multiple_of(index * size, size), size)


def looped(count, body):
    def step(index, carry):
        body(index)
        return carry

    lax.fori_loop(0, count, step, 0)


def vector_row(vecs, row, width):
    lane = lax.broadcasted_iota(jnp.int32, (1, 128), 1)
    pieces = []
    for pair in range(width // 128):
        chunk = row * (width // 64) + 2 * pair
        one = vecs[chunk // 9, chunk % 9 : chunk % 9 + 1, :]
        chunk += 1
        two = vecs[chunk // 9, chunk % 9 : chunk % 9 + 1, :]
        pieces.append(jnp.where(lane < 64, one, pltpu.roll(two, 64, 1)))
    return jnp.concatenate(pieces, axis=1)


def vector_tiles_of(rows, row_up, tiles):
    chunks = rows.shape[1] // 64
    for f in range(tiles.shape[0]):
        for i in range(9):
            row, place = divmod(9 * f + i, chunks)
            if 5 <= row < 9:
                spot = (row - 5) * chunks + place
                piece = row_up[spot // 4, :, 128 * (spot % 4 // 2) : 128 * (spot % 4 // 2) + 128]
            else:
                piece = rows[row : row + 1, 128 * (place // 2) : 128 * (place // 2) + 128]
            tiles[f, i : i + 1, :] = pltpu.roll(piece, 64, 1) if place % 2 else piece


def layer_kernel(length_ref, x_ref, cot_ref, tiles, attn_hbm, up_hbm, down_hbm,
                 out_ref, logs, grad_vec, grad_vec_up, qkv_out, grad_c_out, turned_x_out, grad_r_out, grad_out, grad_up, grad_down,
                 w_attn, w_up, w_down, qkv, context, hat_one, scale_one, normed, active, slope, hidden_low,
                 grad_r, low_e, grad_c, turned_x, turned_n, turned_c, stage_w, stage_t,
                 vec, vec_up, load_sem, wide_sem, tall_sem, save_sem):
    slots, width = x_ref.shape
    length = length_ref[0]
    chunks = w_up.shape[1] // 256
    thirds_of = width // 256
    loads = [pltpu.make_async_copy(source, target, load_sem.at[i])
             for i, (source, target) in enumerate(((attn_hbm, w_attn), (up_hbm, w_up), (down_hbm, w_down)))]
    for load in loads:
        load.start()

    def turn(source, target):
        def one(index):
            target[:, span(index, 128)] = source[span(index, 128), :].T

        looped(slots // 128, one)

    def wide_copy(target, slot, index):
        return pltpu.make_async_copy(stage_w.at[slot], target.at[:, span(index, 256)], wide_sem.at[slot])

    def tall_copy(slot, index):
        return pltpu.make_async_copy(stage_t.at[slot], grad_down.at[span(index, 256), :], tall_sem.at[slot])

    def put_wide(target, index, value, first):
        slot = lax.rem(index, 2)

        @pl.when(jnp.logical_not(first))
        def _():
            wide_copy(target, slot, index).wait()

        stage_w[slot] = value.astype(BF16)
        wide_copy(target, slot, index).start()

    grad_vec[...] = jnp.zeros_like(grad_vec)
    for row in range(12):
        vec[row : row + 1, :] = vector_row(tiles, row, width)
        if 5 <= row < 9:
            for third in range(thirds_of):
                vec_up[(row - 5) * thirds_of + third] = vec[row : row + 1, 256 * third : 256 * (third + 1)]
    turn(x_ref, turned_x)
    loads[0].wait()

    def project(index):
        lanes = span(index, 256)
        part = index // thirds_of
        row = jnp.where(part == 0, vec[0:1, span(lax.rem(index, thirds_of), 256)],
                        jnp.where(part == 2, vec[1:2, span(lax.rem(index, thirds_of), 256)], 0.0))
        qkv[:, lanes] = (jnp.dot(x_ref[...], w_attn[:, lanes], preferred_element_type=F32) + row).astype(BF16)

    looped(3 * thirds_of, project)
    saves = [pltpu.make_async_copy(source, target, save_sem.at[i]) for i, (source, target) in enumerate((
        (qkv, qkv_out), (turned_x, turned_x_out), (grad_c, grad_c_out), (grad_r, grad_r_out)))]
    saves[0].start()
    saves[1].start()

    lane = lax.broadcasted_iota(jnp.int32, (slots, 128), 1)
    tall_lane = lax.broadcasted_iota(jnp.int32, (128, 128), 0)
    seen = lax.broadcasted_iota(jnp.int32, (slots, 128), 0) < length

    def head_lanes(head, value):
        keep = (lane < HEAD_DIM) if head == 0 else (lane >= HEAD_DIM)
        return jnp.where(keep, value, jnp.zeros_like(value))

    def lanes_of(pair, part):
        return pl.ds(pl.multiple_of(part * width + pair * 128, 128), 128)

    def attend(pair):
        key, value = qkv[:, lanes_of(pair, 1)], qkv[:, lanes_of(pair, 2)]
        turned_value = value.T
        keys = [head_lanes(head, key * HEAD_DIM ** (-0.5)) for head in range(2)]
        for block in range(slots // 128):
            rows = slice(128 * block, 128 * (block + 1))
            query = qkv[rows, lanes_of(pair, 0)]
            both = []
            for head in range(2):
                scores = jnp.where(seen, dg(keys[head], query, 1, 1), -1e30)
                top = jnp.max(scores, axis=0, keepdims=True)
                shifted = jnp.exp(scores - top)
                total = jnp.sum(shifted, axis=0, keepdims=True)
                weights = (shifted * (1.0 / total)).astype(BF16)
                both.append(jnp.dot(turned_value, weights, preferred_element_type=F32))
                logs[2 * pair + head, :, rows] = top + jnp.log(total)
            merged = jnp.where(tall_lane < HEAD_DIM, both[0], both[1])
            context[rows, lanes_of(pair, 0)] = merged.T.astype(BF16)

    looped(width // 128, attend)
    turn(context, turned_c)

    def mix(index):
        lanes = span(index, 256)
        away = pl.ds(pl.multiple_of(3 * width + index * 256, 256), 256)
        value = jnp.dot(context[...], w_attn[:, away], preferred_element_type=F32) + vec[2:3, lanes]
        hat_one[:, lanes] = x_ref[:, lanes].astype(F32) + value

    looped(thirds_of, mix)

    def standard(value):
        centered = value - jnp.mean(value, axis=-1, keepdims=True)
        scale = lax.rsqrt(jnp.mean(centered * centered, axis=-1, keepdims=True) + NORM_EPSILON)
        return centered * scale, scale

    def norm_one(index):
        rows = span(index, 128)
        hat, scale = standard(hat_one[rows, :])
        hat_one[rows, :] = hat
        scale_one[rows, :] = jnp.broadcast_to(scale, (128, 128))
        normed[rows, :] = (hat * vec[3:4, :] + vec[4:5, :]).astype(BF16)

    looped(slots // 128, norm_one)
    turn(normed, turned_n)
    loads[1].wait()

    def rise(index):
        lanes = span(index, 256)
        hidden = jnp.dot(normed[...], w_up[:, lanes], preferred_element_type=F32) + vec_up[index]
        below, density = normal_parts(hidden)
        active[:, lanes] = (hidden * below).astype(BF16)
        slope[:, lanes] = below + hidden * density

    looped(chunks, rise)
    loads[2].wait()

    def fall(index):
        lanes = span(index, 256)
        value = jnp.dot(active[...], w_down[:, lanes], preferred_element_type=F32)
        grad_r[:, lanes] = hat_one[:, lanes] * vec[3:4, lanes] + vec[4:5, lanes] + value + vec[9:10, lanes]

    looped(thirds_of, fall)

    def unstandard(grad_hat, hat, scale):
        return scale * (grad_hat - jnp.mean(grad_hat, axis=-1, keepdims=True)
                        - hat * jnp.mean(grad_hat * hat, axis=-1, keepdims=True))

    def add_row(row, value):
        grad_vec[row : row + 1, :] += jnp.sum(value, axis=0, keepdims=True)

    def norm_two(index):
        rows = span(index, 128)
        hat, scale = standard(grad_r[rows, :])
        out_ref[rows, :] = (hat * vec[10:11, :] + vec[11:12, :]).astype(BF16)
        place = lax.broadcasted_iota(jnp.int32, (128, width), 0) + index * 128
        grad = jnp.where(place < length, cot_ref[rows, :].astype(F32), 0.0)
        add_row(10, grad * hat)
        add_row(11, grad)
        back = unstandard(grad * vec[10:11, :], hat, scale)
        add_row(9, back)
        grad_r[rows, :] = back
        low_e[rows, :] = back.astype(BF16)

    looped(slots // 128, norm_two)

    def sink(index):
        lanes = span(index, 256)
        grad = dg(low_e[...], w_down[lanes, :], 1, 1) * slope[:, lanes]
        grad_vec_up[index] = jnp.sum(grad, axis=0, keepdims=True)
        low = grad.astype(BF16)
        hidden_low[:, lanes] = low
        put_wide(grad_up, index, jnp.dot(turned_n[...], low, preferred_element_type=F32), index < 2)
        slot = lax.rem(index, 2)

        @pl.when(index >= 2)
        def _():
            tall_copy(slot, index).wait()

        stage_t[slot] = dg(active[:, lanes], low_e[...], 0, 0).astype(BF16)
        tall_copy(slot, index).start()

    looped(chunks, sink)

    def rise_back(index):
        lanes = span(index, 256)
        grad_r[:, lanes] += dg(hidden_low[...], w_up[lanes, :], 1, 1)

    looped(thirds_of, rise_back)

    def norm_one_back(index):
        rows = span(index, 128)
        hat, grad = hat_one[rows, :], grad_r[rows, :]
        add_row(3, grad * hat)
        add_row(4, grad)
        back = unstandard(grad * vec[3:4, :], hat, scale_one[rows, 0:1])
        add_row(2, back)
        grad_r[rows, :] = back
        low_e[rows, :] = back.astype(BF16)


    def mix_back(index):
        lanes = span(index, 256)
        put_wide(grad_out, index, jnp.dot(turned_c[...], low_e[:, lanes], preferred_element_type=F32), False)
        away = pl.ds(3 * width, width)
        grad_c[:, lanes] = dg(low_e[...], w_attn[lanes, away], 1, 1).astype(BF16)

    looped(slots // 128, norm_one_back)
    saves[3].start()
    looped(thirds_of, mix_back)
    saves[2].start()
    for slot in range(2):
        wide_copy(grad_out, slot, 0).wait()
        tall_copy(slot, 0).wait()
    for save in saves:
        save.wait()


def layer(length, inputs, cotangent, tiles, attn, up, down):
    slots, width = inputs.shape
    tall = down.shape[0]
    anywhere = pl.BlockSpec(memory_space=pl.ANY)
    whole = pl.BlockSpec(memory_space=pltpu.VMEM)
    vmem = pltpu.VMEM
    dma = pltpu.SemaphoreType.DMA
    return pl.pallas_call(
        layer_kernel,
        out_shape=[
            jax.ShapeDtypeStruct((slots, width), BF16),
            jax.ShapeDtypeStruct((width // HEAD_DIM, 1, slots), F32),
            jax.ShapeDtypeStruct((16, width), F32),
            jax.ShapeDtypeStruct((tall // 256, 1, 256), F32),
            jax.ShapeDtypeStruct((slots, 3 * width), BF16),
            jax.ShapeDtypeStruct((slots, width), BF16),
            jax.ShapeDtypeStruct((width, slots), BF16),
            jax.ShapeDtypeStruct((slots, width), F32),
            jax.ShapeDtypeStruct((width, width), BF16),
            jax.ShapeDtypeStruct((width, tall), BF16),
            jax.ShapeDtypeStruct((tall, width), BF16),
        ],
        in_specs=[pl.BlockSpec(memory_space=pltpu.SMEM)] + [whole] * 3 + [anywhere] * 3,
        out_specs=[whole] * 4 + [anywhere] * 7,
        scratch_shapes=[
            vmem((width, 4 * width), BF16), vmem((width, tall), BF16), vmem((tall, width), BF16),
            vmem((slots, 3 * width), BF16), vmem((slots, width), BF16),
            vmem((slots, width), F32), vmem((slots, 128), F32), vmem((slots, width), BF16),
            vmem((slots, tall), BF16), vmem((slots, tall), F32), vmem((slots, tall), BF16),
            vmem((slots, width), F32), vmem((slots, width), BF16), vmem((slots, width), BF16),
            vmem((width, slots), BF16), vmem((width, slots), BF16), vmem((width, slots), BF16),
            vmem((2, width, 256), BF16), vmem((2, 256, width), BF16),
            vmem((16, width), F32), vmem((tall // 256, 1, 256), F32),
            dma((3,)), dma((2,)), dma((2,)), dma((4,)),
        ],
        compiler_params=pltpu.CompilerParams(vmem_limit_bytes=60 * 2**20),
        cost_estimate=pl.CostEstimate(flops=25_000_000_000, bytes_accessed=40_000_000, transcendentals=8_000_000),
        name="layer",
    )(length, inputs, cotangent, tiles, attn, up, down)


def conclude_kernel(chips, share, length_ref, logs, vec_part, vec_up_part, parts, qkv_hbm, grad_c_hbm, turned_x_hbm, grad_r_hbm,
                    attn_hbm, g_out, g_up, g_down,
                    grad_x, vec_sum, early, early_last, late_two, late_one,
                    qkv, grad_c, turned_x, grad_r, w_qkv, grad_heads, probs, dscores, g_qkv, grad_vec, tiles,
                    mine, theirs, ring, crossed, peer, vmine, vring, vpeer, owned,
                    states, items, mat, aug, out_early, out_last, out_two, out_one,
                    load_sem, mine_sem, sib_send, sib_recv, ring_send, ring_recv, cross_send, cross_recv, peer_send, peer_recv,
                    state_send, state_recv, note_send, note_recv, relay_send, relay_recv, keep_sem):
    device, replica, chip, core, place, turn, after, before, sibling = whereabouts(chips)
    count = 2 * chips
    mirror = (device, 1 - replica)
    side = mine.shape[-1]
    width = 2 * side
    slots = qkv.shape[0]
    quarter = side // 4
    last = chips - 1
    part = 128
    panels = side // part
    length = length_ref[0]

    def partner(step):
        return opposite(device, step, count), replica

    barrier = pltpu.get_barrier_semaphore()

    def hail(step, carry):
        pl.semaphore_signal(barrier, inc=1, device_id=partner(step), device_id_type=MESH)
        return carry

    lax.fori_loop(1, count, hail, 0)
    pl.semaphore_signal(barrier, inc=1, device_id=mirror, device_id_type=MESH)

    loads = [pltpu.make_async_copy(source, target, load_sem.at[i]) for i, (source, target) in enumerate((
        (qkv_hbm, qkv), (grad_c_hbm, grad_c), (turned_x_hbm, turned_x), (grad_r_hbm, grad_r),
        (attn_hbm.at[:, : 3 * width], w_qkv)))]


    def quarters(first, number):
        return pl.ds(pl.multiple_of(first * quarter, 16), number * quarter)

    carried = quarters(replica, 3)
    private = quarters(3 * replica, 1)
    foreign = quarters(3 * (1 - replica), 1)

    def column(index):
        return pl.ds(pl.multiple_of(index * side, 128), side)

    def fetch(owner, wanted, start):
        which = owner // 4
        i, j = lax.rem(owner, 4) // 2, lax.rem(owner, 2)
        if 0 in wanted:
            @pl.when(which < 3)
            def _():
                start(0, g_qkv.at[i, :, column(2 * which + j)])

            @pl.when(which == 3)
            def _():
                start(0, g_out.at[i, :, column(j)])

            start(3, tiles.at[owner])
        else:
            start(1, g_up.at[owner // 8, :, column(lax.rem(owner, 8))])
            start(2, g_down.at[owner // 2, :, column(lax.rem(owner, 2))])

    def local(t, slot, source):
        target = vmine.at[0, t] if slot == 3 else mine.at[t, slot]
        return pltpu.make_async_copy(source, target, mine_sem.at[t, slot])

    def to_sibling(t, slot, source):
        target = vmine.at[1, t] if slot == 3 else theirs.at[t, slot]
        return pltpu.make_async_remote_copy(
            src_ref=source, dst_ref=target, send_sem=sib_send.at[t, slot], recv_sem=sib_recv.at[t, slot],
            device_id=sibling, device_id_type=MESH)

    def to_next(t, slot):
        source, target = (vmine.at[0, t], vring.at[t]) if slot == 3 else (mine.at[t, slot, carried, :], ring.at[t, slot])
        return pltpu.make_async_remote_copy(
            src_ref=source, dst_ref=target, send_sem=ring_send.at[t, slot], recv_sem=ring_recv.at[t, slot],
            device_id=after, device_id_type=MESH)

    def across(t, slot):
        return pltpu.make_async_remote_copy(
            src_ref=mine.at[t, slot, foreign, :], dst_ref=crossed.at[t, slot], send_sem=cross_send.at[t, slot],
            recv_sem=cross_recv.at[t, slot], device_id=mirror, device_id_type=MESH)

    def to_mirror(slot):
        source, target = (vmine.at[0, last], vpeer) if slot == 3 else (mine.at[last, slot, carried, :], peer.at[slot, carried, :])
        return pltpu.make_async_remote_copy(
            src_ref=source, dst_ref=target, send_sem=peer_send.at[slot], recv_sem=peer_recv.at[slot],
            device_id=mirror, device_id_type=MESH)

    def begin_own(t, wanted):
        fetch(2 * ring_chip(place - turn * (t + 1), chips) + core, wanted, lambda slot, source: local(t, slot, source).start())

    def begin_sibling(t, wanted):
        fetch(2 * ring_chip(place + turn * (t + 1), chips) + 1 - core, wanted,
              lambda slot, source: to_sibling(t, slot, source).start())

    def begin(t, wanted):
        begin_sibling(t, wanted)
        begin_own(t, wanted)

    def sources(slot):
        return tiles.at[0] if slot == 3 else g_up.at[0, :, :side]

    def pair_up(t, wanted):
        for slot in wanted:
            local(t, slot, sources(slot)).wait()
            to_sibling(t, slot, sources(slot)).wait_recv()
            if slot == 3:
                vmine[0, t] = vmine[0, t] + vmine[1, t]
            else:
                mine[t, slot] = (mine[t, slot].astype(F32) + theirs[t, slot].astype(F32)).astype(BF16)
                across(t, slot).start()

    def add(t, slot, hold, extra):
        mine[t, slot, hold, :] = (mine[t, slot, hold, :].astype(F32) + extra.astype(F32)).astype(BF16)

    def pass_round(t, wanted):
        for slot in wanted:
            if slot < 3:
                across(t, slot).wait_recv()
                add(t, slot, private, crossed[t, slot])

            @pl.when(t > 0)
            def _():
                to_next(t - 1, slot).wait_recv()
                if slot == 3:
                    vmine[0, t] = vmine[0, t] + vring[t - 1]
                else:
                    add(t, slot, carried, ring[t - 1, slot])

            @pl.when(t < last)
            def _():
                to_next(t, slot).start()

            @pl.when(t == last)
            def _():
                to_mirror(slot).start()

    def own_sum(slot):
        to_mirror(slot).wait()
        if slot == 3:
            vec_sum[...] = vmine[0, last] + vpeer[...]
            return
        shared = slice(quarter, 3 * quarter)
        owned[slot, shared, :] = (mine[last, slot, shared, :].astype(F32) + peer[slot, shared, :].astype(F32)).astype(BF16)
        owned[slot, private, :] = mine[last, slot, private, :]
        owned[slot, foreign, :] = peer[slot, foreign, :]

    feed, rest = (1, 2), (3, 0)

    def rest_step(t):
        @pl.when(t + 3 < chips)
        def _():
            begin(t + 3, rest)

        @pl.when(t == 0)
        def _():
            pair_up(1, rest)

        @pl.when(t + 2 < chips)
        def _():
            pair_up(t + 2, rest)

        pass_round(t, rest)


    lane = lax.broadcasted_iota(jnp.int32, (slots, 128), 1)
    seen = lax.broadcasted_iota(jnp.int32, (slots, 128), 0) < length

    def head_lanes(head, value):
        keep = (lane < HEAD_DIM) if head == 0 else (lane >= HEAD_DIM)
        return jnp.where(keep, value, jnp.zeros_like(value))

    def lanes_of(pair, member):
        return pl.ds(pl.multiple_of(member * width + pair * 128, 128), 128)

    def attend_back(pair):
        query, key, value = [qkv[:, lanes_of(pair, member)] for member in range(3)]
        grad = grad_c[:, lanes_of(pair, 0)]
        turned_key = key.T
        found = []
        for head in range(2):
            near_key = head_lanes(head, key * HEAD_DIM ** (-0.5))
            near_value = head_lanes(head, value)
            for block in range(slots // 128):
                rows = slice(128 * block, 128 * (block + 1))
                scores = jnp.where(seen, dg(near_key, query[rows], 1, 1), -1e30)
                weights = jnp.exp(scores - logs[2 * pair + head, :, rows])
                back = dg(near_value, grad[rows], 1, 1)
                scores_back = weights * (back - jnp.sum(back * weights, axis=0, keepdims=True))
                probs[head, :, rows] = weights.astype(BF16)
                dscores[head, :, rows] = scores_back.astype(BF16)
            found.append((
                jnp.dot(turned_key, dscores[head], preferred_element_type=F32),
                jnp.dot(dscores[head], query, preferred_element_type=F32),
                jnp.dot(probs[head], grad, preferred_element_type=F32),
            ))
        top = lax.broadcasted_iota(jnp.int32, (128, slots), 0) < HEAD_DIM
        turned_query = jnp.where(top, found[0][0], found[1][0]) * HEAD_DIM ** (-0.5)
        grad_heads[:, lanes_of(pair, 0)] = turned_query.T.astype(BF16)
        grad_heads[:, lanes_of(pair, 1)] = (jnp.where(lane < HEAD_DIM, found[0][1], found[1][1]) * HEAD_DIM ** (-0.5)).astype(BF16)
        grad_heads[:, lanes_of(pair, 2)] = jnp.where(lane < HEAD_DIM, found[0][2], found[1][2]).astype(BF16)

    def project_back(index):
        lanes = span(index, 256)
        value = jnp.dot(turned_x[...], grad_heads[:, lanes], preferred_element_type=F32)
        g_qkv[:, :, lanes] = value.astype(BF16).reshape(2, side, 256)

    def input_back(index):
        lanes = span(index, 256)
        grad_x[:, lanes] = grad_r[:, lanes] + dg(grad_heads[...], w_qkv[lanes, :], 1, 1)


    def join(pair, carry):
        rows = pl.ds(pl.multiple_of(2 * share * pair, 16), 2 * share)
        for item in range(9):
            two = [parts[2 * pair + index, item].astype(F32) for index in range(2)]
            states[item, rows, :] = jnp.concatenate(two, axis=0).astype(BF16)
        return carry

    def trade(index):
        source = (5 - replica, 3, 8)[index]
        return pltpu.make_async_remote_copy(
            src_ref=states.at[source], dst_ref=states.at[9 + index], send_sem=state_send.at[index],
            recv_sem=state_recv.at[index], device_id=mirror, device_id_type=MESH)

    def update(rotated, left, right, first, second):
        first_new = FIRST_DECAY * first.astype(F32) + (1.0 - FIRST_DECAY) * rotated
        second_new = SECOND_DECAY * second.astype(F32) + (1.0 - SECOND_DECAY) * rotated * rotated
        direction = (
            first_new
            / (1.0 - FIRST_DECAY**ADAM_STEP)
            / (jnp.sqrt(second_new / (1.0 - SECOND_DECAY**ADAM_STEP)) + ADAM_EPSILON)
        )
        back = dg(left, direction.astype(BF16), 1, 0).astype(BF16)
        return dg(back, right, 1, 1)

    def prepare(s):
        for is_right in (False, True):
            @pl.when(replica == int(is_right))
            def _():
                near = 0 if is_right else 1
                g = owned[s]
                outer = dg(g, g, near, near)
                items[(4, 0, 1)[s]] = outer
                mixed = STAT_DECAY * states[s].astype(F32) + (1.0 - STAT_DECAY) * outer
                high, low = halves(mixed)
                mat[s] = dg(high, states[3 + s], 1, 0) + dg(low, states[3 + s], 1, 0)
                if s not in (0, 2 if is_right else 1):
                    return
                other = states[10] if s == 0 else states[9]
                left, right = (other, states[3 + s]) if is_right else (states[3 + s], other)
                rotated = dg(dg(left, g, 0, 0).astype(BF16), right, 1, 0)
                if s > 0:
                    items[2] = rotated
                    items[3] = update(rotated, left, right, states[6], states[7])
                elif is_right:
                    items[5] = update(rotated, left, right, states[8], states[11])
                else:
                    items[5] = rotated

    def rows_of(holder):
        return pl.ds(pl.multiple_of(holder * share, 8), share)

    def outgoing(kind, holder):
        return (out_early, out_last, out_two, out_one)[kind].at[holder]

    def incoming(kind, owner):
        return (early, early_last, late_two, late_one)[kind].at[replica, owner]

    def pack(kind):
        def one(holder, carry):
            rows = rows_of(holder)
            if kind < 2:
                for pair in ((0, 1), (2,))[kind]:
                    two = jnp.concatenate([items[2 * pair, rows, :], items[2 * pair + 1, rows, :]], axis=0)
                    spot = pair if kind == 0 else 0
                    (out_early, out_last)[kind][holder, 2 * share * spot : 2 * share * (spot + 1), :] = two.astype(BF16)
            else:
                columns = ((0, part), (2 * part,))[kind - 2]
                stacked = [mat[s, rows, lo : lo + part] for lo in columns for s in range(3)]
                if kind == 3:
                    stacked.append(jnp.zeros((8, part), F32))
                (out_two, out_one)[kind - 2][holder] = jnp.concatenate(stacked, axis=0).astype(BF16)
            return carry

        lax.fori_loop(0, count, one, 0)

    def note(kind, step):
        target = partner(step)
        return pltpu.make_async_remote_copy(
            src_ref=outgoing(kind, target[0]), dst_ref=incoming(kind, device), send_sem=note_send.at[kind, step],
            recv_sem=note_recv.at[kind, step], device_id=target, device_id_type=MESH)

    def relay(kind, step):
        block = incoming(kind, partner(step)[0])
        return pltpu.make_async_remote_copy(
            src_ref=block, dst_ref=block, send_sem=relay_send.at[kind, step], recv_sem=relay_recv.at[kind, step],
            device_id=mirror, device_id_type=MESH)

    def keep(kind):
        return pltpu.make_async_copy(outgoing(kind, device), incoming(kind, device), keep_sem.at[kind])

    def launch(kind):
        pack(kind)
        keep(kind).start()

        def one(step, carry):
            note(kind, step).start()
            return carry

        lax.fori_loop(1, chips, one, 0)
        near.extend((kind, step) for step in range(chips))
        far.extend((kind, step) for step in range(chips, count))

    def hand_on(kind, step):
        note(kind, step).wait_recv()
        relay(kind, step).start()

    near, far, flying = [], [], []

    def hand_on_near(number):
        for kind, step in near[:number]:
            if step == 0:
                keep(kind).wait()
                relay(kind, 0).start()
            else:
                hand_on(kind, step)
        del near[:number]

    def pump(number):
        for kind, step in far[:number]:
            if len(flying) >= WINDOW:
                hand_on(*flying.pop(0))
            note(kind, step).start()
            flying.append((kind, step))
        del far[:number]


    def first_own(index, carry):
        begin_own(index, feed)
        return carry

    def first_sibling(index, carry):
        begin_sibling(index, feed)
        return carry

    lax.fori_loop(0, 3, first_own, 0)
    for load in loads[:2]:
        load.start()
    lax.fori_loop(0, count // 2, join, 0)
    pl.semaphore_wait(barrier, count)
    lax.fori_loop(0, 3, first_sibling, 0)
    pair_up(0, feed)
    for load in loads[2:]:
        load.start()
    grad_vec[...] = vec_part[...]

    def main(t, carry):
        @pl.when(t + 3 < chips)
        def _():
            begin(t + 3, feed)

        @pl.when(t == 0)
        def _():
            pair_up(1, feed)

        @pl.when(t + 2 < chips)
        def _():
            pair_up(t + 2, feed)

        pass_round(t, feed)

        @pl.when(t == 0)
        def _():
            for load in loads[:2]:
                load.wait()

        @pl.when(t < 2)
        def _():
            def one(third, carry):
                attend_back(3 * t + third)
                return carry

            lax.fori_loop(0, 3, one, 0)

        @pl.when(t == TRADE)
        def _():
            trade(0).start()

        @pl.when(t == 2)
        def _():
            loads[2].wait()
            grad_vec[0:1, :] = jnp.sum(grad_heads[:, :width].astype(F32), axis=0, keepdims=True)
            grad_vec[1:2, :] = jnp.sum(grad_heads[:, 2 * width :].astype(F32), axis=0, keepdims=True)
            looped(3 * width // 256, project_back)
            vector_tiles_of(grad_vec, vec_up_part, tiles)

            def start_rest(index, carry):
                begin(index, rest)
                return carry

            lax.fori_loop(0, 3, start_rest, 0)
            pair_up(0, rest)

        @pl.when(t > 2)
        def _():
            rest_step(t - 3)
        return carry

    lax.fori_loop(0, chips, main, 0)
    trade(1).start()
    trade(2).start()
    trade(0).wait()
    own_sum(1)
    prepare(1)
    rest_step(jnp.int32(chips - 3))
    own_sum(2)
    prepare(2)
    launch(0)
    pump(WINDOW)
    rest_step(jnp.int32(chips - 2))
    hand_on_near(4)
    pump(1)
    for load in loads[3:]:
        load.wait()
    looped(width // 256, input_back)
    pump(1)
    rest_step(jnp.int32(chips - 1))
    hand_on_near(4)
    pump(1)
    own_sum(0)
    trade(1).wait()
    trade(2).wait()
    prepare(0)
    launch(1)

    def between(moment):
        if far and moment % (5, 3, 3, 2)[far[0][0]] == 0:
            pump(1)
        elif near and moment % 2 == 1:
            hand_on_near(1)

    row_index = lax.broadcasted_iota(jnp.int32, (part, part), 0)
    column_index = lax.broadcasted_iota(jnp.int32, (part, part), 1)
    eye = (row_index == column_index).astype(F32)
    for o in range(panels):
        lo = o * part
        for s in range(3):
            block = mat[s, :, lo : lo + part]
            aug[s, :, :part] = mm3(block, block, 0, 0)
            aug[s, :, part:] = eye
        factor_panels(aug, 3, part, lambda p: between(16 * o + p))
        for s in range(3):
            mat[s, :, lo : lo + part] = mm3(mat[s, :, lo : lo + part], aug[s, :, part:], 1, 1)
        if o > 0:
            launch(1 + o)
        if o + 1 < panels:
            for s in range(3):
                q, remaining = mat[s, :, lo : lo + part], mat[s, :, lo + part :]
                mat[s, :, lo + part :] = remaining - mm3(q, mm3(q, remaining, 0, 0), 1, 0)
    while far or near:
        pump(2)
        hand_on_near(2)
    for kind, step in flying:
        hand_on(kind, step)
    own_sum(3)

    def finish(step, carry):
        for kind in range(4):
            relay(kind, step).wait()

            @pl.when(step > 0)
            def _():
                note(kind, step).wait_send()

        @pl.when(step < chips)
        def _():
            for slot in range(4):
                to_sibling(step, slot, sources(slot)).wait_send()
                if slot < 3:
                    across(step, slot).wait_send()

                @pl.when(step < last)
                def _():
                    to_next(step, slot).wait_send()
        return carry

    lax.fori_loop(0, count, finish, 0)


def conclude(length, logs, vec_part, vec_up_part, parts, qkv, grad_c, turned_x, grad_r, attn, g_out, g_up, g_down, share, chips):
    side = g_up.shape[1]
    width, count = 2 * side, 2 * chips
    slots = qkv.shape[0]
    tall = -(-3 * share // 16) * 16
    anywhere = pl.BlockSpec(memory_space=pl.ANY)
    whole = pl.BlockSpec(memory_space=pltpu.VMEM)
    vmem = pltpu.VMEM
    dma = pltpu.SemaphoreType.DMA
    return pl.pallas_call(
        functools.partial(conclude_kernel, chips, share),
        out_shape=[
            jax.ShapeDtypeStruct((slots, width), F32),
            jax.ShapeDtypeStruct((16, 128), F32),
            jax.ShapeDtypeStruct((2, count, 4 * share, side), BF16),
            jax.ShapeDtypeStruct((2, count, 2 * share, side), BF16),
            jax.ShapeDtypeStruct((2, count, 6 * share, 128), BF16),
            jax.ShapeDtypeStruct((2, count, tall, 128), BF16),
        ],
        in_specs=[pl.BlockSpec(memory_space=pltpu.SMEM)] + [whole] * 4 + [anywhere] * 8,
        out_specs=[whole] * 2 + [anywhere] * 4,
        scratch_shapes=[
            vmem((slots, 3 * width), BF16), vmem((slots, width), BF16), vmem((width, slots), BF16), vmem((slots, width), F32),
            vmem((width, 3 * width), BF16), vmem((slots, 3 * width), BF16), vmem((2, slots, slots), BF16),
            vmem((2, slots, slots), BF16), vmem((2, side, 3 * width), BF16), vmem((16, width), F32), vmem((count, 16, 128), F32),
            vmem((chips, 3, side, side), BF16), vmem((chips, 3, side, side), BF16),
            vmem((chips - 1, 3, 3 * side // 4, side), BF16), vmem((chips, 3, side // 4, side), BF16), vmem((3, side, side), BF16),
            vmem((2, chips, 16, 128), F32), vmem((chips - 1, 16, 128), F32), vmem((16, 128), F32), vmem((3, side, side), BF16),
            vmem((12, side, side), BF16), vmem((6, side, side), F32), vmem((3, side, side), F32), vmem((3, 128, 256), F32),
            vmem((count, 4 * share, side), BF16), vmem((count, 2 * share, side), BF16), vmem((count, 6 * share, 128), BF16),
            vmem((count, tall, 128), BF16),
            dma((5,)), dma((chips, 4)), dma((chips, 4)), dma((chips, 4)), dma((chips - 1, 4)), dma((chips - 1, 4)),
            dma((chips, 3)), dma((chips, 3)), dma((4,)), dma((4,)), dma((3,)), dma((3,)),
            dma((4, count)), dma((4, count)), dma((4, count)), dma((4, count)), dma((4,)),
        ],
        compiler_params=pltpu.CompilerParams(collective_id=2, has_side_effects=True, vmem_limit_bytes=62 * 2**20),
        name="conclude",
    )(length, logs, vec_part, vec_up_part, parts, qkv, grad_c, turned_x, grad_r, attn, g_out, g_up, g_down)


def plain_gather(matrices, vectors):
    side = matrices.shape[-1]
    blocks = lax.all_gather(matrices.astype(BF16), "fsdp", axis=1, tiled=True)
    attn = jnp.concatenate([assemble(blocks[4 * part : 4 * part + 4], 2, 2) for part in range(4)], axis=1)
    up = assemble(blocks[16:32], 2, 8)
    down = assemble(blocks[32:], 8, 2)
    rows = lax.all_gather(vectors.astype(BF16), "fsdp", axis=0, tiled=True)
    return attn, up, down, rows.astype(F32).reshape(-1, 2 * side)


def plain_reduce(grad_qkv, grad_out, grad_up, grad_down, vector_grad, capacity):
    shard_count = lax.axis_size("fsdp")
    width = grad_up.shape[0]
    side = width // 2
    blocks = jnp.concatenate(
        [split_blocks(grad_qkv[:, part * width : (part + 1) * width], 2, 2, side) for part in range(3)]
        + [split_blocks(grad_out, 2, 2, side), split_blocks(grad_up, 2, 8, side), split_blocks(grad_down, 8, 2, side)],
        axis=0,
    )
    owned = lax.psum_scatter(
        to_owners(blocks, capacity, shard_count), "fsdp", scatter_dimension=1, tiled=True
    )
    owned = lax.psum(owned, "dp")[:, 0]
    share = lax.psum_scatter(vector_grad, "fsdp", scatter_dimension=0, tiled=True)
    return owned, lax.psum(share, "dp")


def to_owners(blocks, capacity, shard_count):
    spare = capacity * shard_count - blocks.shape[0]
    blocks = jnp.pad(blocks, ((0, spare),) + ((0, 0),) * (blocks.ndim - 1))
    return blocks.reshape((capacity, shard_count) + blocks.shape[1:])


def plain_layer(tokens, cotangent, lengths, attn, up, down, vector_rows):
    sequences, slots, model_width = tokens.shape
    rows_total = sequences * slots
    unit_ratio = FF // model_width

    def shaped(array):
        return array.reshape(sequences, slots, array.shape[-1])

    weight_qkv, weight_out = attn[:, : 3 * model_width], attn[:, 3 * model_width :]
    inputs = tokens.reshape(rows_total, model_width)
    joined = jnp.dot(inputs, weight_qkv, preferred_element_type=F32)
    query_rows = (joined[:, :model_width] + vector_rows[0]).astype(BF16)
    key_rows = joined[:, model_width : 2 * model_width].astype(BF16)
    value_rows = (joined[:, 2 * model_width :] + vector_rows[1]).astype(BF16)
    context, logsum = lax.map(
        attend, (shaped(query_rows), shaped(key_rows), shaped(value_rows), lengths)
    )
    context = context.reshape(rows_total, model_width)
    attended = jnp.dot(context, weight_out, preferred_element_type=F32) + vector_rows[2]
    normed, pull_one = jax.vjp(
        layer_norm, inputs.astype(F32) + attended, vector_rows[3], vector_rows[4]
    )
    normed_low = normed.astype(BF16)
    hidden = jnp.dot(normed_low, up, preferred_element_type=F32) + vector_rows[
        5 : 5 + unit_ratio
    ].reshape(FF)
    active, pull_gelu = jax.vjp(exact_gelu, hidden)
    active_low = active.astype(BF16)
    result = jnp.dot(active_low, down, preferred_element_type=F32) + vector_rows[5 + unit_ratio]
    output, pull_two = jax.vjp(
        layer_norm, normed + result, vector_rows[6 + unit_ratio], vector_rows[7 + unit_ratio]
    )
    block_out = output.reshape(sequences, slots, model_width).astype(BF16)
    visible = (lax.iota(jnp.int32, slots)[None, :] < lengths[:, None]).astype(F32)
    grad_output = (cotangent.astype(F32) * visible[:, :, None]).reshape(rows_total, model_width)
    grad_second, grad_gain_two, grad_shift_two = pull_two(grad_output)
    second_low = grad_second.astype(BF16)
    grad_down = jnp.einsum("tf,td->fd", active_low, second_low, preferred_element_type=F32)
    grad_active = jnp.einsum("td,fd->tf", second_low, down, preferred_element_type=F32)
    (grad_hidden,) = pull_gelu(grad_active)
    hidden_low = grad_hidden.astype(BF16)
    grad_up = jnp.einsum("td,tf->df", normed_low, hidden_low, preferred_element_type=F32)
    grad_normed = grad_second + jnp.einsum("tf,df->td", hidden_low, up, preferred_element_type=F32)
    grad_mixed, grad_gain_one, grad_shift_one = pull_one(grad_normed)
    mixed_low = grad_mixed.astype(BF16)
    grad_out_weight = jnp.einsum("td,te->de", context, mixed_low, preferred_element_type=F32)
    grad_context = jnp.einsum(
        "te,de->td", mixed_low, weight_out, preferred_element_type=F32
    ).astype(BF16)
    grad_query, grad_keys, grad_values = lax.map(
        attend_back,
        (
            shaped(query_rows),
            shaped(key_rows),
            shaped(value_rows),
            logsum,
            shaped(grad_context),
            lengths,
        ),
    )
    grad_joined = jnp.concatenate(
        [
            grad_query.reshape(rows_total, model_width),
            grad_keys.reshape(rows_total, model_width),
            grad_values.reshape(rows_total, model_width),
        ],
        axis=1,
    )
    grad_qkv = jnp.einsum("td,te->de", inputs, grad_joined, preferred_element_type=F32)
    input_grad = grad_mixed + jnp.einsum(
        "te,de->td", grad_joined, weight_qkv, preferred_element_type=F32
    )
    vector_grad = jnp.concatenate(
        [
            jnp.sum(grad_joined[:, :model_width], axis=0, dtype=F32)[None],
            jnp.sum(grad_joined[:, 2 * model_width :], axis=0, dtype=F32)[None],
            jnp.sum(grad_mixed, axis=0)[None],
            grad_gain_one[None],
            grad_shift_one[None],
            jnp.sum(grad_hidden, axis=0).reshape(unit_ratio, model_width),
            jnp.sum(grad_second, axis=0)[None],
            grad_gain_two[None],
            grad_shift_two[None],
        ],
        axis=0,
    ).reshape(-1)
    weight_grads = [part.astype(BF16) for part in (grad_qkv, grad_out_weight, grad_up, grad_down)]
    return block_out, input_grad.reshape(tokens.shape), vector_grad, weight_grads


def shards(
    tokens,
    cotangent,
    lengths,
    matrices,
    first_moment,
    second_moment,
    left_stat,
    right_stat,
    left_basis,
    right_basis,
    vectors,
    vector_first,
    vector_second,
):
    shard_count = lax.axis_size("fsdp")
    replicas = lax.axis_size("dp")
    sequences, slots, model_width = tokens.shape
    block_total, share_rows, block_side = matrices.shape
    capacity = -(-block_total // shard_count)
    ringed = replicas == 2 and sequences == 1 and vectors.shape[0] == 576 and capacity * shard_count == block_total == 48 and share_rows % 8 == 0 and capacity == 3

    right_side = lax.axis_index("dp") % 2 == 1
    if ringed:
        vector_tile = jnp.pad(vectors.reshape(9, 64), ((0, 7), (0, 64)))
        attn, up, down, tiles, states = gather_weights(
            matrices,
            vector_tile,
            (left_stat, right_stat, left_basis, right_basis, first_moment, second_moment),
            shard_count // 2,
        )
        states = lax.all_to_all(states, "fsdp", split_axis=0, concat_axis=0, tiled=True)
        weight_attn = attn.reshape(model_width, 4 * model_width)
        block_out, logs, vec_part, vec_up_part, qkv, grad_c, turned_x, grad_r, *weight_grads = layer(
            lengths,
            tokens[0],
            cotangent[0],
            tiles,
            weight_attn,
            up.reshape(model_width, FF),
            down.reshape(FF, model_width),
        )
        slabs = [part.reshape(-1, block_side, part.shape[1]) for part in weight_grads]
        input_grad, vector_sum, *notes = conclude(
            lengths, logs, vec_part, vec_up_part, states, qkv, grad_c, turned_x, grad_r, weight_attn, *slabs,
            share_rows, shard_count // 2
        )
        block_out, input_grad = block_out[None], input_grad[None]
        vector_sum = vector_sum[:9, :64].reshape(-1)
        local = settle(*notes, matrices, first_moment, second_moment, left_stat, right_stat)
    else:
        chosen = [
            jnp.where(right_side, right_stat, left_stat),
            jnp.where(right_side, right_basis, left_basis),
            jnp.where(right_side, left_basis, right_basis),
            first_moment,
            second_moment,
        ]
        states = jnp.stack([to_owners(part.astype(BF16), capacity, shard_count) for part in chosen])
        attn, up, down, vector_rows = plain_gather(matrices, vectors)
        states = lax.all_to_all(states, "fsdp", split_axis=2, concat_axis=3, tiled=True)[:, :, 0]
        block_out, input_grad, vector_grad, weight_grads = plain_layer(
            tokens, cotangent, lengths, attn, up, down, vector_rows
        )
        owned, vector_sum = plain_reduce(*weight_grads, vector_grad, capacity)
        filler = (lax.iota(jnp.int32, capacity) * shard_count + lax.axis_index("fsdp")) >= block_total
        stat = jnp.where(
            filler[:, None, None], jnp.eye(block_side, dtype=jnp.bfloat16), states[0]
        )
        basis = jnp.where(
            filler[:, None, None], jnp.eye(block_side, dtype=jnp.bfloat16), states[1]
        )
        outer, new_basis, turned, update = soap_blocks(
            owned, stat, basis, states[2], states[3], states[4]
        )
        returned = lax.all_to_all(
            jnp.stack([outer, new_basis, turned, update])[:, :, None],
            "fsdp",
            split_axis=3,
            concat_axis=2,
            tiled=True,
        ).reshape(4, capacity * shard_count, -1, block_side)[:, :block_total]
        mirror = lax.ppermute(
            returned[:2], "dp", [(place, place ^ 1) for place in range(lax.axis_size("dp"))]
        )
        returned = returned.astype(jnp.float32)
        mirror = mirror.astype(jnp.float32)
        left_pair = jnp.where(right_side, mirror, returned[:2])
        right_pair = jnp.where(right_side, returned[:2], mirror)
        turned = returned[2]
        local = [
            returned[3],
            FIRST_DECAY * first_moment + (1.0 - FIRST_DECAY) * turned,
            SECOND_DECAY * second_moment + (1.0 - SECOND_DECAY) * turned * turned,
            STAT_DECAY * left_stat + (1.0 - STAT_DECAY) * left_pair[0],
            STAT_DECAY * right_stat + (1.0 - STAT_DECAY) * right_pair[0],
            left_pair[1],
            right_pair[1],
        ]
        local = [matrices - MATRIX_RATE * (local[0] + WEIGHT_DECAY * matrices)] + local
        local[1] = local[0].astype(BF16)
    vfirst_new = FIRST_DECAY * vector_first + (1.0 - FIRST_DECAY) * vector_sum
    vsecond_new = SECOND_DECAY * vector_second + (1.0 - SECOND_DECAY) * vector_sum * vector_sum
    vector_new = vectors - VECTOR_RATE * (vfirst_new / (1.0 - FIRST_DECAY**ADAM_STEP)) / (
        jnp.sqrt(vsecond_new / (1.0 - SECOND_DECAY**ADAM_STEP)) + ADAM_EPSILON
    )
    return (
        block_out,
        input_grad,
        *local,
        vfirst_new,
        vsecond_new,
        vector_new,
    )


def solution(mesh):
    return jax.shard_map(
        shards,
        mesh=mesh,
        in_specs=(
            P(("fsdp", "dp"), None, None),
            P(("fsdp", "dp"), None, None),
            P(("fsdp", "dp")),
            P(None, "fsdp", None),
            P(None, "fsdp", None),
            P(None, "fsdp", None),
            P(None, "fsdp", None),
            P(None, "fsdp", None),
            P(None, "fsdp", None),
            P(None, "fsdp", None),
            P("fsdp"),
            P("fsdp"),
            P("fsdp"),
        ),
        out_specs=(
            P(("fsdp", "dp"), None, None),
            P(("fsdp", "dp"), None, None),
            P(None, "fsdp", None),
            P(None, "fsdp", None),
            P(None, "fsdp", None),
            P(None, "fsdp", None),
            P(None, "fsdp", None),
            P(None, "fsdp", None),
            P(None, "fsdp", None),
            P(None, "fsdp", None),
            P("fsdp"),
            P("fsdp"),
            P("fsdp"),
        ),
        check_vma=False,
    )
```

```python
import functools

import jax
import jax.numpy as jnp
from jax import lax
from jax.experimental import pallas as pl
from jax.experimental.pallas import tpu as pltpu
from jax.sharding import PartitionSpec as P

F32 = jnp.float32
BF16 = jnp.bfloat16
MESH = pl.DeviceIdType.MESH
TRADE = 1
WINDOW = 4
OWNERS = 4

HEADS = 12
HEAD_DIM = 64
FF = 3072
ADAM_STEP = 10


FIRST_DECAY = 0.9
SECOND_DECAY = 0.999
STAT_DECAY = 0.95
ADAM_EPSILON = 1e-08
NORM_EPSILON = 1e-05
MATRIX_RATE = 0.03
VECTOR_RATE = 0.2
WEIGHT_DECAY = 0.01


def assemble(blocks, row_count, column_count):
    block_side = blocks.shape[-1]
    shaped = blocks.reshape(row_count, column_count, block_side, block_side)
    return shaped.transpose(0, 2, 1, 3).reshape(row_count * block_side, column_count * block_side)


def split_blocks(matrix, row_count, column_count, block_side):
    shaped = matrix.reshape(row_count, block_side, column_count, block_side)
    return shaped.transpose(0, 2, 1, 3).reshape(row_count * column_count, block_side, block_side)


def layer_norm(values, gain_row, shift_row):
    center = jnp.mean(values, axis=-1, keepdims=True)
    centered = values - center
    spread = jnp.mean(centered * centered, axis=-1, keepdims=True)
    return centered * lax.rsqrt(spread + NORM_EPSILON) * gain_row + shift_row


def exact_gelu(hidden):
    return jax.nn.gelu(hidden, approximate=False)


def masked_scores(heads_query, heads_key, length):
    slots = heads_query.shape[0]
    scores = jnp.einsum(
        "qhd,khd->hqk", heads_query, heads_key, preferred_element_type=jnp.float32
    ) * HEAD_DIM ** (-0.5)
    visible = lax.iota(jnp.int32, slots) < length
    return jnp.where(visible[None, None, :], scores, -1e30)


def attend(pieces):
    query_rows, key_rows, value_rows, length = pieces
    slots = query_rows.shape[0]
    heads_query = query_rows.reshape(slots, HEADS, HEAD_DIM)
    heads_key = key_rows.reshape(slots, HEADS, HEAD_DIM)
    heads_value = value_rows.reshape(slots, HEADS, HEAD_DIM)
    scores = masked_scores(heads_query, heads_key, length)
    row_max = jnp.max(scores, axis=-1, keepdims=True)
    shifted = jnp.exp(scores - row_max)
    row_total = jnp.sum(shifted, axis=-1, keepdims=True)
    attention_weights = (shifted / row_total).astype(jnp.bfloat16)
    context = jnp.einsum(
        "hqk,khd->qhd", attention_weights, heads_value, preferred_element_type=jnp.float32
    )
    return (
        context.reshape(slots, -1).astype(jnp.bfloat16),
        row_max[..., 0] + jnp.log(row_total[..., 0]),
    )


def attend_back(pieces):
    query_rows, key_rows, value_rows, logsum, grad_context, length = pieces
    slots = query_rows.shape[0]
    heads_query = query_rows.reshape(slots, HEADS, HEAD_DIM)
    heads_key = key_rows.reshape(slots, HEADS, HEAD_DIM)
    heads_value = value_rows.reshape(slots, HEADS, HEAD_DIM)
    heads_grad = grad_context.reshape(slots, HEADS, HEAD_DIM)
    scores = masked_scores(heads_query, heads_key, length)
    attention_weights = jnp.exp(scores - logsum[..., None])
    weights_low = attention_weights.astype(jnp.bfloat16)
    grad_values = jnp.einsum(
        "hqk,qhd->khd", weights_low, heads_grad, preferred_element_type=jnp.float32
    )
    grad_weights = jnp.einsum(
        "qhd,khd->hqk", heads_grad, heads_value, preferred_element_type=jnp.float32
    )
    grad_scores = attention_weights * (
        grad_weights - jnp.sum(grad_weights * attention_weights, axis=-1, keepdims=True)
    )
    scores_low = grad_scores.astype(jnp.bfloat16)
    grad_query = jnp.einsum(
        "hqk,khd->qhd", scores_low, heads_key, preferred_element_type=jnp.float32
    ) * HEAD_DIM ** (-0.5)
    grad_keys = jnp.einsum(
        "hqk,qhd->khd", scores_low, heads_query, preferred_element_type=jnp.float32
    ) * HEAD_DIM ** (-0.5)
    return (
        grad_query.reshape(slots, -1).astype(jnp.bfloat16),
        grad_keys.reshape(slots, -1).astype(jnp.bfloat16),
        grad_values.reshape(slots, -1).astype(jnp.bfloat16),
    )


def dg(a,b,ca,cb):
    return lax.dot_general(a,b,(((ca,),(cb,)),((),())),preferred_element_type=F32)

def halves(a):
    hi=a.astype(BF16)
    return hi,(a-hi.astype(F32)).astype(BF16)

def mm3(a,b,ca,cb):
    ah,al=halves(a); bh,bl=halves(b)
    return dg(ah,bh,ca,cb)+(dg(ah,bl,ca,cb)+dg(al,bh,ca,cb))

def thirds(u):
    h=u.astype(BF16).astype(F32); r=u-h
    m=r.astype(BF16).astype(F32)
    return h,m,r-m

def factor_panels(aug, slots, side=128, between=None):
    sub=lax.broadcasted_iota(jnp.int32,(8,side),0)
    def spread(v): return jnp.broadcast_to(v,(8,side))
    for p in range(side//8):
        k=8*p
        if between is not None:
            between(p)
        panels=[]
        for s in range(slots):
            pw=aug[s,k:k+8,:side]; pv=aug[s,k:k+8,side:]
            cols=[spread(pw[:,k+i:k+i+1]) for i in range(8)]
            S=[[spread(cols[i][j:j+1,:]) if j>=i else None for i in range(8)] for j in range(8)]
            rw=[spread(pw[i:i+1,:]) for i in range(8)]
            rv=[spread(pv[i:i+1,:]) for i in range(8)]
            panels.append((S,rw,rv))
        for i in range(8):
            for S,rw,rv in panels:
                r=lax.rsqrt(S[i][i])
                for j in range(i+1,8): S[j][i]=S[j][i]*r
                for m in range(i+1,8):
                    for j in range(m,8):
                        S[j][m]=S[j][m]-S[j][i]*S[m][i]
                rw[i]=rw[i]*r; rv[i]=rv[i]*r
                for j in range(i+1,8):
                    rw[j]=rw[j]-S[j][i]*rw[i]
                    rv[j]=rv[j]-S[j][i]*rv[i]
        for s,(S,rw,rv) in enumerate(panels):
            uw,uv=rw[0],rv[0]
            for i in range(1,8):
                uw=jnp.where(sub==i,rw[i],uw); uv=jnp.where(sub==i,rv[i],uv)
            aug[s,k:k+8,side:]=uv
            if k+8<side:
                h,m,l=thirds(uw); vh,vm,vl=thirds(uv)
                a=jnp.concatenate([h,h,m,m,h,l],0).astype(BF16)
                b=jnp.concatenate([jnp.concatenate([h,m,h,m,l,h],0),jnp.concatenate([vh,vm,vh,vm,vl,vh],0)],1).astype(BF16)
                t=dg(a,b,0,0)
                aug[s,k+8:,:]=aug[s,k+8:,:]-t[k+8:,:]

def orthonormal_cols(mat, aug, slots, side=128):
    n=mat.shape[-1]
    r=lax.broadcasted_iota(jnp.int32,(side,side),0); c=lax.broadcasted_iota(jnp.int32,(side,side),1)
    eye=(r==c).astype(F32)
    steps=n//side
    for o in range(steps):
        lo=o*side
        for s in range(slots):
            mo=mat[s,:,lo:lo+side]
            aug[s,:,:side]=mm3(mo,mo,0,0)
            aug[s,:,side:]=eye
        factor_panels(aug,slots,side)
        for s in range(slots):
            q=mm3(mat[s,:,lo:lo+side],aug[s,:,side:],1,1)
            mat[s,:,lo:lo+side]=q
            if o+1<steps:
                rest=mat[s,:,lo+side:]
                mat[s,:,lo+side:]=rest-mm3(q,mm3(q,rest,0,0),1,0)


def soap_kernel(grad, stat, own, other, first, second, outer_out, basis_out, turned_out, update_out, mat, aug):
    slots = grad.shape[0]
    right_side = lax.rem(lax.axis_index("dp"), 2) == 1

    def run(is_right):
        near, far = (0, 1) if is_right else (1, 0)

        def one(s, carry):
            g = grad[s].astype(BF16)
            outer = dg(g, g, near, near)
            outer_out[s] = outer.astype(BF16)
            mixed = STAT_DECAY * stat[s].astype(F32) + (1.0 - STAT_DECAY) * outer
            high, rest = halves(mixed)
            mat[s] = dg(high, own[s], 1, 0) + dg(rest, own[s], 1, 0)
            left, right = (other[s], own[s]) if is_right else (own[s], other[s])
            rotated = dg(dg(left, g, 0, 0).astype(BF16), right, 1, 0)
            turned_out[s] = rotated.astype(BF16)
            first_new = FIRST_DECAY * first[s].astype(F32) + (1.0 - FIRST_DECAY) * rotated
            second_new = SECOND_DECAY * second[s].astype(F32) + (1.0 - SECOND_DECAY) * rotated * rotated
            direction = (
                first_new
                / (1.0 - FIRST_DECAY**ADAM_STEP)
                / (jnp.sqrt(second_new / (1.0 - SECOND_DECAY**ADAM_STEP)) + ADAM_EPSILON)
            )
            back = dg(left, direction.astype(BF16), 1, 0).astype(BF16)
            update_out[s] = dg(back, right, 1, 1).astype(BF16)
            return carry

        lax.fori_loop(0, slots, one, 0)

    @pl.when(right_side)
    def _():
        run(True)

    @pl.when(jnp.logical_not(right_side))
    def _():
        run(False)

    orthonormal_cols(mat, aug, slots)
    basis_out[...] = mat[...].astype(BF16)


def soap_blocks(grad, stat, own, other, first, second):
    slots, side, _ = grad.shape
    shape = jax.ShapeDtypeStruct(grad.shape, BF16)
    whole = pl.BlockSpec(memory_space=pltpu.VMEM)
    return pl.pallas_call(
        soap_kernel,
        out_shape=[shape] * 4,
        in_specs=[whole] * 6,
        out_specs=[whole] * 4,
        scratch_shapes=[
            pltpu.VMEM((slots, side, side), F32),
            pltpu.VMEM((slots, 128, 256), F32),
        ],
        compiler_params=pltpu.CompilerParams(vmem_limit_bytes=60 * 2**20),
        name="soap_blocks",
    )(grad, stat, own, other, first, second)


def ring_place(chip, chips):
    along, across = chip // 2, lax.rem(chip, 2)
    return along * (1 - across) + (chips - 1 - along) * across


def ring_chip(place, chips):
    place = lax.rem(place + 8 * chips, chips)
    across = place // (chips // 2)
    along = place * (1 - across) + (chips - 1 - place) * across
    return 2 * along + across


def whereabouts(chips):
    device, replica = lax.axis_index("fsdp"), lax.axis_index("dp")
    chip, core = device // 2, lax.rem(device, 2)
    place = ring_place(chip, chips)
    turn = 1 - 2 * core
    after = (2 * ring_chip(place + turn, chips) + core, replica)
    before = (2 * ring_chip(place - turn, chips) + core, replica)
    sibling = (2 * chip + 1 - core, replica)
    return device, replica, chip, core, place, turn, after, before, sibling


def greet(neighbours):
    barrier = pltpu.get_barrier_semaphore()
    for neighbour in neighbours:
        pl.semaphore_signal(barrier, inc=1, device_id=neighbour, device_id_type=MESH)
    pl.semaphore_wait(barrier, len(neighbours))


def gather_kernel(chips, share, mat_ref, vec_ref, left_stat, right_stat, left_basis, right_basis, first, second,
                  attn, up, down, vecs, states_out, wide, states, raw_a, raw_u, raw_d, low_a, low_u, low_d,
                  low_v, trade_send, trade_recv, own_sem, ring_send, ring_recv, sib_send, sib_recv, cross_send, cross_recv,
                  vec_send, vec_recv, vec_sib_send, vec_sib_recv, state_sem, out_sem):
    device, replica, chip, core, place, turn, after, before, sibling = whereabouts(chips)
    mirror = (device, 1 - replica)
    side = mat_ref.shape[-1]
    both = 2 * share
    rows = pl.ds(pl.multiple_of(share * core, 8), share)
    barrier = pltpu.get_barrier_semaphore()
    for neighbour in (after, before, sibling, mirror):
        pl.semaphore_signal(barrier, inc=1, device_id=neighbour, device_id_type=MESH)

    def state(source, slot, item):
        return pltpu.make_async_copy(source.at[slot], wide.at[item], state_sem.at[item])

    def fetch_states(stat, basis, spare, mine):
        for slot in range(3):
            state(stat, slot, slot).start()
            state(basis, slot, 3 + slot).start()
        state(first, mine, 6).start()
        state(second, mine, 7).start()
        state(spare, 0, 8).start()

    @pl.when(replica == 0)
    def _():
        fetch_states(left_stat, left_basis, second, 1)

    @pl.when(replica == 1)
    def _():
        fetch_states(right_stat, right_basis, first, 2)

    groups = ((raw_a, low_a, attn), (raw_u, low_u, up), (raw_d, low_d, down))
    for g, (raw, low, out) in enumerate(groups):
        for b in range(16):
            if g == 0:
                raw[(b % 4) // 2, rows, (b // 4) * 2 * side + (b % 2) * side : (b // 4) * 2 * side + (b % 2 + 1) * side] = mat_ref[b]
            elif g == 1:
                raw[b // 8, rows, (b % 8) * side : (b % 8 + 1) * side] = mat_ref[16 + b]
            else:
                raw[b // 2, rows, (b % 2) * side : (b % 2 + 1) * side] = mat_ref[32 + b]
    pl.semaphore_wait(barrier, 4)
    trades = []
    for g, (raw, low, out) in enumerate(groups):
        part = raw.at[:, rows, :]
        trade = pltpu.make_async_remote_copy(
            src_ref=part, dst_ref=part, send_sem=trade_send.at[g], recv_sem=trade_recv.at[g],
            device_id=sibling, device_id_type=MESH)
        trade.start()
        trades.append(trade)
    low_v[...] = vec_ref[...].astype(BF16).astype(F32)

    def cut(ref, g, row, kind):
        first = (4 * replica + core, 2 + core, 4 * (1 - replica) + core)[kind]
        width = ref.shape[-1] // 6
        return ref.at[:, row, pl.ds(pl.multiple_of(first * width, 128), width)]

    def slab(g, origin, kind):
        return cut(groups[g][2], g, pl.ds(pl.multiple_of(origin * both, 16), both), kind)

    def forward(g, t, kind, origin, source):
        return pltpu.make_async_remote_copy(
            src_ref=source, dst_ref=slab(g, origin, kind), send_sem=ring_send.at[t, g, kind],
            recv_sem=ring_recv.at[t, g, kind], device_id=after, device_id_type=MESH)

    def pass_on(g, t, kind, origin):
        part = slab(g, origin, kind)
        return pltpu.make_async_remote_copy(
            src_ref=part, dst_ref=part, send_sem=sib_send.at[t, g, kind], recv_sem=sib_recv.at[t, g, kind],
            device_id=sibling, device_id_type=MESH)

    def across(g, t, origin, kind):
        part = slab(g, origin, kind)
        return pltpu.make_async_remote_copy(
            src_ref=part, dst_ref=part, send_sem=cross_send.at[t, g], recv_sem=cross_recv.at[t, g],
            device_id=mirror, device_id_type=MESH)

    def vec_of(origin):
        return vecs.at[2 * origin + core]

    def vec_forward(t, origin, source):
        return pltpu.make_async_remote_copy(
            src_ref=source, dst_ref=vec_of(origin), send_sem=vec_send.at[t], recv_sem=vec_recv.at[t],
            device_id=after, device_id_type=MESH)

    def vec_pass_on(t, origin, source):
        return pltpu.make_async_remote_copy(
            src_ref=source, dst_ref=vec_of(origin), send_sem=vec_sib_send.at[t], recv_sem=vec_sib_recv.at[t],
            device_id=sibling, device_id_type=MESH)

    vec_forward(0, chip, low_v).start()
    vec_pass_on(0, chip, low_v).start()
    owns = [pltpu.make_async_copy(low_v, vec_of(chip), own_sem.at[3])]
    owns[0].start()
    for g, (raw, low, out) in enumerate(groups):
        trades[g].wait()
        low[...] = raw[...].astype(BF16)
        for kind in range(2):
            forward(g, 0, kind, chip, cut(low, g, slice(None), kind)).start()
        own = pltpu.make_async_copy(low, out.at[:, pl.ds(pl.multiple_of(chip * both, 16), both), :], own_sem.at[g])
        own.start()
        owns.append(own)

    def take_crossed(t):
        origin = ring_chip(place - turn * t, chips)
        for g in range(3):
            across(g, t, origin, 2).wait_recv()
            pass_on(g, t, 2, origin).start()

    def step(t, carry):
        origin = ring_chip(place - turn * t, chips)
        vec_forward(t - 1, origin, vec_of(origin)).wait_recv()

        @pl.when(t < chips - 1)
        def _():
            vec_forward(t, origin, vec_of(origin)).start()

        vec_pass_on(t, origin, vec_of(origin)).start()
        for g in range(3):
            for kind in range(2):
                arrived = slab(g, origin, kind)
                forward(g, t - 1, kind, origin, arrived).wait_recv()

                @pl.when(t < chips - 1)
                def _():
                    forward(g, t, kind, origin, arrived).start()

                if kind == 0:
                    across(g, t, origin, 0).start()
                pass_on(g, t, kind, origin).start()

        @pl.when(t > 1)
        def _():
            take_crossed(t - 1)

        @pl.when(t < 4)
        def _():
            for item in (3 * t - 3, 3 * t - 2, 3 * t - 1):
                state(first, 0, item).wait()
                for holder in range(2 * chips):
                    states[holder, item] = wide[item, holder].astype(BF16)

        @pl.when(t == 4)
        def _():
            pltpu.make_async_copy(states, states_out, out_sem).start()
        return carry

    lax.fori_loop(1, chips, step, 0)
    take_crossed(chips - 1)
    pltpu.make_async_copy(states, states_out, out_sem).wait()
    for own in owns:
        own.wait()

    def finish(t, carry):
        @pl.when(t < chips - 1)
        def _():
            vec_forward(t, chip, vec_of(chip)).wait_send()

        vec_pass_on(t, chip, vec_of(chip)).wait()
        for g in range(3):
            @pl.when(t < chips - 1)
            def _():
                for kind in range(2):
                    forward(g, t, kind, chip, slab(g, chip, kind)).wait_send()

            @pl.when(t > 0)
            def _():
                across(g, t, chip, 0).wait_send()
                for kind in range(3):
                    pass_on(g, t, kind, chip).wait()
        return carry

    lax.fori_loop(0, chips, finish, 0)


def gather_weights(matrices, vector_tile, states, chips):
    total, share, side = matrices.shape
    both = 2 * share
    anywhere = pl.BlockSpec(memory_space=pl.ANY)
    whole = pl.BlockSpec(memory_space=pltpu.VMEM)
    dma = pltpu.SemaphoreType.DMA
    return pl.pallas_call(
        functools.partial(gather_kernel, chips, share),
        out_shape=[
            jax.ShapeDtypeStruct((2, side, 8 * side), BF16),
            jax.ShapeDtypeStruct((2, side, 8 * side), BF16),
            jax.ShapeDtypeStruct((8, side, 2 * side), BF16),
            jax.ShapeDtypeStruct((2 * chips, 16, 128), F32),
            jax.ShapeDtypeStruct((2 * chips, 9, share, side), BF16),
        ],
        in_specs=[whole, whole] + [anywhere] * 6,
        out_specs=[anywhere] * 5,
        scratch_shapes=[
            pltpu.VMEM((9, 2 * chips, share, side), F32),
            pltpu.VMEM((2 * chips, 9, share, side), BF16),
            pltpu.VMEM((2, both, 8 * side), F32),
            pltpu.VMEM((2, both, 8 * side), F32),
            pltpu.VMEM((8, both, 2 * side), F32),
            pltpu.VMEM((2, both, 8 * side), BF16),
            pltpu.VMEM((2, both, 8 * side), BF16),
            pltpu.VMEM((8, both, 2 * side), BF16),
            pltpu.VMEM((16, 128), F32),
            dma((3,)), dma((3,)), dma((4,)),
            dma((chips - 1, 3, 2)), dma((chips - 1, 3, 2)), dma((chips, 3, 3)), dma((chips, 3, 3)),
            dma((chips, 3)), dma((chips, 3)),
            dma((chips - 1,)), dma((chips - 1,)), dma((chips,)), dma((chips,)), dma((9,)), dma,
        ],
        compiler_params=pltpu.CompilerParams(collective_id=1, has_side_effects=True, vmem_limit_bytes=60 * 2**20),
        name="gather_weights",
    )(matrices, vector_tile, *[part.reshape(3, 2 * chips, share, side) for part in states])


def opposite(device, step, count):
    result, bit = 0, 1
    while bit < count:
        one, two = lax.rem(device // bit, 2), lax.rem(step // bit, 2)
        result = result + bit * (one + two - 2 * one * two)
        bit *= 2
    return result


def settle_kernel(early, early_last, late_two, late_one, mat, first, second, left, right, mat_new, mat_low, first_new, second_new, left_new, right_new,
                  left_basis, right_basis):
    share = mat.shape[2]
    for f in range(mat.shape[1]):
        for s in range(3):
            def item(plane, index):
                source, spot = (early, index) if index < 4 else (early_last, index - 4)
                return source[plane, f, spot * share : (spot + 1) * share, :].astype(F32)

            turned = item(*((0, 5), (0, 2), (1, 2))[s])
            update = item(*((1, 5), (0, 3), (1, 3))[s])
            outer = (4, 0, 1)[s]
            fresh = mat[s, f] - MATRIX_RATE * (update + WEIGHT_DECAY * mat[s, f])
            mat_new[s, f] = fresh
            mat_low[s, f] = fresh.astype(BF16)
            first_new[s, f] = FIRST_DECAY * first[s, f] + (1.0 - FIRST_DECAY) * turned
            second_new[s, f] = SECOND_DECAY * second[s, f] + (1.0 - SECOND_DECAY) * turned * turned
            left_new[s, f] = STAT_DECAY * left[s, f] + (1.0 - STAT_DECAY) * item(0, outer)
            right_new[s, f] = STAT_DECAY * right[s, f] + (1.0 - STAT_DECAY) * item(1, outer)
            for panel in range(3):
                lanes = slice(128 * panel, 128 * (panel + 1))
                source, spot = (late_two, 3 * panel + s) if panel < 2 else (late_one, s)
                left_basis[s, f, :, lanes] = source[0, f, spot * share : (spot + 1) * share, :].astype(F32)
                right_basis[s, f, :, lanes] = source[1, f, spot * share : (spot + 1) * share, :].astype(F32)


def settle(early, early_last, late_two, late_one, matrices, first, second, left, right):
    _, count, tall, side = early.shape
    share = matrices.shape[1]
    state = pl.BlockSpec((3, OWNERS, share, side), lambda f: (0, f, 0, 0))
    shape = jax.ShapeDtypeStruct((3, count, share, side), F32)
    low = jax.ShapeDtypeStruct((3, count, share, side), BF16)
    results = pl.pallas_call(
        settle_kernel,
        grid=(count // OWNERS,),
        out_shape=[shape, low] + [shape] * 6,
        in_specs=[
            pl.BlockSpec((2, OWNERS, tall, side), lambda f: (0, f, 0, 0)),
            pl.BlockSpec((2, OWNERS, early_last.shape[2], side), lambda f: (0, f, 0, 0)),
            pl.BlockSpec((2, OWNERS, late_two.shape[2], 128), lambda f: (0, f, 0, 0)),
            pl.BlockSpec((2, OWNERS, late_one.shape[2], 128), lambda f: (0, f, 0, 0)),
        ]
        + [state] * 5,
        out_specs=[state] * 8,
        compiler_params=pltpu.CompilerParams(vmem_limit_bytes=60 * 2**20),
        name="settle",
    )(early, early_last, late_two, late_one, *[part.reshape(3, count, share, side) for part in (matrices, first, second, left, right)])
    return [part.reshape(matrices.shape) for part in results]


def normal_parts(value):
    size = jnp.abs(value) * 0.7071067811865476
    t = 1.0 / (1.0 + 0.3275911 * size)
    bell = jnp.exp(-size * size)
    series = t * (0.254829592 + t * (-0.284496736 + t * (1.421413741 + t * (-1.453152027 + t * 1.061405429))))
    tail = 0.5 * series * bell
    return jnp.where(value >= 0.0, 1.0 - tail, tail), bell * 0.3989422804014327


def span(index, size):
    return pl.ds(pl.multiple_of(index * size, size), size)


def looped(count, body):
    def step(index, carry):
        body(index)
        return carry

    lax.fori_loop(0, count, step, 0)


def vector_row(vecs, row, width):
    lane = lax.broadcasted_iota(jnp.int32, (1, 128), 1)
    pieces = []
    for pair in range(width // 128):
        chunk = row * (width // 64) + 2 * pair
        one = vecs[chunk // 9, chunk % 9 : chunk % 9 + 1, :]
        chunk += 1
        two = vecs[chunk // 9, chunk % 9 : chunk % 9 + 1, :]
        pieces.append(jnp.where(lane < 64, one, pltpu.roll(two, 64, 1)))
    return jnp.concatenate(pieces, axis=1)


def vector_tiles_of(rows, row_up, tiles):
    chunks = rows.shape[1] // 64
    for f in range(tiles.shape[0]):
        for i in range(9):
            row, place = divmod(9 * f + i, chunks)
            if 5 <= row < 9:
                spot = (row - 5) * chunks + place
                piece = row_up[spot // 4, :, 128 * (spot % 4 // 2) : 128 * (spot % 4 // 2) + 128]
            else:
                piece = rows[row : row + 1, 128 * (place // 2) : 128 * (place // 2) + 128]
            tiles[f, i : i + 1, :] = pltpu.roll(piece, 64, 1) if place % 2 else piece


def layer_kernel(length_ref, x_ref, cot_ref, tiles, attn_hbm, up_hbm, down_hbm,
                 out_ref, logs, grad_vec, grad_vec_up, qkv_out, grad_c_out, turned_x_out, grad_r_out, grad_out, grad_up, grad_down,
                 w_attn, w_up, w_down, qkv, context, hat_one, scale_one, normed, active, slope, hidden_low,
                 grad_r, low_e, grad_c, turned_x, turned_n, turned_c, stage_w, stage_t,
                 vec, vec_up, load_sem, wide_sem, tall_sem, save_sem):
    slots, width = x_ref.shape
    length = length_ref[0]
    chunks = w_up.shape[1] // 256
    thirds_of = width // 256
    loads = [pltpu.make_async_copy(source, target, load_sem.at[i])
             for i, (source, target) in enumerate(((attn_hbm, w_attn), (up_hbm, w_up), (down_hbm, w_down)))]
    for load in loads:
        load.start()

    def turn(source, target):
        def one(index):
            target[:, span(index, 128)] = source[span(index, 128), :].T

        looped(slots // 128, one)

    def wide_copy(target, slot, index):
        return pltpu.make_async_copy(stage_w.at[slot], target.at[:, span(index, 256)], wide_sem.at[slot])

    def tall_copy(slot, index):
        return pltpu.make_async_copy(stage_t.at[slot], grad_down.at[span(index, 256), :], tall_sem.at[slot])

    def put_wide(target, index, value, first):
        slot = lax.rem(index, 2)

        @pl.when(jnp.logical_not(first))
        def _():
            wide_copy(target, slot, index).wait()

        stage_w[slot] = value.astype(BF16)
        wide_copy(target, slot, index).start()

    grad_vec[...] = jnp.zeros_like(grad_vec)
    for row in range(12):
        vec[row : row + 1, :] = vector_row(tiles, row, width)
        if 5 <= row < 9:
            for third in range(thirds_of):
                vec_up[(row - 5) * thirds_of + third] = vec[row : row + 1, 256 * third : 256 * (third + 1)]
    turn(x_ref, turned_x)
    loads[0].wait()

    def project(index):
        lanes = span(index, 256)
        part = index // thirds_of
        row = jnp.where(part == 0, vec[0:1, span(lax.rem(index, thirds_of), 256)],
                        jnp.where(part == 2, vec[1:2, span(lax.rem(index, thirds_of), 256)], 0.0))
        qkv[:, lanes] = (jnp.dot(x_ref[...], w_attn[:, lanes], preferred_element_type=F32) + row).astype(BF16)

    looped(3 * thirds_of, project)
    saves = [pltpu.make_async_copy(source, target, save_sem.at[i]) for i, (source, target) in enumerate((
        (qkv, qkv_out), (turned_x, turned_x_out), (grad_c, grad_c_out), (grad_r, grad_r_out)))]
    saves[0].start()
    saves[1].start()

    lane = lax.broadcasted_iota(jnp.int32, (slots, 128), 1)
    tall_lane = lax.broadcasted_iota(jnp.int32, (128, 128), 0)
    seen = lax.broadcasted_iota(jnp.int32, (slots, 128), 0) < length

    def head_lanes(head, value):
        keep = (lane < HEAD_DIM) if head == 0 else (lane >= HEAD_DIM)
        return jnp.where(keep, value, jnp.zeros_like(value))

    def lanes_of(pair, part):
        return pl.ds(pl.multiple_of(part * width + pair * 128, 128), 128)

    def attend(pair):
        key, value = qkv[:, lanes_of(pair, 1)], qkv[:, lanes_of(pair, 2)]
        turned_value = value.T
        keys = [head_lanes(head, key * HEAD_DIM ** (-0.5)) for head in range(2)]
        for block in range(slots // 128):
            rows = slice(128 * block, 128 * (block + 1))
            query = qkv[rows, lanes_of(pair, 0)]
            both = []
            for head in range(2):
                scores = jnp.where(seen, dg(keys[head], query, 1, 1), -1e30)
                top = jnp.max(scores, axis=0, keepdims=True)
                shifted = jnp.exp(scores - top)
                total = jnp.sum(shifted, axis=0, keepdims=True)
                weights = (shifted * (1.0 / total)).astype(BF16)
                both.append(jnp.dot(turned_value, weights, preferred_element_type=F32))
                logs[2 * pair + head, :, rows] = top + jnp.log(total)
            merged = jnp.where(tall_lane < HEAD_DIM, both[0], both[1])
            context[rows, lanes_of(pair, 0)] = merged.T.astype(BF16)

    looped(width // 128, attend)
    turn(context, turned_c)

    def mix(index):
        lanes = span(index, 256)
        away = pl.ds(pl.multiple_of(3 * width + index * 256, 256), 256)
        value = jnp.dot(context[...], w_attn[:, away], preferred_element_type=F32) + vec[2:3, lanes]
        hat_one[:, lanes] = x_ref[:, lanes].astype(F32) + value

    looped(thirds_of, mix)

    def standard(value):
        centered = value - jnp.mean(value, axis=-1, keepdims=True)
        scale = lax.rsqrt(jnp.mean(centered * centered, axis=-1, keepdims=True) + NORM_EPSILON)
        return centered * scale, scale

    def norm_one(index):
        rows = span(index, 128)
        hat, scale = standard(hat_one[rows, :])
        hat_one[rows, :] = hat
        scale_one[rows, :] = jnp.broadcast_to(scale, (128, 128))
        normed[rows, :] = (hat * vec[3:4, :] + vec[4:5, :]).astype(BF16)

    looped(slots // 128, norm_one)
    turn(normed, turned_n)
    loads[1].wait()

    def rise(index):
        lanes = span(index, 256)
        hidden = jnp.dot(normed[...], w_up[:, lanes], preferred_element_type=F32) + vec_up[index]
        below, density = normal_parts(hidden)
        active[:, lanes] = (hidden * below).astype(BF16)
        slope[:, lanes] = below + hidden * density

    looped(chunks, rise)
    loads[2].wait()

    def fall(index):
        lanes = span(index, 256)
        value = jnp.dot(active[...], w_down[:, lanes], preferred_element_type=F32)
        grad_r[:, lanes] = hat_one[:, lanes] * vec[3:4, lanes] + vec[4:5, lanes] + value + vec[9:10, lanes]

    looped(thirds_of, fall)

    def unstandard(grad_hat, hat, scale):
        return scale * (grad_hat - jnp.mean(grad_hat, axis=-1, keepdims=True)
                        - hat * jnp.mean(grad_hat * hat, axis=-1, keepdims=True))

    def add_row(row, value):
        grad_vec[row : row + 1, :] += jnp.sum(value, axis=0, keepdims=True)

    def norm_two(index):
        rows = span(index, 128)
        hat, scale = standard(grad_r[rows, :])
        out_ref[rows, :] = (hat * vec[10:11, :] + vec[11:12, :]).astype(BF16)
        place = lax.broadcasted_iota(jnp.int32, (128, width), 0) + index * 128
        grad = jnp.where(place < length, cot_ref[rows, :].astype(F32), 0.0)
        add_row(10, grad * hat)
        add_row(11, grad)
        back = unstandard(grad * vec[10:11, :], hat, scale)
        add_row(9, back)
        grad_r[rows, :] = back
        low_e[rows, :] = back.astype(BF16)

    looped(slots // 128, norm_two)

    def sink(index):
        lanes = span(index, 256)
        grad = dg(low_e[...], w_down[lanes, :], 1, 1) * slope[:, lanes]
        grad_vec_up[index] = jnp.sum(grad, axis=0, keepdims=True)
        hidden_low[:, lanes] = grad.astype(BF16)

    def weigh(index):
        lanes = span(index, 256)
        put_wide(grad_up, index, jnp.dot(turned_n[...], hidden_low[:, lanes], preferred_element_type=F32), index < 2)
        slot = lax.rem(index, 2)

        @pl.when(index >= 2)
        def _():
            tall_copy(slot, index).wait()

        stage_t[slot] = dg(active[:, lanes], low_e[...], 0, 0).astype(BF16)
        tall_copy(slot, index).start()

    def weigh_and_sink(index):
        slot = lax.rem(index, 2)

        @pl.when(index >= 2)
        def _():
            wide_copy(grad_up, slot, index).wait()
            tall_copy(slot, index).wait()

        lanes = span(index, 256)
        sink(index + 1)
        stage_w[slot] = jnp.dot(turned_n[...], hidden_low[:, lanes], preferred_element_type=F32).astype(BF16)
        stage_t[slot] = dg(active[:, lanes], low_e[...], 0, 0).astype(BF16)
        wide_copy(grad_up, slot, index).start()
        tall_copy(slot, index).start()

    sink(0)
    looped(chunks - 1, weigh_and_sink)
    weigh(jnp.int32(chunks - 1))

    def rise_back(index):
        lanes = span(index, 256)
        grad_r[:, lanes] += dg(hidden_low[...], w_up[lanes, :], 1, 1)

    looped(thirds_of, rise_back)

    def norm_one_back(index):
        rows = span(index, 128)
        hat, grad = hat_one[rows, :], grad_r[rows, :]
        add_row(3, grad * hat)
        add_row(4, grad)
        back = unstandard(grad * vec[3:4, :], hat, scale_one[rows, 0:1])
        add_row(2, back)
        grad_r[rows, :] = back
        low_e[rows, :] = back.astype(BF16)


    def mix_back(index):
        lanes = span(index, 256)
        put_wide(grad_out, index, jnp.dot(turned_c[...], low_e[:, lanes], preferred_element_type=F32), False)
        away = pl.ds(3 * width, width)
        grad_c[:, lanes] = dg(low_e[...], w_attn[lanes, away], 1, 1).astype(BF16)

    looped(slots // 128, norm_one_back)
    saves[3].start()
    looped(thirds_of, mix_back)
    saves[2].start()
    for slot in range(2):
        wide_copy(grad_out, slot, 0).wait()
        tall_copy(slot, 0).wait()
    for save in saves:
        save.wait()


def layer(length, inputs, cotangent, tiles, attn, up, down):
    slots, width = inputs.shape
    tall = down.shape[0]
    anywhere = pl.BlockSpec(memory_space=pl.ANY)
    whole = pl.BlockSpec(memory_space=pltpu.VMEM)
    vmem = pltpu.VMEM
    dma = pltpu.SemaphoreType.DMA
    return pl.pallas_call(
        layer_kernel,
        out_shape=[
            jax.ShapeDtypeStruct((slots, width), BF16),
            jax.ShapeDtypeStruct((width // HEAD_DIM, 1, slots), F32),
            jax.ShapeDtypeStruct((16, width), F32),
            jax.ShapeDtypeStruct((tall // 256, 1, 256), F32),
            jax.ShapeDtypeStruct((slots, 3 * width), BF16),
            jax.ShapeDtypeStruct((slots, width), BF16),
            jax.ShapeDtypeStruct((width, slots), BF16),
            jax.ShapeDtypeStruct((slots, width), F32),
            jax.ShapeDtypeStruct((width, width), BF16),
            jax.ShapeDtypeStruct((width, tall), BF16),
            jax.ShapeDtypeStruct((tall, width), BF16),
        ],
        in_specs=[pl.BlockSpec(memory_space=pltpu.SMEM)] + [whole] * 3 + [anywhere] * 3,
        out_specs=[whole] * 4 + [anywhere] * 7,
        scratch_shapes=[
            vmem((width, 4 * width), BF16), vmem((width, tall), BF16), vmem((tall, width), BF16),
            vmem((slots, 3 * width), BF16), vmem((slots, width), BF16),
            vmem((slots, width), F32), vmem((slots, 128), F32), vmem((slots, width), BF16),
            vmem((slots, tall), BF16), vmem((slots, tall), F32), vmem((slots, tall), BF16),
            vmem((slots, width), F32), vmem((slots, width), BF16), vmem((slots, width), BF16),
            vmem((width, slots), BF16), vmem((width, slots), BF16), vmem((width, slots), BF16),
            vmem((2, width, 256), BF16), vmem((2, 256, width), BF16),
            vmem((16, width), F32), vmem((tall // 256, 1, 256), F32),
            dma((3,)), dma((2,)), dma((2,)), dma((4,)),
        ],
        compiler_params=pltpu.CompilerParams(vmem_limit_bytes=60 * 2**20),
        cost_estimate=pl.CostEstimate(flops=25_000_000_000, bytes_accessed=40_000_000, transcendentals=8_000_000),
        name="layer",
    )(length, inputs, cotangent, tiles, attn, up, down)


def conclude_kernel(chips, share, length_ref, logs, vec_part, vec_up_part, parts, qkv_hbm, grad_c_hbm, turned_x_hbm, grad_r_hbm,
                    attn_hbm, g_out, g_up, g_down,
                    grad_x, vec_sum, early, early_last, late_two, late_one,
                    qkv, grad_c, turned_x, grad_r, w_qkv, grad_heads, probs, dscores, g_qkv, grad_vec, tiles,
                    mine, theirs, ring, crossed, peer, vmine, vring, vpeer, owned,
                    states, items, mat, aug, out_early, out_last, out_two, out_one,
                    load_sem, mine_sem, sib_send, sib_recv, ring_send, ring_recv, cross_send, cross_recv, peer_send, peer_recv,
                    state_send, state_recv, note_send, note_recv, relay_send, relay_recv, keep_sem):
    device, replica, chip, core, place, turn, after, before, sibling = whereabouts(chips)
    count = 2 * chips
    mirror = (device, 1 - replica)
    side = mine.shape[-1]
    width = 2 * side
    slots = qkv.shape[0]
    quarter = side // 4
    last = chips - 1
    part = 128
    panels = side // part
    length = length_ref[0]

    def partner(step):
        return opposite(device, step, count), replica

    barrier = pltpu.get_barrier_semaphore()

    def hail(step, carry):
        pl.semaphore_signal(barrier, inc=1, device_id=partner(step), device_id_type=MESH)
        return carry

    lax.fori_loop(1, count, hail, 0)
    pl.semaphore_signal(barrier, inc=1, device_id=mirror, device_id_type=MESH)

    loads = [pltpu.make_async_copy(source, target, load_sem.at[i]) for i, (source, target) in enumerate((
        (qkv_hbm, qkv), (grad_c_hbm, grad_c), (turned_x_hbm, turned_x), (grad_r_hbm, grad_r),
        (attn_hbm.at[:, : 3 * width], w_qkv)))]


    def quarters(first, number):
        return pl.ds(pl.multiple_of(first * quarter, 16), number * quarter)

    carried = quarters(replica, 3)
    private = quarters(3 * replica, 1)
    foreign = quarters(3 * (1 - replica), 1)

    def column(index):
        return pl.ds(pl.multiple_of(index * side, 128), side)

    def fetch(owner, wanted, start):
        which = owner // 4
        i, j = lax.rem(owner, 4) // 2, lax.rem(owner, 2)
        if 0 in wanted:
            @pl.when(which < 3)
            def _():
                start(0, g_qkv.at[i, :, column(2 * which + j)])

            @pl.when(which == 3)
            def _():
                start(0, g_out.at[i, :, column(j)])

            start(3, tiles.at[owner])
        else:
            start(1, g_up.at[owner // 8, :, column(lax.rem(owner, 8))])
            start(2, g_down.at[owner // 2, :, column(lax.rem(owner, 2))])

    def local(t, slot, source):
        target = vmine.at[0, t] if slot == 3 else mine.at[t, slot]
        return pltpu.make_async_copy(source, target, mine_sem.at[t, slot])

    def to_sibling(t, slot, source):
        target = vmine.at[1, t] if slot == 3 else theirs.at[t, slot]
        return pltpu.make_async_remote_copy(
            src_ref=source, dst_ref=target, send_sem=sib_send.at[t, slot], recv_sem=sib_recv.at[t, slot],
            device_id=sibling, device_id_type=MESH)

    def to_next(t, slot):
        source, target = (vmine.at[0, t], vring.at[t]) if slot == 3 else (mine.at[t, slot, carried, :], ring.at[t, slot])
        return pltpu.make_async_remote_copy(
            src_ref=source, dst_ref=target, send_sem=ring_send.at[t, slot], recv_sem=ring_recv.at[t, slot],
            device_id=after, device_id_type=MESH)

    def across(t, slot):
        return pltpu.make_async_remote_copy(
            src_ref=mine.at[t, slot, foreign, :], dst_ref=crossed.at[t, slot], send_sem=cross_send.at[t, slot],
            recv_sem=cross_recv.at[t, slot], device_id=mirror, device_id_type=MESH)

    def to_mirror(slot):
        source, target = (vmine.at[0, last], vpeer) if slot == 3 else (mine.at[last, slot, carried, :], peer.at[slot, carried, :])
        return pltpu.make_async_remote_copy(
            src_ref=source, dst_ref=target, send_sem=peer_send.at[slot], recv_sem=peer_recv.at[slot],
            device_id=mirror, device_id_type=MESH)

    def begin_own(t, wanted):
        fetch(2 * ring_chip(place - turn * (t + 1), chips) + core, wanted, lambda slot, source: local(t, slot, source).start())

    def begin_sibling(t, wanted):
        fetch(2 * ring_chip(place + turn * (t + 1), chips) + 1 - core, wanted,
              lambda slot, source: to_sibling(t, slot, source).start())

    def begin(t, wanted):
        begin_sibling(t, wanted)
        begin_own(t, wanted)

    def sources(slot):
        return tiles.at[0] if slot == 3 else g_up.at[0, :, :side]

    def pair_up(t, wanted):
        for slot in wanted:
            local(t, slot, sources(slot)).wait()
            to_sibling(t, slot, sources(slot)).wait_recv()
            if slot == 3:
                vmine[0, t] = vmine[0, t] + vmine[1, t]
            else:
                mine[t, slot] = (mine[t, slot].astype(F32) + theirs[t, slot].astype(F32)).astype(BF16)
                across(t, slot).start()

    def add(t, slot, hold, extra):
        mine[t, slot, hold, :] = (mine[t, slot, hold, :].astype(F32) + extra.astype(F32)).astype(BF16)

    def pass_round(t, wanted):
        for slot in wanted:
            if slot < 3:
                across(t, slot).wait_recv()
                add(t, slot, private, crossed[t, slot])

            @pl.when(t > 0)
            def _():
                to_next(t - 1, slot).wait_recv()
                if slot == 3:
                    vmine[0, t] = vmine[0, t] + vring[t - 1]
                else:
                    add(t, slot, carried, ring[t - 1, slot])

            @pl.when(t < last)
            def _():
                to_next(t, slot).start()

            @pl.when(t == last)
            def _():
                to_mirror(slot).start()

    def own_sum(slot):
        to_mirror(slot).wait()
        if slot == 3:
            vec_sum[...] = vmine[0, last] + vpeer[...]
            return
        shared = slice(quarter, 3 * quarter)
        owned[slot, shared, :] = (mine[last, slot, shared, :].astype(F32) + peer[slot, shared, :].astype(F32)).astype(BF16)
        owned[slot, private, :] = mine[last, slot, private, :]
        owned[slot, foreign, :] = peer[slot, foreign, :]

    feed, rest = (1, 2), (3, 0)

    def ahead(t, wanted):
        @pl.when(t + 3 < chips)
        def _():
            begin(t + 3, wanted)

        @pl.when(t == 0)
        def _():
            pair_up(1, wanted)

        @pl.when(t + 2 < chips)
        def _():
            pair_up(t + 2, wanted)

    def rest_step(t):
        pass_round(t, rest)
        ahead(t, rest)


    lane = lax.broadcasted_iota(jnp.int32, (slots, 128), 1)
    seen = lax.broadcasted_iota(jnp.int32, (slots, 128), 0) < length

    def head_lanes(head, value):
        keep = (lane < HEAD_DIM) if head == 0 else (lane >= HEAD_DIM)
        return jnp.where(keep, value, jnp.zeros_like(value))

    def lanes_of(pair, member):
        return pl.ds(pl.multiple_of(member * width + pair * 128, 128), 128)

    def attend_back(pair):
        query, key, value = [qkv[:, lanes_of(pair, member)] for member in range(3)]
        grad = grad_c[:, lanes_of(pair, 0)]
        turned_key = key.T
        found = []
        for head in range(2):
            near_key = head_lanes(head, key * HEAD_DIM ** (-0.5))
            near_value = head_lanes(head, value)
            for block in range(slots // 128):
                rows = slice(128 * block, 128 * (block + 1))
                scores = jnp.where(seen, dg(near_key, query[rows], 1, 1), -1e30)
                weights = jnp.exp(scores - logs[2 * pair + head, :, rows])
                back = dg(near_value, grad[rows], 1, 1)
                scores_back = weights * (back - jnp.sum(back * weights, axis=0, keepdims=True))
                probs[head, :, rows] = weights.astype(BF16)
                dscores[head, :, rows] = scores_back.astype(BF16)
            found.append((
                jnp.dot(turned_key, dscores[head], preferred_element_type=F32),
                jnp.dot(dscores[head], query, preferred_element_type=F32),
                jnp.dot(probs[head], grad, preferred_element_type=F32),
            ))
        top = lax.broadcasted_iota(jnp.int32, (128, slots), 0) < HEAD_DIM
        turned_query = jnp.where(top, found[0][0], found[1][0]) * HEAD_DIM ** (-0.5)
        grad_heads[:, lanes_of(pair, 0)] = turned_query.T.astype(BF16)
        grad_heads[:, lanes_of(pair, 1)] = (jnp.where(lane < HEAD_DIM, found[0][1], found[1][1]) * HEAD_DIM ** (-0.5)).astype(BF16)
        grad_heads[:, lanes_of(pair, 2)] = jnp.where(lane < HEAD_DIM, found[0][2], found[1][2]).astype(BF16)

    def project_back(index):
        lanes = span(index, 256)
        value = jnp.dot(turned_x[...], grad_heads[:, lanes], preferred_element_type=F32)
        g_qkv[:, :, lanes] = value.astype(BF16).reshape(2, side, 256)

    def input_back(index):
        lanes = span(index, 256)
        grad_x[:, lanes] = grad_r[:, lanes] + dg(grad_heads[...], w_qkv[lanes, :], 1, 1)


    def join(pair, carry):
        rows = pl.ds(pl.multiple_of(2 * share * pair, 16), 2 * share)
        for item in range(9):
            two = [parts[2 * pair + index, item].astype(F32) for index in range(2)]
            states[item, rows, :] = jnp.concatenate(two, axis=0).astype(BF16)
        return carry

    def trade(index):
        source = (5 - replica, 3, 8)[index]
        return pltpu.make_async_remote_copy(
            src_ref=states.at[source], dst_ref=states.at[9 + index], send_sem=state_send.at[index],
            recv_sem=state_recv.at[index], device_id=mirror, device_id_type=MESH)

    def update(rotated, left, right, first, second):
        first_new = FIRST_DECAY * first.astype(F32) + (1.0 - FIRST_DECAY) * rotated
        second_new = SECOND_DECAY * second.astype(F32) + (1.0 - SECOND_DECAY) * rotated * rotated
        direction = (
            first_new
            / (1.0 - FIRST_DECAY**ADAM_STEP)
            / (jnp.sqrt(second_new / (1.0 - SECOND_DECAY**ADAM_STEP)) + ADAM_EPSILON)
        )
        back = dg(left, direction.astype(BF16), 1, 0).astype(BF16)
        return dg(back, right, 1, 1)

    def prepare(s):
        for is_right in (False, True):
            @pl.when(replica == int(is_right))
            def _():
                near = 0 if is_right else 1
                g = owned[s]
                outer = dg(g, g, near, near)
                items[(4, 0, 1)[s]] = outer
                mixed = STAT_DECAY * states[s].astype(F32) + (1.0 - STAT_DECAY) * outer
                high, low = halves(mixed)
                mat[s] = dg(high, states[3 + s], 1, 0) + dg(low, states[3 + s], 1, 0)
                if s not in (0, 2 if is_right else 1):
                    return
                other = states[10] if s == 0 else states[9]
                left, right = (other, states[3 + s]) if is_right else (states[3 + s], other)
                rotated = dg(dg(left, g, 0, 0).astype(BF16), right, 1, 0)
                if s > 0:
                    items[2] = rotated
                    items[3] = update(rotated, left, right, states[6], states[7])
                elif is_right:
                    items[5] = update(rotated, left, right, states[8], states[11])
                else:
                    items[5] = rotated

    def rows_of(holder):
        return pl.ds(pl.multiple_of(holder * share, 8), share)

    def outgoing(kind, holder):
        return (out_early, out_last, out_two, out_one)[kind].at[holder]

    def incoming(kind, owner):
        return (early, early_last, late_two, late_one)[kind].at[replica, owner]

    def pack(kind):
        def one(holder, carry):
            rows = rows_of(holder)
            if kind < 2:
                for pair in ((0, 1), (2,))[kind]:
                    two = jnp.concatenate([items[2 * pair, rows, :], items[2 * pair + 1, rows, :]], axis=0)
                    spot = pair if kind == 0 else 0
                    (out_early, out_last)[kind][holder, 2 * share * spot : 2 * share * (spot + 1), :] = two.astype(BF16)
            else:
                columns = ((0, part), (2 * part,))[kind - 2]
                stacked = [mat[s, rows, lo : lo + part] for lo in columns for s in range(3)]
                if kind == 3:
                    stacked.append(jnp.zeros((8, part), F32))
                (out_two, out_one)[kind - 2][holder] = jnp.concatenate(stacked, axis=0).astype(BF16)
            return carry

        lax.fori_loop(0, count, one, 0)

    def note(kind, step):
        target = partner(step)
        return pltpu.make_async_remote_copy(
            src_ref=outgoing(kind, target[0]), dst_ref=incoming(kind, device), send_sem=note_send.at[kind, step],
            recv_sem=note_recv.at[kind, step], device_id=target, device_id_type=MESH)

    def relay(kind, step):
        block = incoming(kind, partner(step)[0])
        return pltpu.make_async_remote_copy(
            src_ref=block, dst_ref=block, send_sem=relay_send.at[kind, step], recv_sem=relay_recv.at[kind, step],
            device_id=mirror, device_id_type=MESH)

    def keep(kind):
        return pltpu.make_async_copy(outgoing(kind, device), incoming(kind, device), keep_sem.at[kind])

    def launch(kind):
        pack(kind)
        keep(kind).start()

        def one(step, carry):
            note(kind, step).start()
            return carry

        lax.fori_loop(1, chips, one, 0)
        near.extend((kind, step) for step in range(chips))
        far.extend((kind, step) for step in range(chips, count))

    def hand_on(kind, step):
        note(kind, step).wait_recv()
        relay(kind, step).start()

    near, far, flying = [], [], []

    def hand_on_near(number):
        for kind, step in near[:number]:
            if step == 0:
                keep(kind).wait()
                relay(kind, 0).start()
            else:
                hand_on(kind, step)
        del near[:number]

    def pump(number):
        for kind, step in far[:number]:
            if len(flying) >= WINDOW:
                hand_on(*flying.pop(0))
            note(kind, step).start()
            flying.append((kind, step))
        del far[:number]


    def first_own(index, carry):
        begin_own(index, feed)
        return carry

    def first_sibling(index, carry):
        begin_sibling(index, feed)
        return carry

    lax.fori_loop(0, 3, first_own, 0)
    for load in loads[:2]:
        load.start()
    lax.fori_loop(0, count // 2, join, 0)
    pl.semaphore_wait(barrier, count)
    lax.fori_loop(0, 3, first_sibling, 0)
    pair_up(0, feed)
    for load in loads[2:]:
        load.start()
    grad_vec[...] = vec_part[...]

    def main(t, carry):
        pass_round(t, feed)

        @pl.when(t > 2)
        def _():
            rest_step(t - 3)

        ahead(t, feed)

        @pl.when(t == 0)
        def _():
            for load in loads[:2]:
                load.wait()

        @pl.when(t < 2)
        def _():
            def one(third, carry):
                attend_back(3 * t + third)
                return carry

            lax.fori_loop(0, 3, one, 0)

        @pl.when(t == TRADE)
        def _():
            trade(0).start()

        @pl.when(t == 2)
        def _():
            loads[2].wait()
            grad_vec[0:1, :] = jnp.sum(grad_heads[:, :width].astype(F32), axis=0, keepdims=True)
            grad_vec[1:2, :] = jnp.sum(grad_heads[:, 2 * width :].astype(F32), axis=0, keepdims=True)
            looped(3 * width // 256, project_back)
            vector_tiles_of(grad_vec, vec_up_part, tiles)

            def start_rest(index, carry):
                begin(index, rest)
                return carry

            lax.fori_loop(0, 3, start_rest, 0)
            pair_up(0, rest)

        return carry

    lax.fori_loop(0, chips, main, 0)
    trade(0).wait()
    own_sum(1)
    prepare(1)
    rest_step(jnp.int32(chips - 3))
    own_sum(2)
    trade(1).start()
    trade(2).start()
    prepare(2)
    launch(0)
    pump(WINDOW)
    rest_step(jnp.int32(chips - 2))
    hand_on_near(4)
    pump(1)
    for load in loads[3:]:
        load.wait()
    looped(width // 256, input_back)
    pump(1)
    rest_step(jnp.int32(chips - 1))
    hand_on_near(4)
    pump(1)
    own_sum(0)
    trade(1).wait()
    trade(2).wait()
    prepare(0)
    launch(1)

    def between(moment):
        if far and moment % (5, 3, 3, 2)[far[0][0]] == 0:
            pump(1)
        elif near and moment % 2 == 1:
            hand_on_near(1)

    row_index = lax.broadcasted_iota(jnp.int32, (part, part), 0)
    column_index = lax.broadcasted_iota(jnp.int32, (part, part), 1)
    eye = (row_index == column_index).astype(F32)
    for o in range(panels):
        lo = o * part
        for s in range(3):
            block = mat[s, :, lo : lo + part]
            aug[s, :, :part] = mm3(block, block, 0, 0)
            aug[s, :, part:] = eye
        factor_panels(aug, 3, part, lambda p: between(16 * o + p))
        for s in range(3):
            mat[s, :, lo : lo + part] = mm3(mat[s, :, lo : lo + part], aug[s, :, part:], 1, 1)
        if o > 0:
            launch(1 + o)
        if o + 1 < panels:
            for s in range(3):
                q, remaining = mat[s, :, lo : lo + part], mat[s, :, lo + part :]
                mat[s, :, lo + part :] = remaining - mm3(q, mm3(q, remaining, 0, 0), 1, 0)
    while far or near:
        pump(2)
        hand_on_near(2)
    for kind, step in flying:
        hand_on(kind, step)
    own_sum(3)

    def finish(step, carry):
        for kind in range(4):
            relay(kind, step).wait()

            @pl.when(step > 0)
            def _():
                note(kind, step).wait_send()

        @pl.when(step < chips)
        def _():
            for slot in range(4):
                to_sibling(step, slot, sources(slot)).wait_send()
                if slot < 3:
                    across(step, slot).wait_send()

                @pl.when(step < last)
                def _():
                    to_next(step, slot).wait_send()
        return carry

    lax.fori_loop(0, count, finish, 0)


def conclude(length, logs, vec_part, vec_up_part, parts, qkv, grad_c, turned_x, grad_r, attn, g_out, g_up, g_down, share, chips):
    side = g_up.shape[1]
    width, count = 2 * side, 2 * chips
    slots = qkv.shape[0]
    tall = -(-3 * share // 16) * 16
    anywhere = pl.BlockSpec(memory_space=pl.ANY)
    whole = pl.BlockSpec(memory_space=pltpu.VMEM)
    vmem = pltpu.VMEM
    dma = pltpu.SemaphoreType.DMA
    return pl.pallas_call(
        functools.partial(conclude_kernel, chips, share),
        out_shape=[
            jax.ShapeDtypeStruct((slots, width), F32),
            jax.ShapeDtypeStruct((16, 128), F32),
            jax.ShapeDtypeStruct((2, count, 4 * share, side), BF16),
            jax.ShapeDtypeStruct((2, count, 2 * share, side), BF16),
            jax.ShapeDtypeStruct((2, count, 6 * share, 128), BF16),
            jax.ShapeDtypeStruct((2, count, tall, 128), BF16),
        ],
        in_specs=[pl.BlockSpec(memory_space=pltpu.SMEM)] + [whole] * 4 + [anywhere] * 8,
        out_specs=[whole] * 2 + [anywhere] * 4,
        scratch_shapes=[
            vmem((slots, 3 * width), BF16), vmem((slots, width), BF16), vmem((width, slots), BF16), vmem((slots, width), F32),
            vmem((width, 3 * width), BF16), vmem((slots, 3 * width), BF16), vmem((2, slots, slots), BF16),
            vmem((2, slots, slots), BF16), vmem((2, side, 3 * width), BF16), vmem((16, width), F32), vmem((count, 16, 128), F32),
            vmem((chips, 3, side, side), BF16), vmem((chips, 3, side, side), BF16),
            vmem((chips - 1, 3, 3 * side // 4, side), BF16), vmem((chips, 3, side // 4, side), BF16), vmem((3, side, side), BF16),
            vmem((2, chips, 16, 128), F32), vmem((chips - 1, 16, 128), F32), vmem((16, 128), F32), vmem((3, side, side), BF16),
            vmem((12, side, side), BF16), vmem((6, side, side), F32), vmem((3, side, side), F32), vmem((3, 128, 256), F32),
            vmem((count, 4 * share, side), BF16), vmem((count, 2 * share, side), BF16), vmem((count, 6 * share, 128), BF16),
            vmem((count, tall, 128), BF16),
            dma((5,)), dma((chips, 4)), dma((chips, 4)), dma((chips, 4)), dma((chips - 1, 4)), dma((chips - 1, 4)),
            dma((chips, 3)), dma((chips, 3)), dma((4,)), dma((4,)), dma((3,)), dma((3,)),
            dma((4, count)), dma((4, count)), dma((4, count)), dma((4, count)), dma((4,)),
        ],
        compiler_params=pltpu.CompilerParams(collective_id=2, has_side_effects=True, vmem_limit_bytes=62 * 2**20),
        name="conclude",
    )(length, logs, vec_part, vec_up_part, parts, qkv, grad_c, turned_x, grad_r, attn, g_out, g_up, g_down)


def plain_gather(matrices, vectors):
    side = matrices.shape[-1]
    blocks = lax.all_gather(matrices.astype(BF16), "fsdp", axis=1, tiled=True)
    attn = jnp.concatenate([assemble(blocks[4 * part : 4 * part + 4], 2, 2) for part in range(4)], axis=1)
    up = assemble(blocks[16:32], 2, 8)
    down = assemble(blocks[32:], 8, 2)
    rows = lax.all_gather(vectors.astype(BF16), "fsdp", axis=0, tiled=True)
    return attn, up, down, rows.astype(F32).reshape(-1, 2 * side)


def plain_reduce(grad_qkv, grad_out, grad_up, grad_down, vector_grad, capacity):
    shard_count = lax.axis_size("fsdp")
    width = grad_up.shape[0]
    side = width // 2
    blocks = jnp.concatenate(
        [split_blocks(grad_qkv[:, part * width : (part + 1) * width], 2, 2, side) for part in range(3)]
        + [split_blocks(grad_out, 2, 2, side), split_blocks(grad_up, 2, 8, side), split_blocks(grad_down, 8, 2, side)],
        axis=0,
    )
    owned = lax.psum_scatter(
        to_owners(blocks, capacity, shard_count), "fsdp", scatter_dimension=1, tiled=True
    )
    owned = lax.psum(owned, "dp")[:, 0]
    share = lax.psum_scatter(vector_grad, "fsdp", scatter_dimension=0, tiled=True)
    return owned, lax.psum(share, "dp")


def to_owners(blocks, capacity, shard_count):
    spare = capacity * shard_count - blocks.shape[0]
    blocks = jnp.pad(blocks, ((0, spare),) + ((0, 0),) * (blocks.ndim - 1))
    return blocks.reshape((capacity, shard_count) + blocks.shape[1:])


def plain_layer(tokens, cotangent, lengths, attn, up, down, vector_rows):
    sequences, slots, model_width = tokens.shape
    rows_total = sequences * slots
    unit_ratio = FF // model_width

    def shaped(array):
        return array.reshape(sequences, slots, array.shape[-1])

    weight_qkv, weight_out = attn[:, : 3 * model_width], attn[:, 3 * model_width :]
    inputs = tokens.reshape(rows_total, model_width)
    joined = jnp.dot(inputs, weight_qkv, preferred_element_type=F32)
    query_rows = (joined[:, :model_width] + vector_rows[0]).astype(BF16)
    key_rows = joined[:, model_width : 2 * model_width].astype(BF16)
    value_rows = (joined[:, 2 * model_width :] + vector_rows[1]).astype(BF16)
    context, logsum = lax.map(
        attend, (shaped(query_rows), shaped(key_rows), shaped(value_rows), lengths)
    )
    context = context.reshape(rows_total, model_width)
    attended = jnp.dot(context, weight_out, preferred_element_type=F32) + vector_rows[2]
    normed, pull_one = jax.vjp(
        layer_norm, inputs.astype(F32) + attended, vector_rows[3], vector_rows[4]
    )
    normed_low = normed.astype(BF16)
    hidden = jnp.dot(normed_low, up, preferred_element_type=F32) + vector_rows[
        5 : 5 + unit_ratio
    ].reshape(FF)
    active, pull_gelu = jax.vjp(exact_gelu, hidden)
    active_low = active.astype(BF16)
    result = jnp.dot(active_low, down, preferred_element_type=F32) + vector_rows[5 + unit_ratio]
    output, pull_two = jax.vjp(
        layer_norm, normed + result, vector_rows[6 + unit_ratio], vector_rows[7 + unit_ratio]
    )
    block_out = output.reshape(sequences, slots, model_width).astype(BF16)
    visible = (lax.iota(jnp.int32, slots)[None, :] < lengths[:, None]).astype(F32)
    grad_output = (cotangent.astype(F32) * visible[:, :, None]).reshape(rows_total, model_width)
    grad_second, grad_gain_two, grad_shift_two = pull_two(grad_output)
    second_low = grad_second.astype(BF16)
    grad_down = jnp.einsum("tf,td->fd", active_low, second_low, preferred_element_type=F32)
    grad_active = jnp.einsum("td,fd->tf", second_low, down, preferred_element_type=F32)
    (grad_hidden,) = pull_gelu(grad_active)
    hidden_low = grad_hidden.astype(BF16)
    grad_up = jnp.einsum("td,tf->df", normed_low, hidden_low, preferred_element_type=F32)
    grad_normed = grad_second + jnp.einsum("tf,df->td", hidden_low, up, preferred_element_type=F32)
    grad_mixed, grad_gain_one, grad_shift_one = pull_one(grad_normed)
    mixed_low = grad_mixed.astype(BF16)
    grad_out_weight = jnp.einsum("td,te->de", context, mixed_low, preferred_element_type=F32)
    grad_context = jnp.einsum(
        "te,de->td", mixed_low, weight_out, preferred_element_type=F32
    ).astype(BF16)
    grad_query, grad_keys, grad_values = lax.map(
        attend_back,
        (
            shaped(query_rows),
            shaped(key_rows),
            shaped(value_rows),
            logsum,
            shaped(grad_context),
            lengths,
        ),
    )
    grad_joined = jnp.concatenate(
        [
            grad_query.reshape(rows_total, model_width),
            grad_keys.reshape(rows_total, model_width),
            grad_values.reshape(rows_total, model_width),
        ],
        axis=1,
    )
    grad_qkv = jnp.einsum("td,te->de", inputs, grad_joined, preferred_element_type=F32)
    input_grad = grad_mixed + jnp.einsum(
        "te,de->td", grad_joined, weight_qkv, preferred_element_type=F32
    )
    vector_grad = jnp.concatenate(
        [
            jnp.sum(grad_joined[:, :model_width], axis=0, dtype=F32)[None],
            jnp.sum(grad_joined[:, 2 * model_width :], axis=0, dtype=F32)[None],
            jnp.sum(grad_mixed, axis=0)[None],
            grad_gain_one[None],
            grad_shift_one[None],
            jnp.sum(grad_hidden, axis=0).reshape(unit_ratio, model_width),
            jnp.sum(grad_second, axis=0)[None],
            grad_gain_two[None],
            grad_shift_two[None],
        ],
        axis=0,
    ).reshape(-1)
    weight_grads = [part.astype(BF16) for part in (grad_qkv, grad_out_weight, grad_up, grad_down)]
    return block_out, input_grad.reshape(tokens.shape), vector_grad, weight_grads


def shards(
    tokens,
    cotangent,
    lengths,
    matrices,
    first_moment,
    second_moment,
    left_stat,
    right_stat,
    left_basis,
    right_basis,
    vectors,
    vector_first,
    vector_second,
):
    shard_count = lax.axis_size("fsdp")
    replicas = lax.axis_size("dp")
    sequences, slots, model_width = tokens.shape
    block_total, share_rows, block_side = matrices.shape
    capacity = -(-block_total // shard_count)
    ringed = replicas == 2 and sequences == 1 and vectors.shape[0] == 576 and capacity * shard_count == block_total == 48 and share_rows % 8 == 0 and capacity == 3

    right_side = lax.axis_index("dp") % 2 == 1
    if ringed:
        vector_tile = jnp.pad(vectors.reshape(9, 64), ((0, 7), (0, 64)))
        attn, up, down, tiles, states = gather_weights(
            matrices,
            vector_tile,
            (left_stat, right_stat, left_basis, right_basis, first_moment, second_moment),
            shard_count // 2,
        )
        states = lax.all_to_all(states, "fsdp", split_axis=0, concat_axis=0, tiled=True)
        weight_attn = attn.reshape(model_width, 4 * model_width)
        block_out, logs, vec_part, vec_up_part, qkv, grad_c, turned_x, grad_r, *weight_grads = layer(
            lengths,
            tokens[0],
            cotangent[0],
            tiles,
            weight_attn,
            up.reshape(model_width, FF),
            down.reshape(FF, model_width),
        )
        slabs = [part.reshape(-1, block_side, part.shape[1]) for part in weight_grads]
        input_grad, vector_sum, *notes = conclude(
            lengths, logs, vec_part, vec_up_part, states, qkv, grad_c, turned_x, grad_r, weight_attn, *slabs,
            share_rows, shard_count // 2
        )
        block_out, input_grad = block_out[None], input_grad[None]
        vector_sum = vector_sum[:9, :64].reshape(-1)
        local = settle(*notes, matrices, first_moment, second_moment, left_stat, right_stat)
    else:
        chosen = [
            jnp.where(right_side, right_stat, left_stat),
            jnp.where(right_side, right_basis, left_basis),
            jnp.where(right_side, left_basis, right_basis),
            first_moment,
            second_moment,
        ]
        states = jnp.stack([to_owners(part.astype(BF16), capacity, shard_count) for part in chosen])
        attn, up, down, vector_rows = plain_gather(matrices, vectors)
        states = lax.all_to_all(states, "fsdp", split_axis=2, concat_axis=3, tiled=True)[:, :, 0]
        block_out, input_grad, vector_grad, weight_grads = plain_layer(
            tokens, cotangent, lengths, attn, up, down, vector_rows
        )
        owned, vector_sum = plain_reduce(*weight_grads, vector_grad, capacity)
        filler = (lax.iota(jnp.int32, capacity) * shard_count + lax.axis_index("fsdp")) >= block_total
        stat = jnp.where(
            filler[:, None, None], jnp.eye(block_side, dtype=jnp.bfloat16), states[0]
        )
        basis = jnp.where(
            filler[:, None, None], jnp.eye(block_side, dtype=jnp.bfloat16), states[1]
        )
        outer, new_basis, turned, update = soap_blocks(
            owned, stat, basis, states[2], states[3], states[4]
        )
        returned = lax.all_to_all(
            jnp.stack([outer, new_basis, turned, update])[:, :, None],
            "fsdp",
            split_axis=3,
            concat_axis=2,
            tiled=True,
        ).reshape(4, capacity * shard_count, -1, block_side)[:, :block_total]
        mirror = lax.ppermute(
            returned[:2], "dp", [(place, place ^ 1) for place in range(lax.axis_size("dp"))]
        )
        returned = returned.astype(jnp.float32)
        mirror = mirror.astype(jnp.float32)
        left_pair = jnp.where(right_side, mirror, returned[:2])
        right_pair = jnp.where(right_side, returned[:2], mirror)
        turned = returned[2]
        local = [
            returned[3],
            FIRST_DECAY * first_moment + (1.0 - FIRST_DECAY) * turned,
            SECOND_DECAY * second_moment + (1.0 - SECOND_DECAY) * turned * turned,
            STAT_DECAY * left_stat + (1.0 - STAT_DECAY) * left_pair[0],
            STAT_DECAY * right_stat + (1.0 - STAT_DECAY) * right_pair[0],
            left_pair[1],
            right_pair[1],
        ]
        local = [matrices - MATRIX_RATE * (local[0] + WEIGHT_DECAY * matrices)] + local
        local[1] = local[0].astype(BF16)
    vfirst_new = FIRST_DECAY * vector_first + (1.0 - FIRST_DECAY) * vector_sum
    vsecond_new = SECOND_DECAY * vector_second + (1.0 - SECOND_DECAY) * vector_sum * vector_sum
    vector_new = vectors - VECTOR_RATE * (vfirst_new / (1.0 - FIRST_DECAY**ADAM_STEP)) / (
        jnp.sqrt(vsecond_new / (1.0 - SECOND_DECAY**ADAM_STEP)) + ADAM_EPSILON
    )
    return (
        block_out,
        input_grad,
        *local,
        vfirst_new,
        vsecond_new,
        vector_new,
    )


def solution(mesh):
    return jax.shard_map(
        shards,
        mesh=mesh,
        in_specs=(
            P(("fsdp", "dp"), None, None),
            P(("fsdp", "dp"), None, None),
            P(("fsdp", "dp")),
            P(None, "fsdp", None),
            P(None, "fsdp", None),
            P(None, "fsdp", None),
            P(None, "fsdp", None),
            P(None, "fsdp", None),
            P(None, "fsdp", None),
            P(None, "fsdp", None),
            P("fsdp"),
            P("fsdp"),
            P("fsdp"),
        ),
        out_specs=(
            P(("fsdp", "dp"), None, None),
            P(("fsdp", "dp"), None, None),
            P(None, "fsdp", None),
            P(None, "fsdp", None),
            P(None, "fsdp", None),
            P(None, "fsdp", None),
            P(None, "fsdp", None),
            P(None, "fsdp", None),
            P(None, "fsdp", None),
            P(None, "fsdp", None),
            P("fsdp"),
            P("fsdp"),
            P("fsdp"),
        ),
        check_vma=False,
    )
```

```python
import functools

import jax
import jax.numpy as jnp
from jax import lax
from jax.experimental import pallas as pl
from jax.experimental.pallas import tpu as pltpu
from jax.sharding import PartitionSpec as P

F32 = jnp.float32
BF16 = jnp.bfloat16
MESH = pl.DeviceIdType.MESH
TRADE = 1
WINDOW = 4
OWNERS = 4

HEADS = 12
HEAD_DIM = 64
FF = 3072
ADAM_STEP = 10


FIRST_DECAY = 0.9
SECOND_DECAY = 0.999
STAT_DECAY = 0.95
ADAM_EPSILON = 1e-08
NORM_EPSILON = 1e-05
MATRIX_RATE = 0.03
VECTOR_RATE = 0.2
WEIGHT_DECAY = 0.01


def assemble(blocks, row_count, column_count):
    block_side = blocks.shape[-1]
    shaped = blocks.reshape(row_count, column_count, block_side, block_side)
    return shaped.transpose(0, 2, 1, 3).reshape(row_count * block_side, column_count * block_side)


def split_blocks(matrix, row_count, column_count, block_side):
    shaped = matrix.reshape(row_count, block_side, column_count, block_side)
    return shaped.transpose(0, 2, 1, 3).reshape(row_count * column_count, block_side, block_side)


def layer_norm(values, gain_row, shift_row):
    center = jnp.mean(values, axis=-1, keepdims=True)
    centered = values - center
    spread = jnp.mean(centered * centered, axis=-1, keepdims=True)
    return centered * lax.rsqrt(spread + NORM_EPSILON) * gain_row + shift_row


def exact_gelu(hidden):
    return jax.nn.gelu(hidden, approximate=False)


def masked_scores(heads_query, heads_key, length):
    slots = heads_query.shape[0]
    scores = jnp.einsum(
        "qhd,khd->hqk", heads_query, heads_key, preferred_element_type=jnp.float32
    ) * HEAD_DIM ** (-0.5)
    visible = lax.iota(jnp.int32, slots) < length
    return jnp.where(visible[None, None, :], scores, -1e30)


def attend(pieces):
    query_rows, key_rows, value_rows, length = pieces
    slots = query_rows.shape[0]
    heads_query = query_rows.reshape(slots, HEADS, HEAD_DIM)
    heads_key = key_rows.reshape(slots, HEADS, HEAD_DIM)
    heads_value = value_rows.reshape(slots, HEADS, HEAD_DIM)
    scores = masked_scores(heads_query, heads_key, length)
    row_max = jnp.max(scores, axis=-1, keepdims=True)
    shifted = jnp.exp(scores - row_max)
    row_total = jnp.sum(shifted, axis=-1, keepdims=True)
    attention_weights = (shifted / row_total).astype(jnp.bfloat16)
    context = jnp.einsum(
        "hqk,khd->qhd", attention_weights, heads_value, preferred_element_type=jnp.float32
    )
    return (
        context.reshape(slots, -1).astype(jnp.bfloat16),
        row_max[..., 0] + jnp.log(row_total[..., 0]),
    )


def attend_back(pieces):
    query_rows, key_rows, value_rows, logsum, grad_context, length = pieces
    slots = query_rows.shape[0]
    heads_query = query_rows.reshape(slots, HEADS, HEAD_DIM)
    heads_key = key_rows.reshape(slots, HEADS, HEAD_DIM)
    heads_value = value_rows.reshape(slots, HEADS, HEAD_DIM)
    heads_grad = grad_context.reshape(slots, HEADS, HEAD_DIM)
    scores = masked_scores(heads_query, heads_key, length)
    attention_weights = jnp.exp(scores - logsum[..., None])
    weights_low = attention_weights.astype(jnp.bfloat16)
    grad_values = jnp.einsum(
        "hqk,qhd->khd", weights_low, heads_grad, preferred_element_type=jnp.float32
    )
    grad_weights = jnp.einsum(
        "qhd,khd->hqk", heads_grad, heads_value, preferred_element_type=jnp.float32
    )
    grad_scores = attention_weights * (
        grad_weights - jnp.sum(grad_weights * attention_weights, axis=-1, keepdims=True)
    )
    scores_low = grad_scores.astype(jnp.bfloat16)
    grad_query = jnp.einsum(
        "hqk,khd->qhd", scores_low, heads_key, preferred_element_type=jnp.float32
    ) * HEAD_DIM ** (-0.5)
    grad_keys = jnp.einsum(
        "hqk,qhd->khd", scores_low, heads_query, preferred_element_type=jnp.float32
    ) * HEAD_DIM ** (-0.5)
    return (
        grad_query.reshape(slots, -1).astype(jnp.bfloat16),
        grad_keys.reshape(slots, -1).astype(jnp.bfloat16),
        grad_values.reshape(slots, -1).astype(jnp.bfloat16),
    )


def dg(a,b,ca,cb):
    return lax.dot_general(a,b,(((ca,),(cb,)),((),())),preferred_element_type=F32)

def halves(a):
    hi=a.astype(BF16)
    return hi,(a-hi.astype(F32)).astype(BF16)

def mm3(a,b,ca,cb):
    ah,al=halves(a); bh,bl=halves(b)
    return dg(ah,bh,ca,cb)+(dg(ah,bl,ca,cb)+dg(al,bh,ca,cb))

def thirds(u):
    h=u.astype(BF16).astype(F32); r=u-h
    m=r.astype(BF16).astype(F32)
    return h,m,r-m

def factor_panels(aug, slots, side=128, between=None):
    sub=lax.broadcasted_iota(jnp.int32,(8,side),0)
    def spread(v): return jnp.broadcast_to(v,(8,side))
    for p in range(side//8):
        k=8*p
        if between is not None:
            between(p)
        panels=[]
        for s in range(slots):
            pw=aug[s,k:k+8,:side]; pv=aug[s,k:k+8,side:]
            cols=[spread(pw[:,k+i:k+i+1]) for i in range(8)]
            S=[[spread(cols[i][j:j+1,:]) if j>=i else None for i in range(8)] for j in range(8)]
            rw=[spread(pw[i:i+1,:]) for i in range(8)]
            rv=[spread(pv[i:i+1,:]) for i in range(8)]
            panels.append((S,rw,rv))
        for i in range(8):
            for S,rw,rv in panels:
                r=lax.rsqrt(S[i][i])
                for j in range(i+1,8): S[j][i]=S[j][i]*r
                for m in range(i+1,8):
                    for j in range(m,8):
                        S[j][m]=S[j][m]-S[j][i]*S[m][i]
                rw[i]=rw[i]*r; rv[i]=rv[i]*r
                for j in range(i+1,8):
                    rw[j]=rw[j]-S[j][i]*rw[i]
                    rv[j]=rv[j]-S[j][i]*rv[i]
        for s,(S,rw,rv) in enumerate(panels):
            uw,uv=rw[0],rv[0]
            for i in range(1,8):
                uw=jnp.where(sub==i,rw[i],uw); uv=jnp.where(sub==i,rv[i],uv)
            aug[s,k:k+8,side:]=uv
            if k+8<side:
                h,m,l=thirds(uw); vh,vm,vl=thirds(uv)
                a=jnp.concatenate([h,h,m,m,h,l],0).astype(BF16)
                b=jnp.concatenate([jnp.concatenate([h,m,h,m,l,h],0),jnp.concatenate([vh,vm,vh,vm,vl,vh],0)],1).astype(BF16)
                t=dg(a,b,0,0)
                aug[s,k+8:,:]=aug[s,k+8:,:]-t[k+8:,:]

def orthonormal_cols(mat, aug, slots, side=128):
    n=mat.shape[-1]
    r=lax.broadcasted_iota(jnp.int32,(side,side),0); c=lax.broadcasted_iota(jnp.int32,(side,side),1)
    eye=(r==c).astype(F32)
    steps=n//side
    for o in range(steps):
        lo=o*side
        for s in range(slots):
            mo=mat[s,:,lo:lo+side]
            aug[s,:,:side]=mm3(mo,mo,0,0)
            aug[s,:,side:]=eye
        factor_panels(aug,slots,side)
        for s in range(slots):
            q=mm3(mat[s,:,lo:lo+side],aug[s,:,side:],1,1)
            mat[s,:,lo:lo+side]=q
            if o+1<steps:
                rest=mat[s,:,lo+side:]
                mat[s,:,lo+side:]=rest-mm3(q,mm3(q,rest,0,0),1,0)


def soap_kernel(grad, stat, own, other, first, second, outer_out, basis_out, turned_out, update_out, mat, aug):
    slots = grad.shape[0]
    right_side = lax.rem(lax.axis_index("dp"), 2) == 1

    def run(is_right):
        near, far = (0, 1) if is_right else (1, 0)

        def one(s, carry):
            g = grad[s].astype(BF16)
            outer = dg(g, g, near, near)
            outer_out[s] = outer.astype(BF16)
            mixed = STAT_DECAY * stat[s].astype(F32) + (1.0 - STAT_DECAY) * outer
            high, rest = halves(mixed)
            mat[s] = dg(high, own[s], 1, 0) + dg(rest, own[s], 1, 0)
            left, right = (other[s], own[s]) if is_right else (own[s], other[s])
            rotated = dg(dg(left, g, 0, 0).astype(BF16), right, 1, 0)
            turned_out[s] = rotated.astype(BF16)
            first_new = FIRST_DECAY * first[s].astype(F32) + (1.0 - FIRST_DECAY) * rotated
            second_new = SECOND_DECAY * second[s].astype(F32) + (1.0 - SECOND_DECAY) * rotated * rotated
            direction = (
                first_new
                / (1.0 - FIRST_DECAY**ADAM_STEP)
                / (jnp.sqrt(second_new / (1.0 - SECOND_DECAY**ADAM_STEP)) + ADAM_EPSILON)
            )
            back = dg(left, direction.astype(BF16), 1, 0).astype(BF16)
            update_out[s] = dg(back, right, 1, 1).astype(BF16)
            return carry

        lax.fori_loop(0, slots, one, 0)

    @pl.when(right_side)
    def _():
        run(True)

    @pl.when(jnp.logical_not(right_side))
    def _():
        run(False)

    orthonormal_cols(mat, aug, slots)
    basis_out[...] = mat[...].astype(BF16)


def soap_blocks(grad, stat, own, other, first, second):
    slots, side, _ = grad.shape
    shape = jax.ShapeDtypeStruct(grad.shape, BF16)
    whole = pl.BlockSpec(memory_space=pltpu.VMEM)
    return pl.pallas_call(
        soap_kernel,
        out_shape=[shape] * 4,
        in_specs=[whole] * 6,
        out_specs=[whole] * 4,
        scratch_shapes=[
            pltpu.VMEM((slots, side, side), F32),
            pltpu.VMEM((slots, 128, 256), F32),
        ],
        compiler_params=pltpu.CompilerParams(vmem_limit_bytes=60 * 2**20),
        name="soap_blocks",
    )(grad, stat, own, other, first, second)


def ring_place(chip, chips):
    along, across = chip // 2, lax.rem(chip, 2)
    return along * (1 - across) + (chips - 1 - along) * across


def ring_chip(place, chips):
    place = lax.rem(place + 8 * chips, chips)
    across = place // (chips // 2)
    along = place * (1 - across) + (chips - 1 - place) * across
    return 2 * along + across


def whereabouts(chips):
    device, replica = lax.axis_index("fsdp"), lax.axis_index("dp")
    chip, core = device // 2, lax.rem(device, 2)
    place = ring_place(chip, chips)
    turn = 1 - 2 * core
    after = (2 * ring_chip(place + turn, chips) + core, replica)
    before = (2 * ring_chip(place - turn, chips) + core, replica)
    sibling = (2 * chip + 1 - core, replica)
    return device, replica, chip, core, place, turn, after, before, sibling


def greet(neighbours):
    barrier = pltpu.get_barrier_semaphore()
    for neighbour in neighbours:
        pl.semaphore_signal(barrier, inc=1, device_id=neighbour, device_id_type=MESH)
    pl.semaphore_wait(barrier, len(neighbours))


def gather_kernel(chips, share, mat_ref, vec_ref, left_stat, right_stat, left_basis, right_basis, first, second,
                  attn, up, down, vecs, states_out, wide, states, raw_a, raw_u, raw_d, low_a, low_u, low_d,
                  low_v, trade_send, trade_recv, own_sem, ring_send, ring_recv, sib_send, sib_recv, cross_send, cross_recv,
                  vec_send, vec_recv, vec_sib_send, vec_sib_recv, state_sem, out_sem):
    device, replica, chip, core, place, turn, after, before, sibling = whereabouts(chips)
    mirror = (device, 1 - replica)
    side = mat_ref.shape[-1]
    both = 2 * share
    rows = pl.ds(pl.multiple_of(share * core, 8), share)
    barrier = pltpu.get_barrier_semaphore()
    for neighbour in (after, before, sibling, mirror):
        pl.semaphore_signal(barrier, inc=1, device_id=neighbour, device_id_type=MESH)

    def state(source, slot, item):
        return pltpu.make_async_copy(source.at[slot], wide.at[item], state_sem.at[item])

    def fetch_states(stat, basis, spare, mine):
        for slot in range(3):
            state(stat, slot, slot).start()
            state(basis, slot, 3 + slot).start()
        state(first, mine, 6).start()
        state(second, mine, 7).start()
        state(spare, 0, 8).start()

    @pl.when(replica == 0)
    def _():
        fetch_states(left_stat, left_basis, second, 1)

    @pl.when(replica == 1)
    def _():
        fetch_states(right_stat, right_basis, first, 2)

    groups = ((raw_a, low_a, attn), (raw_u, low_u, up), (raw_d, low_d, down))
    for g, (raw, low, out) in enumerate(groups):
        for b in range(16):
            if g == 0:
                raw[(b % 4) // 2, rows, (b // 4) * 2 * side + (b % 2) * side : (b // 4) * 2 * side + (b % 2 + 1) * side] = mat_ref[b]
            elif g == 1:
                raw[b // 8, rows, (b % 8) * side : (b % 8 + 1) * side] = mat_ref[16 + b]
            else:
                raw[b // 2, rows, (b % 2) * side : (b % 2 + 1) * side] = mat_ref[32 + b]
    pl.semaphore_wait(barrier, 4)
    trades = []
    for g, (raw, low, out) in enumerate(groups):
        part = raw.at[:, rows, :]
        trade = pltpu.make_async_remote_copy(
            src_ref=part, dst_ref=part, send_sem=trade_send.at[g], recv_sem=trade_recv.at[g],
            device_id=sibling, device_id_type=MESH)
        trade.start()
        trades.append(trade)
    low_v[...] = vec_ref[...].astype(BF16).astype(F32)

    def cut(ref, g, row, kind):
        first = (4 * replica + core, 2 + core, 4 * (1 - replica) + core)[kind]
        width = ref.shape[-1] // 6
        return ref.at[:, row, pl.ds(pl.multiple_of(first * width, 128), width)]

    def slab(g, origin, kind):
        return cut(groups[g][2], g, pl.ds(pl.multiple_of(origin * both, 16), both), kind)

    def forward(g, t, kind, origin, source):
        return pltpu.make_async_remote_copy(
            src_ref=source, dst_ref=slab(g, origin, kind), send_sem=ring_send.at[t, g, kind],
            recv_sem=ring_recv.at[t, g, kind], device_id=after, device_id_type=MESH)

    def pass_on(g, t, kind, origin):
        part = slab(g, origin, kind)
        return pltpu.make_async_remote_copy(
            src_ref=part, dst_ref=part, send_sem=sib_send.at[t, g, kind], recv_sem=sib_recv.at[t, g, kind],
            device_id=sibling, device_id_type=MESH)

    def across(g, t, origin, kind):
        part = slab(g, origin, kind)
        return pltpu.make_async_remote_copy(
            src_ref=part, dst_ref=part, send_sem=cross_send.at[t, g], recv_sem=cross_recv.at[t, g],
            device_id=mirror, device_id_type=MESH)

    def vec_of(origin):
        return vecs.at[2 * origin + core]

    def vec_forward(t, origin, source):
        return pltpu.make_async_remote_copy(
            src_ref=source, dst_ref=vec_of(origin), send_sem=vec_send.at[t], recv_sem=vec_recv.at[t],
            device_id=after, device_id_type=MESH)

    def vec_pass_on(t, origin, source):
        return pltpu.make_async_remote_copy(
            src_ref=source, dst_ref=vec_of(origin), send_sem=vec_sib_send.at[t], recv_sem=vec_sib_recv.at[t],
            device_id=sibling, device_id_type=MESH)

    vec_forward(0, chip, low_v).start()
    vec_pass_on(0, chip, low_v).start()
    owns = [pltpu.make_async_copy(low_v, vec_of(chip), own_sem.at[3])]
    owns[0].start()
    for g, (raw, low, out) in enumerate(groups):
        trades[g].wait()
        low[...] = raw[...].astype(BF16)
        for kind in range(2):
            forward(g, 0, kind, chip, cut(low, g, slice(None), kind)).start()
        own = pltpu.make_async_copy(low, out.at[:, pl.ds(pl.multiple_of(chip * both, 16), both), :], own_sem.at[g])
        own.start()
        owns.append(own)

    def take_crossed(t):
        origin = ring_chip(place - turn * t, chips)
        for g in range(3):
            across(g, t, origin, 2).wait_recv()
            pass_on(g, t, 2, origin).start()

    def step(t, carry):
        origin = ring_chip(place - turn * t, chips)
        vec_forward(t - 1, origin, vec_of(origin)).wait_recv()

        @pl.when(t < chips - 1)
        def _():
            vec_forward(t, origin, vec_of(origin)).start()

        vec_pass_on(t, origin, vec_of(origin)).start()
        for g in range(3):
            for kind in range(2):
                arrived = slab(g, origin, kind)
                forward(g, t - 1, kind, origin, arrived).wait_recv()

                @pl.when(t < chips - 1)
                def _():
                    forward(g, t, kind, origin, arrived).start()

                if kind == 0:
                    across(g, t, origin, 0).start()
                pass_on(g, t, kind, origin).start()

        @pl.when(t > 1)
        def _():
            take_crossed(t - 1)

        @pl.when(t < 4)
        def _():
            for item in (3 * t - 3, 3 * t - 2, 3 * t - 1):
                state(first, 0, item).wait()
                for holder in range(2 * chips):
                    states[holder, item] = wide[item, holder].astype(BF16)

        @pl.when(t == 4)
        def _():
            pltpu.make_async_copy(states, states_out, out_sem).start()
        return carry

    lax.fori_loop(1, chips, step, 0)
    take_crossed(chips - 1)
    pltpu.make_async_copy(states, states_out, out_sem).wait()
    for own in owns:
        own.wait()

    def finish(t, carry):
        @pl.when(t < chips - 1)
        def _():
            vec_forward(t, chip, vec_of(chip)).wait_send()

        vec_pass_on(t, chip, vec_of(chip)).wait()
        for g in range(3):
            @pl.when(t < chips - 1)
            def _():
                for kind in range(2):
                    forward(g, t, kind, chip, slab(g, chip, kind)).wait_send()

            @pl.when(t > 0)
            def _():
                across(g, t, chip, 0).wait_send()
                for kind in range(3):
                    pass_on(g, t, kind, chip).wait()
        return carry

    lax.fori_loop(0, chips, finish, 0)


def gather_weights(matrices, vector_tile, states, chips):
    total, share, side = matrices.shape
    both = 2 * share
    anywhere = pl.BlockSpec(memory_space=pl.ANY)
    whole = pl.BlockSpec(memory_space=pltpu.VMEM)
    dma = pltpu.SemaphoreType.DMA
    return pl.pallas_call(
        functools.partial(gather_kernel, chips, share),
        out_shape=[
            jax.ShapeDtypeStruct((2, side, 8 * side), BF16),
            jax.ShapeDtypeStruct((2, side, 8 * side), BF16),
            jax.ShapeDtypeStruct((8, side, 2 * side), BF16),
            jax.ShapeDtypeStruct((2 * chips, 16, 128), F32),
            jax.ShapeDtypeStruct((2 * chips, 9, share, side), BF16),
        ],
        in_specs=[whole, whole] + [anywhere] * 6,
        out_specs=[anywhere] * 5,
        scratch_shapes=[
            pltpu.VMEM((9, 2 * chips, share, side), F32),
            pltpu.VMEM((2 * chips, 9, share, side), BF16),
            pltpu.VMEM((2, both, 8 * side), F32),
            pltpu.VMEM((2, both, 8 * side), F32),
            pltpu.VMEM((8, both, 2 * side), F32),
            pltpu.VMEM((2, both, 8 * side), BF16),
            pltpu.VMEM((2, both, 8 * side), BF16),
            pltpu.VMEM((8, both, 2 * side), BF16),
            pltpu.VMEM((16, 128), F32),
            dma((3,)), dma((3,)), dma((4,)),
            dma((chips - 1, 3, 2)), dma((chips - 1, 3, 2)), dma((chips, 3, 3)), dma((chips, 3, 3)),
            dma((chips, 3)), dma((chips, 3)),
            dma((chips - 1,)), dma((chips - 1,)), dma((chips,)), dma((chips,)), dma((9,)), dma,
        ],
        compiler_params=pltpu.CompilerParams(collective_id=1, has_side_effects=True, vmem_limit_bytes=60 * 2**20),
        name="gather_weights",
    )(matrices, vector_tile, *[part.reshape(3, 2 * chips, share, side) for part in states])


def opposite(device, step, count):
    result, bit = 0, 1
    while bit < count:
        one, two = lax.rem(device // bit, 2), lax.rem(step // bit, 2)
        result = result + bit * (one + two - 2 * one * two)
        bit *= 2
    return result


def settle_kernel(early, early_last, late_two, late_one, mat, first, second, left, right, mat_new, mat_low, first_new, second_new, left_new, right_new,
                  left_basis, right_basis):
    share = mat.shape[2]
    for f in range(mat.shape[1]):
        for s in range(3):
            def item(plane, index):
                source, spot = (early, index) if index < 4 else (early_last, index - 4)
                return source[plane, f, spot * share : (spot + 1) * share, :].astype(F32)

            turned = item(*((0, 5), (0, 2), (1, 2))[s])
            update = item(*((1, 5), (0, 3), (1, 3))[s])
            outer = (4, 0, 1)[s]
            fresh = mat[s, f] - MATRIX_RATE * (update + WEIGHT_DECAY * mat[s, f])
            mat_new[s, f] = fresh
            mat_low[s, f] = fresh.astype(BF16)
            first_new[s, f] = FIRST_DECAY * first[s, f] + (1.0 - FIRST_DECAY) * turned
            second_new[s, f] = SECOND_DECAY * second[s, f] + (1.0 - SECOND_DECAY) * turned * turned
            left_new[s, f] = STAT_DECAY * left[s, f] + (1.0 - STAT_DECAY) * item(0, outer)
            right_new[s, f] = STAT_DECAY * right[s, f] + (1.0 - STAT_DECAY) * item(1, outer)
            for panel in range(3):
                lanes = slice(128 * panel, 128 * (panel + 1))
                source, spot = (late_two, 3 * panel + s) if panel < 2 else (late_one, s)
                left_basis[s, f, :, lanes] = source[0, f, spot * share : (spot + 1) * share, :].astype(F32)
                right_basis[s, f, :, lanes] = source[1, f, spot * share : (spot + 1) * share, :].astype(F32)


def settle(early, early_last, late_two, late_one, matrices, first, second, left, right):
    _, count, tall, side = early.shape
    share = matrices.shape[1]
    state = pl.BlockSpec((3, OWNERS, share, side), lambda f: (0, f, 0, 0))
    shape = jax.ShapeDtypeStruct((3, count, share, side), F32)
    low = jax.ShapeDtypeStruct((3, count, share, side), BF16)
    results = pl.pallas_call(
        settle_kernel,
        grid=(count // OWNERS,),
        out_shape=[shape, low] + [shape] * 6,
        in_specs=[
            pl.BlockSpec((2, OWNERS, tall, side), lambda f: (0, f, 0, 0)),
            pl.BlockSpec((2, OWNERS, early_last.shape[2], side), lambda f: (0, f, 0, 0)),
            pl.BlockSpec((2, OWNERS, late_two.shape[2], 128), lambda f: (0, f, 0, 0)),
            pl.BlockSpec((2, OWNERS, late_one.shape[2], 128), lambda f: (0, f, 0, 0)),
        ]
        + [state] * 5,
        out_specs=[state] * 8,
        compiler_params=pltpu.CompilerParams(vmem_limit_bytes=60 * 2**20),
        name="settle",
    )(early, early_last, late_two, late_one, *[part.reshape(3, count, share, side) for part in (matrices, first, second, left, right)])
    return [part.reshape(matrices.shape) for part in results]


def normal_parts(value):
    size = jnp.abs(value) * 0.7071067811865476
    t = 1.0 / (1.0 + 0.3275911 * size)
    bell = jnp.exp(-size * size)
    series = t * (0.254829592 + t * (-0.284496736 + t * (1.421413741 + t * (-1.453152027 + t * 1.061405429))))
    tail = 0.5 * series * bell
    return jnp.where(value >= 0.0, 1.0 - tail, tail), bell * 0.3989422804014327


def span(index, size):
    return pl.ds(pl.multiple_of(index * size, size), size)


def looped(count, body):
    def step(index, carry):
        body(index)
        return carry

    lax.fori_loop(0, count, step, 0, unroll=True if count <= 3 else 3 if count % 3 == 0 else 1)


def vector_row(vecs, row, width):
    lane = lax.broadcasted_iota(jnp.int32, (1, 128), 1)
    pieces = []
    for pair in range(width // 128):
        chunk = row * (width // 64) + 2 * pair
        one = vecs[chunk // 9, chunk % 9 : chunk % 9 + 1, :]
        chunk += 1
        two = vecs[chunk // 9, chunk % 9 : chunk % 9 + 1, :]
        pieces.append(jnp.where(lane < 64, one, pltpu.roll(two, 64, 1)))
    return jnp.concatenate(pieces, axis=1)


def vector_tiles_of(rows, row_up, tiles):
    chunks = rows.shape[1] // 64
    for f in range(tiles.shape[0]):
        for i in range(9):
            row, place = divmod(9 * f + i, chunks)
            if 5 <= row < 9:
                spot = (row - 5) * chunks + place
                piece = row_up[spot // 4, :, 128 * (spot % 4 // 2) : 128 * (spot % 4 // 2) + 128]
            else:
                piece = rows[row : row + 1, 128 * (place // 2) : 128 * (place // 2) + 128]
            tiles[f, i : i + 1, :] = pltpu.roll(piece, 64, 1) if place % 2 else piece


def layer_kernel(length_ref, x_ref, cot_ref, tiles, attn_hbm, up_hbm, down_hbm,
                 out_ref, logs, grad_vec, grad_vec_up, qkv_out, grad_c_out, turned_x_out, grad_r_out, grad_out, grad_up, grad_down,
                 w_attn, w_up, w_down, qkv, context, hat_one, scale_one, normed, active, slope, hidden_low,
                 grad_r, low_e, grad_c, turned_x, turned_n, turned_c, stage_w, stage_t,
                 vec, vec_up, load_sem, wide_sem, tall_sem, save_sem):
    slots, width = x_ref.shape
    length = length_ref[0]
    chunks = w_up.shape[1] // 256
    thirds_of = width // 256
    loads = [pltpu.make_async_copy(source, target, load_sem.at[i])
             for i, (source, target) in enumerate(((attn_hbm, w_attn), (up_hbm, w_up), (down_hbm, w_down)))]
    for load in loads:
        load.start()

    def turn(source, target):
        def one(index):
            target[:, span(index, 128)] = source[span(index, 128), :].T

        looped(slots // 128, one)

    def wide_copy(target, slot, index):
        return pltpu.make_async_copy(stage_w.at[slot], target.at[:, span(index, 256)], wide_sem.at[slot])

    def tall_copy(slot, index):
        return pltpu.make_async_copy(stage_t.at[slot], grad_down.at[span(index, 256), :], tall_sem.at[slot])

    def put_wide(target, index, value, first):
        slot = lax.rem(index, 2)

        @pl.when(jnp.logical_not(first))
        def _():
            wide_copy(target, slot, index).wait()

        stage_w[slot] = value.astype(BF16)
        wide_copy(target, slot, index).start()

    grad_vec[...] = jnp.zeros_like(grad_vec)
    for row in range(12):
        vec[row : row + 1, :] = vector_row(tiles, row, width)
        if 5 <= row < 9:
            for third in range(thirds_of):
                vec_up[(row - 5) * thirds_of + third] = vec[row : row + 1, 256 * third : 256 * (third + 1)]
    turn(x_ref, turned_x)
    loads[0].wait()

    def project(index):
        lanes = span(index, 256)
        part = index // thirds_of
        row = jnp.where(part == 0, vec[0:1, span(lax.rem(index, thirds_of), 256)],
                        jnp.where(part == 2, vec[1:2, span(lax.rem(index, thirds_of), 256)], 0.0))
        qkv[:, lanes] = (jnp.dot(x_ref[...], w_attn[:, lanes], preferred_element_type=F32) + row).astype(BF16)

    looped(3 * thirds_of, project)
    saves = [pltpu.make_async_copy(source, target, save_sem.at[i]) for i, (source, target) in enumerate((
        (qkv, qkv_out), (turned_x, turned_x_out), (grad_c, grad_c_out), (grad_r, grad_r_out)))]
    saves[0].start()
    saves[1].start()

    lane = lax.broadcasted_iota(jnp.int32, (slots, 128), 1)
    tall_lane = lax.broadcasted_iota(jnp.int32, (128, 128), 0)
    seen = lax.broadcasted_iota(jnp.int32, (slots, 128), 0) < length

    def head_lanes(head, value):
        keep = (lane < HEAD_DIM) if head == 0 else (lane >= HEAD_DIM)
        return jnp.where(keep, value, jnp.zeros_like(value))

    def lanes_of(pair, part):
        return pl.ds(pl.multiple_of(part * width + pair * 128, 128), 128)

    def attend(pair):
        key, value = qkv[:, lanes_of(pair, 1)], qkv[:, lanes_of(pair, 2)]
        turned_value = value.T
        keys = [head_lanes(head, key * HEAD_DIM ** (-0.5)) for head in range(2)]
        for block in range(slots // 128):
            rows = slice(128 * block, 128 * (block + 1))
            query = qkv[rows, lanes_of(pair, 0)]
            both = []
            for head in range(2):
                scores = jnp.where(seen, dg(keys[head], query, 1, 1), -1e30)
                top = jnp.max(scores, axis=0, keepdims=True)
                shifted = jnp.exp(scores - top)
                total = jnp.sum(shifted, axis=0, keepdims=True)
                weights = (shifted * (1.0 / total)).astype(BF16)
                both.append(jnp.dot(turned_value, weights, preferred_element_type=F32))
                logs[2 * pair + head, :, rows] = top + jnp.log(total)
            merged = jnp.where(tall_lane < HEAD_DIM, both[0], both[1])
            context[rows, lanes_of(pair, 0)] = merged.T.astype(BF16)

    looped(width // 128, attend)
    turn(context, turned_c)

    def mix(index):
        lanes = span(index, 256)
        away = pl.ds(pl.multiple_of(3 * width + index * 256, 256), 256)
        value = jnp.dot(context[...], w_attn[:, away], preferred_element_type=F32) + vec[2:3, lanes]
        hat_one[:, lanes] = x_ref[:, lanes].astype(F32) + value

    looped(thirds_of, mix)

    def standard(value):
        centered = value - jnp.mean(value, axis=-1, keepdims=True)
        scale = lax.rsqrt(jnp.mean(centered * centered, axis=-1, keepdims=True) + NORM_EPSILON)
        return centered * scale, scale

    def norm_one(index):
        rows = span(index, 512)
        hat, scale = standard(hat_one[rows, :])
        hat_one[rows, :] = hat
        scale_one[rows, :] = jnp.broadcast_to(scale, (512, 128))
        normed[rows, :] = (hat * vec[3:4, :] + vec[4:5, :]).astype(BF16)

    looped(slots // 512, norm_one)
    turn(normed, turned_n)
    loads[1].wait()

    def rise(index):
        lanes = span(index, 256)
        hidden = jnp.dot(normed[...], w_up[:, lanes], preferred_element_type=F32) + vec_up[index]
        below, density = normal_parts(hidden)
        active[:, lanes] = (hidden * below).astype(BF16)
        slope[:, lanes] = below + hidden * density

    looped(chunks, rise)
    loads[2].wait()

    def fall(index):
        lanes = span(index, 256)
        value = jnp.dot(active[...], w_down[:, lanes], preferred_element_type=F32)
        grad_r[:, lanes] = hat_one[:, lanes] * vec[3:4, lanes] + vec[4:5, lanes] + value + vec[9:10, lanes]

    looped(thirds_of, fall)

    def unstandard(grad_hat, hat, scale):
        return scale * (grad_hat - jnp.mean(grad_hat, axis=-1, keepdims=True)
                        - hat * jnp.mean(grad_hat * hat, axis=-1, keepdims=True))

    def add_row(row, value):
        grad_vec[row : row + 1, :] += jnp.sum(value, axis=0, keepdims=True)

    def norm_two(index):
        rows = span(index, 512)
        hat, scale = standard(grad_r[rows, :])
        out_ref[rows, :] = (hat * vec[10:11, :] + vec[11:12, :]).astype(BF16)
        place = lax.broadcasted_iota(jnp.int32, (512, width), 0) + index * 512
        grad = jnp.where(place < length, cot_ref[rows, :].astype(F32), 0.0)
        add_row(10, grad * hat)
        add_row(11, grad)
        back = unstandard(grad * vec[10:11, :], hat, scale)
        add_row(9, back)
        grad_r[rows, :] = back
        low_e[rows, :] = back.astype(BF16)

    looped(slots // 512, norm_two)

    def sink(index):
        lanes = span(index, 256)
        grad = dg(low_e[...], w_down[lanes, :], 1, 1) * slope[:, lanes]
        grad_vec_up[index] = jnp.sum(grad, axis=0, keepdims=True)
        hidden_low[:, lanes] = grad.astype(BF16)

    def weigh(index):
        lanes = span(index, 256)
        put_wide(grad_up, index, jnp.dot(turned_n[...], hidden_low[:, lanes], preferred_element_type=F32), index < 2)
        slot = lax.rem(index, 2)

        @pl.when(index >= 2)
        def _():
            tall_copy(slot, index).wait()

        stage_t[slot] = dg(active[:, lanes], low_e[...], 0, 0).astype(BF16)
        tall_copy(slot, index).start()

    def weigh_and_sink(index):
        slot = lax.rem(index, 2)

        @pl.when(index >= 2)
        def _():
            wide_copy(grad_up, slot, index).wait()
            tall_copy(slot, index).wait()

        lanes = span(index, 256)
        sink(index + 1)
        stage_w[slot] = jnp.dot(turned_n[...], hidden_low[:, lanes], preferred_element_type=F32).astype(BF16)
        stage_t[slot] = dg(active[:, lanes], low_e[...], 0, 0).astype(BF16)
        wide_copy(grad_up, slot, index).start()
        tall_copy(slot, index).start()

    sink(0)
    looped(chunks - 1, weigh_and_sink)
    weigh(jnp.int32(chunks - 1))

    def rise_back(index):
        lanes = span(index, 256)
        grad_r[:, lanes] += dg(hidden_low[...], w_up[lanes, :], 1, 1)

    looped(thirds_of, rise_back)

    def norm_one_back(index):
        rows = span(index, 512)
        hat, grad = hat_one[rows, :], grad_r[rows, :]
        add_row(3, grad * hat)
        add_row(4, grad)
        back = unstandard(grad * vec[3:4, :], hat, scale_one[rows, 0:1])
        add_row(2, back)
        grad_r[rows, :] = back
        low_e[rows, :] = back.astype(BF16)


    def mix_back(index):
        lanes = span(index, 256)
        put_wide(grad_out, index, jnp.dot(turned_c[...], low_e[:, lanes], preferred_element_type=F32), False)
        away = pl.ds(3 * width, width)
        grad_c[:, lanes] = dg(low_e[...], w_attn[lanes, away], 1, 1).astype(BF16)

    looped(slots // 512, norm_one_back)
    saves[3].start()
    looped(thirds_of, mix_back)
    saves[2].start()
    for slot in range(2):
        wide_copy(grad_out, slot, 0).wait()
        tall_copy(slot, 0).wait()
    for save in saves:
        save.wait()


def layer(length, inputs, cotangent, tiles, attn, up, down):
    slots, width = inputs.shape
    tall = down.shape[0]
    anywhere = pl.BlockSpec(memory_space=pl.ANY)
    whole = pl.BlockSpec(memory_space=pltpu.VMEM)
    vmem = pltpu.VMEM
    dma = pltpu.SemaphoreType.DMA
    return pl.pallas_call(
        layer_kernel,
        out_shape=[
            jax.ShapeDtypeStruct((slots, width), BF16),
            jax.ShapeDtypeStruct((width // HEAD_DIM, 1, slots), F32),
            jax.ShapeDtypeStruct((16, width), F32),
            jax.ShapeDtypeStruct((tall // 256, 1, 256), F32),
            jax.ShapeDtypeStruct((slots, 3 * width), BF16),
            jax.ShapeDtypeStruct((slots, width), BF16),
            jax.ShapeDtypeStruct((width, slots), BF16),
            jax.ShapeDtypeStruct((slots, width), F32),
            jax.ShapeDtypeStruct((width, width), BF16),
            jax.ShapeDtypeStruct((width, tall), BF16),
            jax.ShapeDtypeStruct((tall, width), BF16),
        ],
        in_specs=[pl.BlockSpec(memory_space=pltpu.SMEM)] + [whole] * 3 + [anywhere] * 3,
        out_specs=[whole] * 4 + [anywhere] * 7,
        scratch_shapes=[
            vmem((width, 4 * width), BF16), vmem((width, tall), BF16), vmem((tall, width), BF16),
            vmem((slots, 3 * width), BF16), vmem((slots, width), BF16),
            vmem((slots, width), F32), vmem((slots, 128), F32), vmem((slots, width), BF16),
            vmem((slots, tall), BF16), vmem((slots, tall), F32), vmem((slots, tall), BF16),
            vmem((slots, width), F32), vmem((slots, width), BF16), vmem((slots, width), BF16),
            vmem((width, slots), BF16), vmem((width, slots), BF16), vmem((width, slots), BF16),
            vmem((2, width, 256), BF16), vmem((2, 256, width), BF16),
            vmem((16, width), F32), vmem((tall // 256, 1, 256), F32),
            dma((3,)), dma((2,)), dma((2,)), dma((4,)),
        ],
        compiler_params=pltpu.CompilerParams(vmem_limit_bytes=60 * 2**20),
        cost_estimate=pl.CostEstimate(flops=25_000_000_000, bytes_accessed=40_000_000, transcendentals=8_000_000),
        name="layer",
    )(length, inputs, cotangent, tiles, attn, up, down)


def conclude_kernel(chips, share, length_ref, logs, vec_part, vec_up_part, parts, qkv_hbm, grad_c_hbm, turned_x_hbm, grad_r_hbm,
                    attn_hbm, g_out, g_up, g_down,
                    grad_x, vec_sum, early, early_last, late_two, late_one,
                    qkv, grad_c, turned_x, grad_r, w_qkv, grad_heads, probs, dscores, g_qkv, grad_vec, tiles,
                    mine, theirs, ring, crossed, peer, vmine, vring, vpeer, owned,
                    states, items, mat, aug, out_early, out_last, out_two, out_one,
                    load_sem, mine_sem, sib_send, sib_recv, ring_send, ring_recv, cross_send, cross_recv, peer_send, peer_recv,
                    state_send, state_recv, note_send, note_recv, relay_send, relay_recv, keep_sem):
    device, replica, chip, core, place, turn, after, before, sibling = whereabouts(chips)
    count = 2 * chips
    mirror = (device, 1 - replica)
    side = mine.shape[-1]
    width = 2 * side
    slots = qkv.shape[0]
    quarter = side // 4
    last = chips - 1
    part = 128
    panels = side // part
    length = length_ref[0]

    def partner(step):
        return opposite(device, step, count), replica

    barrier = pltpu.get_barrier_semaphore()

    def hail(step, carry):
        pl.semaphore_signal(barrier, inc=1, device_id=partner(step), device_id_type=MESH)
        return carry

    lax.fori_loop(1, count, hail, 0)
    pl.semaphore_signal(barrier, inc=1, device_id=mirror, device_id_type=MESH)

    loads = [pltpu.make_async_copy(source, target, load_sem.at[i]) for i, (source, target) in enumerate((
        (qkv_hbm, qkv), (grad_c_hbm, grad_c), (turned_x_hbm, turned_x), (grad_r_hbm, grad_r),
        (attn_hbm.at[:, : 3 * width], w_qkv)))]


    def quarters(first, number):
        return pl.ds(pl.multiple_of(first * quarter, 16), number * quarter)

    carried = quarters(replica, 3)
    private = quarters(3 * replica, 1)
    foreign = quarters(3 * (1 - replica), 1)

    def column(index):
        return pl.ds(pl.multiple_of(index * side, 128), side)

    def fetch(owner, wanted, start):
        which = owner // 4
        i, j = lax.rem(owner, 4) // 2, lax.rem(owner, 2)
        if 0 in wanted:
            @pl.when(which < 3)
            def _():
                start(0, g_qkv.at[i, :, column(2 * which + j)])

            @pl.when(which == 3)
            def _():
                start(0, g_out.at[i, :, column(j)])

            start(3, tiles.at[owner])
        else:
            start(1, g_up.at[owner // 8, :, column(lax.rem(owner, 8))])
            start(2, g_down.at[owner // 2, :, column(lax.rem(owner, 2))])

    def local(t, slot, source):
        target = vmine.at[0, t] if slot == 3 else mine.at[t, slot]
        return pltpu.make_async_copy(source, target, mine_sem.at[t, slot])

    def to_sibling(t, slot, source):
        target = vmine.at[1, t] if slot == 3 else theirs.at[t, slot]
        return pltpu.make_async_remote_copy(
            src_ref=source, dst_ref=target, send_sem=sib_send.at[t, slot], recv_sem=sib_recv.at[t, slot],
            device_id=sibling, device_id_type=MESH)

    def to_next(t, slot):
        source, target = (vmine.at[0, t], vring.at[t]) if slot == 3 else (mine.at[t, slot, carried, :], ring.at[t, slot])
        return pltpu.make_async_remote_copy(
            src_ref=source, dst_ref=target, send_sem=ring_send.at[t, slot], recv_sem=ring_recv.at[t, slot],
            device_id=after, device_id_type=MESH)

    def across(t, slot):
        return pltpu.make_async_remote_copy(
            src_ref=mine.at[t, slot, foreign, :], dst_ref=crossed.at[t, slot], send_sem=cross_send.at[t, slot],
            recv_sem=cross_recv.at[t, slot], device_id=mirror, device_id_type=MESH)

    def to_mirror(slot):
        source, target = (vmine.at[0, last], vpeer) if slot == 3 else (mine.at[last, slot, carried, :], peer.at[slot, carried, :])
        return pltpu.make_async_remote_copy(
            src_ref=source, dst_ref=target, send_sem=peer_send.at[slot], recv_sem=peer_recv.at[slot],
            device_id=mirror, device_id_type=MESH)

    def begin_own(t, wanted):
        fetch(2 * ring_chip(place - turn * (t + 1), chips) + core, wanted, lambda slot, source: local(t, slot, source).start())

    def begin_sibling(t, wanted):
        fetch(2 * ring_chip(place + turn * (t + 1), chips) + 1 - core, wanted,
              lambda slot, source: to_sibling(t, slot, source).start())

    def begin(t, wanted):
        begin_sibling(t, wanted)
        begin_own(t, wanted)

    def sources(slot):
        return tiles.at[0] if slot == 3 else g_up.at[0, :, :side]

    def pair_up(t, wanted):
        for slot in wanted:
            local(t, slot, sources(slot)).wait()
            to_sibling(t, slot, sources(slot)).wait_recv()
            if slot == 3:
                vmine[0, t] = vmine[0, t] + vmine[1, t]
            else:
                mine[t, slot] = (mine[t, slot].astype(F32) + theirs[t, slot].astype(F32)).astype(BF16)
                across(t, slot).start()

    def add(t, slot, hold, extra):
        mine[t, slot, hold, :] = (mine[t, slot, hold, :].astype(F32) + extra.astype(F32)).astype(BF16)

    def pass_round(t, wanted):
        for slot in wanted:
            if slot < 3:
                across(t, slot).wait_recv()
                add(t, slot, private, crossed[t, slot])

            @pl.when(t > 0)
            def _():
                to_next(t - 1, slot).wait_recv()
                if slot == 3:
                    vmine[0, t] = vmine[0, t] + vring[t - 1]
                else:
                    add(t, slot, carried, ring[t - 1, slot])

            @pl.when(t < last)
            def _():
                to_next(t, slot).start()

            @pl.when(t == last)
            def _():
                to_mirror(slot).start()

    def own_sum(slot):
        to_mirror(slot).wait()
        if slot == 3:
            vec_sum[...] = vmine[0, last] + vpeer[...]
            return
        shared = slice(quarter, 3 * quarter)
        owned[slot, shared, :] = (mine[last, slot, shared, :].astype(F32) + peer[slot, shared, :].astype(F32)).astype(BF16)
        owned[slot, private, :] = mine[last, slot, private, :]
        owned[slot, foreign, :] = peer[slot, foreign, :]

    feed, rest = (1, 2), (3, 0)

    def ahead(t, wanted):
        @pl.when(t + 3 < chips)
        def _():
            begin(t + 3, wanted)

        @pl.when(t == 0)
        def _():
            pair_up(1, wanted)

        @pl.when(t + 2 < chips)
        def _():
            pair_up(t + 2, wanted)

    def rest_step(t):
        pass_round(t, rest)
        ahead(t, rest)


    lane = lax.broadcasted_iota(jnp.int32, (slots, 128), 1)
    seen = lax.broadcasted_iota(jnp.int32, (slots, 128), 0) < length

    def head_lanes(head, value):
        keep = (lane < HEAD_DIM) if head == 0 else (lane >= HEAD_DIM)
        return jnp.where(keep, value, jnp.zeros_like(value))

    def lanes_of(pair, member):
        return pl.ds(pl.multiple_of(member * width + pair * 128, 128), 128)

    def attend_back(pair):
        query, key, value = [qkv[:, lanes_of(pair, member)] for member in range(3)]
        grad = grad_c[:, lanes_of(pair, 0)]
        turned_key = key.T
        found = []
        for head in range(2):
            near_key = head_lanes(head, key * HEAD_DIM ** (-0.5))
            near_value = head_lanes(head, value)
            for block in range(slots // 128):
                rows = slice(128 * block, 128 * (block + 1))
                scores = jnp.where(seen, dg(near_key, query[rows], 1, 1), -1e30)
                weights = jnp.exp(scores - logs[2 * pair + head, :, rows])
                back = dg(near_value, grad[rows], 1, 1)
                scores_back = weights * (back - jnp.sum(back * weights, axis=0, keepdims=True))
                probs[head, :, rows] = weights.astype(BF16)
                dscores[head, :, rows] = scores_back.astype(BF16)
            found.append((
                jnp.dot(turned_key, dscores[head], preferred_element_type=F32),
                jnp.dot(dscores[head], query, preferred_element_type=F32),
                jnp.dot(probs[head], grad, preferred_element_type=F32),
            ))
        top = lax.broadcasted_iota(jnp.int32, (128, slots), 0) < HEAD_DIM
        turned_query = jnp.where(top, found[0][0], found[1][0]) * HEAD_DIM ** (-0.5)
        grad_heads[:, lanes_of(pair, 0)] = turned_query.T.astype(BF16)
        grad_heads[:, lanes_of(pair, 1)] = (jnp.where(lane < HEAD_DIM, found[0][1], found[1][1]) * HEAD_DIM ** (-0.5)).astype(BF16)
        grad_heads[:, lanes_of(pair, 2)] = jnp.where(lane < HEAD_DIM, found[0][2], found[1][2]).astype(BF16)

    def project_back(index):
        lanes = span(index, 256)
        value = jnp.dot(turned_x[...], grad_heads[:, lanes], preferred_element_type=F32)
        g_qkv[:, :, lanes] = value.astype(BF16).reshape(2, side, 256)

    def input_back(index):
        lanes = span(index, 256)
        grad_x[:, lanes] = grad_r[:, lanes] + dg(grad_heads[...], w_qkv[lanes, :], 1, 1)


    def join(pair, carry):
        rows = pl.ds(pl.multiple_of(2 * share * pair, 16), 2 * share)
        for item in range(9):
            two = [parts[2 * pair + index, item].astype(F32) for index in range(2)]
            states[item, rows, :] = jnp.concatenate(two, axis=0).astype(BF16)
        return carry

    def trade(index):
        source = (5 - replica, 3, 8)[index]
        return pltpu.make_async_remote_copy(
            src_ref=states.at[source], dst_ref=states.at[9 + index], send_sem=state_send.at[index],
            recv_sem=state_recv.at[index], device_id=mirror, device_id_type=MESH)

    def update(rotated, left, right, first, second):
        first_new = FIRST_DECAY * first.astype(F32) + (1.0 - FIRST_DECAY) * rotated
        second_new = SECOND_DECAY * second.astype(F32) + (1.0 - SECOND_DECAY) * rotated * rotated
        direction = (
            first_new
            / (1.0 - FIRST_DECAY**ADAM_STEP)
            / (jnp.sqrt(second_new / (1.0 - SECOND_DECAY**ADAM_STEP)) + ADAM_EPSILON)
        )
        back = dg(left, direction.astype(BF16), 1, 0).astype(BF16)
        return dg(back, right, 1, 1)

    def prepare(s):
        for is_right in (False, True):
            @pl.when(replica == int(is_right))
            def _():
                near = 0 if is_right else 1
                g = owned[s]
                outer = dg(g, g, near, near)
                items[(4, 0, 1)[s]] = outer
                mixed = STAT_DECAY * states[s].astype(F32) + (1.0 - STAT_DECAY) * outer
                high, low = halves(mixed)
                mat[s] = dg(high, states[3 + s], 1, 0) + dg(low, states[3 + s], 1, 0)
                if s not in (0, 2 if is_right else 1):
                    return
                other = states[10] if s == 0 else states[9]
                left, right = (other, states[3 + s]) if is_right else (states[3 + s], other)
                rotated = dg(dg(left, g, 0, 0).astype(BF16), right, 1, 0)
                if s > 0:
                    items[2] = rotated
                    items[3] = update(rotated, left, right, states[6], states[7])
                elif is_right:
                    items[5] = update(rotated, left, right, states[8], states[11])
                else:
                    items[5] = rotated

    def rows_of(holder):
        return pl.ds(pl.multiple_of(holder * share, 8), share)

    def outgoing(kind, holder):
        return (out_early, out_last, out_two, out_one)[kind].at[holder]

    def incoming(kind, owner):
        return (early, early_last, late_two, late_one)[kind].at[replica, owner]

    def pack(kind):
        def one(holder, carry):
            rows = rows_of(holder)
            if kind < 2:
                for pair in ((0, 1), (2,))[kind]:
                    two = jnp.concatenate([items[2 * pair, rows, :], items[2 * pair + 1, rows, :]], axis=0)
                    spot = pair if kind == 0 else 0
                    (out_early, out_last)[kind][holder, 2 * share * spot : 2 * share * (spot + 1), :] = two.astype(BF16)
            else:
                columns = ((0, part), (2 * part,))[kind - 2]
                stacked = [mat[s, rows, lo : lo + part] for lo in columns for s in range(3)]
                if kind == 3:
                    stacked.append(jnp.zeros((8, part), F32))
                (out_two, out_one)[kind - 2][holder] = jnp.concatenate(stacked, axis=0).astype(BF16)
            return carry

        lax.fori_loop(0, count, one, 0)

    def note(kind, step):
        target = partner(step)
        return pltpu.make_async_remote_copy(
            src_ref=outgoing(kind, target[0]), dst_ref=incoming(kind, device), send_sem=note_send.at[kind, step],
            recv_sem=note_recv.at[kind, step], device_id=target, device_id_type=MESH)

    def relay(kind, step):
        block = incoming(kind, partner(step)[0])
        return pltpu.make_async_remote_copy(
            src_ref=block, dst_ref=block, send_sem=relay_send.at[kind, step], recv_sem=relay_recv.at[kind, step],
            device_id=mirror, device_id_type=MESH)

    def keep(kind):
        return pltpu.make_async_copy(outgoing(kind, device), incoming(kind, device), keep_sem.at[kind])

    def launch(kind):
        pack(kind)
        keep(kind).start()

        def one(step, carry):
            note(kind, step).start()
            return carry

        lax.fori_loop(1, chips, one, 0)
        near.extend((kind, step) for step in range(chips))
        far.extend((kind, step) for step in range(chips, count))

    def hand_on(kind, step):
        note(kind, step).wait_recv()
        relay(kind, step).start()

    near, far, flying = [], [], []

    def hand_on_near(number):
        for kind, step in near[:number]:
            if step == 0:
                keep(kind).wait()
                relay(kind, 0).start()
            else:
                hand_on(kind, step)
        del near[:number]

    def pump(number):
        for kind, step in far[:number]:
            if len(flying) >= WINDOW:
                hand_on(*flying.pop(0))
            note(kind, step).start()
            flying.append((kind, step))
        del far[:number]


    def first_own(index, carry):
        begin_own(index, feed)
        return carry

    def first_sibling(index, carry):
        begin_sibling(index, feed)
        return carry

    lax.fori_loop(0, 3, first_own, 0)
    for load in loads[:2]:
        load.start()
    lax.fori_loop(0, count // 2, join, 0)
    pl.semaphore_wait(barrier, count)
    lax.fori_loop(0, 3, first_sibling, 0)
    pair_up(0, feed)
    for load in loads[2:]:
        load.start()
    grad_vec[...] = vec_part[...]

    def main(t, carry):
        pass_round(t, feed)

        @pl.when(t > 2)
        def _():
            rest_step(t - 3)

        ahead(t, feed)

        @pl.when(t == 0)
        def _():
            for load in loads[:2]:
                load.wait()

        @pl.when(t < 2)
        def _():
            def one(third, carry):
                attend_back(3 * t + third)
                return carry

            lax.fori_loop(0, 3, one, 0)

        @pl.when(t == TRADE)
        def _():
            trade(0).start()

        @pl.when(t == 2)
        def _():
            loads[2].wait()
            grad_vec[0:1, :] = jnp.sum(grad_heads[:, :width].astype(F32), axis=0, keepdims=True)
            grad_vec[1:2, :] = jnp.sum(grad_heads[:, 2 * width :].astype(F32), axis=0, keepdims=True)
            looped(3 * width // 256, project_back)
            vector_tiles_of(grad_vec, vec_up_part, tiles)

            def start_rest(index, carry):
                begin(index, rest)
                return carry

            lax.fori_loop(0, 3, start_rest, 0)
            pair_up(0, rest)

        return carry

    lax.fori_loop(0, chips, main, 0)
    trade(0).wait()
    own_sum(1)
    prepare(1)
    rest_step(jnp.int32(chips - 3))
    own_sum(2)
    trade(1).start()
    trade(2).start()
    prepare(2)
    launch(0)
    pump(WINDOW)
    rest_step(jnp.int32(chips - 2))
    hand_on_near(4)
    pump(1)
    for load in loads[3:]:
        load.wait()
    looped(width // 256, input_back)
    pump(1)
    rest_step(jnp.int32(chips - 1))
    hand_on_near(4)
    pump(1)
    own_sum(0)
    trade(1).wait()
    trade(2).wait()
    prepare(0)
    launch(1)

    def between(moment):
        if far and moment % (5, 3, 3, 2)[far[0][0]] == 0:
            pump(1)
        elif near and moment % 2 == 1:
            hand_on_near(1)

    row_index = lax.broadcasted_iota(jnp.int32, (part, part), 0)
    column_index = lax.broadcasted_iota(jnp.int32, (part, part), 1)
    eye = (row_index == column_index).astype(F32)
    for o in range(panels):
        lo = o * part
        for s in range(3):
            block = mat[s, :, lo : lo + part]
            aug[s, :, :part] = mm3(block, block, 0, 0)
            aug[s, :, part:] = eye
        factor_panels(aug, 3, part, lambda p: between(16 * o + p))
        for s in range(3):
            mat[s, :, lo : lo + part] = mm3(mat[s, :, lo : lo + part], aug[s, :, part:], 1, 1)
        if o > 0:
            launch(1 + o)
        if o + 1 < panels:
            for s in range(3):
                q, remaining = mat[s, :, lo : lo + part], mat[s, :, lo + part :]
                mat[s, :, lo + part :] = remaining - mm3(q, mm3(q, remaining, 0, 0), 1, 0)
    while far or near:
        pump(2)
        hand_on_near(2)
    for kind, step in flying:
        hand_on(kind, step)
    own_sum(3)

    def finish(step, carry):
        for kind in range(4):
            relay(kind, step).wait()

            @pl.when(step > 0)
            def _():
                note(kind, step).wait_send()

        @pl.when(step < chips)
        def _():
            for slot in range(4):
                to_sibling(step, slot, sources(slot)).wait_send()
                if slot < 3:
                    across(step, slot).wait_send()

                @pl.when(step < last)
                def _():
                    to_next(step, slot).wait_send()
        return carry

    lax.fori_loop(0, count, finish, 0)


def conclude(length, logs, vec_part, vec_up_part, parts, qkv, grad_c, turned_x, grad_r, attn, g_out, g_up, g_down, share, chips):
    side = g_up.shape[1]
    width, count = 2 * side, 2 * chips
    slots = qkv.shape[0]
    tall = -(-3 * share // 16) * 16
    anywhere = pl.BlockSpec(memory_space=pl.ANY)
    whole = pl.BlockSpec(memory_space=pltpu.VMEM)
    vmem = pltpu.VMEM
    dma = pltpu.SemaphoreType.DMA
    return pl.pallas_call(
        functools.partial(conclude_kernel, chips, share),
        out_shape=[
            jax.ShapeDtypeStruct((slots, width), F32),
            jax.ShapeDtypeStruct((16, 128), F32),
            jax.ShapeDtypeStruct((2, count, 4 * share, side), BF16),
            jax.ShapeDtypeStruct((2, count, 2 * share, side), BF16),
            jax.ShapeDtypeStruct((2, count, 6 * share, 128), BF16),
            jax.ShapeDtypeStruct((2, count, tall, 128), BF16),
        ],
        in_specs=[pl.BlockSpec(memory_space=pltpu.SMEM)] + [whole] * 4 + [anywhere] * 8,
        out_specs=[whole] * 2 + [anywhere] * 4,
        scratch_shapes=[
            vmem((slots, 3 * width), BF16), vmem((slots, width), BF16), vmem((width, slots), BF16), vmem((slots, width), F32),
            vmem((width, 3 * width), BF16), vmem((slots, 3 * width), BF16), vmem((2, slots, slots), BF16),
            vmem((2, slots, slots), BF16), vmem((2, side, 3 * width), BF16), vmem((16, width), F32), vmem((count, 16, 128), F32),
            vmem((chips, 3, side, side), BF16), vmem((chips, 3, side, side), BF16),
            vmem((chips - 1, 3, 3 * side // 4, side), BF16), vmem((chips, 3, side // 4, side), BF16), vmem((3, side, side), BF16),
            vmem((2, chips, 16, 128), F32), vmem((chips - 1, 16, 128), F32), vmem((16, 128), F32), vmem((3, side, side), BF16),
            vmem((12, side, side), BF16), vmem((6, side, side), F32), vmem((3, side, side), F32), vmem((3, 128, 256), F32),
            vmem((count, 4 * share, side), BF16), vmem((count, 2 * share, side), BF16), vmem((count, 6 * share, 128), BF16),
            vmem((count, tall, 128), BF16),
            dma((5,)), dma((chips, 4)), dma((chips, 4)), dma((chips, 4)), dma((chips - 1, 4)), dma((chips - 1, 4)),
            dma((chips, 3)), dma((chips, 3)), dma((4,)), dma((4,)), dma((3,)), dma((3,)),
            dma((4, count)), dma((4, count)), dma((4, count)), dma((4, count)), dma((4,)),
        ],
        compiler_params=pltpu.CompilerParams(collective_id=2, has_side_effects=True, vmem_limit_bytes=62 * 2**20),
        name="conclude",
    )(length, logs, vec_part, vec_up_part, parts, qkv, grad_c, turned_x, grad_r, attn, g_out, g_up, g_down)


def plain_gather(matrices, vectors):
    side = matrices.shape[-1]
    blocks = lax.all_gather(matrices.astype(BF16), "fsdp", axis=1, tiled=True)
    attn = jnp.concatenate([assemble(blocks[4 * part : 4 * part + 4], 2, 2) for part in range(4)], axis=1)
    up = assemble(blocks[16:32], 2, 8)
    down = assemble(blocks[32:], 8, 2)
    rows = lax.all_gather(vectors.astype(BF16), "fsdp", axis=0, tiled=True)
    return attn, up, down, rows.astype(F32).reshape(-1, 2 * side)


def plain_reduce(grad_qkv, grad_out, grad_up, grad_down, vector_grad, capacity):
    shard_count = lax.axis_size("fsdp")
    width = grad_up.shape[0]
    side = width // 2
    blocks = jnp.concatenate(
        [split_blocks(grad_qkv[:, part * width : (part + 1) * width], 2, 2, side) for part in range(3)]
        + [split_blocks(grad_out, 2, 2, side), split_blocks(grad_up, 2, 8, side), split_blocks(grad_down, 8, 2, side)],
        axis=0,
    )
    owned = lax.psum_scatter(
        to_owners(blocks, capacity, shard_count), "fsdp", scatter_dimension=1, tiled=True
    )
    owned = lax.psum(owned, "dp")[:, 0]
    share = lax.psum_scatter(vector_grad, "fsdp", scatter_dimension=0, tiled=True)
    return owned, lax.psum(share, "dp")


def to_owners(blocks, capacity, shard_count):
    spare = capacity * shard_count - blocks.shape[0]
    blocks = jnp.pad(blocks, ((0, spare),) + ((0, 0),) * (blocks.ndim - 1))
    return blocks.reshape((capacity, shard_count) + blocks.shape[1:])


def plain_layer(tokens, cotangent, lengths, attn, up, down, vector_rows):
    sequences, slots, model_width = tokens.shape
    rows_total = sequences * slots
    unit_ratio = FF // model_width

    def shaped(array):
        return array.reshape(sequences, slots, array.shape[-1])

    weight_qkv, weight_out = attn[:, : 3 * model_width], attn[:, 3 * model_width :]
    inputs = tokens.reshape(rows_total, model_width)
    joined = jnp.dot(inputs, weight_qkv, preferred_element_type=F32)
    query_rows = (joined[:, :model_width] + vector_rows[0]).astype(BF16)
    key_rows = joined[:, model_width : 2 * model_width].astype(BF16)
    value_rows = (joined[:, 2 * model_width :] + vector_rows[1]).astype(BF16)
    context, logsum = lax.map(
        attend, (shaped(query_rows), shaped(key_rows), shaped(value_rows), lengths)
    )
    context = context.reshape(rows_total, model_width)
    attended = jnp.dot(context, weight_out, preferred_element_type=F32) + vector_rows[2]
    normed, pull_one = jax.vjp(
        layer_norm, inputs.astype(F32) + attended, vector_rows[3], vector_rows[4]
    )
    normed_low = normed.astype(BF16)
    hidden = jnp.dot(normed_low, up, preferred_element_type=F32) + vector_rows[
        5 : 5 + unit_ratio
    ].reshape(FF)
    active, pull_gelu = jax.vjp(exact_gelu, hidden)
    active_low = active.astype(BF16)
    result = jnp.dot(active_low, down, preferred_element_type=F32) + vector_rows[5 + unit_ratio]
    output, pull_two = jax.vjp(
        layer_norm, normed + result, vector_rows[6 + unit_ratio], vector_rows[7 + unit_ratio]
    )
    block_out = output.reshape(sequences, slots, model_width).astype(BF16)
    visible = (lax.iota(jnp.int32, slots)[None, :] < lengths[:, None]).astype(F32)
    grad_output = (cotangent.astype(F32) * visible[:, :, None]).reshape(rows_total, model_width)
    grad_second, grad_gain_two, grad_shift_two = pull_two(grad_output)
    second_low = grad_second.astype(BF16)
    grad_down = jnp.einsum("tf,td->fd", active_low, second_low, preferred_element_type=F32)
    grad_active = jnp.einsum("td,fd->tf", second_low, down, preferred_element_type=F32)
    (grad_hidden,) = pull_gelu(grad_active)
    hidden_low = grad_hidden.astype(BF16)
    grad_up = jnp.einsum("td,tf->df", normed_low, hidden_low, preferred_element_type=F32)
    grad_normed = grad_second + jnp.einsum("tf,df->td", hidden_low, up, preferred_element_type=F32)
    grad_mixed, grad_gain_one, grad_shift_one = pull_one(grad_normed)
    mixed_low = grad_mixed.astype(BF16)
    grad_out_weight = jnp.einsum("td,te->de", context, mixed_low, preferred_element_type=F32)
    grad_context = jnp.einsum(
        "te,de->td", mixed_low, weight_out, preferred_element_type=F32
    ).astype(BF16)
    grad_query, grad_keys, grad_values = lax.map(
        attend_back,
        (
            shaped(query_rows),
            shaped(key_rows),
            shaped(value_rows),
            logsum,
            shaped(grad_context),
            lengths,
        ),
    )
    grad_joined = jnp.concatenate(
        [
            grad_query.reshape(rows_total, model_width),
            grad_keys.reshape(rows_total, model_width),
            grad_values.reshape(rows_total, model_width),
        ],
        axis=1,
    )
    grad_qkv = jnp.einsum("td,te->de", inputs, grad_joined, preferred_element_type=F32)
    input_grad = grad_mixed + jnp.einsum(
        "te,de->td", grad_joined, weight_qkv, preferred_element_type=F32
    )
    vector_grad = jnp.concatenate(
        [
            jnp.sum(grad_joined[:, :model_width], axis=0, dtype=F32)[None],
            jnp.sum(grad_joined[:, 2 * model_width :], axis=0, dtype=F32)[None],
            jnp.sum(grad_mixed, axis=0)[None],
            grad_gain_one[None],
            grad_shift_one[None],
            jnp.sum(grad_hidden, axis=0).reshape(unit_ratio, model_width),
            jnp.sum(grad_second, axis=0)[None],
            grad_gain_two[None],
            grad_shift_two[None],
        ],
        axis=0,
    ).reshape(-1)
    weight_grads = [part.astype(BF16) for part in (grad_qkv, grad_out_weight, grad_up, grad_down)]
    return block_out, input_grad.reshape(tokens.shape), vector_grad, weight_grads


def shards(
    tokens,
    cotangent,
    lengths,
    matrices,
    first_moment,
    second_moment,
    left_stat,
    right_stat,
    left_basis,
    right_basis,
    vectors,
    vector_first,
    vector_second,
):
    shard_count = lax.axis_size("fsdp")
    replicas = lax.axis_size("dp")
    sequences, slots, model_width = tokens.shape
    block_total, share_rows, block_side = matrices.shape
    capacity = -(-block_total // shard_count)
    ringed = replicas == 2 and sequences == 1 and vectors.shape[0] == 576 and capacity * shard_count == block_total == 48 and share_rows % 8 == 0 and capacity == 3

    right_side = lax.axis_index("dp") % 2 == 1
    if ringed:
        vector_tile = jnp.pad(vectors.reshape(9, 64), ((0, 7), (0, 64)))
        attn, up, down, tiles, states = gather_weights(
            matrices,
            vector_tile,
            (left_stat, right_stat, left_basis, right_basis, first_moment, second_moment),
            shard_count // 2,
        )
        states = lax.all_to_all(states, "fsdp", split_axis=0, concat_axis=0, tiled=True)
        weight_attn = attn.reshape(model_width, 4 * model_width)
        block_out, logs, vec_part, vec_up_part, qkv, grad_c, turned_x, grad_r, *weight_grads = layer(
            lengths,
            tokens[0],
            cotangent[0],
            tiles,
            weight_attn,
            up.reshape(model_width, FF),
            down.reshape(FF, model_width),
        )
        slabs = [part.reshape(-1, block_side, part.shape[1]) for part in weight_grads]
        input_grad, vector_sum, *notes = conclude(
            lengths, logs, vec_part, vec_up_part, states, qkv, grad_c, turned_x, grad_r, weight_attn, *slabs,
            share_rows, shard_count // 2
        )
        block_out, input_grad = block_out[None], input_grad[None]
        vector_sum = vector_sum[:9, :64].reshape(-1)
        local = settle(*notes, matrices, first_moment, second_moment, left_stat, right_stat)
    else:
        chosen = [
            jnp.where(right_side, right_stat, left_stat),
            jnp.where(right_side, right_basis, left_basis),
            jnp.where(right_side, left_basis, right_basis),
            first_moment,
            second_moment,
        ]
        states = jnp.stack([to_owners(part.astype(BF16), capacity, shard_count) for part in chosen])
        attn, up, down, vector_rows = plain_gather(matrices, vectors)
        states = lax.all_to_all(states, "fsdp", split_axis=2, concat_axis=3, tiled=True)[:, :, 0]
        block_out, input_grad, vector_grad, weight_grads = plain_layer(
            tokens, cotangent, lengths, attn, up, down, vector_rows
        )
        owned, vector_sum = plain_reduce(*weight_grads, vector_grad, capacity)
        filler = (lax.iota(jnp.int32, capacity) * shard_count + lax.axis_index("fsdp")) >= block_total
        stat = jnp.where(
            filler[:, None, None], jnp.eye(block_side, dtype=jnp.bfloat16), states[0]
        )
        basis = jnp.where(
            filler[:, None, None], jnp.eye(block_side, dtype=jnp.bfloat16), states[1]
        )
        outer, new_basis, turned, update = soap_blocks(
            owned, stat, basis, states[2], states[3], states[4]
        )
        returned = lax.all_to_all(
            jnp.stack([outer, new_basis, turned, update])[:, :, None],
            "fsdp",
            split_axis=3,
            concat_axis=2,
            tiled=True,
        ).reshape(4, capacity * shard_count, -1, block_side)[:, :block_total]
        mirror = lax.ppermute(
            returned[:2], "dp", [(place, place ^ 1) for place in range(lax.axis_size("dp"))]
        )
        returned = returned.astype(jnp.float32)
        mirror = mirror.astype(jnp.float32)
        left_pair = jnp.where(right_side, mirror, returned[:2])
        right_pair = jnp.where(right_side, returned[:2], mirror)
        turned = returned[2]
        local = [
            returned[3],
            FIRST_DECAY * first_moment + (1.0 - FIRST_DECAY) * turned,
            SECOND_DECAY * second_moment + (1.0 - SECOND_DECAY) * turned * turned,
            STAT_DECAY * left_stat + (1.0 - STAT_DECAY) * left_pair[0],
            STAT_DECAY * right_stat + (1.0 - STAT_DECAY) * right_pair[0],
            left_pair[1],
            right_pair[1],
        ]
        local = [matrices - MATRIX_RATE * (local[0] + WEIGHT_DECAY * matrices)] + local
        local[1] = local[0].astype(BF16)
    vfirst_new = FIRST_DECAY * vector_first + (1.0 - FIRST_DECAY) * vector_sum
    vsecond_new = SECOND_DECAY * vector_second + (1.0 - SECOND_DECAY) * vector_sum * vector_sum
    vector_new = vectors - VECTOR_RATE * (vfirst_new / (1.0 - FIRST_DECAY**ADAM_STEP)) / (
        jnp.sqrt(vsecond_new / (1.0 - SECOND_DECAY**ADAM_STEP)) + ADAM_EPSILON
    )
    return (
        block_out,
        input_grad,
        *local,
        vfirst_new,
        vsecond_new,
        vector_new,
    )


def solution(mesh):
    return jax.shard_map(
        shards,
        mesh=mesh,
        in_specs=(
            P(("fsdp", "dp"), None, None),
            P(("fsdp", "dp"), None, None),
            P(("fsdp", "dp")),
            P(None, "fsdp", None),
            P(None, "fsdp", None),
            P(None, "fsdp", None),
            P(None, "fsdp", None),
            P(None, "fsdp", None),
            P(None, "fsdp", None),
            P(None, "fsdp", None),
            P("fsdp"),
            P("fsdp"),
            P("fsdp"),
        ),
        out_specs=(
            P(("fsdp", "dp"), None, None),
            P(("fsdp", "dp"), None, None),
            P(None, "fsdp", None),
            P(None, "fsdp", None),
            P(None, "fsdp", None),
            P(None, "fsdp", None),
            P(None, "fsdp", None),
            P(None, "fsdp", None),
            P(None, "fsdp", None),
            P(None, "fsdp", None),
            P("fsdp"),
            P("fsdp"),
            P("fsdp"),
        ),
        check_vma=False,
    )
```
